256 devices in a mesh: gy: 64 (over x, y_lo, z), gx: 4 (over y_hi, core).
Axes of the slice: x: 4, y: 4 (y_hi: 2, y_lo: 2; y = y_hi * 2 + y_lo), z: 8, core: 2. Of those that a mesh axis runs over, the one named last changes fastest.
Arguments:
- cell_index: int32 [3, 98304], P(None, ('gy', 'gx')), may hold values from 0 to 383, as said below
- offsets: float32 [3, 98304], P(None, ('gy', 'gx')), may hold values from 0 to 1
- charges: float32 [98304], P(('gy', 'gx')), may hold values from -6 to 6
- dipoles: float32 [3, 98304], P(None, ('gy', 'gx')), may hold values from -6 to 6
- block_count: int32 [1536], P(('gy', 'gx')), may hold values from 32 to 64, as said below
- shear_cells: int32 [1], replicated, may hold values from 1 to 383
Outputs:
- charge_grad: float32 [98304], P(('gy', 'gx'))
- dipole_grad: float32 [3, 98304], P(None, ('gy', 'gx'))
- position_grad: float32 [3, 98304], P(None, ('gy', 'gx'))
- energy: float32 [1], replicated
The draws below stay inside these ranges and needn't reach their ends.
Inputs may be any that keep to these rules, and one draw needn't show every extreme that they name: `cell_index`: slot s lies in block k = s // 64; block k lies on the device d = k // 6 at gy index d // 4 and gx index d % 4; its atoms have x cells from (d % 4) * 96 + (k % 6) * 16 up to 15 beyond, y cells from (d // 4) * 6 up to 5 beyond, and z cells below 360. The first slot of each block sits at the largest x, y and z cells of that range. Row 0 holds x, row 1 y, row 2 z. The live atoms of a block are its first block_count slots; every device holds a full block.
All inputs are finite; a program needn't handle non-finite values.
Results may differ from the reference program's by a relative error of at most 0.0003.
Values sent between devices are 32-bit elements; how exact they have to be, the bound alone decides.
No kernel may reach another device: no remote copies, remote signals or barrier semaphores. Data moves between devices by JAX's collectives and lax.ppermute only.
A program may use at most 128 MiB of HBM per device.

```python
import math
import jax
import jax.numpy as jnp
from jax import lax

NX = 384
NZ = 360
CY = 6
BX = 16
ATOM_BLK = 64
PENCILS = 4
CX = 96
NY = 384
NB = 6
ATOM_DEV = 384
ATOMS = 98304
BLOCKS = 1536


def draw_cell_index(key, part):
    key = jax.random.fold_in(key, 11)
    subkeys = jax.random.split(key, 3)
    slots = jnp.arange(ATOMS, dtype=jnp.int32)
    device = slots // ATOM_DEV
    row_y = device // PENCILS
    col_x = device % PENCILS
    block_id = slots % ATOM_DEV // ATOM_BLK
    corner = slots % ATOM_BLK == 0
    pick_x = jnp.where(corner, BX - 1, jax.random.randint(subkeys[0], (ATOMS,), 0, BX, dtype=jnp.int32))
    pick_y = jnp.where(corner, CY - 1, jax.random.randint(subkeys[1], (ATOMS,), 0, CY, dtype=jnp.int32))
    pick_z = jnp.where(corner, NZ - 1, jax.random.randint(subkeys[2], (ATOMS,), 0, NZ, dtype=jnp.int32))
    cell_x = col_x * CX + block_id * BX + pick_x
    cell_y = row_y * CY + pick_y
    cell_z = pick_z
    return jnp.stack([cell_x, cell_y, cell_z])


def draw_block_count(key, part):
    key = jax.random.fold_in(key, 23)
    key_low, key_full = jax.random.split(key)
    counts = jax.random.randint(key_low, (BLOCKS,), ATOM_BLK // 2, ATOM_BLK + 1, dtype=jnp.int32)
    full_block = jax.random.randint(key_full, (BLOCKS // NB,), 0, NB, dtype=jnp.int32)
    blocks_all = jnp.arange(BLOCKS, dtype=jnp.int32)
    is_full = blocks_all % NB == full_block[blocks_all // NB]
    return jnp.where(is_full, ATOM_BLK, counts)


def level_of(stream_key, dims, cuts, low, top_value):
    factor_of, own = 1.0, jax.random.fold_in(stream_key, 6)
    for axis_at, shards_of in cuts:
        heights = jnp.exp(jax.random.uniform(jax.random.fold_in(own, axis_at), (shards_of,), jnp.float32, low / len(cuts), top_value / len(cuts)))
        factor_of = factor_of * jnp.repeat(heights, dims[axis_at] // shards_of).reshape([-1 if axis == axis_at else 1 for axis in range(len(dims))])
    return factor_of


def bell_draw(stream_key, dims, spread, most, pieces=(), kind=jnp.bfloat16):
    drawn = jax.random.normal(stream_key, dims, jnp.float32) * spread
    if len(pieces) > 0:
        drawn = level_of(stream_key, dims, pieces, -0.22, 0.18) * drawn
    return jnp.clip(drawn, min=-most, max=most).astype(kind)


def setup_inputs(seed: int = 0) -> dict:
    seeds = jax.random.split(jax.random.key(seed), 7)
    cell_index = draw_cell_index(jax.random.fold_in(seeds[6], 71), 0)
    offsets = jnp.clip(1.0 * jax.random.uniform(seeds[1], (3, ATOMS), jnp.float32) ** level_of(seeds[1], (3, ATOMS), ((1, 256),), -0.2, 0.2), 0.0, 1.0)
    charges = bell_draw(seeds[2], (ATOMS,), 1.0, 6.0, ((0, 256),), jnp.float32)
    dipoles = bell_draw(seeds[3], (3, ATOMS), 1.0, 6.0, ((1, 256),), jnp.float32)
    block_count = draw_block_count(jax.random.fold_in(seeds[6], 71), 0)
    shear_cells = jax.random.randint(seeds[5], (1,), 1, NX).astype(jnp.int32)
    return {"cell_index": cell_index, "offsets": offsets, "charges": charges, "dipoles": dipoles, "block_count": block_count, "shear_cells": shear_cells}


screening = 0.9
combos = ((0, 0, 0), (1, 0, 0), (0, 1, 0), (0, 0, 1), (2, 0, 0), (0, 2, 0), (0, 0, 2), (1, 1, 0), (1, 0, 1), (0, 1, 1))


def spline_tables(fraction):
    levels = {2: [1.0 - fraction, fraction]}
    current = levels[2]
    for n in range(3, 7):
        inverse_n = 1.0 / (n - 1)
        updated = [None] * n
        updated[n - 1] = inverse_n * fraction * current[n - 2]
        for j in range(1, n - 1):
            updated[n - 1 - j] = inverse_n * ((fraction + j) * current[n - 2 - j] + (n - j - fraction) * current[n - 1 - j])
        updated[0] = inverse_n * (1.0 - fraction) * current[0]
        current = updated
        levels[n] = current
    zero_row = jnp.zeros_like(fraction)

    def entry_at(values_list, k):
        return values_list[k] if 0 <= k < len(values_list) else zero_row

    values_w = jnp.stack(levels[6])
    first_w = jnp.stack([entry_at(levels[5], t - 1) - entry_at(levels[5], t) for t in range(6)])
    second_w = jnp.stack([entry_at(levels[4], t - 2) - 2.0 * entry_at(levels[4], t - 1) + entry_at(levels[4], t) for t in range(6)])
    return jnp.stack([values_w, first_w, second_w])


def spline_modulus(angles):
    return (66.0 + 52.0 * jnp.cos(angles) + 2.0 * jnp.cos(2.0 * angles)) / 120.0


def green_values(index_x, index_y, index_z, shear_step, size_x, size_y, size_z):
    fold_x = (index_x + size_x // 2) % size_x - size_x // 2
    fold_y = (index_y + size_y // 2) % size_y - size_y // 2
    fold_z = (index_z + size_z // 2) % size_z - size_z // 2
    float_x = fold_x.astype(jnp.float32)
    float_z = fold_z.astype(jnp.float32)
    wave_y = fold_y.astype(jnp.float32) + float_x * shear_step.astype(jnp.float32) / size_x
    square_norm = (float_x / size_x) ** 2 + (wave_y / size_y) ** 2 + (float_z / size_z) ** 2
    is_zero = (fold_x == 0) & (fold_y == 0) & (fold_z == 0)
    at_edge = (fold_x == -(size_x // 2)) | (fold_y == -(size_y // 2)) | (fold_z == -(size_z // 2))
    safe_norm = jnp.where(is_zero, 1.0, square_norm)
    moduli = spline_modulus(2.0 * math.pi * float_x / size_x) * spline_modulus(2.0 * math.pi * wave_y / size_y) * spline_modulus(2.0 * math.pi * float_z / size_z)
    kernel = jnp.exp(-((math.pi / screening) ** 2) * safe_norm) / (math.pi * safe_norm * moduli * moduli)
    return jnp.where(is_zero | at_edge, 0.0, kernel)


def reference(cell_index, offsets, charges, dipoles, block_count, shear_cells):
    shear_step = shear_cells[0]
    slots = jnp.arange(ATOMS, dtype=jnp.int32)
    live = (slots % ATOM_BLK < jnp.repeat(block_count, ATOM_BLK, total_repeat_length=ATOMS)).astype(jnp.float32)
    charge_live = charges * live
    dipole_live = dipoles * live[None, :]
    weights = jnp.stack([spline_tables(offsets[a]) for a in range(3)])

    def image_cells(offset_id):
        step_x = offset_id // 36
        step_y = (offset_id // 6) % 6
        step_z = offset_id % 6
        raw_y = cell_index[1] + step_y
        wrapped = raw_y >= NY
        cell_y = jnp.where(wrapped, raw_y - NY, raw_y)
        cell_x = (cell_index[0] + step_x + jnp.where(wrapped, shear_step, 0)) % NX
        cell_z = (cell_index[2] + step_z) % NZ
        return cell_x, cell_y, cell_z, weights[0][:, step_x], weights[1][:, step_y], weights[2][:, step_z]

    def spread_step(grid_now, offset_id):
        cell_x, cell_y, cell_z, weight_x, weight_y, weight_z = image_cells(offset_id)
        amount = (charge_live * weight_x[0] * weight_y[0] * weight_z[0]
                  + dipole_live[0] * weight_x[1] * weight_y[0] * weight_z[0]
                  + dipole_live[1] * weight_x[0] * weight_y[1] * weight_z[0]
                  + dipole_live[2] * weight_x[0] * weight_y[0] * weight_z[1])
        return grid_now.at[cell_x, cell_y, cell_z].add(amount), None

    offset_ids = jnp.arange(216, dtype=jnp.int32)
    spread_grid, _ = lax.scan(spread_step, jnp.zeros((NX, NY, NZ), jnp.float32), offset_ids)

    index_x = jnp.arange(NX, dtype=jnp.int32)
    index_y = jnp.arange(NY, dtype=jnp.int32)
    index_z = jnp.arange(NZ, dtype=jnp.int32)
    fold_x = (index_x + NX // 2) % NX - NX // 2
    tick_count = (fold_x[:, None] * shear_step * index_y[None, :]) % (NX * NY)
    angles = (2.0 * math.pi / (NX * NY)) * tick_count.astype(jnp.float32)
    phases = lax.complex(jnp.cos(angles), -jnp.sin(angles))
    spectrum = jnp.fft.fft(jnp.fft.fft(spread_grid, axis=2), axis=0)
    spectrum = jnp.fft.fft(spectrum * phases[:, :, None], axis=1)
    green_k = green_values(index_x[:, None, None], index_y[None, :, None], index_z[None, None, :], shear_step, NX, NY, NZ)
    energy = 0.5 / (NX * NY * NZ) * jnp.sum(green_k * (jnp.real(spectrum) ** 2 + jnp.imag(spectrum) ** 2))
    filtered = jnp.fft.ifft(green_k * spectrum, axis=1) * jnp.conj(phases)[:, :, None]
    potential = jnp.real(jnp.fft.ifft(jnp.fft.ifft(filtered, axis=0), axis=2))

    def read_step(sampled, offset_id):
        cell_x, cell_y, cell_z, weight_x, weight_y, weight_z = image_cells(offset_id)
        sample = potential[cell_x, cell_y, cell_z]
        products = jnp.stack([weight_x[p] * weight_y[r] * weight_z[s] for p, r, s in combos])
        return sampled + products * sample[None, :], None

    sampled, _ = lax.scan(read_step, jnp.zeros((10, ATOMS), jnp.float32), offset_ids)
    charge_grad = live * sampled[0]
    dipole_grad = live[None, :] * sampled[1:4]
    force_x = charge_live * sampled[1] + dipole_live[0] * sampled[4] + dipole_live[1] * sampled[7] + dipole_live[2] * sampled[8]
    force_y = charge_live * sampled[2] + dipole_live[0] * sampled[7] + dipole_live[1] * sampled[5] + dipole_live[2] * sampled[9]
    force_z = charge_live * sampled[3] + dipole_live[0] * sampled[8] + dipole_live[1] * sampled[9] + dipole_live[2] * sampled[6]
    position_grad = live[None, :] * jnp.stack([force_x, force_y, force_z])
    return charge_grad, dipole_grad, position_grad, jnp.reshape(energy, (1,))
```

```python
import math

import jax
import jax.numpy as jnp
import ml_dtypes
import numpy as np
from jax import lax
from jax.experimental import pallas as pl
from jax.experimental.pallas import tpu as pltpu
from jax.sharding import PartitionSpec as P

NX = 384
NY = 384
NZ = 360
CY = 6
CX = 96
PENCILS = 4
SLABS = 64
PART_X = 6
PART_Z = 45
ATOM_BLK = 64
ATOM_DEV = 384
PAIRS = 3
WINDOW = 40
ROWS = 11
HALF = 64
LANES = 128
PADDED_Z = 48
screening = 0.9
f32 = jnp.float32
bf16 = jnp.bfloat16


def split_table(table):
    high = table.astype(ml_dtypes.bfloat16)
    low = (table - high.astype(np.float64)).astype(ml_dtypes.bfloat16)
    return high, low


def wave_tables():
    natural = np.arange(NX)
    angle_x = 2.0 * np.pi / NX * (natural[:, None] * natural[None, :] % NX)
    table_x = np.concatenate([np.cos(angle_x), np.sin(angle_x)], axis=1)
    place_y = np.arange(NY) % SLABS * CY + np.arange(NY) // SLABS
    angle_y = 2.0 * np.pi / NY * (natural[:, None] * place_y[None, :] % NY)
    forward_y = np.concatenate([np.cos(angle_y), np.sin(angle_y)], axis=1)
    inverse_y = np.concatenate([np.cos(angle_y.T), np.sin(angle_y.T)], axis=1)
    return split_table(table_x), split_table(forward_y), split_table(inverse_y)


def spline_rows(fraction):
    levels = {2: [1.0 - fraction, fraction]}
    current = levels[2]
    for n in range(3, 7):
        inverse_n = 1.0 / (n - 1)
        updated = [None] * n
        updated[n - 1] = inverse_n * fraction * current[n - 2]
        for j in range(1, n - 1):
            updated[n - 1 - j] = inverse_n * (
                (fraction + j) * current[n - 2 - j] + (n - j - fraction) * current[n - 1 - j]
            )
        updated[0] = inverse_n * (1.0 - fraction) * current[0]
        current = updated
        levels[n] = current
    zero_row = jnp.zeros_like(fraction)

    def entry_at(values_list, k):
        return values_list[k] if 0 <= k < len(values_list) else zero_row

    first = [entry_at(levels[5], t - 1) - entry_at(levels[5], t) for t in range(6)]
    second = [
        entry_at(levels[4], t - 2) - 2.0 * entry_at(levels[4], t - 1) + entry_at(levels[4], t)
        for t in range(6)
    ]
    return levels[6], first, second


def dense_rows(tables, cell, length):
    away = lax.broadcasted_iota(jnp.int32, (length, cell.shape[1]), 0).astype(f32) - cell
    summed = [jnp.zeros(away.shape, f32) for _ in tables]
    for t in range(6):
        here = away == float(t)
        summed = [jnp.where(here, table[t], so_far) for table, so_far in zip(tables, summed)]
    return summed


def unit_phase(turns):
    turns = turns - jnp.floor(turns + 0.5)
    quarter = jnp.floor(4.0 * turns + 0.5)
    rest = turns - 0.25 * quarter
    theta = (2.0 * math.pi) * rest
    square = theta * theta
    sine = theta * (
        1.0
        + square
        * (-1.0 / 6 + square * (1.0 / 120 + square * (-1.0 / 5040 + square * (1.0 / 362880))))
    )
    cosine = 1.0 + square * (
        -0.5
        + square
        * (1.0 / 24 + square * (-1.0 / 720 + square * (1.0 / 40320 - square * (1.0 / 3628800))))
    )
    odd = jnp.abs(quarter) == 1.0
    cos_out = jnp.where(odd, sine, cosine)
    sin_out = jnp.where(odd, cosine, sine)
    cos_out = jnp.where((quarter == 1.0) | (jnp.abs(quarter) == 2.0), -cos_out, cos_out)
    sin_out = jnp.where((quarter == -1.0) | (jnp.abs(quarter) == 2.0), -sin_out, sin_out)
    return cos_out, sin_out


def halves(value):
    high = value.astype(bf16)
    return high, (value - high.astype(f32)).astype(bf16)


def product(left, right, dims=((1,), (0,))):
    def one(a, b):
        return lax.dot_general(a, b, (dims, ((), ())), preferred_element_type=f32)

    return one(left[0], right[0]) + (one(left[0], right[1]) + one(left[1], right[0]))


def lane_sign(shape):
    return jnp.where(lax.broadcasted_iota(jnp.int32, shape, 1) < HALF, 1.0, -1.0).astype(f32)


def turned(value, sign):
    return pltpu.roll(value, HALF, 1) * sign


def atom_weights(atoms, lanes):
    offset = [atoms[3 + a : 4 + a, lanes] for a in range(3)]
    return [spline_rows(one) for one in offset]


def spread_kernel(
    atoms_ref, base_ref, taps_ref, high_ref, low_ref, cos_ref, sin_ref, out_ref, waves_ref, grid_ref
):
    grid_ref[...] = jnp.zeros_like(grid_ref)
    part = ROWS * LANES
    gap = jnp.zeros((HALF - PADDED_Z, LANES), f32)
    for own in (True, False):
        rows = list(range(CY)) if own else list(range(CY, ROWS))
        start = 0 if own else PENCILS

        def pencil_body(pencil, carry, rows=rows, start=start):
            for i in range(PAIRS):
                atoms = atoms_ref[start + pencil, :, i * LANES : (i + 1) * LANES]
                row = [atoms[a : a + 1] for a in range(10)]
                weights = [spline_rows(row[3 + a]) for a in range(3)]
                charge, dip_x, dip_y, dip_z = row[6:10]
                window = pencil * CX + i * 32
                dense_x = dense_rows(weights[0][:2], row[0] - window.astype(f32), WINDOW)
                dense_y = dense_rows(weights[1][:2], row[1], 16)
                cell_z = row[2]
                turn = base_ref[...] * cell_z
                turn = turn - 360.0 * jnp.floor(turn * (1.0 / 360.0))
                cos_k, sin_k = unit_phase(turn * (1.0 / 360.0))
                turn = 8.0 * cell_z
                turn = turn - 360.0 * jnp.floor(turn * (1.0 / 360.0))
                cos_8, sin_8 = unit_phase(turn * (1.0 / 360.0))
                pieces = [[], [], []]
                pieces_im = [[], [], []]
                for q in range(PADDED_Z // 8):
                    span = slice(q * 8, q * 8 + 8)
                    for s in range(3):
                        real = sum(weights[2][s][t] * taps_ref[t, span, :] for t in range(6))
                        imag = sum(weights[2][s][t] * taps_ref[6 + t, span, :] for t in range(6))
                        pieces[s].append(real * cos_k - imag * sin_k)
                        pieces_im[s].append(-(real * sin_k + imag * cos_k))
                    cos_k, sin_k = cos_k * cos_8 - sin_k * sin_8, sin_k * cos_8 + cos_k * sin_8
                re = [jnp.concatenate(pieces[s], axis=0) for s in range(3)]
                im = [jnp.concatenate(pieces_im[s], axis=0) for s in range(3)]
                pair = (start + pencil) * PAIRS + i
                for s in range(3):
                    waves_ref[pair, s, :PADDED_Z] = re[s]
                    waves_ref[pair, s, PADDED_Z:] = im[s]
                full = []
                for wave_re, wave_im in (
                    (charge * re[0] + dip_z * re[1], charge * im[0] + dip_z * im[1]),
                    (re[0], im[0]),
                ):
                    full.append(
                        jnp.concatenate(
                            [wave_re, gap, wave_im, gap, wave_im, gap, -wave_re, gap], axis=0
                        )
                    )
                right = jnp.concatenate(full, axis=1)
                left = []
                for r in rows:
                    value = dense_y[0][r : r + 1]
                    first = dense_y[1][r : r + 1]
                    left.append(
                        jnp.concatenate(
                            [
                                value * dense_x[0],
                                (dip_x * value) * dense_x[1] + (dip_y * first) * dense_x[0],
                            ],
                            axis=1,
                        )
                    )
                left = jnp.concatenate(left, axis=0)
                added = product(halves(left), halves(right), ((1,), (1,)))
                at = pl.ds(pl.multiple_of(window, 8), WINDOW)
                for n, r in enumerate(rows):
                    piece = added[n * WINDOW : (n + 1) * WINDOW]
                    grid_ref[at, r * LANES : (r + 1) * LANES] += piece[:, :LANES]
                    grid_ref[at, part + r * LANES : part + (r + 1) * LANES] += piece[:, LANES:]
            return carry

        lax.fori_loop(0, PENCILS, pencil_body, 0)
    grid_ref[0:8] += grid_ref[NX : NX + 8]
    table = (high_ref[...], low_ref[...])
    sign = lane_sign((NX, LANES))
    for y in range(CY):
        rows = [y] if y == CY - 1 else [y, CY + y]
        spans = [slice(r * LANES, (r + 1) * LANES) for r in rows]
        top = jnp.concatenate([grid_ref[:NX, span] for span in spans], axis=1)
        low_spans = [slice(part + r * LANES, part + (r + 1) * LANES) for r in rows]
        bottom = jnp.concatenate([grid_ref[:NX, span] for span in low_spans], axis=1)
        line = product(table, halves(jnp.concatenate([top, bottom], axis=0)))
        total = jnp.zeros((NX, LANES), f32)
        for n, r in enumerate(rows):
            one = line[:, n * LANES : (n + 1) * LANES]
            total = total + one * cos_ref[:, r : r + 1] + turned(one, sign) * sin_ref[:, r : r + 1]
        for j in range(PART_X):
            at = (j * CY + y) * LANES
            out_ref[:, at : at + LANES] = total[j * SLABS : (j + 1) * SLABS]


def filter_kernel(
    in_ref, high_ref, low_ref, back_high_ref, back_low_ref, top_ref, norm_ref, mode_ref, out_ref, energy_ref
):
    forward = (high_ref[...], low_ref[...])
    inverse = (back_high_ref[...], back_low_ref[...])
    sign = lane_sign((NY, LANES))
    energy = jnp.zeros((8, LANES), f32)
    for first in range(0, PART_X, 2):
        lines = []
        for j in (first, first + 1):
            lines.append(
                jnp.concatenate(
                    [in_ref[:, (j * CY + y) * LANES : (j * CY + y + 1) * LANES] for y in range(CY)],
                    axis=0,
                )
            )
        stacked = jnp.concatenate(
            [
                jnp.concatenate([one, turned(one, sign)], axis=0)
                for one in lines
            ],
            axis=1,
        )
        spectrum = product(forward, halves(stacked))
        backs = []
        for n in range(2):
            j = first + n
            one = spectrum[:, n * LANES : (n + 1) * LANES]
            square = norm_ref[:, j : j + 1] + mode_ref[1:2, :]
            green = top_ref[:, j : j + 1] * mode_ref[0:1, :] / jnp.where(square == 0.0, 1.0, square)
            green = jnp.where(square == 0.0, 0.0, green)
            scaled = green * one
            share = scaled * one
            energy = energy + sum(share[8 * i : 8 * i + 8] for i in range(NY // 8))
            backs.append(jnp.concatenate([scaled, -turned(scaled, sign)], axis=0))
        potential = product(inverse, halves(jnp.concatenate(backs, axis=1)))
        for n in range(2):
            j = first + n
            for y in range(CY):
                at = (j * CY + y) * LANES
                out_ref[:, at : at + LANES] = potential[
                    y * SLABS : (y + 1) * SLABS, n * LANES : (n + 1) * LANES
                ]
    energy_ref[...] = energy


def sample_kernel(in_ref, atoms_ref, waves_ref, high_ref, low_ref, cos_ref, sin_ref, out_ref, grid_ref):
    table = (high_ref[...], low_ref[...])
    sign = lane_sign((NX, LANES))
    for y in range(CY):
        rows = [y] if y == CY - 1 else [y, CY + y]
        line = jnp.concatenate(
            [in_ref[:, (j * CY + y) * LANES : (j * CY + y + 1) * LANES] for j in range(PART_X)],
            axis=0,
        )
        swapped = turned(line, sign)
        stacked = []
        for r in rows:
            one = line * cos_ref[:, r : r + 1] - swapped * sin_ref[:, r : r + 1]
            stacked.append(jnp.concatenate([one, -turned(one, sign)], axis=0))
        cells = product(table, halves(jnp.concatenate(stacked, axis=1)))
        for n, r in enumerate(rows):
            piece = cells[:, n * LANES : (n + 1) * LANES]
            grid_ref[:NX, r * LANES : (r + 1) * LANES] = piece
            grid_ref[NX:, r * LANES : (r + 1) * LANES] = piece[:8]
    gap = jnp.zeros((HALF - PADDED_Z, LANES), f32)
    for own in (True, False):
        rows = list(range(CY)) if own else list(range(CY, ROWS))
        start = 0 if own else PENCILS

        def pencil_body(pencil, carry, rows=rows, start=start):
            for i in range(PAIRS):
                lanes = slice(i * LANES, (i + 1) * LANES)
                atoms = atoms_ref[start + pencil, :, lanes]
                row = [atoms[a : a + 1] for a in range(11)]
                weights = [spline_rows(row[3 + a]) for a in range(2)]
                window = pencil * CX + i * 32
                dense_x = dense_rows(weights[0], row[0] - window.astype(f32), WINDOW)
                dense_y = dense_rows(weights[1], row[1], 16)
                pair = (start + pencil) * PAIRS + i
                waves = jnp.concatenate(
                    [
                        jnp.concatenate(
                            [waves_ref[pair, s, :PADDED_Z], gap, waves_ref[pair, s, PADDED_Z:], gap],
                            axis=0,
                        )
                        for s in range(3)
                    ],
                    axis=1,
                )
                at = pl.ds(pl.multiple_of(window, 8), WINDOW)
                cells = jnp.concatenate(
                    [grid_ref[at, r * LANES : (r + 1) * LANES] for r in rows], axis=0
                )
                read = product(halves(cells), halves(waves))
                lined = {}
                for order_y, order_z in ((0, 0), (1, 0), (2, 0), (0, 1), (1, 1), (0, 2)):
                    lined[order_y, order_z] = sum(
                        dense_y[order_y][r : r + 1]
                        * read[
                            n * WINDOW : (n + 1) * WINDOW, order_z * LANES : (order_z + 1) * LANES
                        ]
                        for n, r in enumerate(rows)
                    )

                def sampled(p, r, s):
                    return jnp.sum(dense_x[p] * lined[r, s], axis=0, keepdims=True)

                charge, dip_x, dip_y, dip_z, live = row[6:11]
                s100 = sampled(1, 0, 0)
                s010 = sampled(0, 1, 0)
                s001 = sampled(0, 0, 1)
                s110 = sampled(1, 1, 0)
                s101 = sampled(1, 0, 1)
                s011 = sampled(0, 1, 1)
                out = [
                    live * sampled(0, 0, 0),
                    live * s100,
                    live * s010,
                    live * s001,
                    charge * s100 + dip_x * sampled(2, 0, 0) + dip_y * s110 + dip_z * s101,
                    charge * s010 + dip_x * s110 + dip_y * sampled(0, 2, 0) + dip_z * s011,
                    charge * s001 + dip_x * s101 + dip_y * s011 + dip_z * sampled(0, 0, 2),
                    jnp.zeros_like(live),
                ]
                out_ref[start + pencil, :, lanes] = jnp.concatenate(out, axis=0)
            return carry

        lax.fori_loop(0, PENCILS, pencil_body, 0)


def spline_modulus(angles):
    return (66.0 + 52.0 * jnp.cos(angles) + 2.0 * jnp.cos(2.0 * angles)) / 120.0


def folded(index, size):
    return (index + size // 2) % size - size // 2


def call(kernel, out_shape, scratch=(), **cost):
    return pl.pallas_call(
        kernel,
        out_shape=out_shape,
        scratch_shapes=list(scratch),
        compiler_params=pltpu.CompilerParams(vmem_limit_bytes=50 * 1024 * 1024),
        cost_estimate=pl.CostEstimate(transcendentals=0, **cost),
    )


def next_slab(value, back=False):
    step = -1 if back else 1
    return lax.ppermute(value, "gy", [(i, (i + step) % SLABS) for i in range(SLABS)])


def on_device(cell_index, offsets, charges, dipoles, block_count, shear_cells):
    pencil_index = lax.axis_index("gx")
    slab_index = lax.axis_index("gy")
    shear_step = shear_cells[0]
    (x_high, x_low), (y_high, y_low), (back_high, back_low) = wave_tables()

    slot = jnp.arange(ATOM_DEV, dtype=jnp.int32)
    counts = jnp.repeat(block_count, ATOM_BLK, total_repeat_length=ATOM_DEV)
    live = (slot % ATOM_BLK < counts).astype(f32)
    cells = cell_index - jnp.stack([0, slab_index * CY, 0])[:, None]
    mine = jnp.concatenate(
        [
            cells.astype(f32),
            offsets,
            (charges * live)[None],
            dipoles * live[None],
            live[None],
            jnp.zeros((5, ATOM_DEV), f32),
        ],
        axis=0,
    )
    slab_atoms = lax.all_gather(mine, "gx", axis=0, tiled=False)
    atoms = jnp.concatenate([slab_atoms, next_slab(slab_atoms)], axis=0)

    mode_z = pencil_index * PART_Z + jnp.arange(PADDED_Z, dtype=jnp.int32)
    kept = jnp.arange(PADDED_Z) < PART_Z
    ticks = jnp.arange(6, dtype=jnp.int32)[:, None] * mode_z[None, :] % NZ
    angles = 2.0 * math.pi / NZ * ticks.astype(f32)
    taps = jnp.concatenate([jnp.cos(angles), jnp.sin(angles)], axis=0) * kept[None, :]
    taps = jnp.broadcast_to(taps[:, :, None], (12, PADDED_Z, LANES))
    base = jnp.broadcast_to(mode_z[:8, None].astype(f32), (8, LANES))

    index_x = jnp.arange(NX, dtype=jnp.int32)
    above = (slab_index - 1) % SLABS * CY
    rows = jnp.arange(16, dtype=jnp.int32)
    rows = jnp.where(rows < CY, slab_index * CY + rows, above + rows)
    twist = folded(index_x, NX)[:, None] * shear_step * rows[None, :] % (NX * NY)
    angles = 2.0 * math.pi / (NX * NY) * twist.astype(f32)
    cos_t, sin_t = jnp.cos(angles), jnp.sin(angles)

    own_x = folded(jnp.arange(8, dtype=jnp.int32) * SLABS + slab_index, NX)[None, :]
    own_y = folded(jnp.arange(NY, dtype=jnp.int32), NY)[:, None]
    float_x = own_x.astype(f32)
    wave_y = own_y.astype(f32) + float_x * shear_step.astype(f32) / NX
    norm = (float_x / NX) ** 2 + (wave_y / NY) ** 2
    moduli = spline_modulus(2.0 * math.pi * float_x / NX) * spline_modulus(
        2.0 * math.pi * wave_y / NY
    )
    decay = (math.pi / screening) ** 2
    top = jnp.exp(-decay * norm) / (math.pi * moduli * moduli)
    top = jnp.where((own_x == -(NX // 2)) | (own_y == -(NY // 2)), 0.0, top)
    float_z = mode_z.astype(f32)
    norm_z = (float_z / NZ) ** 2
    modulus_z = spline_modulus(2.0 * math.pi * float_z / NZ)
    twice = jnp.where(mode_z == 0, 1.0, 2.0) / (NX * NY * NZ)
    mode_top = jnp.where(kept, twice * jnp.exp(-decay * norm_z) / (modulus_z * modulus_z), 0.0)
    mode_norm = jnp.where(kept, norm_z, 1.0)
    half_rows = jnp.stack([mode_top, mode_norm])
    half_rows = jnp.pad(half_rows, ((0, 6), (0, HALF - PADDED_Z)), constant_values=1.0)
    half_rows = half_rows.at[0, PADDED_Z:].set(0.0)
    mode = jnp.concatenate([half_rows, half_rows], axis=1)

    shape = jax.ShapeDtypeStruct
    wide = PART_X * CY * LANES
    lines, waves = call(
        spread_kernel,
        (shape((SLABS, wide), f32), shape((24, 3, 2 * PADDED_Z, LANES), f32)),
        [pltpu.VMEM((NX + 8, 2 * ROWS * LANES), f32)],
        flops=4_000_000_000,
        bytes_accessed=8_000_000,
    )(atoms, base, taps, x_high, x_low, cos_t, sin_t)
    lines = lax.all_to_all(lines, "gy", split_axis=0, concat_axis=0, tiled=True)
    filtered, energy_rows = call(
        filter_kernel,
        (shape((SLABS, wide), f32), shape((8, LANES), f32)),
        flops=4_000_000_000,
        bytes_accessed=5_000_000,
    )(lines, y_high, y_low, back_high, back_low, top, norm, mode)
    energy = lax.psum(0.5 * jnp.sum(energy_rows), ("gy", "gx"))
    filtered = lax.all_to_all(filtered, "gy", split_axis=0, concat_axis=0, tiled=True)
    shares = call(
        sample_kernel,
        shape((2 * PENCILS, 8, ATOM_DEV), f32),
        [pltpu.VMEM((NX + 8, ROWS * LANES), f32)],
        flops=4_000_000_000,
        bytes_accessed=8_000_000,
    )(filtered, atoms, waves, x_high, x_low, cos_t, sin_t)
    slab_shares = shares[:PENCILS] + next_slab(shares[PENCILS:], back=True)
    own = lax.psum_scatter(slab_shares, "gx", scatter_dimension=0, tiled=False)
    return own[0], own[1:4], own[4:7], jnp.reshape(energy, (1,))


def solution(mesh):
    placed = (
        P(None, ("gy", "gx")),
        P(None, ("gy", "gx")),
        P(("gy", "gx")),
        P(None, ("gy", "gx")),
        P(("gy", "gx")),
        P(),
    )
    return jax.shard_map(
        on_device,
        mesh=mesh,
        in_specs=placed,
        out_specs=(P(("gy", "gx")), P(None, ("gy", "gx")), P(None, ("gy", "gx")), P()),
        check_vma=False,
    )
```

```python
import math

import jax
import jax.numpy as jnp
import ml_dtypes
import numpy as np
from jax import lax
from jax.experimental import pallas as pl
from jax.experimental.pallas import tpu as pltpu
from jax.sharding import PartitionSpec as P

NX = 384
NY = 384
NZ = 360
CY = 6
CX = 96
PENCILS = 4
SLABS = 64
PART_X = 6
PART_Z = 45
ATOM_BLK = 64
ATOM_DEV = 384
PAIRS = 3
WINDOW = 40
ROWS = 11
HALF = 64
LANES = 128
PADDED_Z = 48
screening = 0.9
f32 = jnp.float32
bf16 = jnp.bfloat16


def split_table(table):
    high = table.astype(ml_dtypes.bfloat16)
    low = (table - high.astype(np.float64)).astype(ml_dtypes.bfloat16)
    return high, low


def wave_tables():
    natural = np.arange(NX)
    angle_x = 2.0 * np.pi / NX * (natural[:, None] * natural[None, :] % NX)
    table_x = np.concatenate([np.cos(angle_x), np.sin(angle_x)], axis=1)
    place_y = np.arange(NY) % SLABS * CY + np.arange(NY) // SLABS
    angle_y = 2.0 * np.pi / NY * (natural[:, None] * place_y[None, :] % NY)
    forward_y = np.concatenate([np.cos(angle_y), np.sin(angle_y)], axis=1)
    inverse_y = np.concatenate([np.cos(angle_y.T), np.sin(angle_y.T)], axis=1)
    return split_table(table_x), split_table(forward_y), split_table(inverse_y)


def spline_rows(fraction):
    levels = {2: [1.0 - fraction, fraction]}
    current = levels[2]
    for n in range(3, 7):
        inverse_n = 1.0 / (n - 1)
        updated = [None] * n
        updated[n - 1] = inverse_n * fraction * current[n - 2]
        for j in range(1, n - 1):
            updated[n - 1 - j] = inverse_n * (
                (fraction + j) * current[n - 2 - j] + (n - j - fraction) * current[n - 1 - j]
            )
        updated[0] = inverse_n * (1.0 - fraction) * current[0]
        current = updated
        levels[n] = current
    zero_row = jnp.zeros_like(fraction)

    def entry_at(values_list, k):
        return values_list[k] if 0 <= k < len(values_list) else zero_row

    first = [entry_at(levels[5], t - 1) - entry_at(levels[5], t) for t in range(6)]
    second = [
        entry_at(levels[4], t - 2) - 2.0 * entry_at(levels[4], t - 1) + entry_at(levels[4], t)
        for t in range(6)
    ]
    return levels[6], first, second


def dense_rows(tables, cell, length):
    away = lax.broadcasted_iota(jnp.int32, (length, cell.shape[1]), 0).astype(f32) - cell
    summed = [jnp.zeros(away.shape, f32) for _ in tables]
    for t in range(6):
        here = away == float(t)
        summed = [jnp.where(here, table[t], so_far) for table, so_far in zip(tables, summed)]
    return summed


def unit_phase(turns):
    turns = turns - jnp.floor(turns + 0.5)
    quarter = jnp.floor(4.0 * turns + 0.5)
    rest = turns - 0.25 * quarter
    theta = (2.0 * math.pi) * rest
    square = theta * theta
    sine = theta * (
        1.0
        + square
        * (-1.0 / 6 + square * (1.0 / 120 + square * (-1.0 / 5040 + square * (1.0 / 362880))))
    )
    cosine = 1.0 + square * (
        -0.5
        + square
        * (1.0 / 24 + square * (-1.0 / 720 + square * (1.0 / 40320 - square * (1.0 / 3628800))))
    )
    odd = jnp.abs(quarter) == 1.0
    cos_out = jnp.where(odd, sine, cosine)
    sin_out = jnp.where(odd, cosine, sine)
    cos_out = jnp.where((quarter == 1.0) | (jnp.abs(quarter) == 2.0), -cos_out, cos_out)
    sin_out = jnp.where((quarter == -1.0) | (jnp.abs(quarter) == 2.0), -sin_out, sin_out)
    return cos_out, sin_out


def halves(value):
    high = value.astype(bf16)
    return high, (value - high.astype(f32)).astype(bf16)


def product(left, right, dims=((1,), (0,))):
    def one(a, b):
        return lax.dot_general(a, b, (dims, ((), ())), preferred_element_type=f32)

    return one(left[0], right[0]) + (one(left[0], right[1]) + one(left[1], right[0]))


def lane_sign(shape):
    return jnp.where(lax.broadcasted_iota(jnp.int32, shape, 1) < HALF, 1.0, -1.0).astype(f32)


def turned(value, sign):
    return pltpu.roll(value, HALF, 1) * sign


def atom_weights(atoms, lanes):
    offset = [atoms[3 + a : 4 + a, lanes] for a in range(3)]
    return [spline_rows(one) for one in offset]


PIECES = (0, 16, 32, 64, 80, 96)
GROUPS = PART_X * CY // 4
CARRIERS = 3 * GROUPS


def lane_range(first):
    lane = lax.broadcasted_iota(jnp.int32, (SLABS, LANES), 1)
    return (lane >= first) & (lane < first + 16)


def pack_blocks(blocks):
    carriers = []
    for c in range(3):
        value = blocks[c]
        for half in range(2):
            gap = PADDED_Z + half * HALF
            shift = (gap - PIECES[2 * c + half]) % LANES
            value = jnp.where(lane_range(gap), pltpu.roll(blocks[3], shift, 1), value)
        carriers.append(value)
    return carriers


def unpack_block(carriers):
    value = jnp.zeros((SLABS, LANES), f32)
    for p, source in enumerate(PIECES):
        gap = PADDED_Z + p % 2 * HALF
        shift = (source - gap) % LANES
        value = jnp.where(lane_range(source), pltpu.roll(carriers[p // 2], shift, 1), value)
    return value


def rows_of(carrier):
    return pl.ds(carrier, SLABS, stride=CARRIERS)


def block_at(ref, j, y):
    block = j * CY + y
    group, place = block // 4, block % 4
    if place < 3:
        return ref[rows_of(3 * group + place), :]
    return unpack_block([ref[rows_of(3 * group + c), :] for c in range(3)])


def prepare_kernel(
    where_ref, shear_ref, count_ref, cell_ref, offset_ref, charge_ref, dipole_ref,
    atoms_ref, base_ref, taps_ref, cos_ref, sin_ref
):
    slab, pencil = where_ref[0], where_ref[1]
    slot = lax.broadcasted_iota(jnp.int32, (1, ATOM_DEV), 1)
    live = jnp.zeros((1, ATOM_DEV), f32)
    for b in range(ATOM_DEV // ATOM_BLK):
        inside = (slot >= b * ATOM_BLK) & (slot < b * ATOM_BLK + count_ref[b])
        live = jnp.where(inside, 1.0, live)
    atoms_ref[0:1, :] = cell_ref[0:1, :].astype(f32)
    atoms_ref[1:2, :] = (cell_ref[1:2, :] - slab * CY).astype(f32)
    atoms_ref[2:3, :] = cell_ref[2:3, :].astype(f32)
    atoms_ref[3:6, :] = offset_ref[...]
    atoms_ref[6:7, :] = charge_ref[...] * live
    atoms_ref[7:10, :] = dipole_ref[...] * live
    atoms_ref[10:11, :] = live
    atoms_ref[11:16, :] = jnp.zeros((5, ATOM_DEV), f32)
    first = pencil * PART_Z
    row = lax.broadcasted_iota(jnp.int32, (PADDED_Z, LANES), 0)
    mode = (row + first).astype(f32)
    base_ref[...] = mode[:8]
    for t in range(6):
        cos_t, sin_t = unit_phase(mode * float(t) * (1.0 / NZ))
        taps_ref[t] = jnp.where(row < PART_Z, cos_t, 0.0)
        taps_ref[6 + t] = jnp.where(row < PART_Z, sin_t, 0.0)
    column = lax.broadcasted_iota(jnp.int32, (1, LANES), 1)
    above = jnp.where(slab == 0, SLABS - 1, slab - 1) * CY
    rows = jnp.where(column < CY, slab * CY, above) + jnp.minimum(column, ROWS)
    index = lax.broadcasted_iota(jnp.int32, (NX, LANES), 0)
    folds = jnp.where(index < NX // 2, index, index - NX)
    ticks = folds * (shear_ref[0] * rows)
    whole = jnp.floor(ticks.astype(f32) * (1.0 / (NX * NY))).astype(jnp.int32)
    rest = ticks - whole * (NX * NY)
    cos_t, sin_t = unit_phase(rest.astype(f32) * (1.0 / (NX * NY)))
    cos_ref[...] = cos_t
    sin_ref[...] = sin_t


def spread_kernel(own, *refs):
    if own:
        atoms_ref, base_ref, taps_ref, high_ref, low_ref, cos_ref, sin_ref, out_ref, waves_ref, grid_ref = refs
    else:
        (
            atoms_ref, base_ref, taps_ref, high_ref, low_ref, cos_ref, sin_ref, lines_ref,
            out_ref, waves_ref, grid_ref
        ) = refs
    grid_ref[...] = jnp.zeros_like(grid_ref)
    rows = list(range(CY)) if own else list(range(CY, ROWS))
    part = len(rows) * LANES
    gap = jnp.zeros((HALF - PADDED_Z, LANES), f32)

    def pencil_body(pencil, carry):
        for i in range(PAIRS):
            atoms = atoms_ref[pencil, :, i * LANES : (i + 1) * LANES]
            row = [atoms[a : a + 1] for a in range(10)]
            weights = [spline_rows(row[3 + a]) for a in range(3)]
            charge, dip_x, dip_y, dip_z = row[6:10]
            window = pencil * CX + i * 32
            dense_x = dense_rows(weights[0][:2], row[0] - window.astype(f32), WINDOW)
            dense_y = dense_rows(weights[1][:2], row[1], 16)
            cell_z = row[2]
            turn = base_ref[...] * cell_z
            turn = turn - 360.0 * jnp.floor(turn * (1.0 / 360.0))
            cos_k, sin_k = unit_phase(turn * (1.0 / 360.0))
            turn = 8.0 * cell_z
            turn = turn - 360.0 * jnp.floor(turn * (1.0 / 360.0))
            cos_8, sin_8 = unit_phase(turn * (1.0 / 360.0))
            pieces = [[], [], []]
            pieces_im = [[], [], []]
            for q in range(PADDED_Z // 8):
                span = slice(q * 8, q * 8 + 8)
                for s in range(3):
                    real = sum(weights[2][s][t] * taps_ref[t, span, :] for t in range(6))
                    imag = sum(weights[2][s][t] * taps_ref[6 + t, span, :] for t in range(6))
                    pieces[s].append(real * cos_k - imag * sin_k)
                    pieces_im[s].append(-(real * sin_k + imag * cos_k))
                cos_k, sin_k = cos_k * cos_8 - sin_k * sin_8, sin_k * cos_8 + cos_k * sin_8
            re = [jnp.concatenate(pieces[s], axis=0) for s in range(3)]
            im = [jnp.concatenate(pieces_im[s], axis=0) for s in range(3)]
            pair = pencil * PAIRS + i
            for s in range(3):
                waves_ref[pair, s, :PADDED_Z] = re[s]
                waves_ref[pair, s, PADDED_Z:] = im[s]
            full = []
            for wave_re, wave_im in (
                (charge * re[0] + dip_z * re[1], charge * im[0] + dip_z * im[1]),
                (re[0], im[0]),
            ):
                full.append(
                    jnp.concatenate(
                        [wave_re, gap, wave_im, gap, wave_im, gap, -wave_re, gap], axis=0
                    )
                )
            right = jnp.concatenate(full, axis=1)
            left = []
            for r in rows:
                value = dense_y[0][r : r + 1]
                first = dense_y[1][r : r + 1]
                left.append(
                    jnp.concatenate(
                        [
                            value * dense_x[0],
                            (dip_x * value) * dense_x[1] + (dip_y * first) * dense_x[0],
                        ],
                        axis=1,
                    )
                )
            left = jnp.concatenate(left, axis=0)
            added = product(halves(left), halves(right), ((1,), (1,)))
            at = pl.ds(pl.multiple_of(window, 8), WINDOW)
            for n in range(len(rows)):
                piece = added[n * WINDOW : (n + 1) * WINDOW]
                grid_ref[at, n * LANES : (n + 1) * LANES] += piece[:, :LANES]
                grid_ref[at, part + n * LANES : part + (n + 1) * LANES] += piece[:, LANES:]
        return carry

    lax.fori_loop(0, PENCILS, pencil_body, 0)
    grid_ref[0:8] += grid_ref[NX : NX + 8]
    table = (high_ref[...], low_ref[...])
    sign = lane_sign((NX, LANES))
    totals = []
    for first in range(0, len(rows), 2):
        lanes = slice(first * LANES, min(first + 2, len(rows)) * LANES)
        below = slice(part + lanes.start, part + lanes.stop)
        stacked = jnp.concatenate([grid_ref[:NX, lanes], grid_ref[:NX, below]], axis=0)
        line = product(table, halves(stacked))
        for n, r in enumerate(rows[first : first + 2]):
            one = line[:, n * LANES : (n + 1) * LANES]
            total = one * cos_ref[:, r : r + 1] + turned(one, sign) * sin_ref[:, r : r + 1]
            y = first + n
            if own:
                out_ref[:, y * LANES : (y + 1) * LANES] = total
            else:
                totals.append(total + lines_ref[:, y * LANES : (y + 1) * LANES])
    if own:
        return
    totals.append(lines_ref[:, (CY - 1) * LANES :])
    for group in range(GROUPS):
        blocks = []
        for block in range(4 * group, 4 * group + 4):
            j, y = block // CY, block % CY
            blocks.append(totals[y][j * SLABS : (j + 1) * SLABS])
        for c, carrier in enumerate(pack_blocks(blocks)):
            out_ref[rows_of(3 * group + c), :] = carrier


def filter_kernel(
    in_ref, high_ref, low_ref, back_high_ref, back_low_ref, top_ref, norm_ref, mode_ref, out_ref
):
    forward = (high_ref[...], low_ref[...])
    inverse = (back_high_ref[...], back_low_ref[...])
    sign = lane_sign((NY, LANES))
    energy = jnp.zeros((8, LANES), f32)
    blocks = []
    for first in range(0, PART_X, 2):
        lines = []
        for j in (first, first + 1):
            lines.append(jnp.concatenate([block_at(in_ref, j, y) for y in range(CY)], axis=0))
        stacked = jnp.concatenate(
            [jnp.concatenate([one, turned(one, sign)], axis=0) for one in lines], axis=1
        )
        spectrum = product(forward, halves(stacked))
        backs = []
        for n in range(2):
            j = first + n
            one = spectrum[:, n * LANES : (n + 1) * LANES]
            square = norm_ref[:, j : j + 1] + mode_ref[1:2, :]
            green = top_ref[:, j : j + 1] * mode_ref[0:1, :] / jnp.where(square == 0.0, 1.0, square)
            green = jnp.where(square == 0.0, 0.0, green)
            scaled = green * one
            share = scaled * one
            energy = energy + sum(share[8 * i : 8 * i + 8] for i in range(NY // 8))
            backs.append(jnp.concatenate([scaled, -turned(scaled, sign)], axis=0))
        potential = product(inverse, halves(jnp.concatenate(backs, axis=1)))
        for n in range(2):
            for y in range(CY):
                blocks.append(
                    potential[y * SLABS : (y + 1) * SLABS, n * LANES : (n + 1) * LANES]
                )
        for group in range(first * CY // 4, (first + 2) * CY // 4):
            for c, carrier in enumerate(pack_blocks(blocks[4 * group : 4 * group + 4])):
                out_ref[rows_of(3 * group + c), :] = carrier
    lane = lax.broadcasted_iota(jnp.int32, (SLABS, LANES), 1)
    share = 0.5 * jnp.sum(energy)
    out_ref[rows_of(0), :] = jnp.where(lane == PART_Z, share, out_ref[rows_of(0), :])


def sample_kernel(own, in_ref, atoms_ref, waves_ref, high_ref, low_ref, cos_ref, sin_ref, out_ref, grid_ref):
    table = (high_ref[...], low_ref[...])
    sign = lane_sign((NX, LANES))
    rows = list(range(CY)) if own else list(range(CY, ROWS))
    for first in range(0, len(rows), 2):
        stacked = []
        for y in range(first, min(first + 2, len(rows))):
            line = jnp.concatenate([block_at(in_ref, j, y) for j in range(PART_X)], axis=0)
            r = rows[y]
            one = line * cos_ref[:, r : r + 1] - turned(line, sign) * sin_ref[:, r : r + 1]
            stacked.append(jnp.concatenate([one, -turned(one, sign)], axis=0))
        cells = product(table, halves(jnp.concatenate(stacked, axis=1)))
        lanes = slice(first * LANES, (first + len(stacked)) * LANES)
        grid_ref[:NX, lanes] = cells
        grid_ref[NX:, lanes] = cells[:8]
    gap = jnp.zeros((HALF - PADDED_Z, LANES), f32)
    if own:
        lane = lax.broadcasted_iota(jnp.int32, (SLABS, LANES), 1)
        energy = jnp.sum(jnp.where(lane == PART_Z, in_ref[rows_of(0), :], 0.0))
    else:
        energy = 0.0

    def pencil_body(pencil, carry):
        for i in range(PAIRS):
            lanes = slice(i * LANES, (i + 1) * LANES)
            atoms = atoms_ref[pencil, :, lanes]
            row = [atoms[a : a + 1] for a in range(11)]
            weights = [spline_rows(row[3 + a]) for a in range(2)]
            window = pencil * CX + i * 32
            dense_x = dense_rows(weights[0], row[0] - window.astype(f32), WINDOW)
            dense_y = dense_rows(weights[1], row[1], 16)
            pair = pencil * PAIRS + i
            waves = jnp.concatenate(
                [
                    jnp.concatenate(
                        [waves_ref[pair, s, :PADDED_Z], gap, waves_ref[pair, s, PADDED_Z:], gap],
                        axis=0,
                    )
                    for s in range(3)
                ],
                axis=1,
            )
            at = pl.ds(pl.multiple_of(window, 8), WINDOW)
            cells = jnp.concatenate(
                [grid_ref[at, n * LANES : (n + 1) * LANES] for n in range(len(rows))], axis=0
            )
            read = product(halves(cells), halves(waves))
            lined = {}
            for order_y, order_z in ((0, 0), (1, 0), (2, 0), (0, 1), (1, 1), (0, 2)):
                lined[order_y, order_z] = sum(
                    dense_y[order_y][r : r + 1]
                    * read[n * WINDOW : (n + 1) * WINDOW, order_z * LANES : (order_z + 1) * LANES]
                    for n, r in enumerate(rows)
                )

            def sampled(p, r, s):
                return jnp.sum(dense_x[p] * lined[r, s], axis=0, keepdims=True)

            charge, dip_x, dip_y, dip_z, live = row[6:11]
            s100 = sampled(1, 0, 0)
            s010 = sampled(0, 1, 0)
            s001 = sampled(0, 0, 1)
            s110 = sampled(1, 1, 0)
            s101 = sampled(1, 0, 1)
            s011 = sampled(0, 1, 1)
            out = [
                live * sampled(0, 0, 0),
                live * s100,
                live * s010,
                live * s001,
                charge * s100 + dip_x * sampled(2, 0, 0) + dip_y * s110 + dip_z * s101,
                charge * s010 + dip_x * s110 + dip_y * sampled(0, 2, 0) + dip_z * s011,
                charge * s001 + dip_x * s101 + dip_y * s011 + dip_z * sampled(0, 0, 2),
                jnp.full(live.shape, energy, f32),
            ]
            out_ref[pencil, :, lanes] = jnp.concatenate(out, axis=0)
        return carry

    lax.fori_loop(0, PENCILS, pencil_body, 0)


def finish_kernel(in_ref, charge_ref, dipole_ref, position_ref, energy_ref):
    total = (in_ref[0] + in_ref[1]) + (in_ref[2] + in_ref[3])
    charge_ref[...] = total[0:1]
    dipole_ref[...] = total[1:4]
    position_ref[...] = total[4:7]
    energy_ref[...] = total[7:8, 0:1]


def spline_modulus(angles):
    return (66.0 + 52.0 * jnp.cos(angles) + 2.0 * jnp.cos(2.0 * angles)) / 120.0


def folded(index, size):
    return (index + size // 2) % size - size // 2


def call(kernel, out_shape, scratch=(), in_smem=0, inputs=0, flops=0, bytes_accessed=0):
    more = {}
    if in_smem:
        whole = pl.BlockSpec(memory_space=pltpu.VMEM)
        scalars = pl.BlockSpec(memory_space=pltpu.SMEM)
        more["in_specs"] = [scalars] * in_smem + [whole] * (inputs - in_smem)
    return pl.pallas_call(
        kernel,
        out_shape=out_shape,
        scratch_shapes=list(scratch),
        compiler_params=pltpu.CompilerParams(vmem_limit_bytes=32 * 1024 * 1024),
        cost_estimate=pl.CostEstimate(
            transcendentals=0, flops=flops, bytes_accessed=bytes_accessed
        ),
        **more,
    )


def next_slab(value, back=False):
    step = -1 if back else 1
    return lax.ppermute(value, "gy", [(i, (i + step) % SLABS) for i in range(SLABS)])


def swap_slabs(lines):
    lines = lines.reshape(SLABS, CARRIERS, 1, LANES)
    lines = lax.all_to_all(lines, "gy", split_axis=0, concat_axis=0, tiled=True)
    return lines.reshape(SLABS * CARRIERS, LANES)


def on_device(cell_index, offsets, charges, dipoles, block_count, shear_cells):
    pencil_index = lax.axis_index("gx")
    slab_index = lax.axis_index("gy")
    shear_step = shear_cells[0]
    (x_high, x_low), (y_high, y_low), (back_high, back_low) = wave_tables()
    shape = jax.ShapeDtypeStruct
    work = {"flops": 2_000_000_000, "bytes_accessed": 8_000_000}

    mine, base, taps, cos_t, sin_t = call(
        prepare_kernel,
        (
            shape((16, ATOM_DEV), f32),
            shape((8, LANES), f32),
            shape((12, PADDED_Z, LANES), f32),
            shape((NX, LANES), f32),
            shape((NX, LANES), f32),
        ),
        in_smem=3,
        inputs=7,
    )(
        jnp.stack([slab_index, pencil_index]),
        shear_cells,
        block_count,
        cell_index,
        offsets,
        charges[None],
        dipoles,
    )
    atoms = lax.all_gather(mine, "gx", axis=0, tiled=False)
    below_atoms = next_slab(atoms)

    own_x = folded(jnp.arange(8, dtype=jnp.int32) * SLABS + slab_index, NX)[None, :]
    own_y = folded(jnp.arange(NY, dtype=jnp.int32), NY)[:, None]
    float_x = own_x.astype(f32)
    wave_y = own_y.astype(f32) + float_x * shear_step.astype(f32) / NX
    norm = (float_x / NX) ** 2 + (wave_y / NY) ** 2
    moduli = spline_modulus(2.0 * math.pi * float_x / NX) * spline_modulus(
        2.0 * math.pi * wave_y / NY
    )
    decay = (math.pi / screening) ** 2
    top = jnp.exp(-decay * norm) / (math.pi * moduli * moduli)
    top = jnp.where((own_x == -(NX // 2)) | (own_y == -(NY // 2)), 0.0, top)
    lane = jnp.arange(LANES, dtype=jnp.int32) % HALF
    mode_z = pencil_index * PART_Z + lane
    kept = lane < PART_Z
    float_z = mode_z.astype(f32)
    norm_z = (float_z / NZ) ** 2
    modulus_z = spline_modulus(2.0 * math.pi * float_z / NZ)
    twice = jnp.where(mode_z == 0, 1.0, 2.0) / (NX * NY * NZ)
    mode_top = jnp.where(kept, twice * jnp.exp(-decay * norm_z) / (modulus_z * modulus_z), 0.0)
    mode_norm = jnp.where(kept, norm_z, 1.0)
    mode = jnp.stack([mode_top, mode_norm])

    waves_shape = shape((PENCILS * PAIRS, 3, 2 * PADDED_Z, LANES), f32)
    packed = shape((SLABS * CARRIERS, LANES), f32)
    own_lines, waves = call(
        lambda *refs: spread_kernel(True, *refs),
        (shape((NX, CY * LANES), f32), waves_shape),
        [pltpu.VMEM((NX + 8, 2 * CY * LANES), f32)],
        **work,
    )(atoms, base, taps, x_high, x_low, cos_t, sin_t)
    lines, below_waves = call(
        lambda *refs: spread_kernel(False, *refs),
        (packed, waves_shape),
        [pltpu.VMEM((NX + 8, 2 * (ROWS - CY) * LANES), f32)],
        **work,
    )(below_atoms, base, taps, x_high, x_low, cos_t, sin_t, own_lines)
    lines = swap_slabs(lines)
    filtered = call(filter_kernel, packed, **work)(
        lines, y_high, y_low, back_high, back_low, top, norm, mode
    )
    filtered = swap_slabs(filtered)
    below_shares = call(
        lambda *refs: sample_kernel(False, *refs),
        shape((PENCILS, 8, ATOM_DEV), f32),
        [pltpu.VMEM((NX + 8, (ROWS - CY) * LANES), f32)],
        **work,
    )(filtered, below_atoms, below_waves, x_high, x_low, cos_t, sin_t)
    below_shares = next_slab(below_shares, back=True)
    shares = call(
        lambda *refs: sample_kernel(True, *refs),
        shape((PENCILS, 8, ATOM_DEV), f32),
        [pltpu.VMEM((NX + 8, CY * LANES), f32)],
        **work,
    )(filtered, atoms, waves, x_high, x_low, cos_t, sin_t)
    shares = lax.all_to_all(shares + below_shares, "gx", split_axis=0, concat_axis=0, tiled=True)
    charge_grad, dipole_grad, position_grad, energy = call(
        finish_kernel,
        (
            shape((1, ATOM_DEV), f32),
            shape((3, ATOM_DEV), f32),
            shape((3, ATOM_DEV), f32),
            shape((1, 1), f32),
        ),
    )(shares)
    return charge_grad[0], dipole_grad, position_grad, energy[0]


def solution(mesh):
    placed = (
        P(None, ("gy", "gx")),
        P(None, ("gy", "gx")),
        P(("gy", "gx")),
        P(None, ("gy", "gx")),
        P(("gy", "gx")),
        P(),
    )
    return jax.shard_map(
        on_device,
        mesh=mesh,
        in_specs=placed,
        out_specs=(P(("gy", "gx")), P(None, ("gy", "gx")), P(None, ("gy", "gx")), P()),
        check_vma=False,
    )
```

```python
import math

import jax
import jax.numpy as jnp
import ml_dtypes
import numpy as np
from jax import lax
from jax.experimental import pallas as pl
from jax.experimental.pallas import tpu as pltpu
from jax.sharding import PartitionSpec as P

NX = 384
NY = 384
NZ = 360
CY = 6
CX = 96
PENCILS = 4
SLABS = 64
PART_X = 6
PART_Z = 45
ATOM_BLK = 64
ATOM_DEV = 384
PAIRS = 3
WINDOW = 40
ROWS = 11
HALF = 64
LANES = 128
PADDED_Z = 48
QUARTER = 96
screening = 0.9
f32 = jnp.float32
bf16 = jnp.bfloat16


def split_table(table):
    high = table.astype(ml_dtypes.bfloat16)
    low = (table - high.astype(np.float64)).astype(ml_dtypes.bfloat16)
    return np.stack([high, low])


def wave_tables():
    quarter = np.arange(QUARTER)
    mode = np.arange(4)[:, None] + 4 * quarter[None, :]
    row_y = CY * (quarter % 16) + quarter // 16
    tables = []
    for place in (quarter, row_y):
        ticks = mode[:, :, None] * place % NX
        for table in (ticks, ticks.transpose(0, 2, 1)):
            angle = 2.0 * np.pi / NX * table.reshape(NX, QUARTER)
            tables.append(split_table(np.concatenate([np.cos(angle), np.sin(angle)], axis=1)))
    return tables


def spline_rows(fraction):
    levels = {2: [1.0 - fraction, fraction]}
    current = levels[2]
    for n in range(3, 7):
        inverse_n = 1.0 / (n - 1)
        updated = [None] * n
        updated[n - 1] = inverse_n * fraction * current[n - 2]
        for j in range(1, n - 1):
            updated[n - 1 - j] = inverse_n * (
                (fraction + j) * current[n - 2 - j] + (n - j - fraction) * current[n - 1 - j]
            )
        updated[0] = inverse_n * (1.0 - fraction) * current[0]
        current = updated
        levels[n] = current
    zero_row = jnp.zeros_like(fraction)

    def entry_at(values_list, k):
        return values_list[k] if 0 <= k < len(values_list) else zero_row

    first = [entry_at(levels[5], t - 1) - entry_at(levels[5], t) for t in range(6)]
    second = [
        entry_at(levels[4], t - 2) - 2.0 * entry_at(levels[4], t - 1) + entry_at(levels[4], t)
        for t in range(6)
    ]
    return levels[6], first, second


def dense_rows(tables, cell, length):
    away = lax.broadcasted_iota(jnp.int32, (length, cell.shape[1]), 0).astype(f32) - cell
    summed = [jnp.zeros(away.shape, f32) for _ in tables]
    for t in range(6):
        here = away == float(t)
        summed = [jnp.where(here, table[t], so_far) for table, so_far in zip(tables, summed)]
    return summed


def unit_phase(turns):
    turns = turns - jnp.floor(turns + 0.5)
    quarter = jnp.floor(4.0 * turns + 0.5)
    rest = turns - 0.25 * quarter
    theta = (2.0 * math.pi) * rest
    square = theta * theta
    sine = theta * (
        1.0
        + square
        * (-1.0 / 6 + square * (1.0 / 120 + square * (-1.0 / 5040 + square * (1.0 / 362880))))
    )
    cosine = 1.0 + square * (
        -0.5
        + square
        * (1.0 / 24 + square * (-1.0 / 720 + square * (1.0 / 40320 - square * (1.0 / 3628800))))
    )
    odd = jnp.abs(quarter) == 1.0
    cos_out = jnp.where(odd, sine, cosine)
    sin_out = jnp.where(odd, cosine, sine)
    cos_out = jnp.where((quarter == 1.0) | (jnp.abs(quarter) == 2.0), -cos_out, cos_out)
    sin_out = jnp.where((quarter == -1.0) | (jnp.abs(quarter) == 2.0), -sin_out, sin_out)
    return cos_out, sin_out


def halves(value):
    high = value.astype(bf16)
    return high, (value - high.astype(f32)).astype(bf16)


def product(left, right, dims=((1,), (0,))):
    def one(a, b):
        return lax.dot_general(a, b, (dims, ((), ())), preferred_element_type=f32)

    return one(left[0], right[0]) + (one(left[0], right[1]) + one(left[1], right[0]))


def lane_sign(shape):
    return jnp.where(lax.broadcasted_iota(jnp.int32, shape, 1) < HALF, 1.0, -1.0).astype(f32)


def turned(value, sign):
    return pltpu.roll(value, HALF, 1) * sign


def fetch(source, target, semaphore):
    copy = pltpu.make_async_copy(source, target, semaphore)
    copy.start()
    return copy


def table_rows(table_ref, r):
    rows = slice(r * QUARTER, (r + 1) * QUARTER)
    return table_ref[0, rows], table_ref[1, rows]


def forward_line(table_ref, quarters, turned_quarters):
    g, h = quarters, turned_quarters
    a, b, c, d = g[0] + g[2], g[0] - g[2], g[1] + g[3], g[1] - g[3]
    ta, tb, tc, td = h[0] + h[2], h[0] - h[2], h[1] + h[3], h[1] - h[3]
    lines = []
    for r, (one, other) in enumerate(
        ((a + c, ta + tc), (b + td, tb - d), (a - c, ta - tc), (b - td, tb + d))
    ):
        stacked = jnp.concatenate([one, other], axis=0)
        lines.append(product(table_rows(table_ref, r), halves(stacked)))
    return lines


def inverse_line(table_ref, modes, turned_modes):
    z = []
    for r in range(4):
        stacked = jnp.concatenate([modes[r], -turned_modes[r]], axis=0)
        z.append(product(table_rows(table_ref, r), halves(stacked)))
    a, b, c, d = z[0] + z[2], z[0] - z[2], z[1] + z[3], z[1] - z[3]
    width = d.shape[1]
    sign = lane_sign((QUARTER, LANES))
    td = jnp.concatenate(
        [turned(d[:, n : n + LANES], sign) for n in range(0, width, LANES)], axis=1
    )
    return [a + c, b - td, a - c, b + td]


def quarters_of(value):
    return [value[r * QUARTER : (r + 1) * QUARTER] for r in range(4)]


PIECES = (0, 16, 32, 64, 80, 96)
GROUPS = PART_X * CY // 4
CARRIERS = 3 * GROUPS


def lane_range(first):
    lane = lax.broadcasted_iota(jnp.int32, (SLABS, LANES), 1)
    return (lane >= first) & (lane < first + 16)


def pack_blocks(blocks):
    carriers = []
    for c in range(3):
        value = blocks[c]
        for half in range(2):
            gap = PADDED_Z + half * HALF
            shift = (gap - PIECES[2 * c + half]) % LANES
            value = jnp.where(lane_range(gap), pltpu.roll(blocks[3], shift, 1), value)
        carriers.append(value)
    return carriers


def unpack_block(carriers):
    value = jnp.zeros((SLABS, LANES), f32)
    for p, source in enumerate(PIECES):
        gap = PADDED_Z + p % 2 * HALF
        shift = (source - gap) % LANES
        value = jnp.where(lane_range(source), pltpu.roll(carriers[p // 2], shift, 1), value)
    return value


def rows_of(carrier):
    return pl.ds(carrier, SLABS, stride=CARRIERS)


def block_at(ref, j, y):
    block = j * CY + y
    group, place = block // 4, block % 4
    if place < 3:
        return ref[rows_of(3 * group + place), :]
    return unpack_block([ref[rows_of(3 * group + c), :] for c in range(3)])


def prepare_kernel(
    where_ref, shear_ref, counts_ref, cells_ref, offsets_ref, charges_ref, dipoles_ref,
    atoms_ref, base_ref, taps_ref, cos_ref, sin_ref,
    count_ref, cell_ref, offset_ref, charge_ref, dipole_ref, semaphores
):
    copies = [
        fetch(source, target, semaphores.at[n])
        for n, (source, target) in enumerate(
            (
                (counts_ref, count_ref),
                (cells_ref, cell_ref),
                (offsets_ref, offset_ref),
                (charges_ref, charge_ref),
                (dipoles_ref, dipole_ref),
            )
        )
    ]
    slab, pencil = where_ref[0], where_ref[1]
    first = pencil * PART_Z
    row = lax.broadcasted_iota(jnp.int32, (PADDED_Z, LANES), 0)
    mode = (row + first).astype(f32)
    base_ref[...] = mode[:8]
    for t in range(6):
        cos_t, sin_t = unit_phase(mode * float(t) * (1.0 / NZ))
        taps_ref[t] = jnp.where(row < PART_Z, cos_t, 0.0)
        taps_ref[6 + t] = jnp.where(row < PART_Z, sin_t, 0.0)
    column = lax.broadcasted_iota(jnp.int32, (1, LANES), 1)
    above = jnp.where(slab == 0, SLABS - 1, slab - 1) * CY
    rows = jnp.where(column < CY, slab * CY, above) + jnp.minimum(column, ROWS)
    index = lax.broadcasted_iota(jnp.int32, (NX, LANES), 0)
    residue = (
        (index >= QUARTER).astype(jnp.int32)
        + (index >= 2 * QUARTER).astype(jnp.int32)
        + (index >= 3 * QUARTER).astype(jnp.int32)
    )
    mode_x = 4 * (index - QUARTER * residue) + residue
    folds = jnp.where(mode_x < NX // 2, mode_x, mode_x - NX)
    ticks = folds * (shear_ref[0] * rows)
    whole = jnp.floor(ticks.astype(f32) * (1.0 / (NX * NY))).astype(jnp.int32)
    rest = ticks - whole * (NX * NY)
    cos_t, sin_t = unit_phase(rest.astype(f32) * (1.0 / (NX * NY)))
    cos_ref[...] = cos_t
    sin_ref[...] = sin_t
    for copy in copies:
        copy.wait()
    slot = lax.broadcasted_iota(jnp.int32, (1, ATOM_DEV), 1)
    live = jnp.zeros((1, ATOM_DEV), f32)
    for b in range(ATOM_DEV // ATOM_BLK):
        inside = (slot >= b * ATOM_BLK) & (slot < b * ATOM_BLK + count_ref[b])
        live = jnp.where(inside, 1.0, live)
    atoms_ref[0:1, :] = cell_ref[0:1, :].astype(f32)
    atoms_ref[1:2, :] = (cell_ref[1:2, :] - slab * CY).astype(f32)
    atoms_ref[2:3, :] = cell_ref[2:3, :].astype(f32)
    atoms_ref[3:6, :] = offset_ref[...]
    atoms_ref[6:7, :] = charge_ref[...] * live
    atoms_ref[7:10, :] = dipole_ref[...] * live
    atoms_ref[10:11, :] = live
    atoms_ref[11:16, :] = jnp.zeros((5, ATOM_DEV), f32)


def spread_kernel(own, *refs):
    atoms_ref, base_ref, taps_ref, tables_ref, cos_ref, sin_ref = refs[:6]
    out_ref, waves_out_ref, grid_ref, table_ref, waves_ref, semaphores = refs[-6:]
    lines_ref = None if own else refs[6]
    table_copy = fetch(tables_ref, table_ref, semaphores.at[0])
    grid_ref[...] = jnp.zeros_like(grid_ref)
    rows = list(range(CY)) if own else list(range(CY, ROWS))
    part = len(rows) * LANES
    gap = jnp.zeros((HALF - PADDED_Z, LANES), f32)

    def pencil_body(pencil, carry):
        for i in range(PAIRS):
            atoms = atoms_ref[pencil, :, i * LANES : (i + 1) * LANES]
            row = [atoms[a : a + 1] for a in range(10)]
            weights = [spline_rows(row[3 + a]) for a in range(3)]
            charge, dip_x, dip_y, dip_z = row[6:10]
            window = pencil * CX + i * 32
            dense_x = dense_rows(weights[0][:2], row[0] - window.astype(f32), WINDOW)
            dense_y = dense_rows(weights[1][:2], row[1], 16)
            cell_z = row[2]
            turn = base_ref[...] * cell_z
            turn = turn - 360.0 * jnp.floor(turn * (1.0 / 360.0))
            cos_k, sin_k = unit_phase(turn * (1.0 / 360.0))
            turn = 8.0 * cell_z
            turn = turn - 360.0 * jnp.floor(turn * (1.0 / 360.0))
            cos_8, sin_8 = unit_phase(turn * (1.0 / 360.0))
            pieces = [[], [], []]
            pieces_im = [[], [], []]
            for q in range(PADDED_Z // 8):
                span = slice(q * 8, q * 8 + 8)
                for s in range(3):
                    real = sum(weights[2][s][t] * taps_ref[t, span, :] for t in range(6))
                    imag = sum(weights[2][s][t] * taps_ref[6 + t, span, :] for t in range(6))
                    pieces[s].append(real * cos_k - imag * sin_k)
                    pieces_im[s].append(-(real * sin_k + imag * cos_k))
                cos_k, sin_k = cos_k * cos_8 - sin_k * sin_8, sin_k * cos_8 + cos_k * sin_8
            re = [jnp.concatenate(pieces[s], axis=0) for s in range(3)]
            im = [jnp.concatenate(pieces_im[s], axis=0) for s in range(3)]
            pair = pencil * PAIRS + i
            for s in range(3):
                waves_ref[pair, s, :PADDED_Z] = re[s]
                waves_ref[pair, s, PADDED_Z:] = im[s]
            full = []
            for wave_re, wave_im in (
                (charge * re[0] + dip_z * re[1], charge * im[0] + dip_z * im[1]),
                (re[0], im[0]),
            ):
                full.append(
                    jnp.concatenate(
                        [wave_re, gap, wave_im, gap, wave_im, gap, -wave_re, gap], axis=0
                    )
                )
            right = jnp.concatenate(full, axis=1)
            left = []
            for r in rows:
                value = dense_y[0][r : r + 1]
                first = dense_y[1][r : r + 1]
                left.append(
                    jnp.concatenate(
                        [
                            value * dense_x[0],
                            (dip_x * value) * dense_x[1] + (dip_y * first) * dense_x[0],
                        ],
                        axis=1,
                    )
                )
            left = jnp.concatenate(left, axis=0)
            added = product(halves(left), halves(right), ((1,), (1,)))
            at = pl.ds(pl.multiple_of(window, 8), WINDOW)
            for n in range(len(rows)):
                piece = added[n * WINDOW : (n + 1) * WINDOW]
                grid_ref[at, n * LANES : (n + 1) * LANES] += piece[:, :LANES]
                grid_ref[at, part + n * LANES : part + (n + 1) * LANES] += piece[:, LANES:]
        return carry

    lax.fori_loop(0, PENCILS, pencil_body, 0)
    grid_ref[0:8] += grid_ref[NX : NX + 8]
    waves_copy = fetch(waves_ref, waves_out_ref, semaphores.at[1])
    table_copy.wait()
    sign = lane_sign((NX, LANES))
    totals = []
    for first in range(0, len(rows), 2):
        lanes = slice(first * LANES, min(first + 2, len(rows)) * LANES)
        below = slice(part + lanes.start, part + lanes.stop)
        line = jnp.concatenate(
            forward_line(
                table_ref, quarters_of(grid_ref[:NX, lanes]), quarters_of(grid_ref[:NX, below])
            ),
            axis=0,
        )
        for n, r in enumerate(rows[first : first + 2]):
            one = line[:, n * LANES : (n + 1) * LANES]
            total = one * cos_ref[:, r : r + 1] + turned(one, sign) * sin_ref[:, r : r + 1]
            y = first + n
            if own:
                out_ref[:, y * LANES : (y + 1) * LANES] = total
            else:
                totals.append(total + lines_ref[:, y * LANES : (y + 1) * LANES])
    if own:
        waves_copy.wait()
        return
    totals.append(lines_ref[:, (CY - 1) * LANES :])
    for group in range(GROUPS):
        blocks = []
        for block in range(4 * group, 4 * group + 4):
            j, y = block // CY, block % CY
            blocks.append(totals[y][j * SLABS : (j + 1) * SLABS])
        for c, carrier in enumerate(pack_blocks(blocks)):
            out_ref[rows_of(3 * group + c), :] = carrier
    waves_copy.wait()


def filter_kernel(
    in_ref, tables_ref, backs_ref, top_ref, norm_ref, mode_ref, out_ref, table_ref, back_ref, semaphores
):
    copies = [
        fetch(tables_ref, table_ref, semaphores.at[0]),
        fetch(backs_ref, back_ref, semaphores.at[1]),
    ]
    sign = lane_sign((NY, LANES))
    energy = jnp.zeros((8, LANES), f32)
    blocks = []
    for first in range(0, PART_X, 2):
        lines = []
        for j in (first, first + 1):
            found = [block_at(in_ref, j, y) for y in range(CY)]
            lines.append(
                jnp.concatenate(
                    [one[16 * part : 16 * part + 16] for part in range(4) for one in found], axis=0
                )
            )
        swapped = jnp.concatenate([turned(one, sign) for one in lines], axis=1)
        lines = jnp.concatenate(lines, axis=1)
        if first == 0:
            copies[0].wait()
        spectrum = jnp.concatenate(
            forward_line(table_ref, quarters_of(lines), quarters_of(swapped)), axis=0
        )
        modes = []
        for n in range(2):
            j = first + n
            one = spectrum[:, n * LANES : (n + 1) * LANES]
            square = norm_ref[:, j : j + 1] + mode_ref[1:2, :]
            green = top_ref[:, j : j + 1] * mode_ref[0:1, :] / jnp.where(square == 0.0, 1.0, square)
            green = jnp.where(square == 0.0, 0.0, green)
            scaled = green * one
            share = scaled * one
            energy = energy + sum(share[8 * i : 8 * i + 8] for i in range(NY // 8))
            modes.append(scaled)
        swapped = jnp.concatenate([turned(one, sign) for one in modes], axis=1)
        modes = jnp.concatenate(modes, axis=1)
        if first == 0:
            copies[1].wait()
        parts = inverse_line(back_ref, quarters_of(modes), quarters_of(swapped))
        for n in range(2):
            for y in range(CY):
                blocks.append(
                    jnp.concatenate(
                        [
                            one[16 * y : 16 * y + 16, n * LANES : (n + 1) * LANES]
                            for one in parts
                        ],
                        axis=0,
                    )
                )
        for group in range(first * CY // 4, (first + 2) * CY // 4):
            for c, carrier in enumerate(pack_blocks(blocks[4 * group : 4 * group + 4])):
                out_ref[rows_of(3 * group + c), :] = carrier
    lane = lax.broadcasted_iota(jnp.int32, (SLABS, LANES), 1)
    share = 0.5 * jnp.sum(energy)
    out_ref[rows_of(0), :] = jnp.where(lane == PART_Z, share, out_ref[rows_of(0), :])


def sample_kernel(
    own, in_ref, atoms_ref, waves_in_ref, tables_ref, cos_ref, sin_ref, out_ref,
    grid_ref, table_ref, waves_ref, semaphores
):
    table_copy = fetch(tables_ref, table_ref, semaphores.at[0])
    waves_copy = fetch(waves_in_ref, waves_ref, semaphores.at[1])
    sign = lane_sign((NX, LANES))
    rows = list(range(CY)) if own else list(range(CY, ROWS))
    for first in range(0, len(rows), 2):
        modes = []
        for y in range(first, min(first + 2, len(rows))):
            line = jnp.concatenate([block_at(in_ref, j, y) for j in range(PART_X)], axis=0)
            r = rows[y]
            modes.append(line * cos_ref[:, r : r + 1] - turned(line, sign) * sin_ref[:, r : r + 1])
        swapped = jnp.concatenate([turned(one, sign) for one in modes], axis=1)
        stacked = modes
        modes = jnp.concatenate(modes, axis=1)
        if first == 0:
            table_copy.wait()
        cells = jnp.concatenate(
            inverse_line(table_ref, quarters_of(modes), quarters_of(swapped)), axis=0
        )
        lanes = slice(first * LANES, (first + len(stacked)) * LANES)
        grid_ref[:NX, lanes] = cells
        grid_ref[NX:, lanes] = cells[:8]
    gap = jnp.zeros((HALF - PADDED_Z, LANES), f32)
    if own:
        lane = lax.broadcasted_iota(jnp.int32, (SLABS, LANES), 1)
        energy = jnp.sum(jnp.where(lane == PART_Z, in_ref[rows_of(0), :], 0.0))
    else:
        energy = 0.0

    waves_copy.wait()

    def pencil_body(pencil, carry):
        for i in range(PAIRS):
            lanes = slice(i * LANES, (i + 1) * LANES)
            atoms = atoms_ref[pencil, :, lanes]
            row = [atoms[a : a + 1] for a in range(11)]
            weights = [spline_rows(row[3 + a]) for a in range(2)]
            window = pencil * CX + i * 32
            dense_x = dense_rows(weights[0], row[0] - window.astype(f32), WINDOW)
            dense_y = dense_rows(weights[1], row[1], 16)
            pair = pencil * PAIRS + i
            waves = jnp.concatenate(
                [
                    jnp.concatenate(
                        [waves_ref[pair, s, :PADDED_Z], gap, waves_ref[pair, s, PADDED_Z:], gap],
                        axis=0,
                    )
                    for s in range(3)
                ],
                axis=1,
            )
            at = pl.ds(pl.multiple_of(window, 8), WINDOW)
            cells = jnp.concatenate(
                [grid_ref[at, n * LANES : (n + 1) * LANES] for n in range(len(rows))], axis=0
            )
            read = product(halves(cells), halves(waves))
            lined = {}
            for order_y, order_z in ((0, 0), (1, 0), (2, 0), (0, 1), (1, 1), (0, 2)):
                lined[order_y, order_z] = sum(
                    dense_y[order_y][r : r + 1]
                    * read[n * WINDOW : (n + 1) * WINDOW, order_z * LANES : (order_z + 1) * LANES]
                    for n, r in enumerate(rows)
                )

            def sampled(p, r, s):
                return jnp.sum(dense_x[p] * lined[r, s], axis=0, keepdims=True)

            charge, dip_x, dip_y, dip_z, live = row[6:11]
            s100 = sampled(1, 0, 0)
            s010 = sampled(0, 1, 0)
            s001 = sampled(0, 0, 1)
            s110 = sampled(1, 1, 0)
            s101 = sampled(1, 0, 1)
            s011 = sampled(0, 1, 1)
            out = [
                live * sampled(0, 0, 0),
                live * s100,
                live * s010,
                live * s001,
                charge * s100 + dip_x * sampled(2, 0, 0) + dip_y * s110 + dip_z * s101,
                charge * s010 + dip_x * s110 + dip_y * sampled(0, 2, 0) + dip_z * s011,
                charge * s001 + dip_x * s101 + dip_y * s011 + dip_z * sampled(0, 0, 2),
                jnp.full(live.shape, energy, f32),
            ]
            out_ref[pencil, :, lanes] = jnp.concatenate(out, axis=0)
        return carry

    lax.fori_loop(0, PENCILS, pencil_body, 0)


def finish_kernel(in_ref, charge_ref, dipole_ref, position_ref, energy_ref):
    total = (in_ref[0] + in_ref[1]) + (in_ref[2] + in_ref[3])
    charge_ref[...] = total[0:1]
    dipole_ref[...] = total[1:4]
    position_ref[...] = total[4:7]
    energy_ref[...] = total[7:8, 0:1]


def spline_modulus(angles):
    return (66.0 + 52.0 * jnp.cos(angles) + 2.0 * jnp.cos(2.0 * angles)) / 120.0


def mode_of(row):
    return 4 * (row % QUARTER) + row // QUARTER


def folded(index, size):
    return (index + size // 2) % size - size // 2


SPACES = {"v": pltpu.VMEM, "h": pltpu.HBM, "s": pltpu.SMEM}
WORK = {"flops": 1_000_000_000, "bytes_accessed": 8_000_000}


def call(kernel, inputs, outputs, out_shape, scratch=()):
    return pl.pallas_call(
        kernel,
        out_shape=out_shape,
        in_specs=[pl.BlockSpec(memory_space=SPACES[one]) for one in inputs],
        out_specs=tuple(pl.BlockSpec(memory_space=SPACES[one]) for one in outputs),
        scratch_shapes=list(scratch),
        compiler_params=pltpu.CompilerParams(vmem_limit_bytes=32 * 1024 * 1024),
        cost_estimate=pl.CostEstimate(transcendentals=0, **WORK),
    )


def next_slab(value, back=False):
    step = -1 if back else 1
    return lax.ppermute(value, "gy", [(i, (i + step) % SLABS) for i in range(SLABS)])


def swap_slabs(lines):
    lines = lines.reshape(SLABS, CARRIERS, 1, LANES)
    lines = lax.all_to_all(lines, "gy", split_axis=0, concat_axis=0, tiled=True)
    return lines.reshape(SLABS * CARRIERS, LANES)


def on_device(cell_index, offsets, charges, dipoles, block_count, shear_cells):
    pencil_index = lax.axis_index("gx")
    slab_index = lax.axis_index("gy")
    shear_step = shear_cells[0]
    x_forward, x_inverse, y_forward, y_inverse = wave_tables()
    shape = jax.ShapeDtypeStruct

    mine, base, taps, cos_t, sin_t = call(
        prepare_kernel,
        "sshhhhh",
        "vvvvv",
        (
            shape((16, ATOM_DEV), f32),
            shape((8, LANES), f32),
            shape((12, PADDED_Z, LANES), f32),
            shape((NX, LANES), f32),
            shape((NX, LANES), f32),
        ),
        [
            pltpu.SMEM(block_count.shape, jnp.int32),
            pltpu.VMEM((3, ATOM_DEV), jnp.int32),
            pltpu.VMEM((3, ATOM_DEV), f32),
            pltpu.VMEM((1, ATOM_DEV), f32),
            pltpu.VMEM((3, ATOM_DEV), f32),
            pltpu.SemaphoreType.DMA((5,)),
        ],
    )(
        jnp.stack([slab_index, pencil_index]),
        shear_cells,
        block_count,
        cell_index,
        offsets,
        charges[None],
        dipoles,
    )
    atoms = lax.all_gather(mine, "gx", axis=0, tiled=False)
    below_atoms = next_slab(atoms)

    own_x = folded(mode_of(jnp.arange(8, dtype=jnp.int32) * SLABS + slab_index), NX)[None, :]
    own_y = folded(mode_of(jnp.arange(NY, dtype=jnp.int32)), NY)[:, None]
    float_x = own_x.astype(f32)
    wave_y = own_y.astype(f32) + float_x * shear_step.astype(f32) / NX
    norm = (float_x / NX) ** 2 + (wave_y / NY) ** 2
    moduli = spline_modulus(2.0 * math.pi * float_x / NX) * spline_modulus(
        2.0 * math.pi * wave_y / NY
    )
    decay = (math.pi / screening) ** 2
    top = jnp.exp(-decay * norm) / (math.pi * moduli * moduli)
    top = jnp.where((own_x == -(NX // 2)) | (own_y == -(NY // 2)), 0.0, top)
    lane = jnp.arange(LANES, dtype=jnp.int32) % HALF
    mode_z = pencil_index * PART_Z + lane
    kept = lane < PART_Z
    float_z = mode_z.astype(f32)
    norm_z = (float_z / NZ) ** 2
    modulus_z = spline_modulus(2.0 * math.pi * float_z / NZ)
    twice = jnp.where(mode_z == 0, 1.0, 2.0) / (NX * NY * NZ)
    mode_top = jnp.where(kept, twice * jnp.exp(-decay * norm_z) / (modulus_z * modulus_z), 0.0)
    mode_norm = jnp.where(kept, norm_z, 1.0)
    mode = jnp.stack([mode_top, mode_norm])

    waves_shape = shape((PENCILS * PAIRS, 3, 2 * PADDED_Z, LANES), f32)
    packed = shape((SLABS * CARRIERS, LANES), f32)
    table_space = pltpu.VMEM((2, NX, 2 * QUARTER), bf16)
    waves_space = pltpu.VMEM(waves_shape.shape, f32)
    two = pltpu.SemaphoreType.DMA((2,))
    own_lines, waves = call(
        lambda *refs: spread_kernel(True, *refs),
        "vvvhvv",
        "vh",
        (shape((NX, CY * LANES), f32), waves_shape),
        [pltpu.VMEM((NX + 8, 2 * CY * LANES), f32), table_space, waves_space, two],
    )(atoms, base, taps, x_forward, cos_t, sin_t)
    lines, below_waves = call(
        lambda *refs: spread_kernel(False, *refs),
        "vvvhvvv",
        "vh",
        (packed, waves_shape),
        [pltpu.VMEM((NX + 8, 2 * (ROWS - CY) * LANES), f32), table_space, waves_space, two],
    )(below_atoms, base, taps, x_forward, cos_t, sin_t, own_lines)
    lines = swap_slabs(lines)
    (filtered,) = call(filter_kernel, "vhhvvv", "v", (packed,), [table_space, table_space, two])(
        lines, y_forward, y_inverse, top, norm, mode
    )
    filtered = swap_slabs(filtered)
    shares_shape = shape((PENCILS, 8, ATOM_DEV), f32)
    (below_shares,) = call(
        lambda *refs: sample_kernel(False, *refs),
        "vvhhvv",
        "v",
        (shares_shape,),
        [pltpu.VMEM((NX + 8, (ROWS - CY) * LANES), f32), table_space, waves_space, two],
    )(filtered, below_atoms, below_waves, x_inverse, cos_t, sin_t)
    below_shares = next_slab(below_shares, back=True)
    (shares,) = call(
        lambda *refs: sample_kernel(True, *refs),
        "vvhhvv",
        "v",
        (shares_shape,),
        [pltpu.VMEM((NX + 8, CY * LANES), f32), table_space, waves_space, two],
    )(filtered, atoms, waves, x_inverse, cos_t, sin_t)
    shares = lax.all_to_all(shares + below_shares, "gx", split_axis=0, concat_axis=0, tiled=True)
    charge_grad, dipole_grad, position_grad, energy = call(
        finish_kernel,
        "v",
        "vvvv",
        (
            shape((1, ATOM_DEV), f32),
            shape((3, ATOM_DEV), f32),
            shape((3, ATOM_DEV), f32),
            shape((1, 1), f32),
        ),
    )(shares)
    return charge_grad[0], dipole_grad, position_grad, energy[0]


def solution(mesh):
    placed = (
        P(None, ("gy", "gx")),
        P(None, ("gy", "gx")),
        P(("gy", "gx")),
        P(None, ("gy", "gx")),
        P(("gy", "gx")),
        P(),
    )
    return jax.shard_map(
        on_device,
        mesh=mesh,
        in_specs=placed,
        out_specs=(P(("gy", "gx")), P(None, ("gy", "gx")), P(None, ("gy", "gx")), P()),
        check_vma=False,
    )
```

```python
import math

import jax
import jax.numpy as jnp
import ml_dtypes
import numpy as np
from jax import lax
from jax.experimental import pallas as pl
from jax.experimental.pallas import tpu as pltpu
from jax.sharding import PartitionSpec as P

NX = 384
NY = 384
NZ = 360
CY = 6
CX = 96
PENCILS = 4
SLABS = 64
PART_X = 6
PART_Z = 45
ATOM_BLK = 64
ATOM_DEV = 384
PAIRS = 3
WINDOW = 40
ROWS = 11
HALF = 64
LANES = 128
PADDED_Z = 48
QUARTER = 96
screening = 0.9
f32 = jnp.float32
bf16 = jnp.bfloat16


def split_table(table):
    high = table.astype(ml_dtypes.bfloat16)
    low = (table - high.astype(np.float64)).astype(ml_dtypes.bfloat16)
    return np.concatenate([high, high, low], axis=1)


def wave_tables():
    quarter = np.arange(QUARTER)
    mode = np.arange(4)[:, None] + 4 * quarter[None, :]
    row_y = CY * (quarter % 16) + quarter // 16
    tables = []
    for place in (quarter, row_y):
        ticks = mode[:, :, None] * place % NX
        for table in (ticks, ticks.transpose(0, 2, 1)):
            angle = 2.0 * np.pi / NX * table.reshape(NX, QUARTER)
            tables.append(split_table(np.concatenate([np.cos(angle), np.sin(angle)], axis=1)))
    return tables


def spline_rows(fraction):
    levels = {2: [1.0 - fraction, fraction]}
    current = levels[2]
    for n in range(3, 7):
        inverse_n = 1.0 / (n - 1)
        updated = [None] * n
        updated[n - 1] = inverse_n * fraction * current[n - 2]
        for j in range(1, n - 1):
            updated[n - 1 - j] = inverse_n * (
                (fraction + j) * current[n - 2 - j] + (n - j - fraction) * current[n - 1 - j]
            )
        updated[0] = inverse_n * (1.0 - fraction) * current[0]
        current = updated
        levels[n] = current
    zero_row = jnp.zeros_like(fraction)

    def entry_at(values_list, k):
        return values_list[k] if 0 <= k < len(values_list) else zero_row

    first = [entry_at(levels[5], t - 1) - entry_at(levels[5], t) for t in range(6)]
    second = [
        entry_at(levels[4], t - 2) - 2.0 * entry_at(levels[4], t - 1) + entry_at(levels[4], t)
        for t in range(6)
    ]
    return levels[6], first, second


def dense_rows(tables, cell, length):
    away = lax.broadcasted_iota(jnp.int32, (length, cell.shape[1]), 0).astype(f32) - cell
    summed = [jnp.zeros(away.shape, f32) for _ in tables]
    for t in range(6):
        here = away == float(t)
        summed = [jnp.where(here, table[t], so_far) for table, so_far in zip(tables, summed)]
    return summed


def unit_phase(turns):
    turns = turns - jnp.floor(turns + 0.5)
    quarter = jnp.floor(4.0 * turns + 0.5)
    rest = turns - 0.25 * quarter
    theta = (2.0 * math.pi) * rest
    square = theta * theta
    sine = theta * (
        1.0
        + square
        * (-1.0 / 6 + square * (1.0 / 120 + square * (-1.0 / 5040 + square * (1.0 / 362880))))
    )
    cosine = 1.0 + square * (
        -0.5
        + square
        * (1.0 / 24 + square * (-1.0 / 720 + square * (1.0 / 40320 - square * (1.0 / 3628800))))
    )
    odd = jnp.abs(quarter) == 1.0
    cos_out = jnp.where(odd, sine, cosine)
    sin_out = jnp.where(odd, cosine, sine)
    cos_out = jnp.where((quarter == 1.0) | (jnp.abs(quarter) == 2.0), -cos_out, cos_out)
    sin_out = jnp.where((quarter == -1.0) | (jnp.abs(quarter) == 2.0), -sin_out, sin_out)
    return cos_out, sin_out


def halves(value):
    high = value.astype(bf16)
    return high, (value - high.astype(f32)).astype(bf16)


def joined(left, right):
    return (
        jnp.concatenate([left[0], left[0], left[1]], axis=1),
        jnp.concatenate([right[0], right[1], right[0]], axis=0),
    )


def product(left, right):
    left, right = joined(left, right)
    return jnp.dot(left, right, preferred_element_type=f32)


def product3(left, right):
    def one(a, b):
        return jnp.dot(a, b, preferred_element_type=f32)

    return one(left[0], right[0]) + (one(left[0], right[1]) + one(left[1], right[0]))


def lane_sign(shape):
    return jnp.where(lax.broadcasted_iota(jnp.int32, shape, 1) < HALF, 1.0, -1.0).astype(f32)


def turned(value, sign):
    return pltpu.roll(value, HALF, 1) * sign


def fetch(source, target, semaphore):
    copy = pltpu.make_async_copy(source, target, semaphore)
    copy.start()
    return copy


def line_product(table_ref, r, value):
    rows = slice(r * QUARTER, (r + 1) * QUARTER)
    table = table_ref[rows, : 2 * QUARTER], table_ref[rows, 4 * QUARTER :]
    return product3(table, halves(value))


def forward_line(table_ref, quarters, turned_quarters):
    g, h = quarters, turned_quarters
    a, b, c, d = g[0] + g[2], g[0] - g[2], g[1] + g[3], g[1] - g[3]
    ta, tb, tc, td = h[0] + h[2], h[0] - h[2], h[1] + h[3], h[1] - h[3]
    lines = []
    for r, (one, other) in enumerate(
        ((a + c, ta + tc), (b + td, tb - d), (a - c, ta - tc), (b - td, tb + d))
    ):
        stacked = jnp.concatenate([one, other], axis=0)
        lines.append(line_product(table_ref, r, stacked))
    return lines


def inverse_line(table_ref, modes, turned_modes):
    z = []
    for r in range(4):
        stacked = jnp.concatenate([modes[r], -turned_modes[r]], axis=0)
        z.append(line_product(table_ref, r, stacked))
    a, b, c, d = z[0] + z[2], z[0] - z[2], z[1] + z[3], z[1] - z[3]
    width = d.shape[1]
    sign = lane_sign((QUARTER, LANES))
    td = jnp.concatenate(
        [turned(d[:, n : n + LANES], sign) for n in range(0, width, LANES)], axis=1
    )
    return [a + c, b - td, a - c, b + td]


def quarters_of(value):
    return [value[r * QUARTER : (r + 1) * QUARTER] for r in range(4)]


PIECES = (0, 16, 32, 64, 80, 96)
GROUPS = PART_X * CY // 4
CARRIERS = 3 * GROUPS


def lane_range(first):
    lane = lax.broadcasted_iota(jnp.int32, (SLABS, LANES), 1)
    return (lane >= first) & (lane < first + 16)


def pack_blocks(blocks):
    carriers = []
    for c in range(3):
        value = blocks[c]
        for half in range(2):
            gap = PADDED_Z + half * HALF
            shift = (gap - PIECES[2 * c + half]) % LANES
            value = jnp.where(lane_range(gap), pltpu.roll(blocks[3], shift, 1), value)
        carriers.append(value)
    return carriers


def unpack_block(carriers):
    value = jnp.zeros((SLABS, LANES), f32)
    for p, source in enumerate(PIECES):
        gap = PADDED_Z + p % 2 * HALF
        shift = (source - gap) % LANES
        value = jnp.where(lane_range(source), pltpu.roll(carriers[p // 2], shift, 1), value)
    return value


def rows_of(carrier):
    return pl.ds(carrier, SLABS, stride=CARRIERS)


def block_at(ref, j, y):
    block = j * CY + y
    group, place = block // 4, block % 4
    if place < 3:
        return ref[rows_of(3 * group + place), :]
    return unpack_block([ref[rows_of(3 * group + c), :] for c in range(3)])


def prepare_kernel(
    where_ref, shear_ref, counts_ref, cells_ref, offsets_ref, charges_ref, dipoles_ref,
    atoms_ref, base_ref, taps_ref, cos_ref, sin_ref,
    count_ref, cell_ref, offset_ref, charge_ref, dipole_ref, semaphores
):
    copies = [
        fetch(source, target, semaphores.at[n])
        for n, (source, target) in enumerate(
            (
                (counts_ref, count_ref),
                (cells_ref, cell_ref),
                (offsets_ref, offset_ref),
                (charges_ref, charge_ref),
                (dipoles_ref, dipole_ref),
            )
        )
    ]
    slab, pencil = where_ref[0], where_ref[1]
    first = pencil * PART_Z
    row = lax.broadcasted_iota(jnp.int32, (PADDED_Z, LANES), 0)
    mode = (row + first).astype(f32)
    base_ref[...] = mode[:8]
    for t in range(6):
        cos_t, sin_t = unit_phase(mode * float(t) * (1.0 / NZ))
        taps_ref[t] = jnp.where(row < PART_Z, cos_t, 0.0)
        taps_ref[6 + t] = jnp.where(row < PART_Z, sin_t, 0.0)
    column = lax.broadcasted_iota(jnp.int32, (1, LANES), 1)
    above = jnp.where(slab == 0, SLABS - 1, slab - 1) * CY
    rows = jnp.where(column < CY, slab * CY, above) + jnp.minimum(column, ROWS)
    index = lax.broadcasted_iota(jnp.int32, (NX, LANES), 0)
    residue = (
        (index >= QUARTER).astype(jnp.int32)
        + (index >= 2 * QUARTER).astype(jnp.int32)
        + (index >= 3 * QUARTER).astype(jnp.int32)
    )
    mode_x = 4 * (index - QUARTER * residue) + residue
    folds = jnp.where(mode_x < NX // 2, mode_x, mode_x - NX)
    ticks = folds * (shear_ref[0] * rows)
    whole = jnp.floor(ticks.astype(f32) * (1.0 / (NX * NY))).astype(jnp.int32)
    rest = ticks - whole * (NX * NY)
    cos_t, sin_t = unit_phase(rest.astype(f32) * (1.0 / (NX * NY)))
    cos_ref[...] = cos_t
    sin_ref[...] = sin_t
    for copy in copies:
        copy.wait()
    slot = lax.broadcasted_iota(jnp.int32, (1, ATOM_DEV), 1)
    live = jnp.zeros((1, ATOM_DEV), f32)
    for b in range(ATOM_DEV // ATOM_BLK):
        inside = (slot >= b * ATOM_BLK) & (slot < b * ATOM_BLK + count_ref[b])
        live = jnp.where(inside, 1.0, live)
    atoms_ref[0:1, :] = cell_ref[0:1, :].astype(f32)
    atoms_ref[1:2, :] = (cell_ref[1:2, :] - slab * CY).astype(f32)
    atoms_ref[2:3, :] = cell_ref[2:3, :].astype(f32)
    atoms_ref[3:6, :] = offset_ref[...]
    atoms_ref[6:7, :] = charge_ref[...] * live
    atoms_ref[7:10, :] = dipole_ref[...] * live
    atoms_ref[10:11, :] = live
    atoms_ref[11:16, :] = jnp.zeros((5, ATOM_DEV), f32)


def spline_table(atoms_ref, table_ref, orders):
    def pencil_body(pencil, carry):
        tables = spline_rows(atoms_ref[pencil, 3:6, :])
        for o in range(orders):
            for t in range(6):
                table_ref[pencil, o * 6 + t, 0:3, :] = tables[o][t]
        return carry

    lax.fori_loop(0, PENCILS, pencil_body, 0)


def weight_rows(table_ref, pencil, lanes, dim, orders):
    row = slice(dim, dim + 1)
    return [[table_ref[pencil, o * 6 + t, row, lanes] for t in range(6)] for o in range(orders)]


def pair_place(pair):
    pencil = pair // PAIRS
    return pencil, pl.ds(pl.multiple_of(pair % PAIRS * LANES, LANES), LANES)


def z_waves(cell_z, weights, base_ref, taps_ref):
    turn = base_ref[...] * cell_z
    turn = turn - 360.0 * jnp.floor(turn * (1.0 / 360.0))
    cos_k, sin_k = unit_phase(turn * (1.0 / 360.0))
    turn = 8.0 * cell_z
    turn = turn - 360.0 * jnp.floor(turn * (1.0 / 360.0))
    cos_8, sin_8 = unit_phase(jnp.broadcast_to(turn * (1.0 / 360.0), cos_k.shape))
    pieces = [[] for _ in weights]
    pieces_im = [[] for _ in weights]
    for q in range(PADDED_Z // 8):
        span = slice(q * 8, q * 8 + 8)
        cos_t = [taps_ref[t, span, :] for t in range(6)]
        sin_t = [taps_ref[6 + t, span, :] for t in range(6)]
        for s, weight in enumerate(weights):
            real = weight[0] * cos_t[0] + sum(weight[t] * cos_t[t] for t in range(1, 6))
            imag = sum(weight[t] * sin_t[t] for t in range(1, 6))
            pieces[s].append(real * cos_k - imag * sin_k)
            pieces_im[s].append(-(real * sin_k + imag * cos_k))
        cos_k, sin_k = cos_k * cos_8 - sin_k * sin_8, sin_k * cos_8 + cos_k * sin_8
    return [
        (jnp.concatenate(re, axis=0), jnp.concatenate(im, axis=0))
        for re, im in zip(pieces, pieces_im)
    ]


def spread_kernel(own, *refs):
    atoms_ref, base_ref, taps_ref, tables_ref, cos_ref, sin_ref = refs[:6]
    out_ref, grid_ref, table_ref, weights_ref, semaphores = refs[-5:]
    lines_ref = None if own else refs[6]
    table_copy = fetch(tables_ref, table_ref, semaphores.at[0])
    grid_ref[...] = jnp.zeros_like(grid_ref)
    rows = list(range(CY)) if own else list(range(CY, ROWS))
    part = len(rows) * LANES
    gap = jnp.zeros((HALF - PADDED_Z, LANES), bf16)
    spline_table(atoms_ref, weights_ref, 2)

    def pair_body(pair, carry):
        pencil, lanes = pair_place(pair)
        row = [atoms_ref[pencil, a : a + 1, lanes] for a in range(10)]
        charge, dip_x, dip_y, dip_z = row[6:10]
        window = pair * 32
        dense_x = dense_rows(
            weight_rows(weights_ref, pencil, lanes, 0, 2), row[0] - window.astype(f32), WINDOW
        )
        dense_y = dense_rows(weight_rows(weights_ref, pencil, lanes, 1, 2), row[1], 16)
        value, first = weight_rows(weights_ref, pencil, lanes, 2, 2)
        mixed = [charge * value[t] + dip_z * first[t] for t in range(6)]
        right = []
        for re, im in z_waves(row[2], (mixed, value), base_ref, taps_ref):
            re, im = halves(re), halves(im)
            right.append(
                [
                    jnp.concatenate([re[n], gap, im[n], gap, im[n], gap, -re[n], gap], axis=0)
                    for n in range(2)
                ]
            )
        high, low = [jnp.concatenate([right[0][n], right[1][n]], axis=1) for n in range(2)]
        right = jnp.concatenate([high, low, high], axis=1)
        left = []
        for r in rows:
            value, first = dense_y[0][r : r + 1], dense_y[1][r : r + 1]
            left.append(
                jnp.concatenate(
                    [
                        value * dense_x[0],
                        (dip_x * value) * dense_x[1] + (dip_y * first) * dense_x[0],
                    ],
                    axis=1,
                )
            )
        high, low = halves(jnp.concatenate(left, axis=0))
        left = jnp.concatenate([high, high, low], axis=1)
        added = lax.dot_general(
            left, right, (((1,), (1,)), ((), ())), preferred_element_type=f32
        )
        at = pl.ds(pl.multiple_of(window, 8), WINDOW)
        for n in range(len(rows)):
            piece = added[n * WINDOW : (n + 1) * WINDOW]
            grid_ref[at, n * LANES : (n + 1) * LANES] += piece[:, :LANES]
            grid_ref[at, part + n * LANES : part + (n + 1) * LANES] += piece[:, LANES:]
        return carry

    lax.fori_loop(0, PENCILS * PAIRS, pair_body, 0, unroll=6)
    grid_ref[0:8] += grid_ref[NX : NX + 8]
    table_copy.wait()
    sign = lane_sign((NX, LANES))
    totals = []
    for first in range(0, len(rows), 2):
        lanes = slice(first * LANES, min(first + 2, len(rows)) * LANES)
        below = slice(part + lanes.start, part + lanes.stop)
        line = jnp.concatenate(
            forward_line(
                table_ref, quarters_of(grid_ref[:NX, lanes]), quarters_of(grid_ref[:NX, below])
            ),
            axis=0,
        )
        for n, r in enumerate(rows[first : first + 2]):
            one = line[:, n * LANES : (n + 1) * LANES]
            total = one * cos_ref[:, r : r + 1] + turned(one, sign) * sin_ref[:, r : r + 1]
            y = first + n
            if own:
                out_ref[:, y * LANES : (y + 1) * LANES] = total
            else:
                totals.append(total + lines_ref[:, y * LANES : (y + 1) * LANES])
    if own:
        return
    totals.append(lines_ref[:, (CY - 1) * LANES :])
    for group in range(GROUPS):
        blocks = []
        for block in range(4 * group, 4 * group + 4):
            j, y = block // CY, block % CY
            blocks.append(totals[y][j * SLABS : (j + 1) * SLABS])
        for c, carrier in enumerate(pack_blocks(blocks)):
            out_ref[rows_of(3 * group + c), :] = carrier


def weights_kernel(
    atoms_ref, below_ref, base_ref, taps_ref, waves_ref, x_ref, y_ref, weights_ref, below_weights_ref
):
    for start, some_ref, table_ref in (
        (0, atoms_ref, weights_ref),
        (PENCILS * PAIRS, below_ref, below_weights_ref),
    ):
        spline_table(some_ref, table_ref, 3)

        def pair_body(pair, carry, start=start, some_ref=some_ref, table_ref=table_ref):
            pencil, lanes = pair_place(pair)
            row = [some_ref[pencil, a : a + 1, lanes] for a in range(3)]
            window = (pair * 32).astype(f32)
            dense_x = dense_rows(
                weight_rows(table_ref, pencil, lanes, 0, 3), row[0] - window, WINDOW
            )
            dense_y = dense_rows(weight_rows(table_ref, pencil, lanes, 1, 3), row[1], 16)
            for p in range(3):
                x_ref[start + pair, p] = dense_x[p]
                y_ref[start + pair, p] = dense_y[p]
            waves = z_waves(
                row[2], weight_rows(table_ref, pencil, lanes, 2, 3), base_ref, taps_ref
            )
            for s, (re, im) in enumerate(waves):
                re, im = halves(re), halves(im)
                columns = slice(s * LANES, (s + 1) * LANES)
                for n in range(2):
                    waves_ref[start + pair, n, :PADDED_Z, columns] = re[n]
                    waves_ref[start + pair, n, PADDED_Z:, columns] = im[n]
            return carry

        lax.fori_loop(0, PENCILS * PAIRS, pair_body, 0, unroll=6)


def green_kernel(top_ref, norm_ref, mode_ref, out_ref):
    for j in range(PART_X):
        square = norm_ref[:, j : j + 1] + mode_ref[1:2, :]
        green = top_ref[:, j : j + 1] * mode_ref[0:1, :] / jnp.where(square == 0.0, 1.0, square)
        out_ref[:, j * LANES : (j + 1) * LANES] = jnp.where(square == 0.0, 0.0, green)


def filter_kernel(
    in_ref, tables_ref, backs_ref, green_ref, out_ref, table_ref, back_ref, semaphores
):
    copies = [
        fetch(tables_ref, table_ref, semaphores.at[0]),
        fetch(backs_ref, back_ref, semaphores.at[1]),
    ]
    sign = lane_sign((NY, LANES))
    energy = jnp.zeros((8, LANES), f32)
    blocks = []
    for first in range(0, PART_X, 2):
        lines = []
        for j in (first, first + 1):
            found = [block_at(in_ref, j, y) for y in range(CY)]
            lines.append(
                jnp.concatenate(
                    [one[16 * part : 16 * part + 16] for part in range(4) for one in found], axis=0
                )
            )
        swapped = jnp.concatenate([turned(one, sign) for one in lines], axis=1)
        lines = jnp.concatenate(lines, axis=1)
        if first == 0:
            copies[0].wait()
        spectrum = jnp.concatenate(
            forward_line(table_ref, quarters_of(lines), quarters_of(swapped)), axis=0
        )
        modes = []
        for n in range(2):
            j = first + n
            one = spectrum[:, n * LANES : (n + 1) * LANES]
            scaled = green_ref[:, j * LANES : (j + 1) * LANES] * one
            share = scaled * one
            energy = energy + sum(share[8 * i : 8 * i + 8] for i in range(NY // 8))
            modes.append(scaled)
        swapped = jnp.concatenate([turned(one, sign) for one in modes], axis=1)
        modes = jnp.concatenate(modes, axis=1)
        if first == 0:
            copies[1].wait()
        parts = inverse_line(back_ref, quarters_of(modes), quarters_of(swapped))
        for n in range(2):
            for y in range(CY):
                blocks.append(
                    jnp.concatenate(
                        [
                            one[16 * y : 16 * y + 16, n * LANES : (n + 1) * LANES]
                            for one in parts
                        ],
                        axis=0,
                    )
                )
        for group in range(first * CY // 4, (first + 2) * CY // 4):
            for c, carrier in enumerate(pack_blocks(blocks[4 * group : 4 * group + 4])):
                out_ref[rows_of(3 * group + c), :] = carrier
    lane = lax.broadcasted_iota(jnp.int32, (SLABS, LANES), 1)
    share = 0.5 * jnp.sum(energy)
    out_ref[rows_of(0), :] = jnp.where(lane == PART_Z, share, out_ref[rows_of(0), :])


def sample_kernel(
    own, in_ref, atoms_ref, waves_ref, x_ref, y_ref, tables_ref, cos_ref, sin_ref, out_ref,
    grid_ref, table_ref, semaphores
):
    table_copy = fetch(tables_ref, table_ref, semaphores.at[0])
    sign = lane_sign((NX, LANES))
    rows = list(range(CY)) if own else list(range(CY, ROWS))
    for first in range(0, len(rows), 2):
        modes, swapped = [], []
        for y in range(first, min(first + 2, len(rows))):
            line = jnp.concatenate([block_at(in_ref, j, y) for j in range(PART_X)], axis=0)
            other = turned(line, sign)
            r = rows[y]
            cos_r, sin_r = cos_ref[:, r : r + 1], sin_ref[:, r : r + 1]
            modes.append(line * cos_r - other * sin_r)
            swapped.append(other * cos_r + line * sin_r)
        swapped = jnp.concatenate(swapped, axis=1)
        stacked = modes
        modes = jnp.concatenate(modes, axis=1)
        if first == 0:
            table_copy.wait()
        cells = jnp.concatenate(
            inverse_line(table_ref, quarters_of(modes), quarters_of(swapped)), axis=0
        )
        lanes = slice(first * LANES, (first + len(stacked)) * LANES)
        grid_ref[:NX, lanes] = cells
        grid_ref[NX:, lanes] = cells[:8]
    gap = jnp.zeros((HALF - PADDED_Z, 3 * LANES), bf16)
    if own:
        lane = lax.broadcasted_iota(jnp.int32, (SLABS, LANES), 1)
        energy = jnp.sum(jnp.where(lane == PART_Z, in_ref[rows_of(0), :], 0.0))
    else:
        energy = 0.0

    start = 0 if own else PENCILS * PAIRS

    def pair_body(pair, carry):
        pencil, lanes = pair_place(pair)
        waves = [
            jnp.concatenate(
                [waves_ref[start + pair, n, :PADDED_Z], gap, waves_ref[start + pair, n, PADDED_Z:], gap],
                axis=0,
            )
            for n in range(2)
        ]
        at = pl.ds(pl.multiple_of(pair * 32, 8), WINDOW)
        cells = jnp.concatenate(
            [grid_ref[at, n * LANES : (n + 1) * LANES] for n in range(len(rows))], axis=0
        )
        read = product(halves(cells), waves)
        dense_x = [x_ref[start + pair, p] for p in range(3)]
        dense_y = [y_ref[start + pair, p] for p in range(3)]
        lined = {}
        for order_y, order_z in ((0, 0), (1, 0), (2, 0), (0, 1), (1, 1), (0, 2)):
            lined[order_y, order_z] = sum(
                dense_y[order_y][r : r + 1]
                * read[n * WINDOW : (n + 1) * WINDOW, order_z * LANES : (order_z + 1) * LANES]
                for n, r in enumerate(rows)
            )

        def sampled(p, r, s):
            return jnp.sum(dense_x[p] * lined[r, s], axis=0, keepdims=True)

        charge, dip_x, dip_y, dip_z, live = [
            atoms_ref[pencil, a : a + 1, lanes] for a in range(6, 11)
        ]
        s100 = sampled(1, 0, 0)
        s010 = sampled(0, 1, 0)
        s001 = sampled(0, 0, 1)
        s110 = sampled(1, 1, 0)
        s101 = sampled(1, 0, 1)
        s011 = sampled(0, 1, 1)
        out = [
            live * sampled(0, 0, 0),
            live * s100,
            live * s010,
            live * s001,
            charge * s100 + dip_x * sampled(2, 0, 0) + dip_y * s110 + dip_z * s101,
            charge * s010 + dip_x * s110 + dip_y * sampled(0, 2, 0) + dip_z * s011,
            charge * s001 + dip_x * s101 + dip_y * s011 + dip_z * sampled(0, 0, 2),
            jnp.full(live.shape, energy, f32),
        ]
        out_ref[pencil, :, lanes] = jnp.concatenate(out, axis=0)
        return carry

    lax.fori_loop(0, PENCILS * PAIRS, pair_body, 0, unroll=6)


def finish_kernel(in_ref, charge_ref, dipole_ref, position_ref, energy_ref):
    total = (in_ref[0] + in_ref[1]) + (in_ref[2] + in_ref[3])
    charge_ref[...] = total[0:1]
    dipole_ref[...] = total[1:4]
    position_ref[...] = total[4:7]
    energy_ref[...] = total[7:8, 0:1]


def spline_modulus(angles):
    return (66.0 + 52.0 * jnp.cos(angles) + 2.0 * jnp.cos(2.0 * angles)) / 120.0


def mode_of(row):
    return 4 * (row % QUARTER) + row // QUARTER


def folded(index, size):
    return (index + size // 2) % size - size // 2


SPACES = {"v": pltpu.VMEM, "h": pltpu.HBM, "s": pltpu.SMEM}
WORK = {"flops": 1_000_000_000, "bytes_accessed": 8_000_000}


def call(kernel, inputs, out_shape, scratch=()):
    def run(*operands):
        placed = [
            pltpu.with_memory_space_constraint(one, pltpu.HBM) if where == "h" else one
            for one, where in zip(operands, inputs)
        ]
        return pl.pallas_call(
            kernel,
            out_shape=out_shape,
            in_specs=[pl.BlockSpec(memory_space=SPACES[one]) for one in inputs],
            scratch_shapes=list(scratch),
            compiler_params=pltpu.CompilerParams(vmem_limit_bytes=20 * 1024 * 1024),
            cost_estimate=pl.CostEstimate(transcendentals=0, **WORK),
        )(*placed)

    return run


def next_slab(value, back=False):
    step = -1 if back else 1
    return lax.ppermute(value, "gy", [(i, (i + step) % SLABS) for i in range(SLABS)])


def swap_slabs(lines):
    lines = lines.reshape(SLABS, CARRIERS, 1, LANES)
    lines = lax.all_to_all(lines, "gy", split_axis=0, concat_axis=0, tiled=True)
    return lines.reshape(SLABS * CARRIERS, LANES)


def on_device(cell_index, offsets, charges, dipoles, block_count, shear_cells):
    pencil_index = lax.axis_index("gx")
    slab_index = lax.axis_index("gy")
    shear_step = shear_cells[0]
    x_forward, x_inverse, y_forward, y_inverse = wave_tables()
    shape = jax.ShapeDtypeStruct

    mine, base, taps, cos_t, sin_t = call(
        prepare_kernel,
        "sshhhhh",
        (
            shape((16, ATOM_DEV), f32),
            shape((8, LANES), f32),
            shape((12, PADDED_Z, LANES), f32),
            shape((NX, LANES), f32),
            shape((NX, LANES), f32),
        ),
        [
            pltpu.SMEM(block_count.shape, jnp.int32),
            pltpu.VMEM((3, ATOM_DEV), jnp.int32),
            pltpu.VMEM((3, ATOM_DEV), f32),
            pltpu.VMEM((1, ATOM_DEV), f32),
            pltpu.VMEM((3, ATOM_DEV), f32),
            pltpu.SemaphoreType.DMA((5,)),
        ],
    )(
        jnp.stack([slab_index, pencil_index]),
        shear_cells,
        block_count,
        cell_index,
        offsets,
        charges[None],
        dipoles,
    )
    atoms = lax.all_gather(mine, "gx", axis=0, tiled=False)
    below_atoms = next_slab(atoms)

    own_x = folded(mode_of(jnp.arange(8, dtype=jnp.int32) * SLABS + slab_index), NX)[None, :]
    own_y = folded(mode_of(jnp.arange(NY, dtype=jnp.int32)), NY)[:, None]
    float_x = own_x.astype(f32)
    wave_y = own_y.astype(f32) + float_x * shear_step.astype(f32) / NX
    norm = (float_x / NX) ** 2 + (wave_y / NY) ** 2
    moduli = spline_modulus(2.0 * math.pi * float_x / NX) * spline_modulus(
        2.0 * math.pi * wave_y / NY
    )
    decay = (math.pi / screening) ** 2
    top = jnp.exp(-decay * norm) / (math.pi * moduli * moduli)
    top = jnp.where((own_x == -(NX // 2)) | (own_y == -(NY // 2)), 0.0, top)
    lane = jnp.arange(LANES, dtype=jnp.int32) % HALF
    mode_z = pencil_index * PART_Z + lane
    kept = lane < PART_Z
    float_z = mode_z.astype(f32)
    norm_z = (float_z / NZ) ** 2
    modulus_z = spline_modulus(2.0 * math.pi * float_z / NZ)
    twice = jnp.where(mode_z == 0, 1.0, 2.0) / (NX * NY * NZ)
    mode_top = jnp.where(kept, twice * jnp.exp(-decay * norm_z) / (modulus_z * modulus_z), 0.0)
    mode_norm = jnp.where(kept, norm_z, 1.0)
    mode = jnp.stack([mode_top, mode_norm])

    packed = shape((SLABS * CARRIERS, LANES), f32)
    table_space = pltpu.VMEM((NX, 6 * QUARTER), bf16)
    two = pltpu.SemaphoreType.DMA((2,))
    own_lines = call(
        lambda *refs: spread_kernel(True, *refs),
        "vvvhvv",
        shape((NX, CY * LANES), f32),
        [
            pltpu.VMEM((NX + 8, 2 * CY * LANES), f32),
            table_space,
            pltpu.VMEM((PENCILS, 12, 8, ATOM_DEV), f32),
            two,
        ],
    )(atoms, base, taps, x_forward, cos_t, sin_t)
    lines = call(
        lambda *refs: spread_kernel(False, *refs),
        "vvvhvvv",
        packed,
        [
            pltpu.VMEM((NX + 8, 2 * (ROWS - CY) * LANES), f32),
            table_space,
            pltpu.VMEM((PENCILS, 12, 8, ATOM_DEV), f32),
            two,
        ],
    )(below_atoms, base, taps, x_forward, cos_t, sin_t, own_lines)
    lines, atoms, below_atoms, top = lax.optimization_barrier((lines, atoms, below_atoms, top))
    pairs = 2 * PENCILS * PAIRS
    waves, dense_x, dense_y = call(
        weights_kernel,
        "vvvv",
        (
            shape((pairs, 2, 2 * PADDED_Z, 3 * LANES), bf16),
            shape((pairs, 3, WINDOW, LANES), f32),
            shape((pairs, 3, 16, LANES), f32),
        ),
        [pltpu.VMEM((PENCILS, 18, 8, ATOM_DEV), f32)] * 2,
    )(atoms, below_atoms, base, taps)
    green = call(green_kernel, "vvv", shape((NY, PART_X * LANES), f32))(top, norm, mode)
    lines = swap_slabs(lines)
    filtered = call(filter_kernel, "vhhv", packed, [table_space, table_space, two])(
        lines, y_forward, y_inverse, green
    )
    filtered = swap_slabs(filtered)
    shares_shape = shape((PENCILS, 8, ATOM_DEV), f32)
    below_shares = call(
        lambda *refs: sample_kernel(False, *refs),
        "vvvvvhvv",
        shares_shape,
        [pltpu.VMEM((NX + 8, (ROWS - CY) * LANES), f32), table_space, two],
    )(filtered, below_atoms, waves, dense_x, dense_y, x_inverse, cos_t, sin_t)
    below_shares = next_slab(below_shares, back=True)
    shares = call(
        lambda *refs: sample_kernel(True, *refs),
        "vvvvvhvv",
        shares_shape,
        [pltpu.VMEM((NX + 8, CY * LANES), f32), table_space, two],
    )(filtered, atoms, waves, dense_x, dense_y, x_inverse, cos_t, sin_t)
    shares = lax.all_to_all(shares + below_shares, "gx", split_axis=0, concat_axis=0, tiled=True)
    charge_grad, dipole_grad, position_grad, energy = call(
        finish_kernel,
        "v",
        (
            shape((1, ATOM_DEV), f32),
            shape((3, ATOM_DEV), f32),
            shape((3, ATOM_DEV), f32),
            shape((1, 1), f32),
        ),
    )(shares)
    return charge_grad[0], dipole_grad, position_grad, energy[0]


def solution(mesh):
    placed = (
        P(None, ("gy", "gx")),
        P(None, ("gy", "gx")),
        P(("gy", "gx")),
        P(None, ("gy", "gx")),
        P(("gy", "gx")),
        P(),
    )
    return jax.shard_map(
        on_device,
        mesh=mesh,
        in_specs=placed,
        out_specs=(P(("gy", "gx")), P(None, ("gy", "gx")), P(None, ("gy", "gx")), P()),
        check_vma=False,
    )
```

```python
import math

import jax
import jax.numpy as jnp
import ml_dtypes
import numpy as np
from jax import lax
from jax.experimental import pallas as pl
from jax.experimental.pallas import tpu as pltpu
from jax.sharding import PartitionSpec as P

NX = 384
NY = 384
NZ = 360
CY = 6
CX = 96
PENCILS = 4
SLABS = 64
PART_X = 6
PART_Z = 45
ATOM_BLK = 64
ATOM_DEV = 384
PAIRS = 3
WINDOW = 40
ROWS = 11
HALF = 64
LANES = 128
PADDED_Z = 48
QUARTER = 96
screening = 0.9
f32 = jnp.float32
bf16 = jnp.bfloat16


def split_table(table):
    high = table.astype(ml_dtypes.bfloat16)
    low = (table - high.astype(np.float64)).astype(ml_dtypes.bfloat16)
    return np.concatenate([high, high, low], axis=1)


def wave_tables():
    quarter = np.arange(QUARTER)
    mode = np.arange(4)[:, None] + 4 * quarter[None, :]
    row_y = CY * (quarter % 16) + quarter // 16
    tables = []
    for place in (quarter, row_y):
        ticks = mode[:, :, None] * place % NX
        for table in (ticks, ticks.transpose(0, 2, 1)):
            angle = 2.0 * np.pi / NX * table.reshape(NX, QUARTER)
            tables.append(split_table(np.concatenate([np.cos(angle), np.sin(angle)], axis=1)))
    return tables


def spline_rows(fraction):
    levels = {2: [1.0 - fraction, fraction]}
    current = levels[2]
    for n in range(3, 7):
        inverse_n = 1.0 / (n - 1)
        updated = [None] * n
        updated[n - 1] = inverse_n * fraction * current[n - 2]
        for j in range(1, n - 1):
            updated[n - 1 - j] = inverse_n * (
                (fraction + j) * current[n - 2 - j] + (n - j - fraction) * current[n - 1 - j]
            )
        updated[0] = inverse_n * (1.0 - fraction) * current[0]
        current = updated
        levels[n] = current
    zero_row = jnp.zeros_like(fraction)

    def entry_at(values_list, k):
        return values_list[k] if 0 <= k < len(values_list) else zero_row

    first = [entry_at(levels[5], t - 1) - entry_at(levels[5], t) for t in range(6)]
    second = [
        entry_at(levels[4], t - 2) - 2.0 * entry_at(levels[4], t - 1) + entry_at(levels[4], t)
        for t in range(6)
    ]
    return levels[6], first, second


def dense_rows(tables, cell, length):
    away = lax.broadcasted_iota(jnp.int32, (length, cell.shape[1]), 0).astype(f32) - cell
    summed = [jnp.zeros(away.shape, f32) for _ in tables]
    for t in range(6):
        here = away == float(t)
        summed = [jnp.where(here, table[t], so_far) for table, so_far in zip(tables, summed)]
    return summed


def unit_phase(turns):
    turns = turns - jnp.floor(turns + 0.5)
    quarter = jnp.floor(4.0 * turns + 0.5)
    rest = turns - 0.25 * quarter
    theta = (2.0 * math.pi) * rest
    square = theta * theta
    sine = theta * (
        1.0
        + square
        * (-1.0 / 6 + square * (1.0 / 120 + square * (-1.0 / 5040 + square * (1.0 / 362880))))
    )
    cosine = 1.0 + square * (
        -0.5
        + square
        * (1.0 / 24 + square * (-1.0 / 720 + square * (1.0 / 40320 - square * (1.0 / 3628800))))
    )
    odd = jnp.abs(quarter) == 1.0
    cos_out = jnp.where(odd, sine, cosine)
    sin_out = jnp.where(odd, cosine, sine)
    cos_out = jnp.where((quarter == 1.0) | (jnp.abs(quarter) == 2.0), -cos_out, cos_out)
    sin_out = jnp.where((quarter == -1.0) | (jnp.abs(quarter) == 2.0), -sin_out, sin_out)
    return cos_out, sin_out


def halves(value):
    high = value.astype(bf16)
    return high, (value - high.astype(f32)).astype(bf16)


def joined(left, right):
    return (
        jnp.concatenate([left[0], left[0], left[1]], axis=1),
        jnp.concatenate([right[0], right[1], right[0]], axis=0),
    )


def product(left, right):
    left, right = joined(left, right)
    return jnp.dot(left, right, preferred_element_type=f32)


def product3(left, right):
    def one(a, b):
        return jnp.dot(a, b, preferred_element_type=f32)

    return one(left[0], right[0]) + (one(left[0], right[1]) + one(left[1], right[0]))


def lane_sign(shape):
    return jnp.where(lax.broadcasted_iota(jnp.int32, shape, 1) < HALF, 1.0, -1.0).astype(f32)


def turned(value, sign):
    return pltpu.roll(value, HALF, 1) * sign


def fetch(source, target, semaphore):
    copy = pltpu.make_async_copy(source, target, semaphore)
    copy.start()
    return copy


def line_product(table_ref, r, value):
    rows = slice(r * QUARTER, (r + 1) * QUARTER)
    table = table_ref[rows, : 2 * QUARTER], table_ref[rows, 4 * QUARTER :]
    return product3(table, halves(value))


def forward_line(table_ref, quarters, turned_quarters):
    g, h = quarters, turned_quarters
    a, b, c, d = g[0] + g[2], g[0] - g[2], g[1] + g[3], g[1] - g[3]
    ta, tb, tc, td = h[0] + h[2], h[0] - h[2], h[1] + h[3], h[1] - h[3]
    lines = []
    for r, (one, other) in enumerate(
        ((a + c, ta + tc), (b + td, tb - d), (a - c, ta - tc), (b - td, tb + d))
    ):
        stacked = jnp.concatenate([one, other], axis=0)
        lines.append(line_product(table_ref, r, stacked))
    return lines


def inverse_line(table_ref, modes, turned_modes):
    z = []
    for r in range(4):
        stacked = jnp.concatenate([modes[r], -turned_modes[r]], axis=0)
        z.append(line_product(table_ref, r, stacked))
    a, b, c, d = z[0] + z[2], z[0] - z[2], z[1] + z[3], z[1] - z[3]
    width = d.shape[1]
    sign = lane_sign((QUARTER, LANES))
    td = jnp.concatenate(
        [turned(d[:, n : n + LANES], sign) for n in range(0, width, LANES)], axis=1
    )
    return [a + c, b - td, a - c, b + td]


def quarters_of(value):
    return [value[r * QUARTER : (r + 1) * QUARTER] for r in range(4)]


PIECES = (0, 16, 32, 64, 80, 96)
GROUPS = PART_X * CY // 4
CARRIERS = 3 * GROUPS


def lane_range(first):
    lane = lax.broadcasted_iota(jnp.int32, (SLABS, LANES), 1)
    return (lane >= first) & (lane < first + 16)


def pack_blocks(blocks):
    carriers = []
    for c in range(3):
        value = blocks[c]
        for half in range(2):
            gap = PADDED_Z + half * HALF
            shift = (gap - PIECES[2 * c + half]) % LANES
            value = jnp.where(lane_range(gap), pltpu.roll(blocks[3], shift, 1), value)
        carriers.append(value)
    return carriers


def unpack_block(carriers):
    value = jnp.zeros((SLABS, LANES), f32)
    for p, source in enumerate(PIECES):
        gap = PADDED_Z + p % 2 * HALF
        shift = (source - gap) % LANES
        value = jnp.where(lane_range(source), pltpu.roll(carriers[p // 2], shift, 1), value)
    return value


def rows_of(carrier):
    return pl.ds(carrier, SLABS, stride=CARRIERS)


def block_at(ref, j, y):
    block = j * CY + y
    group, place = block // 4, block % 4
    if place < 3:
        return ref[rows_of(3 * group + place), :]
    return unpack_block([ref[rows_of(3 * group + c), :] for c in range(3)])


def prepare_kernel(
    where_ref, shear_ref, counts_ref, cells_ref, offsets_ref, charges_ref, dipoles_ref,
    atoms_ref, base_ref, taps_ref, cos_ref, sin_ref,
    count_ref, cell_ref, offset_ref, charge_ref, dipole_ref, semaphores
):
    copies = [
        fetch(source, target, semaphores.at[n])
        for n, (source, target) in enumerate(
            (
                (counts_ref, count_ref),
                (cells_ref, cell_ref),
                (offsets_ref, offset_ref),
                (charges_ref, charge_ref.at[0]),
                (dipoles_ref, dipole_ref),
            )
        )
    ]
    slab, pencil = where_ref[0], where_ref[1]
    first = pencil * PART_Z
    row = lax.broadcasted_iota(jnp.int32, (PADDED_Z, LANES), 0)
    mode = (row + first).astype(f32)
    base_ref[...] = mode[:8]
    for t in range(6):
        cos_t, sin_t = unit_phase(mode * float(t) * (1.0 / NZ))
        taps_ref[t] = jnp.where(row < PART_Z, cos_t, 0.0)
        taps_ref[6 + t] = jnp.where(row < PART_Z, sin_t, 0.0)
    column = lax.broadcasted_iota(jnp.int32, (1, LANES), 1)
    above = jnp.where(slab == 0, SLABS - 1, slab - 1) * CY
    rows = jnp.where(column < CY, slab * CY, above) + jnp.minimum(column, ROWS)
    index = lax.broadcasted_iota(jnp.int32, (NX, LANES), 0)
    residue = (
        (index >= QUARTER).astype(jnp.int32)
        + (index >= 2 * QUARTER).astype(jnp.int32)
        + (index >= 3 * QUARTER).astype(jnp.int32)
    )
    mode_x = 4 * (index - QUARTER * residue) + residue
    folds = jnp.where(mode_x < NX // 2, mode_x, mode_x - NX)
    ticks = folds * (shear_ref[0] * rows)
    whole = jnp.floor(ticks.astype(f32) * (1.0 / (NX * NY))).astype(jnp.int32)
    rest = ticks - whole * (NX * NY)
    cos_t, sin_t = unit_phase(rest.astype(f32) * (1.0 / (NX * NY)))
    cos_ref[...] = cos_t
    sin_ref[...] = sin_t
    for copy in copies:
        copy.wait()
    slot = lax.broadcasted_iota(jnp.int32, (1, ATOM_DEV), 1)
    live = jnp.zeros((1, ATOM_DEV), f32)
    for b in range(ATOM_DEV // ATOM_BLK):
        inside = (slot >= b * ATOM_BLK) & (slot < b * ATOM_BLK + count_ref[b])
        live = jnp.where(inside, 1.0, live)
    atoms_ref[0:1, :] = cell_ref[0:1, :].astype(f32)
    atoms_ref[1:2, :] = (cell_ref[1:2, :] - slab * CY).astype(f32)
    atoms_ref[2:3, :] = cell_ref[2:3, :].astype(f32)
    atoms_ref[3:6, :] = offset_ref[...]
    atoms_ref[6:7, :] = charge_ref[...] * live
    atoms_ref[7:10, :] = dipole_ref[...] * live
    atoms_ref[10:11, :] = live
    atoms_ref[11:16, :] = jnp.zeros((5, ATOM_DEV), f32)


def spline_table(atoms_ref, table_ref, orders):
    def pencil_body(pencil, carry):
        tables = spline_rows(atoms_ref[pencil, 3:6, :])
        for o in range(orders):
            for t in range(6):
                table_ref[pencil, o * 6 + t, 0:3, :] = tables[o][t]
        return carry

    lax.fori_loop(0, PENCILS, pencil_body, 0)


def weight_rows(table_ref, pencil, lanes, dim, orders):
    row = slice(dim, dim + 1)
    return [[table_ref[pencil, o * 6 + t, row, lanes] for t in range(6)] for o in range(orders)]


def pair_place(pair):
    pencil = pair // PAIRS
    return pencil, pl.ds(pl.multiple_of(pair % PAIRS * LANES, LANES), LANES)


def z_waves(cell_z, weights, base_ref, taps_ref):
    turn = base_ref[...] * cell_z
    turn = turn - 360.0 * jnp.floor(turn * (1.0 / 360.0))
    cos_k, sin_k = unit_phase(turn * (1.0 / 360.0))
    turn = 8.0 * cell_z
    turn = turn - 360.0 * jnp.floor(turn * (1.0 / 360.0))
    cos_8, sin_8 = unit_phase(jnp.broadcast_to(turn * (1.0 / 360.0), cos_k.shape))
    pieces = [[] for _ in weights]
    pieces_im = [[] for _ in weights]
    for q in range(PADDED_Z // 8):
        span = slice(q * 8, q * 8 + 8)
        cos_t = [taps_ref[t, span, :] for t in range(6)]
        sin_t = [taps_ref[6 + t, span, :] for t in range(6)]
        for s, weight in enumerate(weights):
            real = weight[0] * cos_t[0] + sum(weight[t] * cos_t[t] for t in range(1, 6))
            imag = sum(weight[t] * sin_t[t] for t in range(1, 6))
            pieces[s].append(real * cos_k - imag * sin_k)
            pieces_im[s].append(-(real * sin_k + imag * cos_k))
        cos_k, sin_k = cos_k * cos_8 - sin_k * sin_8, sin_k * cos_8 + cos_k * sin_8
    return [
        (jnp.concatenate(re, axis=0), jnp.concatenate(im, axis=0))
        for re, im in zip(pieces, pieces_im)
    ]


def sampling_weights(start, some_ref, table_ref, base_ref, taps_ref, waves_ref, x_ref, y_ref):
    spline_table(some_ref, table_ref, 3)

    def pair_body(pair, carry):
        pencil, lanes = pair_place(pair)
        row = [some_ref[pencil, a : a + 1, lanes] for a in range(3)]
        window = (pair * 32).astype(f32)
        dense_x = dense_rows(weight_rows(table_ref, pencil, lanes, 0, 3), row[0] - window, WINDOW)
        dense_y = dense_rows(weight_rows(table_ref, pencil, lanes, 1, 3), row[1], 16)
        for p in range(3):
            x_ref[start + pair, p] = dense_x[p]
            y_ref[start + pair, p] = dense_y[p]
        waves = z_waves(row[2], weight_rows(table_ref, pencil, lanes, 2, 3), base_ref, taps_ref)
        for s, (re, im) in enumerate(waves):
            re, im = halves(re), halves(im)
            columns = slice(s * LANES, (s + 1) * LANES)
            for n in range(2):
                waves_ref[start + pair, n, :PADDED_Z, columns] = re[n]
                waves_ref[start + pair, n, PADDED_Z:, columns] = im[n]
        return carry

    lax.fori_loop(0, PENCILS * PAIRS, pair_body, 0, unroll=2)


def spread_kernel(own, *refs):
    atoms_ref, base_ref, taps_ref, tables_ref, cos_ref, sin_ref = refs[:6]
    if own:
        out_ref, grid_ref, table_ref, weights_ref, semaphores = refs[6:]
    else:
        lines_ref, where_ref, slab_atoms_ref, out_ref = refs[6:10]
        results, kept = refs[10:13], refs[13:16]
        grid_ref, table_ref, weights_ref, semaphores = refs[16:]
    table_copy = fetch(tables_ref, table_ref, semaphores.at[0])
    grid_ref[...] = jnp.zeros_like(grid_ref)
    rows = list(range(CY)) if own else list(range(CY, ROWS))
    part = len(rows) * LANES
    gap = jnp.zeros((HALF - PADDED_Z, LANES), bf16)
    spline_table(atoms_ref, weights_ref, 2)

    def pair_body(pair, carry):
        pencil, lanes = pair_place(pair)
        row = [atoms_ref[pencil, a : a + 1, lanes] for a in range(10)]
        charge, dip_x, dip_y, dip_z = row[6:10]
        window = pair * 32
        dense_x = dense_rows(
            weight_rows(weights_ref, pencil, lanes, 0, 2), row[0] - window.astype(f32), WINDOW
        )
        dense_y = dense_rows(weight_rows(weights_ref, pencil, lanes, 1, 2), row[1], 16)
        value, first = weight_rows(weights_ref, pencil, lanes, 2, 2)
        mixed = [charge * value[t] + dip_z * first[t] for t in range(6)]
        right = []
        for re, im in z_waves(row[2], (mixed, value), base_ref, taps_ref):
            re, im = halves(re), halves(im)
            right.append(
                [
                    jnp.concatenate([re[n], gap, im[n], gap, im[n], gap, -re[n], gap], axis=0)
                    for n in range(2)
                ]
            )
        high, low = [jnp.concatenate([right[0][n], right[1][n]], axis=1) for n in range(2)]
        right = jnp.concatenate([high, low, high], axis=1)
        left = []
        for r in rows:
            value, first = dense_y[0][r : r + 1], dense_y[1][r : r + 1]
            left.append(
                jnp.concatenate(
                    [
                        value * dense_x[0],
                        (dip_x * value) * dense_x[1] + (dip_y * first) * dense_x[0],
                    ],
                    axis=1,
                )
            )
        high, low = halves(jnp.concatenate(left, axis=0))
        left = jnp.concatenate([high, high, low], axis=1)
        added = lax.dot_general(
            left, right, (((1,), (1,)), ((), ())), preferred_element_type=f32
        )
        at = pl.ds(pl.multiple_of(window, 8), WINDOW)
        for n in range(len(rows)):
            piece = added[n * WINDOW : (n + 1) * WINDOW]
            grid_ref[at, n * LANES : (n + 1) * LANES] += piece[:, :LANES]
            grid_ref[at, part + n * LANES : part + (n + 1) * LANES] += piece[:, LANES:]
        return carry

    lax.fori_loop(0, PENCILS * PAIRS, pair_body, 0, unroll=6)
    grid_ref[0:8] += grid_ref[NX : NX + 8]
    table_copy.wait()
    sign = lane_sign((NX, LANES))
    totals = []
    for first in range(0, len(rows), 2):
        lanes = slice(first * LANES, min(first + 2, len(rows)) * LANES)
        below = slice(part + lanes.start, part + lanes.stop)
        line = jnp.concatenate(
            forward_line(
                table_ref, quarters_of(grid_ref[:NX, lanes]), quarters_of(grid_ref[:NX, below])
            ),
            axis=0,
        )
        for n, r in enumerate(rows[first : first + 2]):
            one = line[:, n * LANES : (n + 1) * LANES]
            total = one * cos_ref[:, r : r + 1] + turned(one, sign) * sin_ref[:, r : r + 1]
            y = first + n
            if own:
                out_ref[:, y * LANES : (y + 1) * LANES] = total
            else:
                totals.append(total + lines_ref[:, y * LANES : (y + 1) * LANES])
    if own:
        return
    totals.append(lines_ref[:, (CY - 1) * LANES :])
    for group in range(GROUPS):
        blocks = []
        for block in range(4 * group, 4 * group + 4):
            j, y = block // CY, block % CY
            blocks.append(totals[y][j * SLABS : (j + 1) * SLABS])
        for c, carrier in enumerate(pack_blocks(blocks)):
            out_ref[rows_of(3 * group + c), :] = carrier

    @pl.when(where_ref[1] % 2 == 1)
    def _():
        for start, some_ref in ((0, slab_atoms_ref), (PENCILS * PAIRS, atoms_ref)):
            sampling_weights(start, some_ref, weights_ref, base_ref, taps_ref, *kept)
        copies = [fetch(kept[n], results[n], semaphores.at[n]) for n in range(3)]
        for copy in copies:
            copy.wait()


def green_kernel(top_ref, norm_ref, mode_ref, out_ref):
    for j in range(PART_X):
        square = norm_ref[:, j : j + 1] + mode_ref[1:2, :]
        green = top_ref[:, j : j + 1] * mode_ref[0:1, :] / jnp.where(square == 0.0, 1.0, square)
        out_ref[:, j * LANES : (j + 1) * LANES] = jnp.where(square == 0.0, 0.0, green)


def filter_kernel(
    in_ref, tables_ref, backs_ref, green_ref, out_ref, table_ref, back_ref, semaphores
):
    copies = [
        fetch(tables_ref, table_ref, semaphores.at[0]),
        fetch(backs_ref, back_ref, semaphores.at[1]),
    ]
    sign = lane_sign((NY, LANES))
    energy = jnp.zeros((8, LANES), f32)
    blocks = []
    for first in range(0, PART_X, 2):
        lines = []
        for j in (first, first + 1):
            found = [block_at(in_ref, j, y) for y in range(CY)]
            lines.append(
                jnp.concatenate(
                    [one[16 * part : 16 * part + 16] for part in range(4) for one in found], axis=0
                )
            )
        swapped = jnp.concatenate([turned(one, sign) for one in lines], axis=1)
        lines = jnp.concatenate(lines, axis=1)
        if first == 0:
            copies[0].wait()
        spectrum = jnp.concatenate(
            forward_line(table_ref, quarters_of(lines), quarters_of(swapped)), axis=0
        )
        modes = []
        for n in range(2):
            j = first + n
            one = spectrum[:, n * LANES : (n + 1) * LANES]
            scaled = green_ref[:, j * LANES : (j + 1) * LANES] * one
            share = scaled * one
            energy = energy + sum(share[8 * i : 8 * i + 8] for i in range(NY // 8))
            modes.append(scaled)
        swapped = jnp.concatenate([turned(one, sign) for one in modes], axis=1)
        modes = jnp.concatenate(modes, axis=1)
        if first == 0:
            copies[1].wait()
        parts = inverse_line(back_ref, quarters_of(modes), quarters_of(swapped))
        for n in range(2):
            for y in range(CY):
                blocks.append(
                    jnp.concatenate(
                        [
                            one[16 * y : 16 * y + 16, n * LANES : (n + 1) * LANES]
                            for one in parts
                        ],
                        axis=0,
                    )
                )
        for group in range(first * CY // 4, (first + 2) * CY // 4):
            for c, carrier in enumerate(pack_blocks(blocks[4 * group : 4 * group + 4])):
                out_ref[rows_of(3 * group + c), :] = carrier
    lane = lax.broadcasted_iota(jnp.int32, (SLABS, LANES), 1)
    share = 0.5 * jnp.sum(energy)
    out_ref[rows_of(0), :] = jnp.where(lane == PART_Z, share, out_ref[rows_of(0), :])


def sample_kernel(
    own, in_ref, atoms_ref, where_ref, base_ref, taps_ref, cos_ref, sin_ref, tables_ref,
    waves_in_ref, x_in_ref, y_in_ref, out_ref,
    grid_ref, table_ref, waves_ref, x_ref, y_ref, weights_ref, semaphores
):
    table_copy = fetch(tables_ref, table_ref, semaphores.at[3])
    later = where_ref[1] % 2 == 0
    start = 0 if own else PENCILS * PAIRS
    some = pl.ds(start, PENCILS * PAIRS)
    copies = [
        pltpu.make_async_copy(source.at[some], target, semaphores.at[n])
        for n, (source, target) in enumerate(
            ((waves_in_ref, waves_ref), (x_in_ref, x_ref), (y_in_ref, y_ref))
        )
    ]

    @pl.when(later)
    def _():
        sampling_weights(0, atoms_ref, weights_ref, base_ref, taps_ref, waves_ref, x_ref, y_ref)

    @pl.when(jnp.logical_not(later))
    def _():
        for copy in copies:
            copy.start()

    sign = lane_sign((NX, LANES))
    rows = list(range(CY)) if own else list(range(CY, ROWS))
    for first in range(0, len(rows), 2):
        modes, swapped = [], []
        for y in range(first, min(first + 2, len(rows))):
            line = jnp.concatenate([block_at(in_ref, j, y) for j in range(PART_X)], axis=0)
            other = turned(line, sign)
            r = rows[y]
            cos_r, sin_r = cos_ref[:, r : r + 1], sin_ref[:, r : r + 1]
            modes.append(line * cos_r - other * sin_r)
            swapped.append(other * cos_r + line * sin_r)
        swapped = jnp.concatenate(swapped, axis=1)
        stacked = modes
        modes = jnp.concatenate(modes, axis=1)
        if first == 0:
            table_copy.wait()
        cells = jnp.concatenate(
            inverse_line(table_ref, quarters_of(modes), quarters_of(swapped)), axis=0
        )
        lanes = slice(first * LANES, (first + len(stacked)) * LANES)
        grid_ref[:NX, lanes] = cells
        grid_ref[NX:, lanes] = cells[:8]
    gap = jnp.zeros((HALF - PADDED_Z, 3 * LANES), bf16)
    if own:
        lane = lax.broadcasted_iota(jnp.int32, (SLABS, LANES), 1)
        energy = jnp.sum(jnp.where(lane == PART_Z, in_ref[rows_of(0), :], 0.0))
    else:
        energy = 0.0

    @pl.when(jnp.logical_not(later))
    def _():
        for copy in copies:
            copy.wait()

    def pair_body(pair, carry):
        pencil, lanes = pair_place(pair)
        waves = [
            jnp.concatenate(
                [waves_ref[pair, n, :PADDED_Z], gap, waves_ref[pair, n, PADDED_Z:], gap],
                axis=0,
            )
            for n in range(2)
        ]
        at = pl.ds(pl.multiple_of(pair * 32, 8), WINDOW)
        cells = jnp.concatenate(
            [grid_ref[at, n * LANES : (n + 1) * LANES] for n in range(len(rows))], axis=0
        )
        read = product(halves(cells), waves)
        dense_x = [x_ref[pair, p] for p in range(3)]
        dense_y = [y_ref[pair, p] for p in range(3)]
        lined = {}
        for order_y, order_z in ((0, 0), (1, 0), (2, 0), (0, 1), (1, 1), (0, 2)):
            lined[order_y, order_z] = sum(
                dense_y[order_y][r : r + 1]
                * read[n * WINDOW : (n + 1) * WINDOW, order_z * LANES : (order_z + 1) * LANES]
                for n, r in enumerate(rows)
            )

        def sampled(p, r, s):
            return jnp.sum(dense_x[p] * lined[r, s], axis=0, keepdims=True)

        charge, dip_x, dip_y, dip_z, live = [
            atoms_ref[pencil, a : a + 1, lanes] for a in range(6, 11)
        ]
        s100 = sampled(1, 0, 0)
        s010 = sampled(0, 1, 0)
        s001 = sampled(0, 0, 1)
        s110 = sampled(1, 1, 0)
        s101 = sampled(1, 0, 1)
        s011 = sampled(0, 1, 1)
        out = [
            live * sampled(0, 0, 0),
            live * s100,
            live * s010,
            live * s001,
            charge * s100 + dip_x * sampled(2, 0, 0) + dip_y * s110 + dip_z * s101,
            charge * s010 + dip_x * s110 + dip_y * sampled(0, 2, 0) + dip_z * s011,
            charge * s001 + dip_x * s101 + dip_y * s011 + dip_z * sampled(0, 0, 2),
            jnp.full(live.shape, energy, f32),
        ]
        out_ref[pencil, :, lanes] = jnp.concatenate(out, axis=0)
        return carry

    lax.fori_loop(0, PENCILS * PAIRS, pair_body, 0, unroll=6)


def finish_kernel(in_ref, charge_ref, dipole_ref, position_ref, energy_ref, row_ref, semaphore):
    total = (in_ref[0] + in_ref[1]) + (in_ref[2] + in_ref[3])
    row_ref[...] = total[0:1]
    copy = fetch(row_ref.at[0], charge_ref, semaphore)
    dipole_ref[...] = total[1:4]
    position_ref[...] = total[4:7]
    energy_ref[...] = total[7:8, 0:1]
    copy.wait()


def spline_modulus(angles):
    return (66.0 + 52.0 * jnp.cos(angles) + 2.0 * jnp.cos(2.0 * angles)) / 120.0


def mode_of(row):
    return 4 * (row % QUARTER) + row // QUARTER


def folded(index, size):
    return (index + size // 2) % size - size // 2


SPACES = {"v": pltpu.VMEM, "h": pltpu.HBM, "s": pltpu.SMEM}
WORK = {"flops": 1_000_000_000, "bytes_accessed": 8_000_000}


def out_place(shape):
    pinned = isinstance(shape, type(pltpu.HBM((8, LANES), f32)))
    return pl.BlockSpec(memory_space=pltpu.HBM if pinned else pltpu.VMEM)


def call(kernel, inputs, out_shape, scratch=()):
    def run(*operands):
        placed = [
            pltpu.with_memory_space_constraint(one, pltpu.HBM) if where == "h" else one
            for one, where in zip(operands, inputs)
        ]
        return pl.pallas_call(
            kernel,
            out_shape=out_shape,
            in_specs=[pl.BlockSpec(memory_space=SPACES[one]) for one in inputs],
            out_specs=jax.tree.map(out_place, out_shape),
            scratch_shapes=list(scratch),
            compiler_params=pltpu.CompilerParams(vmem_limit_bytes=28 * 1024 * 1024),
            cost_estimate=pl.CostEstimate(transcendentals=0, **WORK),
        )(*placed)

    return run


def next_slab(value, back=False):
    step = -1 if back else 1
    return lax.ppermute(value, "gy", [(i, (i + step) % SLABS) for i in range(SLABS)])


def swap_slabs(lines):
    lines = lines.reshape(SLABS, CARRIERS, 1, LANES)
    lines = lax.all_to_all(lines, "gy", split_axis=0, concat_axis=0, tiled=True)
    return lines.reshape(SLABS * CARRIERS, LANES)


def on_device(cell_index, offsets, charges, dipoles, block_count, shear_cells):
    pencil_index = lax.axis_index("gx")
    slab_index = lax.axis_index("gy")
    x_forward, x_inverse, y_forward, y_inverse = wave_tables()
    shape = jax.ShapeDtypeStruct
    where = jnp.stack([slab_index, pencil_index])

    mine, base, taps, cos_t, sin_t = call(
        prepare_kernel,
        "sshhhhh",
        (
            shape((16, ATOM_DEV), f32),
            shape((8, LANES), f32),
            shape((12, PADDED_Z, LANES), f32),
            shape((NX, LANES), f32),
            shape((NX, LANES), f32),
        ),
        [
            pltpu.SMEM(block_count.shape, jnp.int32),
            pltpu.VMEM((3, ATOM_DEV), jnp.int32),
            pltpu.VMEM((3, ATOM_DEV), f32),
            pltpu.VMEM((1, ATOM_DEV), f32),
            pltpu.VMEM((3, ATOM_DEV), f32),
            pltpu.SemaphoreType.DMA((5,)),
        ],
    )(
        where,
        shear_cells,
        block_count,
        cell_index,
        offsets,
        charges,
        dipoles,
    )
    atoms = lax.all_gather(mine, "gx", axis=0, tiled=False)
    below_atoms = next_slab(atoms)

    packed = shape((SLABS * CARRIERS, LANES), f32)
    table_space = pltpu.VMEM((NX, 6 * QUARTER), bf16)
    two = pltpu.SemaphoreType.DMA((2,))
    pairs = 2 * PENCILS * PAIRS
    held = [
        ((2, 2 * PADDED_Z, 3 * LANES), bf16),
        ((3, WINDOW, LANES), f32),
        ((3, 16, LANES), f32),
    ]
    weights_space = pltpu.VMEM((PENCILS, 18, 8, ATOM_DEV), f32)
    four = pltpu.SemaphoreType.DMA((4,))
    own_lines = call(
        lambda *refs: spread_kernel(True, *refs),
        "vvvhvv",
        shape((NX, CY * LANES), f32),
        [pltpu.VMEM((NX + 8, 2 * CY * LANES), f32), table_space, weights_space, two],
    )(atoms, base, taps, x_forward, cos_t, sin_t)
    lines, *weights = call(
        lambda *refs: spread_kernel(False, *refs),
        "vvvhvvvsv",
        (packed, *(pltpu.HBM((pairs, *dims), kind) for dims, kind in held)),
        [
            *(pltpu.VMEM((pairs, *dims), kind) for dims, kind in held),
            pltpu.VMEM((NX + 8, 2 * (ROWS - CY) * LANES), f32),
            table_space,
            weights_space,
            four,
        ],
    )(below_atoms, base, taps, x_forward, cos_t, sin_t, own_lines, where, atoms)
    lines, shear_cells = lax.optimization_barrier((lines, shear_cells))
    shear_step = shear_cells[0]

    own_x = folded(mode_of(jnp.arange(8, dtype=jnp.int32) * SLABS + slab_index), NX)[None, :]
    own_y = folded(mode_of(jnp.arange(NY, dtype=jnp.int32)), NY)[:, None]
    float_x = own_x.astype(f32)
    wave_y = own_y.astype(f32) + float_x * shear_step.astype(f32) / NX
    norm = (float_x / NX) ** 2 + (wave_y / NY) ** 2
    moduli = spline_modulus(2.0 * math.pi * float_x / NX) * spline_modulus(
        2.0 * math.pi * wave_y / NY
    )
    decay = (math.pi / screening) ** 2
    top = jnp.exp(-decay * norm) / (math.pi * moduli * moduli)
    top = jnp.where((own_x == -(NX // 2)) | (own_y == -(NY // 2)), 0.0, top)
    lane = jnp.arange(LANES, dtype=jnp.int32) % HALF
    mode_z = pencil_index * PART_Z + lane
    kept = lane < PART_Z
    float_z = mode_z.astype(f32)
    norm_z = (float_z / NZ) ** 2
    modulus_z = spline_modulus(2.0 * math.pi * float_z / NZ)
    twice = jnp.where(mode_z == 0, 1.0, 2.0) / (NX * NY * NZ)
    mode_top = jnp.where(kept, twice * jnp.exp(-decay * norm_z) / (modulus_z * modulus_z), 0.0)
    mode_norm = jnp.where(kept, norm_z, 1.0)
    mode = jnp.stack([mode_top, mode_norm])

    green = call(green_kernel, "vvv", shape((NY, PART_X * LANES), f32))(top, norm, mode)
    lines = swap_slabs(lines)
    filtered = call(filter_kernel, "vhhv", packed, [table_space, table_space, two])(
        lines, y_forward, y_inverse, green
    )
    filtered = swap_slabs(filtered)
    shares_shape = shape((PENCILS, 8, ATOM_DEV), f32)
    sample_spaces = [
        table_space,
        *(pltpu.VMEM((pairs // 2, *dims), kind) for dims, kind in held),
        weights_space,
        four,
    ]
    below_shares = call(
        lambda *refs: sample_kernel(False, *refs),
        "vvsvvvvhhhh",
        shares_shape,
        [pltpu.VMEM((NX + 8, (ROWS - CY) * LANES), f32), *sample_spaces],
    )(filtered, below_atoms, where, base, taps, cos_t, sin_t, x_inverse, *weights)
    below_shares = next_slab(below_shares, back=True)
    shares = call(
        lambda *refs: sample_kernel(True, *refs),
        "vvsvvvvhhhh",
        shares_shape,
        [pltpu.VMEM((NX + 8, CY * LANES), f32), *sample_spaces],
    )(filtered, atoms, where, base, taps, cos_t, sin_t, x_inverse, *weights)
    shares = lax.all_to_all(shares + below_shares, "gx", split_axis=0, concat_axis=0, tiled=True)
    charge_grad, dipole_grad, position_grad, energy = call(
        finish_kernel,
        "v",
        (
            pltpu.HBM((ATOM_DEV,), f32),
            shape((3, ATOM_DEV), f32),
            shape((3, ATOM_DEV), f32),
            shape((1, 1), f32),
        ),
        [pltpu.VMEM((1, ATOM_DEV), f32), pltpu.SemaphoreType.DMA],
    )(shares)
    return charge_grad, dipole_grad, position_grad, energy[0]


def solution(mesh):
    placed = (
        P(None, ("gy", "gx")),
        P(None, ("gy", "gx")),
        P(("gy", "gx")),
        P(None, ("gy", "gx")),
        P(("gy", "gx")),
        P(),
    )
    return jax.shard_map(
        on_device,
        mesh=mesh,
        in_specs=placed,
        out_specs=(P(("gy", "gx")), P(None, ("gy", "gx")), P(None, ("gy", "gx")), P()),
        check_vma=False,
    )
```

```python
import math

import jax
import jax.numpy as jnp
import ml_dtypes
import numpy as np
from jax import lax
from jax.experimental import pallas as pl
from jax.experimental.pallas import tpu as pltpu
from jax.sharding import PartitionSpec as P

NX = 384
NY = 384
NZ = 360
CY = 6
CX = 96
PENCILS = 4
SLABS = 64
PART_X = 6
PART_Z = 45
ATOM_BLK = 64
ATOM_DEV = 384
PAIRS = 3
WINDOW = 40
WIDE = 48
EXTENDED = NX + WIDE
HALF = 64
LANES = 128
PADDED_Z = 48
QUARTER = 96
screening = 0.9
f32 = jnp.float32
bf16 = jnp.bfloat16


def split_table(table):
    high = table.astype(ml_dtypes.bfloat16)
    low = (table - high.astype(np.float64)).astype(ml_dtypes.bfloat16)
    return np.concatenate([high, high, low], axis=1)


def wave_tables():
    quarter = np.arange(QUARTER)
    mode = np.arange(4)[:, None] + 4 * quarter[None, :]
    row_y = CY * (quarter % 16) + quarter // 16
    tables = []
    for place in (quarter, row_y):
        ticks = mode[:, :, None] * place % NX
        for table in (ticks, ticks.transpose(0, 2, 1)):
            angle = 2.0 * np.pi / NX * table.reshape(NX, QUARTER)
            tables.append(split_table(np.concatenate([np.cos(angle), np.sin(angle)], axis=1)))
    return tables


def spline_rows(fraction):
    levels = {2: [1.0 - fraction, fraction]}
    current = levels[2]
    for n in range(3, 7):
        inverse_n = 1.0 / (n - 1)
        updated = [None] * n
        updated[n - 1] = inverse_n * fraction * current[n - 2]
        for j in range(1, n - 1):
            updated[n - 1 - j] = inverse_n * (
                (fraction + j) * current[n - 2 - j] + (n - j - fraction) * current[n - 1 - j]
            )
        updated[0] = inverse_n * (1.0 - fraction) * current[0]
        current = updated
        levels[n] = current
    zero_row = jnp.zeros_like(fraction)

    def entry_at(values_list, k):
        return values_list[k] if 0 <= k < len(values_list) else zero_row

    first = [entry_at(levels[5], t - 1) - entry_at(levels[5], t) for t in range(6)]
    second = [
        entry_at(levels[4], t - 2) - 2.0 * entry_at(levels[4], t - 1) + entry_at(levels[4], t)
        for t in range(6)
    ]
    return levels[6], first, second


def dense_rows(tables, cell, length):
    away = lax.broadcasted_iota(jnp.int32, (length, cell.shape[1]), 0).astype(f32) - cell
    summed = [jnp.zeros(away.shape, f32) for _ in tables]
    for t in range(6):
        here = away == float(t)
        summed = [jnp.where(here, table[t], so_far) for table, so_far in zip(tables, summed)]
    return summed


def unit_phase(turns):
    turns = turns - jnp.floor(turns + 0.5)
    quarter = jnp.floor(4.0 * turns + 0.5)
    rest = turns - 0.25 * quarter
    theta = (2.0 * math.pi) * rest
    square = theta * theta
    sine = theta * (
        1.0
        + square
        * (-1.0 / 6 + square * (1.0 / 120 + square * (-1.0 / 5040 + square * (1.0 / 362880))))
    )
    cosine = 1.0 + square * (
        -0.5
        + square
        * (1.0 / 24 + square * (-1.0 / 720 + square * (1.0 / 40320 - square * (1.0 / 3628800))))
    )
    odd = jnp.abs(quarter) == 1.0
    cos_out = jnp.where(odd, sine, cosine)
    sin_out = jnp.where(odd, cosine, sine)
    cos_out = jnp.where((quarter == 1.0) | (jnp.abs(quarter) == 2.0), -cos_out, cos_out)
    sin_out = jnp.where((quarter == -1.0) | (jnp.abs(quarter) == 2.0), -sin_out, sin_out)
    return cos_out, sin_out


def halves(value):
    high = value.astype(bf16)
    return high, (value - high.astype(f32)).astype(bf16)


def joined(left, right):
    return (
        jnp.concatenate([left[0], left[0], left[1]], axis=1),
        jnp.concatenate([right[0], right[1], right[0]], axis=0),
    )


def product(left, right):
    left, right = joined(left, right)
    return jnp.dot(left, right, preferred_element_type=f32)


def product3(left, right):
    def one(a, b):
        return jnp.dot(a, b, preferred_element_type=f32)

    return one(left[0], right[0]) + (one(left[0], right[1]) + one(left[1], right[0]))


def lane_sign(shape):
    return jnp.where(lax.broadcasted_iota(jnp.int32, shape, 1) < HALF, 1.0, -1.0).astype(f32)


def turned(value, sign):
    return pltpu.roll(value, HALF, 1) * sign


def fetch(source, target, semaphore):
    copy = pltpu.make_async_copy(source, target, semaphore)
    copy.start()
    return copy


def line_product(table_ref, r, value):
    rows = slice(r * QUARTER, (r + 1) * QUARTER)
    table = table_ref[rows, : 2 * QUARTER], table_ref[rows, 4 * QUARTER :]
    return product3(table, halves(value))


def forward_line(table_ref, quarters, turned_quarters):
    g, h = quarters, turned_quarters
    a, b, c, d = g[0] + g[2], g[0] - g[2], g[1] + g[3], g[1] - g[3]
    ta, tb, tc, td = h[0] + h[2], h[0] - h[2], h[1] + h[3], h[1] - h[3]
    lines = []
    for r, (one, other) in enumerate(
        ((a + c, ta + tc), (b + td, tb - d), (a - c, ta - tc), (b - td, tb + d))
    ):
        stacked = jnp.concatenate([one, other], axis=0)
        lines.append(line_product(table_ref, r, stacked))
    return lines


def inverse_line(table_ref, modes, turned_modes):
    z = []
    for r in range(4):
        stacked = jnp.concatenate([modes[r], -turned_modes[r]], axis=0)
        z.append(line_product(table_ref, r, stacked))
    a, b, c, d = z[0] + z[2], z[0] - z[2], z[1] + z[3], z[1] - z[3]
    width = d.shape[1]
    sign = lane_sign((QUARTER, LANES))
    td = jnp.concatenate(
        [turned(d[:, n : n + LANES], sign) for n in range(0, width, LANES)], axis=1
    )
    return [a + c, b - td, a - c, b + td]


def quarters_of(value):
    return [value[r * QUARTER : (r + 1) * QUARTER] for r in range(4)]


PIECES = (0, 16, 32, 64, 80, 96)
GROUPS = PART_X * CY // 4
CARRIERS = 3 * GROUPS


def lane_range(first):
    lane = lax.broadcasted_iota(jnp.int32, (SLABS, LANES), 1)
    return (lane >= first) & (lane < first + 16)


def pack_blocks(blocks):
    carriers = []
    for c in range(3):
        value = blocks[c]
        for half in range(2):
            gap = PADDED_Z + half * HALF
            shift = (gap - PIECES[2 * c + half]) % LANES
            value = jnp.where(lane_range(gap), pltpu.roll(blocks[3], shift, 1), value)
        carriers.append(value)
    return carriers


def unpack_block(carriers):
    value = jnp.zeros((SLABS, LANES), f32)
    for p, source in enumerate(PIECES):
        gap = PADDED_Z + p % 2 * HALF
        shift = (source - gap) % LANES
        value = jnp.where(lane_range(source), pltpu.roll(carriers[p // 2], shift, 1), value)
    return value


def rows_of(carrier):
    return pl.ds(carrier, SLABS, stride=CARRIERS)


def block_at(ref, j, y):
    block = j * CY + y
    group, place = block // 4, block % 4
    if place < 3:
        return ref[rows_of(3 * group + place), :]
    return unpack_block([ref[rows_of(3 * group + c), :] for c in range(3)])


def prepare_kernel(
    where_ref, shear_ref, counts_ref, cells_ref, offsets_ref, charges_ref, dipoles_ref,
    atoms_ref, base_ref, taps_ref, cos_ref, sin_ref,
    count_ref, cell_ref, offset_ref, charge_ref, dipole_ref, semaphores
):
    copies = [
        fetch(source, target, semaphores.at[n])
        for n, (source, target) in enumerate(
            (
                (counts_ref, count_ref),
                (cells_ref, cell_ref),
                (offsets_ref, offset_ref),
                (charges_ref, charge_ref.at[0]),
                (dipoles_ref, dipole_ref),
            )
        )
    ]
    slab, pencil = where_ref[0], where_ref[1]
    first = pencil * PART_Z
    row = lax.broadcasted_iota(jnp.int32, (PADDED_Z, LANES), 0)
    mode = (row + first).astype(f32)
    base_ref[...] = mode[:8]
    for t in range(6):
        cos_t, sin_t = unit_phase(mode * float(t) * (1.0 / NZ))
        taps_ref[t] = jnp.where(row < PART_Z, cos_t, 0.0)
        taps_ref[6 + t] = jnp.where(row < PART_Z, sin_t, 0.0)
    column = lax.broadcasted_iota(jnp.int32, (1, LANES), 1)
    rows = slab * CY + jnp.minimum(column, CY)
    index = lax.broadcasted_iota(jnp.int32, (NX, LANES), 0)
    residue = (
        (index >= QUARTER).astype(jnp.int32)
        + (index >= 2 * QUARTER).astype(jnp.int32)
        + (index >= 3 * QUARTER).astype(jnp.int32)
    )
    mode_x = 4 * (index - QUARTER * residue) + residue
    folds = jnp.where(mode_x < NX // 2, mode_x, mode_x - NX)
    ticks = folds * (shear_ref[0] * rows)
    whole = jnp.floor(ticks.astype(f32) * (1.0 / (NX * NY))).astype(jnp.int32)
    rest = ticks - whole * (NX * NY)
    cos_t, sin_t = unit_phase(rest.astype(f32) * (1.0 / (NX * NY)))
    cos_ref[...] = cos_t
    sin_ref[...] = sin_t
    for copy in copies:
        copy.wait()
    slot = lax.broadcasted_iota(jnp.int32, (1, ATOM_DEV), 1)
    live = jnp.zeros((1, ATOM_DEV), f32)
    for b in range(ATOM_DEV // ATOM_BLK):
        inside = (slot >= b * ATOM_BLK) & (slot < b * ATOM_BLK + count_ref[b])
        live = jnp.where(inside, 1.0, live)
    atoms_ref[0:1, :] = cell_ref[0:1, :].astype(f32)
    atoms_ref[1:2, :] = (cell_ref[1:2, :] - slab * CY).astype(f32)
    atoms_ref[2:3, :] = cell_ref[2:3, :].astype(f32)
    atoms_ref[3:6, :] = offset_ref[...]
    atoms_ref[6:7, :] = charge_ref[...] * live
    atoms_ref[7:10, :] = dipole_ref[...] * live
    atoms_ref[10:11, :] = live
    atoms_ref[11:16, :] = jnp.zeros((5, ATOM_DEV), f32)


def spline_table(atoms_ref, table_ref, orders):
    def pencil_body(pencil, carry):
        tables = spline_rows(atoms_ref[pencil, 3:6, :])
        for o in range(orders):
            for t in range(6):
                table_ref[pencil, o * 6 + t, 0:3, :] = tables[o][t]
        return carry

    lax.fori_loop(0, PENCILS, pencil_body, 0)


def weight_rows(table_ref, pencil, lanes, dim, orders):
    row = slice(dim, dim + 1)
    return [[table_ref[pencil, o * 6 + t, row, lanes] for t in range(6)] for o in range(orders)]


def pair_place(pair):
    pencil = pair // PAIRS
    return pencil, pl.ds(pl.multiple_of(pair % PAIRS * LANES, LANES), LANES)


def pair_window(pair, own, where_ref):
    if own:
        return pl.multiple_of(pair * 32, 8), WINDOW, (pair * 32).astype(f32)
    place = pair * 32 + where_ref[2]
    place = jnp.where(place >= NX, place - NX, place)
    first = place // 8 * 8
    return pl.multiple_of(first, 8), WIDE, (pair * 32 - (place - first)).astype(f32)


def z_waves(cell_z, weights, base_ref, taps_ref):
    turn = base_ref[...] * cell_z
    turn = turn - 360.0 * jnp.floor(turn * (1.0 / 360.0))
    cos_k, sin_k = unit_phase(turn * (1.0 / 360.0))
    turn = 8.0 * cell_z
    turn = turn - 360.0 * jnp.floor(turn * (1.0 / 360.0))
    cos_8, sin_8 = unit_phase(jnp.broadcast_to(turn * (1.0 / 360.0), cos_k.shape))
    pieces = [[] for _ in weights]
    pieces_im = [[] for _ in weights]
    for q in range(PADDED_Z // 8):
        span = slice(q * 8, q * 8 + 8)
        cos_t = [taps_ref[t, span, :] for t in range(6)]
        sin_t = [taps_ref[6 + t, span, :] for t in range(6)]
        for s, weight in enumerate(weights):
            real = weight[0] * cos_t[0] + sum(weight[t] * cos_t[t] for t in range(1, 6))
            imag = sum(weight[t] * sin_t[t] for t in range(1, 6))
            pieces[s].append(real * cos_k - imag * sin_k)
            pieces_im[s].append(-(real * sin_k + imag * cos_k))
        cos_k, sin_k = cos_k * cos_8 - sin_k * sin_8, sin_k * cos_8 + cos_k * sin_8
    return [
        (jnp.concatenate(re, axis=0), jnp.concatenate(im, axis=0))
        for re, im in zip(pieces, pieces_im)
    ]


def sampling_weights(
    start, own, where_ref, some_ref, table_ref, base_ref, taps_ref, waves_ref, x_ref, y_ref
):
    spline_table(some_ref, table_ref, 3)

    def pair_body(pair, carry):
        pencil, lanes = pair_place(pair)
        row = [some_ref[pencil, a : a + 1, lanes] for a in range(3)]
        _, window, origin = pair_window(pair, own, where_ref)
        dense_x = dense_rows(weight_rows(table_ref, pencil, lanes, 0, 3), row[0] - origin, window)
        dense_y = dense_rows(weight_rows(table_ref, pencil, lanes, 1, 3), row[1], 16)
        for p in range(3):
            x_ref[start + pair, p, :window] = dense_x[p]
            y_ref[start + pair, p] = dense_y[p]
        waves = z_waves(row[2], weight_rows(table_ref, pencil, lanes, 2, 3), base_ref, taps_ref)
        for s, (re, im) in enumerate(waves):
            re, im = halves(re), halves(im)
            columns = slice(s * LANES, (s + 1) * LANES)
            for n in range(2):
                waves_ref[start + pair, n, :PADDED_Z, columns] = re[n]
                waves_ref[start + pair, n, PADDED_Z:, columns] = im[n]
        return carry

    lax.fori_loop(0, PENCILS * PAIRS, pair_body, 0, unroll=2)


def spread_kernel(own, *refs):
    atoms_ref, where_ref, base_ref, taps_ref = refs[:4]
    if own:
        grid_ref, weights_ref = refs[4:]
        grid_ref[...] = jnp.zeros_like(grid_ref)
    else:
        slab_grid_ref, tables_ref, cos_ref, sin_ref, slab_atoms_ref, out_ref = refs[4:10]
        results, kept = refs[10:13], refs[13:16]
        grid_ref, table_ref, weights_ref, semaphores = refs[16:]
        table_copy = fetch(tables_ref, table_ref, semaphores.at[0])
        grid_ref[...] = slab_grid_ref[...]
    rows = list(range(CY)) if own else list(range(CY, 2 * CY - 1))
    part = CY * LANES
    gap = jnp.zeros((HALF - PADDED_Z, LANES), bf16)
    spline_table(atoms_ref, weights_ref, 2)

    def pair_body(pair, carry):
        pencil, lanes = pair_place(pair)
        row = [atoms_ref[pencil, a : a + 1, lanes] for a in range(10)]
        charge, dip_x, dip_y, dip_z = row[6:10]
        first_row, window, origin = pair_window(pair, own, where_ref)
        dense_x = dense_rows(
            weight_rows(weights_ref, pencil, lanes, 0, 2), row[0] - origin, window
        )
        dense_y = dense_rows(weight_rows(weights_ref, pencil, lanes, 1, 2), row[1], 16)
        value, first = weight_rows(weights_ref, pencil, lanes, 2, 2)
        mixed = [charge * value[t] + dip_z * first[t] for t in range(6)]
        right = []
        for re, im in z_waves(row[2], (mixed, value), base_ref, taps_ref):
            re, im = halves(re), halves(im)
            right.append(
                [
                    jnp.concatenate([re[n], gap, im[n], gap, im[n], gap, -re[n], gap], axis=0)
                    for n in range(2)
                ]
            )
        high, low = [jnp.concatenate([right[0][n], right[1][n]], axis=1) for n in range(2)]
        right = jnp.concatenate([high, low, high], axis=1)
        left = []
        for r in rows:
            value, first = dense_y[0][r : r + 1], dense_y[1][r : r + 1]
            left.append(
                jnp.concatenate(
                    [
                        value * dense_x[0],
                        (dip_x * value) * dense_x[1] + (dip_y * first) * dense_x[0],
                    ],
                    axis=1,
                )
            )
        high, low = halves(jnp.concatenate(left, axis=0))
        left = jnp.concatenate([high, high, low], axis=1)
        added = lax.dot_general(
            left, right, (((1,), (1,)), ((), ())), preferred_element_type=f32
        )
        at = pl.ds(first_row, window)
        for n in range(len(rows)):
            piece = added[n * window : (n + 1) * window]
            grid_ref[at, n * LANES : (n + 1) * LANES] += piece[:, :LANES]
            grid_ref[at, part + n * LANES : part + (n + 1) * LANES] += piece[:, LANES:]
        return carry

    lax.fori_loop(0, PENCILS * PAIRS, pair_body, 0, unroll=6)
    if own:
        return
    grid_ref[0:WIDE] += grid_ref[NX:EXTENDED]
    table_copy.wait()
    sign = lane_sign((NX, LANES))
    totals = []
    for first in range(0, CY, 2):
        lanes = slice(first * LANES, (first + 2) * LANES)
        below = slice(part + lanes.start, part + lanes.stop)
        line = jnp.concatenate(
            forward_line(
                table_ref, quarters_of(grid_ref[:NX, lanes]), quarters_of(grid_ref[:NX, below])
            ),
            axis=0,
        )
        for n, y in enumerate((first, first + 1)):
            one = line[:, n * LANES : (n + 1) * LANES]
            totals.append(one * cos_ref[:, y : y + 1] + turned(one, sign) * sin_ref[:, y : y + 1])
    for group in range(GROUPS):
        blocks = []
        for block in range(4 * group, 4 * group + 4):
            j, y = block // CY, block % CY
            blocks.append(totals[y][j * SLABS : (j + 1) * SLABS])
        for c, carrier in enumerate(pack_blocks(blocks)):
            out_ref[rows_of(3 * group + c), :] = carrier

    @pl.when(where_ref[1] % 2 == 1)
    def _():
        for start, some_ref in ((0, slab_atoms_ref), (PENCILS * PAIRS, atoms_ref)):
            sampling_weights(
                start, start == 0, where_ref, some_ref, weights_ref, base_ref, taps_ref, *kept
            )
        copies = [fetch(kept[n], results[n], semaphores.at[n]) for n in range(3)]
        for copy in copies:
            copy.wait()


def green_kernel(top_ref, norm_ref, mode_ref, out_ref):
    for j in range(PART_X):
        square = norm_ref[:, j : j + 1] + mode_ref[1:2, :]
        green = top_ref[:, j : j + 1] * mode_ref[0:1, :] / jnp.where(square == 0.0, 1.0, square)
        out_ref[:, j * LANES : (j + 1) * LANES] = jnp.where(square == 0.0, 0.0, green)


def filter_kernel(
    in_ref, tables_ref, backs_ref, green_ref, out_ref, table_ref, back_ref, semaphores
):
    copies = [
        fetch(tables_ref, table_ref, semaphores.at[0]),
        fetch(backs_ref, back_ref, semaphores.at[1]),
    ]
    sign = lane_sign((NY, LANES))
    energy = jnp.zeros((8, LANES), f32)
    blocks = []
    for first in range(0, PART_X, 2):
        lines = []
        for j in (first, first + 1):
            found = [block_at(in_ref, j, y) for y in range(CY)]
            lines.append(
                jnp.concatenate(
                    [one[16 * part : 16 * part + 16] for part in range(4) for one in found], axis=0
                )
            )
        swapped = jnp.concatenate([turned(one, sign) for one in lines], axis=1)
        lines = jnp.concatenate(lines, axis=1)
        if first == 0:
            copies[0].wait()
        spectrum = jnp.concatenate(
            forward_line(table_ref, quarters_of(lines), quarters_of(swapped)), axis=0
        )
        modes = []
        for n in range(2):
            j = first + n
            one = spectrum[:, n * LANES : (n + 1) * LANES]
            scaled = green_ref[:, j * LANES : (j + 1) * LANES] * one
            share = scaled * one
            energy = energy + sum(share[8 * i : 8 * i + 8] for i in range(NY // 8))
            modes.append(scaled)
        swapped = jnp.concatenate([turned(one, sign) for one in modes], axis=1)
        modes = jnp.concatenate(modes, axis=1)
        if first == 0:
            copies[1].wait()
        parts = inverse_line(back_ref, quarters_of(modes), quarters_of(swapped))
        for n in range(2):
            for y in range(CY):
                blocks.append(
                    jnp.concatenate(
                        [
                            one[16 * y : 16 * y + 16, n * LANES : (n + 1) * LANES]
                            for one in parts
                        ],
                        axis=0,
                    )
                )
        for group in range(first * CY // 4, (first + 2) * CY // 4):
            for c, carrier in enumerate(pack_blocks(blocks[4 * group : 4 * group + 4])):
                out_ref[rows_of(3 * group + c), :] = carrier
    lane = lax.broadcasted_iota(jnp.int32, (SLABS, LANES), 1)
    share = 0.5 * jnp.sum(energy)
    out_ref[rows_of(0), :] = jnp.where(lane == PART_Z, share, out_ref[rows_of(0), :])


def sample_kernel(own, *refs):
    atoms_ref, where_ref, base_ref, taps_ref, waves_in_ref, x_in_ref, y_in_ref = refs[:7]
    if own:
        grid_ref, out_ref = refs[7:9]
    else:
        in_ref, cos_ref, sin_ref, tables_ref, out_ref, grid_ref, table_ref = refs[7:14]
    waves_ref, x_ref, y_ref, weights_ref, semaphores = refs[-5:]
    if not own:
        table_copy = fetch(tables_ref, table_ref, semaphores.at[3])
    later = where_ref[1] % 2 == 0
    start = 0 if own else PENCILS * PAIRS
    some = pl.ds(start, PENCILS * PAIRS)
    copies = [
        pltpu.make_async_copy(source.at[some], target, semaphores.at[n])
        for n, (source, target) in enumerate(
            ((waves_in_ref, waves_ref), (x_in_ref, x_ref), (y_in_ref, y_ref))
        )
    ]

    @pl.when(later)
    def _():
        sampling_weights(
            0, own, where_ref, atoms_ref, weights_ref, base_ref, taps_ref, waves_ref, x_ref, y_ref
        )

    @pl.when(jnp.logical_not(later))
    def _():
        for copy in copies:
            copy.start()

    rows = list(range(CY)) if own else list(range(CY, 2 * CY - 1))
    energy = 0.0
    if not own:
        sign = lane_sign((NX, LANES))
        for first in range(0, CY, 2):
            modes, swapped = [], []
            for y in range(first, first + 2):
                line = jnp.concatenate([block_at(in_ref, j, y) for j in range(PART_X)], axis=0)
                other = turned(line, sign)
                cos_y, sin_y = cos_ref[:, y : y + 1], sin_ref[:, y : y + 1]
                modes.append(line * cos_y - other * sin_y)
                swapped.append(other * cos_y + line * sin_y)
            swapped = jnp.concatenate(swapped, axis=1)
            modes = jnp.concatenate(modes, axis=1)
            if first == 0:
                table_copy.wait()
            cells = jnp.concatenate(
                inverse_line(table_ref, quarters_of(modes), quarters_of(swapped)), axis=0
            )
            lanes = slice(first * LANES, (first + 2) * LANES)
            grid_ref[:NX, lanes] = cells
            grid_ref[NX:, lanes] = cells[:WIDE]
        lane = lax.broadcasted_iota(jnp.int32, (SLABS, LANES), 1)
        energy = jnp.sum(jnp.where(lane == PART_Z, in_ref[rows_of(0), :], 0.0))
    gap = jnp.zeros((HALF - PADDED_Z, 3 * LANES), bf16)

    @pl.when(jnp.logical_not(later))
    def _():
        for copy in copies:
            copy.wait()

    def pair_body(pair, carry):
        pencil, lanes = pair_place(pair)
        waves = [
            jnp.concatenate(
                [waves_ref[pair, n, :PADDED_Z], gap, waves_ref[pair, n, PADDED_Z:], gap],
                axis=0,
            )
            for n in range(2)
        ]
        first_row, window, _ = pair_window(pair, own, where_ref)
        at = pl.ds(first_row, window)
        cells = jnp.concatenate(
            [grid_ref[at, n * LANES : (n + 1) * LANES] for n in range(len(rows))], axis=0
        )
        read = product(halves(cells), waves)
        dense_x = [x_ref[pair, p, :window] for p in range(3)]
        dense_y = [y_ref[pair, p] for p in range(3)]
        lined = {}
        for order_y, order_z in ((0, 0), (1, 0), (2, 0), (0, 1), (1, 1), (0, 2)):
            lined[order_y, order_z] = sum(
                dense_y[order_y][r : r + 1]
                * read[n * window : (n + 1) * window, order_z * LANES : (order_z + 1) * LANES]
                for n, r in enumerate(rows)
            )

        def sampled(p, r, s):
            return jnp.sum(dense_x[p] * lined[r, s], axis=0, keepdims=True)

        charge, dip_x, dip_y, dip_z, live = [
            atoms_ref[pencil, a : a + 1, lanes] for a in range(6, 11)
        ]
        s100 = sampled(1, 0, 0)
        s010 = sampled(0, 1, 0)
        s001 = sampled(0, 0, 1)
        s110 = sampled(1, 1, 0)
        s101 = sampled(1, 0, 1)
        s011 = sampled(0, 1, 1)
        out = [
            live * sampled(0, 0, 0),
            live * s100,
            live * s010,
            live * s001,
            charge * s100 + dip_x * sampled(2, 0, 0) + dip_y * s110 + dip_z * s101,
            charge * s010 + dip_x * s110 + dip_y * sampled(0, 2, 0) + dip_z * s011,
            charge * s001 + dip_x * s101 + dip_y * s011 + dip_z * sampled(0, 0, 2),
            jnp.full(live.shape, energy, f32),
        ]
        out_ref[pencil, :, lanes] = jnp.concatenate(out, axis=0)
        return carry

    lax.fori_loop(0, PENCILS * PAIRS, pair_body, 0, unroll=6)


def finish_kernel(in_ref, charge_ref, dipole_ref, position_ref, energy_ref, row_ref, semaphore):
    total = (in_ref[0] + in_ref[1]) + (in_ref[2] + in_ref[3])
    row_ref[...] = total[0:1]
    copy = fetch(row_ref.at[0], charge_ref, semaphore)
    dipole_ref[...] = total[1:4]
    position_ref[...] = total[4:7]
    energy_ref[...] = total[7:8, 0:1]
    copy.wait()


def spline_modulus(angles):
    return (66.0 + 52.0 * jnp.cos(angles) + 2.0 * jnp.cos(2.0 * angles)) / 120.0


def mode_of(row):
    return 4 * (row % QUARTER) + row // QUARTER


def folded(index, size):
    return (index + size // 2) % size - size // 2


SPACES = {"v": pltpu.VMEM, "h": pltpu.HBM, "s": pltpu.SMEM}
WORK = {"flops": 1_000_000_000, "bytes_accessed": 8_000_000}


def out_place(shape):
    pinned = isinstance(shape, type(pltpu.HBM((8, LANES), f32)))
    return pl.BlockSpec(memory_space=pltpu.HBM if pinned else pltpu.VMEM)


def call(kernel, inputs, out_shape, scratch=()):
    def run(*operands):
        placed = [
            pltpu.with_memory_space_constraint(one, pltpu.HBM) if where == "h" else one
            for one, where in zip(operands, inputs)
        ]
        return pl.pallas_call(
            kernel,
            out_shape=out_shape,
            in_specs=[pl.BlockSpec(memory_space=SPACES[one]) for one in inputs],
            out_specs=jax.tree.map(out_place, out_shape),
            scratch_shapes=list(scratch),
            compiler_params=pltpu.CompilerParams(vmem_limit_bytes=28 * 1024 * 1024),
            cost_estimate=pl.CostEstimate(transcendentals=0, **WORK),
        )(*placed)

    return run


def next_slab(value, back=False):
    step = -1 if back else 1
    return lax.ppermute(value, "gy", [(i, (i + step) % SLABS) for i in range(SLABS)])


def swap_slabs(lines):
    lines = lines.reshape(SLABS, CARRIERS, 1, LANES)
    lines = lax.all_to_all(lines, "gy", split_axis=0, concat_axis=0, tiled=True)
    return lines.reshape(SLABS * CARRIERS, LANES)


def on_device(cell_index, offsets, charges, dipoles, block_count, shear_cells):
    pencil_index = lax.axis_index("gx")
    slab_index = lax.axis_index("gy")
    x_forward, x_inverse, y_forward, y_inverse = wave_tables()
    shape = jax.ShapeDtypeStruct
    shift = jnp.where(slab_index == 0, shear_cells[0], 0)
    where = jnp.stack([slab_index, pencil_index, shift])

    mine, base, taps, cos_t, sin_t = call(
        prepare_kernel,
        "sshhhhh",
        (
            shape((16, ATOM_DEV), f32),
            shape((8, LANES), f32),
            shape((12, PADDED_Z, LANES), f32),
            shape((NX, LANES), f32),
            shape((NX, LANES), f32),
        ),
        [
            pltpu.SMEM(block_count.shape, jnp.int32),
            pltpu.VMEM((3, ATOM_DEV), jnp.int32),
            pltpu.VMEM((3, ATOM_DEV), f32),
            pltpu.VMEM((1, ATOM_DEV), f32),
            pltpu.VMEM((3, ATOM_DEV), f32),
            pltpu.SemaphoreType.DMA((5,)),
        ],
    )(
        where,
        shear_cells,
        block_count,
        cell_index,
        offsets,
        charges,
        dipoles,
    )
    atoms = lax.all_gather(mine, "gx", axis=0, tiled=False)
    below_atoms = next_slab(atoms)

    packed = shape((SLABS * CARRIERS, LANES), f32)
    table_space = pltpu.VMEM((NX, 6 * QUARTER), bf16)
    two = pltpu.SemaphoreType.DMA((2,))
    pairs = 2 * PENCILS * PAIRS
    held = [
        ((2, 2 * PADDED_Z, 3 * LANES), bf16),
        ((3, WIDE, LANES), f32),
        ((3, 16, LANES), f32),
    ]
    weights_space = pltpu.VMEM((PENCILS, 18, 8, ATOM_DEV), f32)
    four = pltpu.SemaphoreType.DMA((4,))
    slab_grid = call(
        lambda *refs: spread_kernel(True, *refs),
        "vsvv",
        shape((EXTENDED, 2 * CY * LANES), f32),
        [weights_space],
    )(atoms, where, base, taps)
    lines, *weights = call(
        lambda *refs: spread_kernel(False, *refs),
        "vsvvvhvvv",
        (packed, *(pltpu.HBM((pairs, *dims), kind) for dims, kind in held)),
        [
            *(pltpu.VMEM((pairs, *dims), kind) for dims, kind in held),
            pltpu.VMEM((EXTENDED, 2 * CY * LANES), f32),
            table_space,
            weights_space,
            four,
        ],
    )(below_atoms, where, base, taps, slab_grid, x_forward, cos_t, sin_t, atoms)
    lines, shear_cells = lax.optimization_barrier((lines, shear_cells))
    shear_step = shear_cells[0]

    own_x = folded(mode_of(jnp.arange(8, dtype=jnp.int32) * SLABS + slab_index), NX)[None, :]
    own_y = folded(mode_of(jnp.arange(NY, dtype=jnp.int32)), NY)[:, None]
    float_x = own_x.astype(f32)
    wave_y = own_y.astype(f32) + float_x * shear_step.astype(f32) / NX
    norm = (float_x / NX) ** 2 + (wave_y / NY) ** 2
    moduli = spline_modulus(2.0 * math.pi * float_x / NX) * spline_modulus(
        2.0 * math.pi * wave_y / NY
    )
    decay = (math.pi / screening) ** 2
    top = jnp.exp(-decay * norm) / (math.pi * moduli * moduli)
    top = jnp.where((own_x == -(NX // 2)) | (own_y == -(NY // 2)), 0.0, top)
    lane = jnp.arange(LANES, dtype=jnp.int32) % HALF
    mode_z = pencil_index * PART_Z + lane
    kept = lane < PART_Z
    float_z = mode_z.astype(f32)
    norm_z = (float_z / NZ) ** 2
    modulus_z = spline_modulus(2.0 * math.pi * float_z / NZ)
    twice = jnp.where(mode_z == 0, 1.0, 2.0) / (NX * NY * NZ)
    mode_top = jnp.where(kept, twice * jnp.exp(-decay * norm_z) / (modulus_z * modulus_z), 0.0)
    mode_norm = jnp.where(kept, norm_z, 1.0)
    mode = jnp.stack([mode_top, mode_norm])

    green = call(green_kernel, "vvv", shape((NY, PART_X * LANES), f32))(top, norm, mode)
    lines = swap_slabs(lines)
    filtered = call(filter_kernel, "vhhv", packed, [table_space, table_space, two])(
        lines, y_forward, y_inverse, green
    )
    filtered = swap_slabs(filtered)
    shares_shape = shape((PENCILS, 8, ATOM_DEV), f32)
    sample_spaces = [
        *(pltpu.VMEM((pairs // 2, *dims), kind) for dims, kind in held),
        weights_space,
        four,
    ]
    below_shares, potential = call(
        lambda *refs: sample_kernel(False, *refs),
        "vsvvhhhvvvh",
        (shares_shape, shape((EXTENDED, CY * LANES), f32)),
        [table_space, *sample_spaces],
    )(below_atoms, where, base, taps, *weights, filtered, cos_t, sin_t, x_inverse)
    below_shares = next_slab(below_shares, back=True)
    shares = call(
        lambda *refs: sample_kernel(True, *refs), "vsvvhhhv", shares_shape, sample_spaces
    )(atoms, where, base, taps, *weights, potential)
    shares = lax.all_to_all(shares + below_shares, "gx", split_axis=0, concat_axis=0, tiled=True)
    charge_grad, dipole_grad, position_grad, energy = call(
        finish_kernel,
        "v",
        (
            pltpu.HBM((ATOM_DEV,), f32),
            shape((3, ATOM_DEV), f32),
            shape((3, ATOM_DEV), f32),
            shape((1, 1), f32),
        ),
        [pltpu.VMEM((1, ATOM_DEV), f32), pltpu.SemaphoreType.DMA],
    )(shares)
    return charge_grad, dipole_grad, position_grad, energy[0]


def solution(mesh):
    placed = (
        P(None, ("gy", "gx")),
        P(None, ("gy", "gx")),
        P(("gy", "gx")),
        P(None, ("gy", "gx")),
        P(("gy", "gx")),
        P(),
    )
    return jax.shard_map(
        on_device,
        mesh=mesh,
        in_specs=placed,
        out_specs=(P(("gy", "gx")), P(None, ("gy", "gx")), P(None, ("gy", "gx")), P()),
        check_vma=False,
    )
```

```python
import math

import jax
import jax.numpy as jnp
import ml_dtypes
import numpy as np
from jax import lax
from jax.experimental import pallas as pl
from jax.experimental.pallas import tpu as pltpu
from jax.sharding import PartitionSpec as P

NX = 384
NY = 384
NZ = 360
CY = 6
CX = 96
PENCILS = 4
SLABS = 64
PART_X = 6
PART_Z = 45
ATOM_BLK = 64
ATOM_DEV = 384
PAIRS = 3
WINDOW = 40
WIDE = 48
EXTENDED = NX + WIDE
HALF = 64
LANES = 128
PADDED_Z = 48
QUARTER = 96
screening = 0.9
f32 = jnp.float32
bf16 = jnp.bfloat16


def split_table(table):
    high = table.astype(ml_dtypes.bfloat16)
    low = (table - high.astype(np.float64)).astype(ml_dtypes.bfloat16)
    return np.concatenate([high, high, low], axis=1)


def wave_tables():
    quarter = np.arange(QUARTER)
    mode = np.arange(4)[:, None] + 4 * quarter[None, :]
    row_y = CY * (quarter % 16) + quarter // 16
    tables = []
    for place in (quarter, row_y):
        ticks = mode[:, :, None] * place % NX
        for table in (ticks, ticks.transpose(0, 2, 1)):
            angle = 2.0 * np.pi / NX * table.reshape(NX, QUARTER)
            tables.append(split_table(np.concatenate([np.cos(angle), np.sin(angle)], axis=1)))
    return tables


def spline_rows(fraction):
    levels = {2: [1.0 - fraction, fraction]}
    current = levels[2]
    for n in range(3, 7):
        inverse_n = 1.0 / (n - 1)
        updated = [None] * n
        updated[n - 1] = inverse_n * fraction * current[n - 2]
        for j in range(1, n - 1):
            updated[n - 1 - j] = inverse_n * (
                (fraction + j) * current[n - 2 - j] + (n - j - fraction) * current[n - 1 - j]
            )
        updated[0] = inverse_n * (1.0 - fraction) * current[0]
        current = updated
        levels[n] = current
    zero_row = jnp.zeros_like(fraction)

    def entry_at(values_list, k):
        return values_list[k] if 0 <= k < len(values_list) else zero_row

    first = [entry_at(levels[5], t - 1) - entry_at(levels[5], t) for t in range(6)]
    second = [
        entry_at(levels[4], t - 2) - 2.0 * entry_at(levels[4], t - 1) + entry_at(levels[4], t)
        for t in range(6)
    ]
    return levels[6], first, second


def dense_rows(tables, cell, length):
    away = lax.broadcasted_iota(jnp.int32, (length, cell.shape[1]), 0).astype(f32) - cell
    summed = [jnp.zeros(away.shape, f32) for _ in tables]
    for t in range(6):
        here = away == float(t)
        summed = [jnp.where(here, table[t], so_far) for table, so_far in zip(tables, summed)]
    return summed


def unit_phase(turns):
    turns = turns - jnp.floor(turns + 0.5)
    quarter = jnp.floor(4.0 * turns + 0.5)
    rest = turns - 0.25 * quarter
    theta = (2.0 * math.pi) * rest
    square = theta * theta
    sine = theta * (
        1.0
        + square
        * (-1.0 / 6 + square * (1.0 / 120 + square * (-1.0 / 5040 + square * (1.0 / 362880))))
    )
    cosine = 1.0 + square * (
        -0.5
        + square
        * (1.0 / 24 + square * (-1.0 / 720 + square * (1.0 / 40320 - square * (1.0 / 3628800))))
    )
    odd = jnp.abs(quarter) == 1.0
    cos_out = jnp.where(odd, sine, cosine)
    sin_out = jnp.where(odd, cosine, sine)
    cos_out = jnp.where((quarter == 1.0) | (jnp.abs(quarter) == 2.0), -cos_out, cos_out)
    sin_out = jnp.where((quarter == -1.0) | (jnp.abs(quarter) == 2.0), -sin_out, sin_out)
    return cos_out, sin_out


def halves(value):
    high = value.astype(bf16)
    return high, (value - high.astype(f32)).astype(bf16)


def joined(left, right):
    return (
        jnp.concatenate([left[0], left[0], left[1]], axis=1),
        jnp.concatenate([right[0], right[1], right[0]], axis=0),
    )


def product(left, right):
    left, right = joined(left, right)
    return jnp.dot(left, right, preferred_element_type=f32)


def product3(left, right):
    def one(a, b):
        return jnp.dot(a, b, preferred_element_type=f32)

    return one(left[0], right[0]) + (one(left[0], right[1]) + one(left[1], right[0]))


def lane_sign(shape):
    return jnp.where(lax.broadcasted_iota(jnp.int32, shape, 1) < HALF, 1.0, -1.0).astype(f32)


def turned(value, sign):
    return pltpu.roll(value, HALF, 1) * sign


def fetch(source, target, semaphore):
    copy = pltpu.make_async_copy(source, target, semaphore)
    copy.start()
    return copy


def line_product(table_ref, r, value):
    rows = slice(r * QUARTER, (r + 1) * QUARTER)
    table = table_ref[rows, : 2 * QUARTER], table_ref[rows, 4 * QUARTER :]
    return product3(table, halves(value))


def forward_line(table_ref, quarters, turned_quarters):
    g, h = quarters, turned_quarters
    a, b, c, d = g[0] + g[2], g[0] - g[2], g[1] + g[3], g[1] - g[3]
    ta, tb, tc, td = h[0] + h[2], h[0] - h[2], h[1] + h[3], h[1] - h[3]
    lines = []
    for r, (one, other) in enumerate(
        ((a + c, ta + tc), (b + td, tb - d), (a - c, ta - tc), (b - td, tb + d))
    ):
        stacked = jnp.concatenate([one, other], axis=0)
        lines.append(line_product(table_ref, r, stacked))
    return lines


def inverse_line(table_ref, modes, turned_modes):
    z = []
    for r in range(4):
        stacked = jnp.concatenate([modes[r], -turned_modes[r]], axis=0)
        z.append(line_product(table_ref, r, stacked))
    a, b, c, d = z[0] + z[2], z[0] - z[2], z[1] + z[3], z[1] - z[3]
    width = d.shape[1]
    sign = lane_sign((QUARTER, LANES))
    td = jnp.concatenate(
        [turned(d[:, n : n + LANES], sign) for n in range(0, width, LANES)], axis=1
    )
    return [a + c, b - td, a - c, b + td]


def quarters_of(value):
    return [value[r * QUARTER : (r + 1) * QUARTER] for r in range(4)]


PIECES = (0, 16, 32, 64, 80, 96)
GROUPS = PART_X * CY // 4
CARRIERS = 3 * GROUPS


def lane_range(first):
    lane = lax.broadcasted_iota(jnp.int32, (SLABS, LANES), 1)
    return (lane >= first) & (lane < first + 16)


def pack_blocks(blocks):
    carriers = []
    for c in range(3):
        value = blocks[c]
        for half in range(2):
            gap = PADDED_Z + half * HALF
            shift = (gap - PIECES[2 * c + half]) % LANES
            value = jnp.where(lane_range(gap), pltpu.roll(blocks[3], shift, 1), value)
        carriers.append(value)
    return carriers


def unpack_block(carriers):
    value = jnp.zeros((SLABS, LANES), f32)
    for p, source in enumerate(PIECES):
        gap = PADDED_Z + p % 2 * HALF
        shift = (source - gap) % LANES
        value = jnp.where(lane_range(source), pltpu.roll(carriers[p // 2], shift, 1), value)
    return value


def rows_of(carrier):
    return pl.ds(carrier, SLABS, stride=CARRIERS)


def block_at(ref, j, y):
    block = j * CY + y
    group, place = block // 4, block % 4
    if place < 3:
        return ref[rows_of(3 * group + place), :]
    return unpack_block([ref[rows_of(3 * group + c), :] for c in range(3)])


def prepare_kernel(
    where_ref, shear_ref, counts_ref, cells_ref, offsets_ref, charges_ref, dipoles_ref,
    atoms_ref, base_ref, taps_ref, cos_ref, sin_ref,
    count_ref, cell_ref, offset_ref, charge_ref, dipole_ref, semaphores
):
    copies = [
        fetch(source, target, semaphores.at[n])
        for n, (source, target) in enumerate(
            (
                (counts_ref, count_ref),
                (cells_ref, cell_ref),
                (offsets_ref, offset_ref),
                (charges_ref, charge_ref.at[0]),
                (dipoles_ref, dipole_ref),
            )
        )
    ]
    slab, pencil = where_ref[0], where_ref[1]
    first = pencil * PART_Z
    row = lax.broadcasted_iota(jnp.int32, (PADDED_Z, LANES), 0)
    mode = (row + first).astype(f32)
    base_ref[...] = mode[:8]
    for t in range(6):
        cos_t, sin_t = unit_phase(mode * float(t) * (1.0 / NZ))
        taps_ref[t] = jnp.where(row < PART_Z, cos_t, 0.0)
        taps_ref[6 + t] = jnp.where(row < PART_Z, sin_t, 0.0)
    column = lax.broadcasted_iota(jnp.int32, (1, LANES), 1)
    rows = slab * CY + jnp.minimum(column, CY)
    index = lax.broadcasted_iota(jnp.int32, (NX, LANES), 0)
    residue = (
        (index >= QUARTER).astype(jnp.int32)
        + (index >= 2 * QUARTER).astype(jnp.int32)
        + (index >= 3 * QUARTER).astype(jnp.int32)
    )
    mode_x = 4 * (index - QUARTER * residue) + residue
    folds = jnp.where(mode_x < NX // 2, mode_x, mode_x - NX)
    ticks = folds * (shear_ref[0] * rows)
    whole = jnp.floor(ticks.astype(f32) * (1.0 / (NX * NY))).astype(jnp.int32)
    rest = ticks - whole * (NX * NY)
    cos_t, sin_t = unit_phase(rest.astype(f32) * (1.0 / (NX * NY)))
    cos_ref[...] = cos_t
    sin_ref[...] = sin_t
    for copy in copies:
        copy.wait()
    slot = lax.broadcasted_iota(jnp.int32, (1, ATOM_DEV), 1)
    live = jnp.zeros((1, ATOM_DEV), f32)
    for b in range(ATOM_DEV // ATOM_BLK):
        inside = (slot >= b * ATOM_BLK) & (slot < b * ATOM_BLK + count_ref[b])
        live = jnp.where(inside, 1.0, live)
    atoms_ref[0:1, :] = cell_ref[0:1, :].astype(f32)
    atoms_ref[1:2, :] = (cell_ref[1:2, :] - slab * CY).astype(f32)
    atoms_ref[2:3, :] = cell_ref[2:3, :].astype(f32)
    atoms_ref[3:6, :] = offset_ref[...]
    atoms_ref[6:7, :] = charge_ref[...] * live
    atoms_ref[7:10, :] = dipole_ref[...] * live
    atoms_ref[10:11, :] = live
    atoms_ref[11:16, :] = jnp.zeros((5, ATOM_DEV), f32)


def spline_table(atoms_ref, table_ref, orders):
    def pencil_body(pencil, carry):
        tables = spline_rows(atoms_ref[pencil, 3:6, :])
        for o in range(orders):
            for t in range(6):
                table_ref[pencil, o * 6 + t, 0:3, :] = tables[o][t]
        return carry

    lax.fori_loop(0, PENCILS, pencil_body, 0)


def weight_rows(table_ref, pencil, lanes, dim, orders):
    row = slice(dim, dim + 1)
    return [[table_ref[pencil, o * 6 + t, row, lanes] for t in range(6)] for o in range(orders)]


def pair_place(pair):
    pencil = pair // PAIRS
    return pencil, pl.ds(pl.multiple_of(pair % PAIRS * LANES, LANES), LANES)


def pair_window(pair, own, where_ref):
    if own:
        return pl.multiple_of(pair * 32, 8), WINDOW, (pair * 32).astype(f32)
    place = pair * 32 + where_ref[2]
    place = jnp.where(place >= NX, place - NX, place)
    first = place // 8 * 8
    return pl.multiple_of(first, 8), WIDE, (pair * 32 - (place - first)).astype(f32)


def z_waves(cell_z, weights, base_ref, taps_ref):
    turn = base_ref[...] * cell_z
    turn = turn - 360.0 * jnp.floor(turn * (1.0 / 360.0))
    cos_k, sin_k = unit_phase(turn * (1.0 / 360.0))
    turn = 8.0 * cell_z
    turn = turn - 360.0 * jnp.floor(turn * (1.0 / 360.0))
    cos_8, sin_8 = unit_phase(jnp.broadcast_to(turn * (1.0 / 360.0), cos_k.shape))
    pieces = [[] for _ in weights]
    pieces_im = [[] for _ in weights]
    for q in range(PADDED_Z // 8):
        span = slice(q * 8, q * 8 + 8)
        cos_t = [taps_ref[t, span, :] for t in range(6)]
        sin_t = [taps_ref[6 + t, span, :] for t in range(6)]
        for s, weight in enumerate(weights):
            real = weight[0] * cos_t[0] + sum(weight[t] * cos_t[t] for t in range(1, 6))
            imag = sum(weight[t] * sin_t[t] for t in range(1, 6))
            pieces[s].append(real * cos_k - imag * sin_k)
            pieces_im[s].append(-(real * sin_k + imag * cos_k))
        cos_k, sin_k = cos_k * cos_8 - sin_k * sin_8, sin_k * cos_8 + cos_k * sin_8
    return [
        (jnp.concatenate(re, axis=0), jnp.concatenate(im, axis=0))
        for re, im in zip(pieces, pieces_im)
    ]


def sampling_weights(
    start, own, where_ref, some_ref, table_ref, base_ref, taps_ref, waves_ref, x_ref, y_ref
):
    spline_table(some_ref, table_ref, 3)

    def pair_body(pair, carry):
        pencil, lanes = pair_place(pair)
        row = [some_ref[pencil, a : a + 1, lanes] for a in range(3)]
        _, window, origin = pair_window(pair, own, where_ref)
        dense_x = dense_rows(weight_rows(table_ref, pencil, lanes, 0, 3), row[0] - origin, window)
        dense_y = dense_rows(weight_rows(table_ref, pencil, lanes, 1, 3), row[1], 16)
        for p in range(3):
            x_ref[start + pair, p, :window] = dense_x[p]
            y_ref[start + pair, p] = dense_y[p]
        waves = z_waves(row[2], weight_rows(table_ref, pencil, lanes, 2, 3), base_ref, taps_ref)
        for s, (re, im) in enumerate(waves):
            re, im = halves(re), halves(im)
            columns = slice(s * LANES, (s + 1) * LANES)
            for n in range(2):
                waves_ref[start + pair, n, :PADDED_Z, columns] = re[n]
                waves_ref[start + pair, n, PADDED_Z:, columns] = im[n]
        return carry

    lax.fori_loop(0, PENCILS * PAIRS, pair_body, 0, unroll=2)


def keep_weights(atoms, where_ref, weights_ref, base_ref, taps_ref, kept, results, semaphores):
    for start, some_ref in zip((0, PENCILS * PAIRS), atoms):
        sampling_weights(
            start, start == 0, where_ref, some_ref, weights_ref, base_ref, taps_ref, *kept
        )
    copies = [fetch(kept[n], results[n], semaphores.at[n]) for n in range(3)]
    for copy in copies:
        copy.wait()


def spread_kernel(own, *refs):
    atoms_ref, where_ref, base_ref, taps_ref = refs[:4]
    if own:
        grid_ref, weights_ref = refs[4:]
        grid_ref[...] = jnp.zeros_like(grid_ref)
    else:
        slab_grid_ref, tables_ref, cos_ref, sin_ref, slab_atoms_ref, out_ref = refs[4:10]
        results, kept = refs[10:13], refs[13:16]
        grid_ref, table_ref, weights_ref, semaphores = refs[16:]
        table_copy = fetch(tables_ref, table_ref, semaphores.at[0])
        grid_ref[...] = slab_grid_ref[...]
    rows = list(range(CY)) if own else list(range(CY, 2 * CY - 1))
    part = CY * LANES
    gap = jnp.zeros((HALF - PADDED_Z, LANES), bf16)
    spline_table(atoms_ref, weights_ref, 2)

    def pair_body(pair, carry):
        pencil, lanes = pair_place(pair)
        row = [atoms_ref[pencil, a : a + 1, lanes] for a in range(10)]
        charge, dip_x, dip_y, dip_z = row[6:10]
        first_row, window, origin = pair_window(pair, own, where_ref)
        dense_x = dense_rows(
            weight_rows(weights_ref, pencil, lanes, 0, 2), row[0] - origin, window
        )
        dense_y = dense_rows(weight_rows(weights_ref, pencil, lanes, 1, 2), row[1], 16)
        value, first = weight_rows(weights_ref, pencil, lanes, 2, 2)
        mixed = [charge * value[t] + dip_z * first[t] for t in range(6)]
        right = []
        for re, im in z_waves(row[2], (mixed, value), base_ref, taps_ref):
            re, im = halves(re), halves(im)
            right.append(
                [
                    jnp.concatenate([re[n], gap, im[n], gap, im[n], gap, -re[n], gap], axis=0)
                    for n in range(2)
                ]
            )
        high, low = [jnp.concatenate([right[0][n], right[1][n]], axis=1) for n in range(2)]
        right = jnp.concatenate([high, low, high], axis=1)
        left = []
        for r in rows:
            value, first = dense_y[0][r : r + 1], dense_y[1][r : r + 1]
            left.append(
                jnp.concatenate(
                    [
                        value * dense_x[0],
                        (dip_x * value) * dense_x[1] + (dip_y * first) * dense_x[0],
                    ],
                    axis=1,
                )
            )
        high, low = halves(jnp.concatenate(left, axis=0))
        left = jnp.concatenate([high, high, low], axis=1)
        added = lax.dot_general(
            left, right, (((1,), (1,)), ((), ())), preferred_element_type=f32
        )
        at = pl.ds(first_row, window)
        for n in range(len(rows)):
            piece = added[n * window : (n + 1) * window]
            grid_ref[at, n * LANES : (n + 1) * LANES] += piece[:, :LANES]
            grid_ref[at, part + n * LANES : part + (n + 1) * LANES] += piece[:, LANES:]
        return carry

    lax.fori_loop(0, PENCILS * PAIRS, pair_body, 0, unroll=6)
    if own:
        return
    grid_ref[0:WIDE] += grid_ref[NX:EXTENDED]
    table_copy.wait()
    sign = lane_sign((NX, LANES))
    totals = []
    for first in range(0, CY, 2):
        lanes = slice(first * LANES, (first + 2) * LANES)
        below = slice(part + lanes.start, part + lanes.stop)
        line = jnp.concatenate(
            forward_line(
                table_ref, quarters_of(grid_ref[:NX, lanes]), quarters_of(grid_ref[:NX, below])
            ),
            axis=0,
        )
        for n, y in enumerate((first, first + 1)):
            one = line[:, n * LANES : (n + 1) * LANES]
            totals.append(one * cos_ref[:, y : y + 1] + turned(one, sign) * sin_ref[:, y : y + 1])
    for group in range(GROUPS):
        blocks = []
        for block in range(4 * group, 4 * group + 4):
            j, y = block // CY, block % CY
            blocks.append(totals[y][j * SLABS : (j + 1) * SLABS])
        for c, carrier in enumerate(pack_blocks(blocks)):
            out_ref[rows_of(3 * group + c), :] = carrier

    @pl.when(where_ref[1] % 2 == 1)
    def _():
        keep_weights(
            (slab_atoms_ref, atoms_ref), where_ref, weights_ref, base_ref, taps_ref,
            kept, results, semaphores
        )


def weights_kernel(
    atoms_ref, below_ref, where_ref, base_ref, taps_ref, waves_in_ref, x_in_ref, y_in_ref, *refs
):
    results, kept, weights_ref, semaphores = refs[:3], refs[3:6], refs[6], refs[7]

    @pl.when(where_ref[1] % 2 == 0)
    def _():
        keep_weights(
            (atoms_ref, below_ref), where_ref, weights_ref, base_ref, taps_ref,
            kept, results, semaphores
        )


def green_kernel(top_ref, norm_ref, mode_ref, out_ref):
    for j in range(PART_X):
        square = norm_ref[:, j : j + 1] + mode_ref[1:2, :]
        green = top_ref[:, j : j + 1] * mode_ref[0:1, :] / jnp.where(square == 0.0, 1.0, square)
        out_ref[:, j * LANES : (j + 1) * LANES] = jnp.where(square == 0.0, 0.0, green)


def filter_kernel(
    in_ref, tables_ref, backs_ref, green_ref, out_ref, table_ref, back_ref, semaphores
):
    copies = [
        fetch(tables_ref, table_ref, semaphores.at[0]),
        fetch(backs_ref, back_ref, semaphores.at[1]),
    ]
    sign = lane_sign((NY, LANES))
    energy = jnp.zeros((8, LANES), f32)
    blocks = []
    for first in range(0, PART_X, 2):
        lines = []
        for j in (first, first + 1):
            found = [block_at(in_ref, j, y) for y in range(CY)]
            lines.append(
                jnp.concatenate(
                    [one[16 * part : 16 * part + 16] for part in range(4) for one in found], axis=0
                )
            )
        swapped = jnp.concatenate([turned(one, sign) for one in lines], axis=1)
        lines = jnp.concatenate(lines, axis=1)
        if first == 0:
            copies[0].wait()
        spectrum = jnp.concatenate(
            forward_line(table_ref, quarters_of(lines), quarters_of(swapped)), axis=0
        )
        modes = []
        for n in range(2):
            j = first + n
            one = spectrum[:, n * LANES : (n + 1) * LANES]
            scaled = green_ref[:, j * LANES : (j + 1) * LANES] * one
            share = scaled * one
            energy = energy + sum(share[8 * i : 8 * i + 8] for i in range(NY // 8))
            modes.append(scaled)
        swapped = jnp.concatenate([turned(one, sign) for one in modes], axis=1)
        modes = jnp.concatenate(modes, axis=1)
        if first == 0:
            copies[1].wait()
        parts = inverse_line(back_ref, quarters_of(modes), quarters_of(swapped))
        for n in range(2):
            for y in range(CY):
                blocks.append(
                    jnp.concatenate(
                        [
                            one[16 * y : 16 * y + 16, n * LANES : (n + 1) * LANES]
                            for one in parts
                        ],
                        axis=0,
                    )
                )
        for group in range(first * CY // 4, (first + 2) * CY // 4):
            for c, carrier in enumerate(pack_blocks(blocks[4 * group : 4 * group + 4])):
                out_ref[rows_of(3 * group + c), :] = carrier
    lane = lax.broadcasted_iota(jnp.int32, (SLABS, LANES), 1)
    share = 0.5 * jnp.sum(energy)
    out_ref[rows_of(0), :] = jnp.where(lane == PART_Z, share, out_ref[rows_of(0), :])


def sample_kernel(own, *refs):
    atoms_ref, where_ref, waves_in_ref, x_in_ref, y_in_ref = refs[:5]
    if own:
        grid_ref, out_ref = refs[5:7]
    else:
        in_ref, cos_ref, sin_ref, tables_ref, out_ref, grid_ref, table_ref = refs[5:12]
    waves_ref, x_ref, y_ref, semaphores = refs[-4:]
    if not own:
        table_copy = fetch(tables_ref, table_ref, semaphores.at[3, 0])
    start = 0 if own else PENCILS * PAIRS

    def pair_copies(pair):
        return [
            pltpu.make_async_copy(source.at[start + pair], target.at[pair], semaphores.at[n, pair])
            for n, (source, target) in enumerate(
                ((waves_in_ref, waves_ref), (x_in_ref, x_ref), (y_in_ref, y_ref))
            )
        ]

    for pair in range(PENCILS * PAIRS):
        for copy in pair_copies(pair):
            copy.start()

    rows = list(range(CY)) if own else list(range(CY, 2 * CY - 1))
    energy = 0.0
    if not own:
        sign = lane_sign((NX, LANES))
        for first in range(0, CY, 2):
            modes, swapped = [], []
            for y in range(first, first + 2):
                line = jnp.concatenate([block_at(in_ref, j, y) for j in range(PART_X)], axis=0)
                other = turned(line, sign)
                cos_y, sin_y = cos_ref[:, y : y + 1], sin_ref[:, y : y + 1]
                modes.append(line * cos_y - other * sin_y)
                swapped.append(other * cos_y + line * sin_y)
            swapped = jnp.concatenate(swapped, axis=1)
            modes = jnp.concatenate(modes, axis=1)
            if first == 0:
                table_copy.wait()
            cells = jnp.concatenate(
                inverse_line(table_ref, quarters_of(modes), quarters_of(swapped)), axis=0
            )
            lanes = slice(first * LANES, (first + 2) * LANES)
            grid_ref[:NX, lanes] = cells
            grid_ref[NX:, lanes] = cells[:WIDE]
        lane = lax.broadcasted_iota(jnp.int32, (SLABS, LANES), 1)
        energy = jnp.sum(jnp.where(lane == PART_Z, in_ref[rows_of(0), :], 0.0))
    gap = jnp.zeros((HALF - PADDED_Z, 3 * LANES), bf16)

    def pair_body(pair, carry):
        pencil, lanes = pair_place(pair)
        for copy in pair_copies(pair):
            copy.wait()
        waves = [
            jnp.concatenate(
                [waves_ref[pair, n, :PADDED_Z], gap, waves_ref[pair, n, PADDED_Z:], gap],
                axis=0,
            )
            for n in range(2)
        ]
        first_row, window, _ = pair_window(pair, own, where_ref)
        at = pl.ds(first_row, window)
        cells = jnp.concatenate(
            [grid_ref[at, n * LANES : (n + 1) * LANES] for n in range(len(rows))], axis=0
        )
        read = product(halves(cells), waves)
        dense_x = [x_ref[pair, p, :window] for p in range(3)]
        dense_y = [y_ref[pair, p] for p in range(3)]
        lined = {}
        for order_y, order_z in ((0, 0), (1, 0), (2, 0), (0, 1), (1, 1), (0, 2)):
            lined[order_y, order_z] = sum(
                dense_y[order_y][r : r + 1]
                * read[n * window : (n + 1) * window, order_z * LANES : (order_z + 1) * LANES]
                for n, r in enumerate(rows)
            )

        def sampled(p, r, s):
            return jnp.sum(dense_x[p] * lined[r, s], axis=0, keepdims=True)

        charge, dip_x, dip_y, dip_z, live = [
            atoms_ref[pencil, a : a + 1, lanes] for a in range(6, 11)
        ]
        s100 = sampled(1, 0, 0)
        s010 = sampled(0, 1, 0)
        s001 = sampled(0, 0, 1)
        s110 = sampled(1, 1, 0)
        s101 = sampled(1, 0, 1)
        s011 = sampled(0, 1, 1)
        out = [
            live * sampled(0, 0, 0),
            live * s100,
            live * s010,
            live * s001,
            charge * s100 + dip_x * sampled(2, 0, 0) + dip_y * s110 + dip_z * s101,
            charge * s010 + dip_x * s110 + dip_y * sampled(0, 2, 0) + dip_z * s011,
            charge * s001 + dip_x * s101 + dip_y * s011 + dip_z * sampled(0, 0, 2),
            jnp.full(live.shape, energy, f32),
        ]
        out_ref[pencil, :, lanes] = jnp.concatenate(out, axis=0)
        return carry

    lax.fori_loop(0, PENCILS * PAIRS, pair_body, 0, unroll=6)


def finish_kernel(in_ref, charge_ref, dipole_ref, position_ref, energy_ref, row_ref, semaphore):
    total = (in_ref[0] + in_ref[1]) + (in_ref[2] + in_ref[3])
    row_ref[...] = total[0:1]
    copy = fetch(row_ref.at[0], charge_ref, semaphore)
    dipole_ref[...] = total[1:4]
    position_ref[...] = total[4:7]
    energy_ref[...] = total[7:8, 0:1]
    copy.wait()


def spline_modulus(angles):
    return (66.0 + 52.0 * jnp.cos(angles) + 2.0 * jnp.cos(2.0 * angles)) / 120.0


def mode_of(row):
    return 4 * (row % QUARTER) + row // QUARTER


def folded(index, size):
    return (index + size // 2) % size - size // 2


SPACES = {"v": pltpu.VMEM, "h": pltpu.HBM, "s": pltpu.SMEM}
WORK = {"flops": 1_000_000_000, "bytes_accessed": 8_000_000}


def out_place(shape):
    pinned = isinstance(shape, type(pltpu.HBM((8, LANES), f32)))
    return pl.BlockSpec(memory_space=pltpu.HBM if pinned else pltpu.VMEM)


def call(kernel, inputs, out_shape, scratch=(), aliases=()):
    def run(*operands):
        placed = [
            pltpu.with_memory_space_constraint(one, pltpu.HBM) if where == "h" else one
            for one, where in zip(operands, inputs)
        ]
        return pl.pallas_call(
            kernel,
            out_shape=out_shape,
            in_specs=[pl.BlockSpec(memory_space=SPACES[one]) for one in inputs],
            out_specs=jax.tree.map(out_place, out_shape),
            scratch_shapes=list(scratch),
            input_output_aliases=dict(aliases),
            compiler_params=pltpu.CompilerParams(vmem_limit_bytes=28 * 1024 * 1024),
            cost_estimate=pl.CostEstimate(transcendentals=0, **WORK),
        )(*placed)

    return run


def next_slab(value, back=False):
    step = -1 if back else 1
    return lax.ppermute(value, "gy", [(i, (i + step) % SLABS) for i in range(SLABS)])


def swap_slabs(lines):
    lines = lines.reshape(SLABS, CARRIERS, 1, LANES)
    lines = lax.all_to_all(lines, "gy", split_axis=0, concat_axis=0, tiled=True)
    return lines.reshape(SLABS * CARRIERS, LANES)


def on_device(cell_index, offsets, charges, dipoles, block_count, shear_cells):
    pencil_index = lax.axis_index("gx")
    slab_index = lax.axis_index("gy")
    x_forward, x_inverse, y_forward, y_inverse = wave_tables()
    shape = jax.ShapeDtypeStruct
    shift = jnp.where(slab_index == 0, shear_cells[0], 0)
    where = jnp.stack([slab_index, pencil_index, shift])

    mine, base, taps, cos_t, sin_t = call(
        prepare_kernel,
        "sshhhhh",
        (
            shape((16, ATOM_DEV), f32),
            shape((8, LANES), f32),
            shape((12, PADDED_Z, LANES), f32),
            shape((NX, LANES), f32),
            shape((NX, LANES), f32),
        ),
        [
            pltpu.SMEM(block_count.shape, jnp.int32),
            pltpu.VMEM((3, ATOM_DEV), jnp.int32),
            pltpu.VMEM((3, ATOM_DEV), f32),
            pltpu.VMEM((1, ATOM_DEV), f32),
            pltpu.VMEM((3, ATOM_DEV), f32),
            pltpu.SemaphoreType.DMA((5,)),
        ],
    )(
        where,
        shear_cells,
        block_count,
        cell_index,
        offsets,
        charges,
        dipoles,
    )
    atoms = lax.all_gather(mine, "gx", axis=0, tiled=False)
    below_atoms = next_slab(atoms)

    packed = shape((SLABS * CARRIERS, LANES), f32)
    table_space = pltpu.VMEM((NX, 6 * QUARTER), bf16)
    two = pltpu.SemaphoreType.DMA((2,))
    pairs = 2 * PENCILS * PAIRS
    held = [
        ((2, 2 * PADDED_Z, 3 * LANES), bf16),
        ((3, WIDE, LANES), f32),
        ((3, 16, LANES), f32),
    ]
    weights_space = pltpu.VMEM((PENCILS, 18, 8, ATOM_DEV), f32)
    four = pltpu.SemaphoreType.DMA((4,))
    slab_grid = call(
        lambda *refs: spread_kernel(True, *refs),
        "vsvv",
        shape((EXTENDED, 2 * CY * LANES), f32),
        [weights_space],
    )(atoms, where, base, taps)
    lines, *weights = call(
        lambda *refs: spread_kernel(False, *refs),
        "vsvvvhvvv",
        (packed, *(pltpu.HBM((pairs, *dims), kind) for dims, kind in held)),
        [
            *(pltpu.VMEM((pairs, *dims), kind) for dims, kind in held),
            pltpu.VMEM((EXTENDED, 2 * CY * LANES), f32),
            table_space,
            weights_space,
            four,
        ],
    )(below_atoms, where, base, taps, slab_grid, x_forward, cos_t, sin_t, atoms)
    lines, shear_cells = lax.optimization_barrier((lines, shear_cells))
    shear_step = shear_cells[0]

    own_x = folded(mode_of(jnp.arange(8, dtype=jnp.int32) * SLABS + slab_index), NX)[None, :]
    own_y = folded(mode_of(jnp.arange(NY, dtype=jnp.int32)), NY)[:, None]
    float_x = own_x.astype(f32)
    wave_y = own_y.astype(f32) + float_x * shear_step.astype(f32) / NX
    norm = (float_x / NX) ** 2 + (wave_y / NY) ** 2
    moduli = spline_modulus(2.0 * math.pi * float_x / NX) * spline_modulus(
        2.0 * math.pi * wave_y / NY
    )
    decay = (math.pi / screening) ** 2
    top = jnp.exp(-decay * norm) / (math.pi * moduli * moduli)
    top = jnp.where((own_x == -(NX // 2)) | (own_y == -(NY // 2)), 0.0, top)
    lane = jnp.arange(LANES, dtype=jnp.int32) % HALF
    mode_z = pencil_index * PART_Z + lane
    kept = lane < PART_Z
    float_z = mode_z.astype(f32)
    norm_z = (float_z / NZ) ** 2
    modulus_z = spline_modulus(2.0 * math.pi * float_z / NZ)
    twice = jnp.where(mode_z == 0, 1.0, 2.0) / (NX * NY * NZ)
    mode_top = jnp.where(kept, twice * jnp.exp(-decay * norm_z) / (modulus_z * modulus_z), 0.0)
    mode_norm = jnp.where(kept, norm_z, 1.0)
    mode = jnp.stack([mode_top, mode_norm])

    green = call(green_kernel, "vvv", shape((NY, PART_X * LANES), f32))(top, norm, mode)
    lines = swap_slabs(lines)
    filtered = call(filter_kernel, "vhhv", packed, [table_space, table_space, two])(
        lines, y_forward, y_inverse, green
    )
    filtered, atoms, below_atoms = lax.optimization_barrier((filtered, atoms, below_atoms))
    weights = call(
        weights_kernel,
        "vvsvvhhh",
        tuple(pltpu.HBM((pairs, *dims), kind) for dims, kind in held),
        [*(pltpu.VMEM((pairs, *dims), kind) for dims, kind in held), weights_space, four],
        ((5, 0), (6, 1), (7, 2)),
    )(atoms, below_atoms, where, base, taps, *weights)
    filtered = swap_slabs(filtered)
    shares_shape = shape((PENCILS, 8, ATOM_DEV), f32)
    sample_spaces = [
        *(pltpu.VMEM((pairs // 2, *dims), kind) for dims, kind in held),
        pltpu.SemaphoreType.DMA((4, pairs // 2)),
    ]
    below_shares, potential = call(
        lambda *refs: sample_kernel(False, *refs),
        "vshhhvvvh",
        (shares_shape, shape((EXTENDED, CY * LANES), f32)),
        [table_space, *sample_spaces],
    )(below_atoms, where, *weights, filtered, cos_t, sin_t, x_inverse)
    below_shares = next_slab(below_shares, back=True)
    shares = call(
        lambda *refs: sample_kernel(True, *refs), "vshhhv", shares_shape, sample_spaces
    )(atoms, where, *weights, potential)
    shares = lax.all_to_all(shares + below_shares, "gx", split_axis=0, concat_axis=0, tiled=True)
    charge_grad, dipole_grad, position_grad, energy = call(
        finish_kernel,
        "v",
        (
            pltpu.HBM((ATOM_DEV,), f32),
            shape((3, ATOM_DEV), f32),
            shape((3, ATOM_DEV), f32),
            shape((1, 1), f32),
        ),
        [pltpu.VMEM((1, ATOM_DEV), f32), pltpu.SemaphoreType.DMA],
    )(shares)
    return charge_grad, dipole_grad, position_grad, energy[0]


def solution(mesh):
    placed = (
        P(None, ("gy", "gx")),
        P(None, ("gy", "gx")),
        P(("gy", "gx")),
        P(None, ("gy", "gx")),
        P(("gy", "gx")),
        P(),
    )
    return jax.shard_map(
        on_device,
        mesh=mesh,
        in_specs=placed,
        out_specs=(P(("gy", "gx")), P(None, ("gy", "gx")), P(None, ("gy", "gx")), P()),
        check_vma=False,
    )
```

```python
import math

import jax
import jax.numpy as jnp
import ml_dtypes
import numpy as np
from jax import lax
from jax.experimental import pallas as pl
from jax.experimental.pallas import tpu as pltpu
from jax.sharding import PartitionSpec as P

NX = 384
NY = 384
NZ = 360
CY = 6
CX = 96
PENCILS = 4
SLABS = 64
PART_X = 6
PART_Z = 45
ATOM_BLK = 64
ATOM_DEV = 384
PAIRS = 3
WINDOW = 40
WIDE = 48
EXTENDED = NX + WIDE
HALF = 64
LANES = 128
PADDED_Z = 48
QUARTER = 96
screening = 0.9
f32 = jnp.float32
bf16 = jnp.bfloat16


def split_table(table):
    high = table.astype(ml_dtypes.bfloat16)
    low = (table - high.astype(np.float64)).astype(ml_dtypes.bfloat16)
    return np.concatenate([high, high, low], axis=1)


def wave_tables():
    quarter = np.arange(QUARTER)
    mode = np.arange(4)[:, None] + 4 * quarter[None, :]
    row_y = CY * (quarter % 16) + quarter // 16
    tables = []
    for place in (quarter, row_y):
        ticks = mode[:, :, None] * place % NX
        for table in (ticks, ticks.transpose(0, 2, 1)):
            angle = 2.0 * np.pi / NX * table.reshape(NX, QUARTER)
            tables.append(split_table(np.concatenate([np.cos(angle), np.sin(angle)], axis=1)))
    return tables


def spline_rows(fraction):
    levels = {2: [1.0 - fraction, fraction]}
    current = levels[2]
    for n in range(3, 7):
        inverse_n = 1.0 / (n - 1)
        updated = [None] * n
        updated[n - 1] = inverse_n * fraction * current[n - 2]
        for j in range(1, n - 1):
            updated[n - 1 - j] = inverse_n * (
                (fraction + j) * current[n - 2 - j] + (n - j - fraction) * current[n - 1 - j]
            )
        updated[0] = inverse_n * (1.0 - fraction) * current[0]
        current = updated
        levels[n] = current
    zero_row = jnp.zeros_like(fraction)

    def entry_at(values_list, k):
        return values_list[k] if 0 <= k < len(values_list) else zero_row

    first = [entry_at(levels[5], t - 1) - entry_at(levels[5], t) for t in range(6)]
    second = [
        entry_at(levels[4], t - 2) - 2.0 * entry_at(levels[4], t - 1) + entry_at(levels[4], t)
        for t in range(6)
    ]
    return levels[6], first, second


def dense_rows(tables, cell, length):
    away = lax.broadcasted_iota(jnp.int32, (length, cell.shape[1]), 0).astype(f32) - cell
    summed = [jnp.zeros(away.shape, f32) for _ in tables]
    for t in range(6):
        here = away == float(t)
        summed = [jnp.where(here, table[t], so_far) for table, so_far in zip(tables, summed)]
    return summed


def unit_phase(turns):
    turns = turns - jnp.floor(turns + 0.5)
    quarter = jnp.floor(4.0 * turns + 0.5)
    rest = turns - 0.25 * quarter
    theta = (2.0 * math.pi) * rest
    square = theta * theta
    sine = theta * (
        1.0
        + square
        * (-1.0 / 6 + square * (1.0 / 120 + square * (-1.0 / 5040 + square * (1.0 / 362880))))
    )
    cosine = 1.0 + square * (
        -0.5
        + square
        * (1.0 / 24 + square * (-1.0 / 720 + square * (1.0 / 40320 - square * (1.0 / 3628800))))
    )
    odd = jnp.abs(quarter) == 1.0
    cos_out = jnp.where(odd, sine, cosine)
    sin_out = jnp.where(odd, cosine, sine)
    cos_out = jnp.where((quarter == 1.0) | (jnp.abs(quarter) == 2.0), -cos_out, cos_out)
    sin_out = jnp.where((quarter == -1.0) | (jnp.abs(quarter) == 2.0), -sin_out, sin_out)
    return cos_out, sin_out


def halves(value):
    high = value.astype(bf16)
    return high, (value - high.astype(f32)).astype(bf16)


def joined(left, right):
    return (
        jnp.concatenate([left[0], left[0], left[1]], axis=1),
        jnp.concatenate([right[0], right[1], right[0]], axis=0),
    )


def product(left, right):
    left, right = joined(left, right)
    return jnp.dot(left, right, preferred_element_type=f32)


def product3(left, right):
    def one(a, b):
        return jnp.dot(a, b, preferred_element_type=f32)

    return one(left[0], right[0]) + (one(left[0], right[1]) + one(left[1], right[0]))


def lane_sign(shape):
    return jnp.where(lax.broadcasted_iota(jnp.int32, shape, 1) < HALF, 1.0, -1.0).astype(f32)


def turned(value, sign):
    return pltpu.roll(value, HALF, 1) * sign


def fetch(source, target, semaphore):
    copy = pltpu.make_async_copy(source, target, semaphore)
    copy.start()
    return copy


def line_product(table_ref, r, value):
    rows = slice(r * QUARTER, (r + 1) * QUARTER)
    table = table_ref[rows, : 2 * QUARTER], table_ref[rows, 4 * QUARTER :]
    return product3(table, halves(value))


def forward_line(table_ref, quarters, turned_quarters):
    g, h = quarters, turned_quarters
    a, b, c, d = g[0] + g[2], g[0] - g[2], g[1] + g[3], g[1] - g[3]
    ta, tb, tc, td = h[0] + h[2], h[0] - h[2], h[1] + h[3], h[1] - h[3]
    lines = []
    for r, (one, other) in enumerate(
        ((a + c, ta + tc), (b + td, tb - d), (a - c, ta - tc), (b - td, tb + d))
    ):
        stacked = jnp.concatenate([one, other], axis=0)
        lines.append(line_product(table_ref, r, stacked))
    return lines


def inverse_line(table_ref, modes, turned_modes):
    z = []
    for r in range(4):
        stacked = jnp.concatenate([modes[r], -turned_modes[r]], axis=0)
        z.append(line_product(table_ref, r, stacked))
    a, b, c, d = z[0] + z[2], z[0] - z[2], z[1] + z[3], z[1] - z[3]
    width = d.shape[1]
    sign = lane_sign((QUARTER, LANES))
    td = jnp.concatenate(
        [turned(d[:, n : n + LANES], sign) for n in range(0, width, LANES)], axis=1
    )
    return [a + c, b - td, a - c, b + td]


def quarters_of(value):
    return [value[r * QUARTER : (r + 1) * QUARTER] for r in range(4)]


PIECES = (0, 16, 32, 64, 80, 96)
GROUPS = PART_X * CY // 4
CARRIERS = 3 * GROUPS


def lane_range(first):
    lane = lax.broadcasted_iota(jnp.int32, (SLABS, LANES), 1)
    return (lane >= first) & (lane < first + 16)


def pack_blocks(blocks):
    carriers = []
    for c in range(3):
        value = blocks[c]
        for half in range(2):
            gap = PADDED_Z + half * HALF
            shift = (gap - PIECES[2 * c + half]) % LANES
            value = jnp.where(lane_range(gap), pltpu.roll(blocks[3], shift, 1), value)
        carriers.append(value)
    return carriers


def unpack_block(carriers):
    value = jnp.zeros((SLABS, LANES), f32)
    for p, source in enumerate(PIECES):
        gap = PADDED_Z + p % 2 * HALF
        shift = (source - gap) % LANES
        value = jnp.where(lane_range(source), pltpu.roll(carriers[p // 2], shift, 1), value)
    return value


def rows_of(carrier):
    return pl.ds(carrier, SLABS, stride=CARRIERS)


def block_at(ref, j, y):
    block = j * CY + y
    group, place = block // 4, block % 4
    if place < 3:
        return ref[rows_of(3 * group + place), :]
    return unpack_block([ref[rows_of(3 * group + c), :] for c in range(3)])


def prepare_kernel(
    where_ref, shear_ref, counts_ref, cells_ref, offsets_ref, charges_ref, dipoles_ref,
    atoms_ref, base_ref, taps_ref, cos_ref, sin_ref,
    count_ref, cell_ref, offset_ref, charge_ref, dipole_ref, semaphores
):
    copies = [
        fetch(source, target, semaphores.at[n])
        for n, (source, target) in enumerate(
            (
                (counts_ref, count_ref),
                (cells_ref, cell_ref),
                (offsets_ref, offset_ref),
                (charges_ref, charge_ref.at[0]),
                (dipoles_ref, dipole_ref),
            )
        )
    ]
    slab, pencil = where_ref[0], where_ref[1]
    first = pencil * PART_Z
    row = lax.broadcasted_iota(jnp.int32, (PADDED_Z, LANES), 0)
    mode = (row + first).astype(f32)
    base_ref[...] = mode[:8]
    for t in range(6):
        cos_t, sin_t = unit_phase(mode * float(t) * (1.0 / NZ))
        taps_ref[t] = jnp.where(row < PART_Z, cos_t, 0.0)
        taps_ref[6 + t] = jnp.where(row < PART_Z, sin_t, 0.0)
    column = lax.broadcasted_iota(jnp.int32, (1, LANES), 1)
    rows = slab * CY + jnp.minimum(column, CY)
    index = lax.broadcasted_iota(jnp.int32, (NX, LANES), 0)
    residue = (
        (index >= QUARTER).astype(jnp.int32)
        + (index >= 2 * QUARTER).astype(jnp.int32)
        + (index >= 3 * QUARTER).astype(jnp.int32)
    )
    mode_x = 4 * (index - QUARTER * residue) + residue
    folds = jnp.where(mode_x < NX // 2, mode_x, mode_x - NX)
    ticks = folds * (shear_ref[0] * rows)
    whole = jnp.floor(ticks.astype(f32) * (1.0 / (NX * NY))).astype(jnp.int32)
    rest = ticks - whole * (NX * NY)
    cos_t, sin_t = unit_phase(rest.astype(f32) * (1.0 / (NX * NY)))
    cos_ref[...] = cos_t
    sin_ref[...] = sin_t
    for copy in copies:
        copy.wait()
    slot = lax.broadcasted_iota(jnp.int32, (1, ATOM_DEV), 1)
    live = jnp.zeros((1, ATOM_DEV), f32)
    for b in range(ATOM_DEV // ATOM_BLK):
        inside = (slot >= b * ATOM_BLK) & (slot < b * ATOM_BLK + count_ref[b])
        live = jnp.where(inside, 1.0, live)
    atoms_ref[0:1, :] = cell_ref[0:1, :].astype(f32)
    atoms_ref[1:2, :] = (cell_ref[1:2, :] - slab * CY).astype(f32)
    atoms_ref[2:3, :] = cell_ref[2:3, :].astype(f32)
    atoms_ref[3:6, :] = offset_ref[...]
    atoms_ref[6:7, :] = charge_ref[...] * live
    atoms_ref[7:10, :] = dipole_ref[...] * live
    atoms_ref[10:11, :] = live
    atoms_ref[11:16, :] = jnp.zeros((5, ATOM_DEV), f32)


def spline_table(atoms_ref, table_ref, orders):
    def pencil_body(pencil, carry):
        tables = spline_rows(atoms_ref[pencil, 3:6, :])
        for o in range(orders):
            for t in range(6):
                table_ref[pencil, o * 6 + t, 0:3, :] = tables[o][t]
        return carry

    lax.fori_loop(0, PENCILS, pencil_body, 0)


def weight_rows(table_ref, pencil, lanes, dim, orders):
    row = slice(dim, dim + 1)
    return [[table_ref[pencil, o * 6 + t, row, lanes] for t in range(6)] for o in range(orders)]


def pair_place(pair):
    pencil = pair // PAIRS
    return pencil, pl.ds(pl.multiple_of(pair % PAIRS * LANES, LANES), LANES)


def pair_window(pair, own, where_ref):
    if own:
        return pl.multiple_of(pair * 32, 8), WINDOW, (pair * 32).astype(f32)
    place = pair * 32 + where_ref[2]
    place = jnp.where(place >= NX, place - NX, place)
    first = place // 8 * 8
    return pl.multiple_of(first, 8), WIDE, (pair * 32 - (place - first)).astype(f32)


def z_waves(cell_z, weights, base_ref, taps_ref):
    turn = base_ref[...] * cell_z
    turn = turn - 360.0 * jnp.floor(turn * (1.0 / 360.0))
    cos_k, sin_k = unit_phase(turn * (1.0 / 360.0))
    turn = 8.0 * cell_z
    turn = turn - 360.0 * jnp.floor(turn * (1.0 / 360.0))
    cos_8, sin_8 = unit_phase(jnp.broadcast_to(turn * (1.0 / 360.0), cos_k.shape))
    pieces = [[] for _ in weights]
    pieces_im = [[] for _ in weights]
    for q in range(PADDED_Z // 8):
        span = slice(q * 8, q * 8 + 8)
        cos_t = [taps_ref[t, span, :] for t in range(6)]
        sin_t = [taps_ref[6 + t, span, :] for t in range(6)]
        for s, weight in enumerate(weights):
            real = weight[0] * cos_t[0] + sum(weight[t] * cos_t[t] for t in range(1, 6))
            imag = sum(weight[t] * sin_t[t] for t in range(1, 6))
            pieces[s].append(real * cos_k - imag * sin_k)
            pieces_im[s].append(-(real * sin_k + imag * cos_k))
        cos_k, sin_k = cos_k * cos_8 - sin_k * sin_8, sin_k * cos_8 + cos_k * sin_8
    return [
        (jnp.concatenate(re, axis=0), jnp.concatenate(im, axis=0))
        for re, im in zip(pieces, pieces_im)
    ]


def sampling_weights(
    start, own, where_ref, some_ref, table_ref, base_ref, taps_ref, waves_ref, x_ref, y_ref
):
    spline_table(some_ref, table_ref, 3)

    def pair_body(pair, carry):
        pencil, lanes = pair_place(pair)
        row = [some_ref[pencil, a : a + 1, lanes] for a in range(3)]
        _, window, origin = pair_window(pair, own, where_ref)
        dense_x = dense_rows(weight_rows(table_ref, pencil, lanes, 0, 3), row[0] - origin, window)
        dense_y = dense_rows(weight_rows(table_ref, pencil, lanes, 1, 3), row[1], 16)
        for p in range(3):
            x_ref[start + pair, p, :window] = dense_x[p]
            y_ref[start + pair, p] = dense_y[p]
        waves = z_waves(row[2], weight_rows(table_ref, pencil, lanes, 2, 3), base_ref, taps_ref)
        for s, (re, im) in enumerate(waves):
            re, im = halves(re), halves(im)
            columns = slice(s * LANES, (s + 1) * LANES)
            for n in range(2):
                waves_ref[start + pair, n, :PADDED_Z, columns] = re[n]
                waves_ref[start + pair, n, PADDED_Z:, columns] = im[n]
        return carry

    lax.fori_loop(0, PENCILS * PAIRS, pair_body, 0, unroll=2)


def spread_kernel(own, *refs):
    atoms_ref, where_ref, base_ref, taps_ref = refs[:4]
    if own:
        grid_ref, weights_ref = refs[4:]
        grid_ref[...] = jnp.zeros_like(grid_ref)
    else:
        _, tables_ref, cos_ref, sin_ref, slab_atoms_ref, grid_ref, out_ref = refs[4:11]
        results, kept = refs[11:14], refs[14:17]
        table_ref, weights_ref, semaphores = refs[17:]
        table_copy = fetch(tables_ref, table_ref, semaphores.at[0])
    rows = list(range(CY)) if own else list(range(CY, 2 * CY - 1))
    part = CY * LANES
    gap = jnp.zeros((HALF - PADDED_Z, LANES), bf16)
    spline_table(atoms_ref, weights_ref, 2)

    def pair_body(pair, carry):
        pencil, lanes = pair_place(pair)
        row = [atoms_ref[pencil, a : a + 1, lanes] for a in range(10)]
        charge, dip_x, dip_y, dip_z = row[6:10]
        first_row, window, origin = pair_window(pair, own, where_ref)
        dense_x = dense_rows(
            weight_rows(weights_ref, pencil, lanes, 0, 2), row[0] - origin, window
        )
        dense_y = dense_rows(weight_rows(weights_ref, pencil, lanes, 1, 2), row[1], 16)
        value, first = weight_rows(weights_ref, pencil, lanes, 2, 2)
        mixed = [charge * value[t] + dip_z * first[t] for t in range(6)]
        right = []
        for re, im in z_waves(row[2], (mixed, value), base_ref, taps_ref):
            re, im = halves(re), halves(im)
            right.append(
                [
                    jnp.concatenate([re[n], gap, im[n], gap, im[n], gap, -re[n], gap], axis=0)
                    for n in range(2)
                ]
            )
        high, low = [jnp.concatenate([right[0][n], right[1][n]], axis=1) for n in range(2)]
        right = jnp.concatenate([high, low, high], axis=1)
        left = []
        for r in rows:
            value, first = dense_y[0][r : r + 1], dense_y[1][r : r + 1]
            left.append(
                jnp.concatenate(
                    [
                        value * dense_x[0],
                        (dip_x * value) * dense_x[1] + (dip_y * first) * dense_x[0],
                    ],
                    axis=1,
                )
            )
        high, low = halves(jnp.concatenate(left, axis=0))
        left = jnp.concatenate([high, high, low], axis=1)
        added = lax.dot_general(
            left, right, (((1,), (1,)), ((), ())), preferred_element_type=f32
        )
        at = pl.ds(first_row, window)
        for n in range(len(rows)):
            piece = added[n * window : (n + 1) * window]
            grid_ref[at, n * LANES : (n + 1) * LANES] += piece[:, :LANES]
            grid_ref[at, part + n * LANES : part + (n + 1) * LANES] += piece[:, LANES:]
        return carry

    lax.fori_loop(0, PENCILS * PAIRS, pair_body, 0, unroll=6)
    if own:
        return
    grid_ref[0:WIDE] += grid_ref[NX:EXTENDED]
    table_copy.wait()
    sign = lane_sign((NX, LANES))
    totals = []
    for first in range(0, CY, 2):
        lanes = slice(first * LANES, (first + 2) * LANES)
        below = slice(part + lanes.start, part + lanes.stop)
        line = jnp.concatenate(
            forward_line(
                table_ref, quarters_of(grid_ref[:NX, lanes]), quarters_of(grid_ref[:NX, below])
            ),
            axis=0,
        )
        for n, y in enumerate((first, first + 1)):
            one = line[:, n * LANES : (n + 1) * LANES]
            totals.append(one * cos_ref[:, y : y + 1] + turned(one, sign) * sin_ref[:, y : y + 1])
    for group in range(GROUPS):
        blocks = []
        for block in range(4 * group, 4 * group + 4):
            j, y = block // CY, block % CY
            blocks.append(totals[y][j * SLABS : (j + 1) * SLABS])
        for c, carrier in enumerate(pack_blocks(blocks)):
            out_ref[rows_of(3 * group + c), :] = carrier

    @pl.when(where_ref[1] % 2 == 1)
    def _():
        for start, some_ref in ((0, slab_atoms_ref), (PENCILS * PAIRS, atoms_ref)):
            sampling_weights(
                start, start == 0, where_ref, some_ref, weights_ref, base_ref, taps_ref, *kept
            )
        copies = [fetch(kept[n], results[n], semaphores.at[n]) for n in range(3)]
        for copy in copies:
            copy.wait()


def green_kernel(top_ref, norm_ref, mode_ref, out_ref):
    for j in range(PART_X):
        square = norm_ref[:, j : j + 1] + mode_ref[1:2, :]
        green = top_ref[:, j : j + 1] * mode_ref[0:1, :] / jnp.where(square == 0.0, 1.0, square)
        out_ref[:, j * LANES : (j + 1) * LANES] = jnp.where(square == 0.0, 0.0, green)


def filter_kernel(
    in_ref, tables_ref, backs_ref, green_ref, out_ref, table_ref, back_ref, semaphores
):
    copies = [
        fetch(tables_ref, table_ref, semaphores.at[0]),
        fetch(backs_ref, back_ref, semaphores.at[1]),
    ]
    sign = lane_sign((NY, LANES))
    energy = jnp.zeros((8, LANES), f32)
    blocks = []
    for first in range(0, PART_X, 2):
        lines = []
        for j in (first, first + 1):
            found = [block_at(in_ref, j, y) for y in range(CY)]
            lines.append(
                jnp.concatenate(
                    [one[16 * part : 16 * part + 16] for part in range(4) for one in found], axis=0
                )
            )
        swapped = jnp.concatenate([turned(one, sign) for one in lines], axis=1)
        lines = jnp.concatenate(lines, axis=1)
        if first == 0:
            copies[0].wait()
        spectrum = jnp.concatenate(
            forward_line(table_ref, quarters_of(lines), quarters_of(swapped)), axis=0
        )
        modes = []
        for n in range(2):
            j = first + n
            one = spectrum[:, n * LANES : (n + 1) * LANES]
            scaled = green_ref[:, j * LANES : (j + 1) * LANES] * one
            share = scaled * one
            energy = energy + sum(share[8 * i : 8 * i + 8] for i in range(NY // 8))
            modes.append(scaled)
        swapped = jnp.concatenate([turned(one, sign) for one in modes], axis=1)
        modes = jnp.concatenate(modes, axis=1)
        if first == 0:
            copies[1].wait()
        parts = inverse_line(back_ref, quarters_of(modes), quarters_of(swapped))
        for n in range(2):
            for y in range(CY):
                blocks.append(
                    jnp.concatenate(
                        [
                            one[16 * y : 16 * y + 16, n * LANES : (n + 1) * LANES]
                            for one in parts
                        ],
                        axis=0,
                    )
                )
        for group in range(first * CY // 4, (first + 2) * CY // 4):
            for c, carrier in enumerate(pack_blocks(blocks[4 * group : 4 * group + 4])):
                out_ref[rows_of(3 * group + c), :] = carrier
    lane = lax.broadcasted_iota(jnp.int32, (SLABS, LANES), 1)
    share = 0.5 * jnp.sum(energy)
    out_ref[rows_of(0), :] = jnp.where(lane == PART_Z, share, out_ref[rows_of(0), :])


def sample_kernel(own, *refs):
    if own:
        atoms_ref, where_ref, waves_ref, x_ref, y_ref, grid_ref, out_ref = refs
    else:
        atoms_ref, where_ref, base_ref, taps_ref = refs[:4]
        kept = refs[4:7]
        in_ref, cos_ref, sin_ref, tables_ref, slab_atoms_ref, out_ref, grid_ref = refs[7:14]
        slab_weights, below_weights = refs[14:17], refs[17:20]
        waves_ref, x_ref, y_ref = below_weights
        table_ref, weights_ref, semaphores = refs[20:]
        table_copy = fetch(tables_ref, table_ref, semaphores.at[6])
        later = where_ref[1] % 2 == 0
        pairs = PENCILS * PAIRS
        copies = [
            pltpu.make_async_copy(source.at[pl.ds(start, pairs)], target, semaphores.at[n])
            for n, (source, start, target) in enumerate(
                [(kept[n], pairs, below_weights[n]) for n in range(3)]
                + [(kept[n], 0, slab_weights[n]) for n in range(3)]
            )
        ]

        @pl.when(later)
        def _():
            for slab, some_ref, targets in (
                (False, atoms_ref, below_weights),
                (True, slab_atoms_ref, slab_weights),
            ):
                sampling_weights(
                    0, slab, where_ref, some_ref, weights_ref, base_ref, taps_ref, *targets
                )

        @pl.when(jnp.logical_not(later))
        def _():
            for copy in copies:
                copy.start()

    rows = list(range(CY)) if own else list(range(CY, 2 * CY - 1))
    energy = 0.0
    if not own:
        sign = lane_sign((NX, LANES))
        for first in range(0, CY, 2):
            modes, swapped = [], []
            for y in range(first, first + 2):
                line = jnp.concatenate([block_at(in_ref, j, y) for j in range(PART_X)], axis=0)
                other = turned(line, sign)
                cos_y, sin_y = cos_ref[:, y : y + 1], sin_ref[:, y : y + 1]
                modes.append(line * cos_y - other * sin_y)
                swapped.append(other * cos_y + line * sin_y)
            swapped = jnp.concatenate(swapped, axis=1)
            modes = jnp.concatenate(modes, axis=1)
            if first == 0:
                table_copy.wait()
            cells = jnp.concatenate(
                inverse_line(table_ref, quarters_of(modes), quarters_of(swapped)), axis=0
            )
            lanes = slice(first * LANES, (first + 2) * LANES)
            grid_ref[:NX, lanes] = cells
            grid_ref[NX:, lanes] = cells[:WIDE]
        lane = lax.broadcasted_iota(jnp.int32, (SLABS, LANES), 1)
        energy = jnp.sum(jnp.where(lane == PART_Z, in_ref[rows_of(0), :], 0.0))
    gap = jnp.zeros((HALF - PADDED_Z, 3 * LANES), bf16)

    if not own:

        @pl.when(jnp.logical_not(later))
        def _():
            for copy in copies[:3]:
                copy.wait()

    def pair_body(pair, carry):
        pencil, lanes = pair_place(pair)
        waves = [
            jnp.concatenate(
                [waves_ref[pair, n, :PADDED_Z], gap, waves_ref[pair, n, PADDED_Z:], gap],
                axis=0,
            )
            for n in range(2)
        ]
        first_row, window, _ = pair_window(pair, own, where_ref)
        at = pl.ds(first_row, window)
        cells = jnp.concatenate(
            [grid_ref[at, n * LANES : (n + 1) * LANES] for n in range(len(rows))], axis=0
        )
        read = product(halves(cells), waves)
        dense_x = [x_ref[pair, p, :window] for p in range(3)]
        dense_y = [y_ref[pair, p] for p in range(3)]
        lined = {}
        for order_y, order_z in ((0, 0), (1, 0), (2, 0), (0, 1), (1, 1), (0, 2)):
            lined[order_y, order_z] = sum(
                dense_y[order_y][r : r + 1]
                * read[n * window : (n + 1) * window, order_z * LANES : (order_z + 1) * LANES]
                for n, r in enumerate(rows)
            )

        def sampled(p, r, s):
            return jnp.sum(dense_x[p] * lined[r, s], axis=0, keepdims=True)

        charge, dip_x, dip_y, dip_z, live = [
            atoms_ref[pencil, a : a + 1, lanes] for a in range(6, 11)
        ]
        s100 = sampled(1, 0, 0)
        s010 = sampled(0, 1, 0)
        s001 = sampled(0, 0, 1)
        s110 = sampled(1, 1, 0)
        s101 = sampled(1, 0, 1)
        s011 = sampled(0, 1, 1)
        out = [
            live * sampled(0, 0, 0),
            live * s100,
            live * s010,
            live * s001,
            charge * s100 + dip_x * sampled(2, 0, 0) + dip_y * s110 + dip_z * s101,
            charge * s010 + dip_x * s110 + dip_y * sampled(0, 2, 0) + dip_z * s011,
            charge * s001 + dip_x * s101 + dip_y * s011 + dip_z * sampled(0, 0, 2),
            jnp.full(live.shape, energy, f32),
        ]
        out_ref[pencil, :, lanes] = jnp.concatenate(out, axis=0)
        return carry

    lax.fori_loop(0, PENCILS * PAIRS, pair_body, 0, unroll=6)
    if not own:

        @pl.when(jnp.logical_not(later))
        def _():
            for copy in copies[3:]:
                copy.wait()


def finish_kernel(in_ref, charge_ref, dipole_ref, position_ref, energy_ref, row_ref, semaphore):
    total = (in_ref[0] + in_ref[1]) + (in_ref[2] + in_ref[3])
    row_ref[...] = total[0:1]
    copy = fetch(row_ref.at[0], charge_ref, semaphore)
    dipole_ref[...] = total[1:4]
    position_ref[...] = total[4:7]
    energy_ref[...] = total[7:8, 0:1]
    copy.wait()


def spline_modulus(angles):
    return (66.0 + 52.0 * jnp.cos(angles) + 2.0 * jnp.cos(2.0 * angles)) / 120.0


def mode_of(row):
    return 4 * (row % QUARTER) + row // QUARTER


def folded(index, size):
    return (index + size // 2) % size - size // 2


SPACES = {"v": pltpu.VMEM, "h": pltpu.HBM, "s": pltpu.SMEM}
WORK = {"flops": 1_000_000_000, "bytes_accessed": 8_000_000}


def out_place(shape):
    pinned = isinstance(shape, type(pltpu.HBM((8, LANES), f32)))
    return pl.BlockSpec(memory_space=pltpu.HBM if pinned else pltpu.VMEM)


def call(kernel, inputs, out_shape, scratch=(), aliases=()):
    def run(*operands):
        placed = [
            pltpu.with_memory_space_constraint(one, pltpu.HBM) if where == "h" else one
            for one, where in zip(operands, inputs)
        ]
        return pl.pallas_call(
            kernel,
            out_shape=out_shape,
            in_specs=[pl.BlockSpec(memory_space=SPACES[one]) for one in inputs],
            out_specs=jax.tree.map(out_place, out_shape),
            scratch_shapes=list(scratch),
            input_output_aliases=dict(aliases),
            compiler_params=pltpu.CompilerParams(vmem_limit_bytes=28 * 1024 * 1024),
            cost_estimate=pl.CostEstimate(transcendentals=0, **WORK),
        )(*placed)

    return run


def next_slab(value, back=False):
    step = -1 if back else 1
    return lax.ppermute(value, "gy", [(i, (i + step) % SLABS) for i in range(SLABS)])


def swap_slabs(lines):
    lines = lines.reshape(SLABS, CARRIERS, 1, LANES)
    lines = lax.all_to_all(lines, "gy", split_axis=0, concat_axis=0, tiled=True)
    return lines.reshape(SLABS * CARRIERS, LANES)


def on_device(cell_index, offsets, charges, dipoles, block_count, shear_cells):
    pencil_index = lax.axis_index("gx")
    slab_index = lax.axis_index("gy")
    x_forward, x_inverse, y_forward, y_inverse = wave_tables()
    shape = jax.ShapeDtypeStruct
    shift = jnp.where(slab_index == 0, shear_cells[0], 0)
    where = jnp.stack([slab_index, pencil_index, shift])

    mine, base, taps, cos_t, sin_t = call(
        prepare_kernel,
        "sshhhhh",
        (
            shape((16, ATOM_DEV), f32),
            shape((8, LANES), f32),
            shape((12, PADDED_Z, LANES), f32),
            shape((NX, LANES), f32),
            shape((NX, LANES), f32),
        ),
        [
            pltpu.SMEM(block_count.shape, jnp.int32),
            pltpu.VMEM((3, ATOM_DEV), jnp.int32),
            pltpu.VMEM((3, ATOM_DEV), f32),
            pltpu.VMEM((1, ATOM_DEV), f32),
            pltpu.VMEM((3, ATOM_DEV), f32),
            pltpu.SemaphoreType.DMA((5,)),
        ],
    )(
        where,
        shear_cells,
        block_count,
        cell_index,
        offsets,
        charges,
        dipoles,
    )
    atoms = lax.all_gather(mine, "gx", axis=0, tiled=False)
    below_atoms = next_slab(atoms)

    packed = shape((SLABS * CARRIERS, LANES), f32)
    table_space = pltpu.VMEM((NX, 6 * QUARTER), bf16)
    two = pltpu.SemaphoreType.DMA((2,))
    pairs = 2 * PENCILS * PAIRS
    held = [
        ((2, 2 * PADDED_Z, 3 * LANES), bf16),
        ((3, WIDE, LANES), f32),
        ((3, 16, LANES), f32),
    ]
    weights_space = pltpu.VMEM((PENCILS, 18, 8, ATOM_DEV), f32)
    four = pltpu.SemaphoreType.DMA((4,))
    grid_shape = shape((EXTENDED, 2 * CY * LANES), f32)
    slab_grid = call(
        lambda *refs: spread_kernel(True, *refs),
        "vsvv",
        grid_shape,
        [weights_space],
    )(atoms, where, base, taps)
    _, lines, *weights = call(
        lambda *refs: spread_kernel(False, *refs),
        "vsvvvhvvv",
        (grid_shape, packed, *(pltpu.HBM((pairs, *dims), kind) for dims, kind in held)),
        [
            *(pltpu.VMEM((pairs, *dims), kind) for dims, kind in held),
            table_space,
            weights_space,
            four,
        ],
        ((4, 0),),
    )(below_atoms, where, base, taps, slab_grid, x_forward, cos_t, sin_t, atoms)
    lines, shear_cells = lax.optimization_barrier((lines, shear_cells))
    shear_step = shear_cells[0]

    own_x = folded(mode_of(jnp.arange(8, dtype=jnp.int32) * SLABS + slab_index), NX)[None, :]
    own_y = folded(mode_of(jnp.arange(NY, dtype=jnp.int32)), NY)[:, None]
    float_x = own_x.astype(f32)
    wave_y = own_y.astype(f32) + float_x * shear_step.astype(f32) / NX
    norm = (float_x / NX) ** 2 + (wave_y / NY) ** 2
    moduli = spline_modulus(2.0 * math.pi * float_x / NX) * spline_modulus(
        2.0 * math.pi * wave_y / NY
    )
    decay = (math.pi / screening) ** 2
    top = jnp.exp(-decay * norm) / (math.pi * moduli * moduli)
    top = jnp.where((own_x == -(NX // 2)) | (own_y == -(NY // 2)), 0.0, top)
    lane = jnp.arange(LANES, dtype=jnp.int32) % HALF
    mode_z = pencil_index * PART_Z + lane
    kept = lane < PART_Z
    float_z = mode_z.astype(f32)
    norm_z = (float_z / NZ) ** 2
    modulus_z = spline_modulus(2.0 * math.pi * float_z / NZ)
    twice = jnp.where(mode_z == 0, 1.0, 2.0) / (NX * NY * NZ)
    mode_top = jnp.where(kept, twice * jnp.exp(-decay * norm_z) / (modulus_z * modulus_z), 0.0)
    mode_norm = jnp.where(kept, norm_z, 1.0)
    mode = jnp.stack([mode_top, mode_norm])

    green = call(green_kernel, "vvv", shape((NY, PART_X * LANES), f32))(top, norm, mode)
    lines = swap_slabs(lines)
    filtered = call(filter_kernel, "vhhv", packed, [table_space, table_space, two])(
        lines, y_forward, y_inverse, green
    )
    filtered = swap_slabs(filtered)
    shares_shape = shape((PENCILS, 8, ATOM_DEV), f32)
    below_shares, potential, *weights = call(
        lambda *refs: sample_kernel(False, *refs),
        "vsvvhhhvvvhv",
        (
            shares_shape,
            shape((EXTENDED, CY * LANES), f32),
            *(shape((pairs // 2, *dims), kind) for dims, kind in held),
        ),
        [
            *(pltpu.VMEM((pairs // 2, *dims), kind) for dims, kind in held),
            table_space,
            weights_space,
            pltpu.SemaphoreType.DMA((7,)),
        ],
    )(below_atoms, where, base, taps, *weights, filtered, cos_t, sin_t, x_inverse, atoms)
    below_shares = next_slab(below_shares, back=True)
    shares = call(lambda *refs: sample_kernel(True, *refs), "vsvvvv", shares_shape)(
        atoms, where, *weights, potential
    )
    shares = lax.all_to_all(shares + below_shares, "gx", split_axis=0, concat_axis=0, tiled=True)
    charge_grad, dipole_grad, position_grad, energy = call(
        finish_kernel,
        "v",
        (
            pltpu.HBM((ATOM_DEV,), f32),
            shape((3, ATOM_DEV), f32),
            shape((3, ATOM_DEV), f32),
            shape((1, 1), f32),
        ),
        [pltpu.VMEM((1, ATOM_DEV), f32), pltpu.SemaphoreType.DMA],
    )(shares)
    return charge_grad, dipole_grad, position_grad, energy[0]


def solution(mesh):
    placed = (
        P(None, ("gy", "gx")),
        P(None, ("gy", "gx")),
        P(("gy", "gx")),
        P(None, ("gy", "gx")),
        P(("gy", "gx")),
        P(),
    )
    return jax.shard_map(
        on_device,
        mesh=mesh,
        in_specs=placed,
        out_specs=(P(("gy", "gx")), P(None, ("gy", "gx")), P(None, ("gy", "gx")), P()),
        check_vma=False,
    )
```

```python
import math

import jax
import jax.numpy as jnp
import ml_dtypes
import numpy as np
from jax import lax
from jax.experimental import pallas as pl
from jax.experimental.pallas import tpu as pltpu
from jax.sharding import PartitionSpec as P

NX = 384
NY = 384
NZ = 360
CY = 6
CX = 96
PENCILS = 4
SLABS = 64
PART_X = 6
PART_Z = 45
ATOM_BLK = 64
ATOM_DEV = 384
PAIRS = 3
WINDOW = 40
WIDE = 48
EXTENDED = NX + WIDE
HALF = 64
LANES = 128
PADDED_Z = 48
QUARTER = 96
screening = 0.9
f32 = jnp.float32
bf16 = jnp.bfloat16


def split_table(table):
    high = table.astype(ml_dtypes.bfloat16)
    low = (table - high.astype(np.float64)).astype(ml_dtypes.bfloat16)
    return np.concatenate([high, high, low], axis=1)


def wave_tables():
    quarter = np.arange(QUARTER)
    mode = np.arange(4)[:, None] + 4 * quarter[None, :]
    row_y = CY * (quarter % 16) + quarter // 16
    tables = []
    for place in (quarter, row_y):
        ticks = mode[:, :, None] * place % NX
        for table in (ticks, ticks.transpose(0, 2, 1)):
            angle = 2.0 * np.pi / NX * table.reshape(NX, QUARTER)
            tables.append(split_table(np.concatenate([np.cos(angle), np.sin(angle)], axis=1)))
    return tables


def spline_rows(fraction):
    levels = {2: [1.0 - fraction, fraction]}
    current = levels[2]
    for n in range(3, 7):
        inverse_n = 1.0 / (n - 1)
        updated = [None] * n
        updated[n - 1] = inverse_n * fraction * current[n - 2]
        for j in range(1, n - 1):
            updated[n - 1 - j] = inverse_n * (
                (fraction + j) * current[n - 2 - j] + (n - j - fraction) * current[n - 1 - j]
            )
        updated[0] = inverse_n * (1.0 - fraction) * current[0]
        current = updated
        levels[n] = current
    zero_row = jnp.zeros_like(fraction)

    def entry_at(values_list, k):
        return values_list[k] if 0 <= k < len(values_list) else zero_row

    first = [entry_at(levels[5], t - 1) - entry_at(levels[5], t) for t in range(6)]
    second = [
        entry_at(levels[4], t - 2) - 2.0 * entry_at(levels[4], t - 1) + entry_at(levels[4], t)
        for t in range(6)
    ]
    return levels[6], first, second


def dense_rows(tables, cell, length):
    away = lax.broadcasted_iota(jnp.int32, (length, cell.shape[1]), 0).astype(f32) - cell
    summed = [jnp.zeros(away.shape, f32) for _ in tables]
    for t in range(6):
        here = away == float(t)
        summed = [jnp.where(here, table[t], so_far) for table, so_far in zip(tables, summed)]
    return summed


def unit_phase(turns):
    turns = turns - jnp.floor(turns + 0.5)
    quarter = jnp.floor(4.0 * turns + 0.5)
    rest = turns - 0.25 * quarter
    theta = (2.0 * math.pi) * rest
    square = theta * theta
    sine = theta * (
        1.0
        + square
        * (-1.0 / 6 + square * (1.0 / 120 + square * (-1.0 / 5040 + square * (1.0 / 362880))))
    )
    cosine = 1.0 + square * (
        -0.5
        + square
        * (1.0 / 24 + square * (-1.0 / 720 + square * (1.0 / 40320 - square * (1.0 / 3628800))))
    )
    odd = jnp.abs(quarter) == 1.0
    cos_out = jnp.where(odd, sine, cosine)
    sin_out = jnp.where(odd, cosine, sine)
    cos_out = jnp.where((quarter == 1.0) | (jnp.abs(quarter) == 2.0), -cos_out, cos_out)
    sin_out = jnp.where((quarter == -1.0) | (jnp.abs(quarter) == 2.0), -sin_out, sin_out)
    return cos_out, sin_out


def halves(value):
    high = value.astype(bf16)
    return high, (value - high.astype(f32)).astype(bf16)


def joined(left, right):
    return (
        jnp.concatenate([left[0], left[0], left[1]], axis=1),
        jnp.concatenate([right[0], right[1], right[0]], axis=0),
    )


def product(left, right):
    left, right = joined(left, right)
    return jnp.dot(left, right, preferred_element_type=f32)


def product3(left, right):
    def one(a, b):
        return jnp.dot(a, b, preferred_element_type=f32)

    return one(left[0], right[0]) + (one(left[0], right[1]) + one(left[1], right[0]))


def lane_sign(shape):
    return jnp.where(lax.broadcasted_iota(jnp.int32, shape, 1) < HALF, 1.0, -1.0).astype(f32)


def turned(value, sign):
    return pltpu.roll(value, HALF, 1) * sign


def fetch(source, target, semaphore):
    copy = pltpu.make_async_copy(source, target, semaphore)
    copy.start()
    return copy


def line_product(table_ref, r, value):
    rows = slice(r * QUARTER, (r + 1) * QUARTER)
    table = table_ref[rows, : 2 * QUARTER], table_ref[rows, 4 * QUARTER :]
    return product3(table, halves(value))


def forward_line(table_ref, quarters, turned_quarters):
    g, h = quarters, turned_quarters
    a, b, c, d = g[0] + g[2], g[0] - g[2], g[1] + g[3], g[1] - g[3]
    ta, tb, tc, td = h[0] + h[2], h[0] - h[2], h[1] + h[3], h[1] - h[3]
    lines = []
    for r, (one, other) in enumerate(
        ((a + c, ta + tc), (b + td, tb - d), (a - c, ta - tc), (b - td, tb + d))
    ):
        stacked = jnp.concatenate([one, other], axis=0)
        lines.append(line_product(table_ref, r, stacked))
    return lines


def inverse_line(table_ref, modes, turned_modes):
    z = []
    for r in range(4):
        stacked = jnp.concatenate([modes[r], -turned_modes[r]], axis=0)
        z.append(line_product(table_ref, r, stacked))
    a, b, c, d = z[0] + z[2], z[0] - z[2], z[1] + z[3], z[1] - z[3]
    width = d.shape[1]
    sign = lane_sign((QUARTER, LANES))
    td = jnp.concatenate(
        [turned(d[:, n : n + LANES], sign) for n in range(0, width, LANES)], axis=1
    )
    return [a + c, b - td, a - c, b + td]


def quarters_of(value):
    return [value[r * QUARTER : (r + 1) * QUARTER] for r in range(4)]


PIECES = (0, 16, 32, 64, 80, 96)
GROUPS = PART_X * CY // 4
CARRIERS = 3 * GROUPS


def lane_range(first):
    lane = lax.broadcasted_iota(jnp.int32, (SLABS, LANES), 1)
    return (lane >= first) & (lane < first + 16)


def pack_blocks(blocks):
    carriers = []
    for c in range(3):
        value = blocks[c]
        for half in range(2):
            gap = PADDED_Z + half * HALF
            shift = (gap - PIECES[2 * c + half]) % LANES
            value = jnp.where(lane_range(gap), pltpu.roll(blocks[3], shift, 1), value)
        carriers.append(value)
    return carriers


def unpack_block(carriers):
    value = jnp.zeros((SLABS, LANES), f32)
    for p, source in enumerate(PIECES):
        gap = PADDED_Z + p % 2 * HALF
        shift = (source - gap) % LANES
        value = jnp.where(lane_range(source), pltpu.roll(carriers[p // 2], shift, 1), value)
    return value


def rows_of(carrier):
    return pl.ds(carrier, SLABS, stride=CARRIERS)


def block_at(ref, j, y):
    block = j * CY + y
    group, place = block // 4, block % 4
    if place < 3:
        return ref[rows_of(3 * group + place), :]
    return unpack_block([ref[rows_of(3 * group + c), :] for c in range(3)])


def prepare_kernel(
    where_ref, shear_ref, counts_ref, cells_ref, offsets_ref, charges_ref, dipoles_ref,
    atoms_ref, base_ref, taps_ref, cos_ref, sin_ref,
    count_ref, cell_ref, offset_ref, charge_ref, dipole_ref, semaphores
):
    copies = [
        fetch(source, target, semaphores.at[n])
        for n, (source, target) in enumerate(
            (
                (counts_ref, count_ref),
                (cells_ref, cell_ref),
                (offsets_ref, offset_ref),
                (charges_ref, charge_ref.at[0]),
                (dipoles_ref, dipole_ref),
            )
        )
    ]
    slab, pencil = where_ref[0], where_ref[1]
    first = pencil * PART_Z
    row = lax.broadcasted_iota(jnp.int32, (PADDED_Z, LANES), 0)
    mode = (row + first).astype(f32)
    base_ref[...] = mode[:8]
    for t in range(6):
        cos_t, sin_t = unit_phase(mode * float(t) * (1.0 / NZ))
        taps_ref[t] = jnp.where(row < PART_Z, cos_t, 0.0)
        taps_ref[6 + t] = jnp.where(row < PART_Z, sin_t, 0.0)
    column = lax.broadcasted_iota(jnp.int32, (1, LANES), 1)
    rows = slab * CY + jnp.minimum(column, CY)
    index = lax.broadcasted_iota(jnp.int32, (NX, LANES), 0)
    folds = folded_mode(index)
    ticks = folds * (shear_ref[0] * rows)
    whole = jnp.floor(ticks.astype(f32) * (1.0 / (NX * NY))).astype(jnp.int32)
    rest = ticks - whole * (NX * NY)
    cos_t, sin_t = unit_phase(rest.astype(f32) * (1.0 / (NX * NY)))
    cos_ref[...] = cos_t
    sin_ref[...] = sin_t
    for copy in copies:
        copy.wait()
    slot = lax.broadcasted_iota(jnp.int32, (1, ATOM_DEV), 1)
    live = jnp.zeros((1, ATOM_DEV), f32)
    for b in range(ATOM_DEV // ATOM_BLK):
        inside = (slot >= b * ATOM_BLK) & (slot < b * ATOM_BLK + count_ref[b])
        live = jnp.where(inside, 1.0, live)
    atoms_ref[0:1, :] = cell_ref[0:1, :].astype(f32)
    atoms_ref[1:2, :] = (cell_ref[1:2, :] - slab * CY).astype(f32)
    atoms_ref[2:3, :] = cell_ref[2:3, :].astype(f32)
    atoms_ref[3:6, :] = offset_ref[...]
    atoms_ref[6:7, :] = charge_ref[...] * live
    atoms_ref[7:10, :] = dipole_ref[...] * live
    atoms_ref[10:11, :] = live
    atoms_ref[11:16, :] = jnp.zeros((5, ATOM_DEV), f32)


def spline_table(atoms_ref, table_ref, orders):
    def pencil_body(pencil, carry):
        tables = spline_rows(atoms_ref[pencil, 3:6, :])
        for o in range(orders):
            for t in range(6):
                table_ref[pencil, o * 6 + t, 0:3, :] = tables[o][t]
        return carry

    lax.fori_loop(0, PENCILS, pencil_body, 0)


def weight_rows(table_ref, pencil, lanes, dim, orders):
    row = slice(dim, dim + 1)
    return [[table_ref[pencil, o * 6 + t, row, lanes] for t in range(6)] for o in range(orders)]


def pair_place(pair):
    pencil = pair // PAIRS
    return pencil, pl.ds(pl.multiple_of(pair % PAIRS * LANES, LANES), LANES)


def pair_window(pair, own, where_ref):
    if own:
        return pl.multiple_of(pair * 32, 8), WINDOW, (pair * 32).astype(f32)
    place = pair * 32 + where_ref[2]
    place = jnp.where(place >= NX, place - NX, place)
    first = place // 8 * 8
    return pl.multiple_of(first, 8), WIDE, (pair * 32 - (place - first)).astype(f32)


def z_waves(cell_z, weights, base_ref, taps_ref):
    turn = base_ref[...] * cell_z
    turn = turn - 360.0 * jnp.floor(turn * (1.0 / 360.0))
    cos_k, sin_k = unit_phase(turn * (1.0 / 360.0))
    turn = 8.0 * cell_z
    turn = turn - 360.0 * jnp.floor(turn * (1.0 / 360.0))
    cos_8, sin_8 = unit_phase(jnp.broadcast_to(turn * (1.0 / 360.0), cos_k.shape))
    pieces = [[] for _ in weights]
    pieces_im = [[] for _ in weights]
    for q in range(PADDED_Z // 8):
        span = slice(q * 8, q * 8 + 8)
        cos_t = [taps_ref[t, span, :] for t in range(6)]
        sin_t = [taps_ref[6 + t, span, :] for t in range(6)]
        for s, weight in enumerate(weights):
            real = weight[0] * cos_t[0] + sum(weight[t] * cos_t[t] for t in range(1, 6))
            imag = sum(weight[t] * sin_t[t] for t in range(1, 6))
            pieces[s].append(real * cos_k - imag * sin_k)
            pieces_im[s].append(-(real * sin_k + imag * cos_k))
        cos_k, sin_k = cos_k * cos_8 - sin_k * sin_8, sin_k * cos_8 + cos_k * sin_8
    return [
        (jnp.concatenate(re, axis=0), jnp.concatenate(im, axis=0))
        for re, im in zip(pieces, pieces_im)
    ]


def sampling_weights(
    start, own, where_ref, some_ref, table_ref, base_ref, taps_ref, waves_ref, x_ref, y_ref
):
    spline_table(some_ref, table_ref, 3)

    def pair_body(pair, carry):
        pencil, lanes = pair_place(pair)
        row = [some_ref[pencil, a : a + 1, lanes] for a in range(3)]
        _, window, origin = pair_window(pair, own, where_ref)
        dense_x = dense_rows(weight_rows(table_ref, pencil, lanes, 0, 3), row[0] - origin, window)
        dense_y = dense_rows(weight_rows(table_ref, pencil, lanes, 1, 3), row[1], 16)
        for p in range(3):
            x_ref[start + pair, p, :window] = dense_x[p]
            y_ref[start + pair, p] = dense_y[p]
        waves = z_waves(row[2], weight_rows(table_ref, pencil, lanes, 2, 3), base_ref, taps_ref)
        for s, (re, im) in enumerate(waves):
            re, im = halves(re), halves(im)
            columns = slice(s * LANES, (s + 1) * LANES)
            for n in range(2):
                waves_ref[start + pair, n, :PADDED_Z, columns] = re[n]
                waves_ref[start + pair, n, PADDED_Z:, columns] = im[n]
        return carry

    lax.fori_loop(0, PENCILS * PAIRS, pair_body, 0, unroll=2)


def spread_kernel(own, *refs):
    atoms_ref, where_ref, base_ref, taps_ref = refs[:4]
    if own:
        grid_ref, weights_ref = refs[4:]
        grid_ref[...] = jnp.zeros_like(grid_ref)
    else:
        _, tables_ref, cos_ref, sin_ref, slab_atoms_ref, grid_ref, out_ref = refs[4:11]
        results, green_out_ref, kept = refs[11:14], refs[14], refs[15:18]
        green_ref, table_ref, weights_ref, semaphores = refs[18:]
        table_copy = fetch(tables_ref, table_ref, semaphores.at[0])
    rows = list(range(CY)) if own else list(range(CY, 2 * CY - 1))
    part = CY * LANES
    gap = jnp.zeros((HALF - PADDED_Z, LANES), bf16)
    spline_table(atoms_ref, weights_ref, 2)

    def pair_body(pair, carry):
        pencil, lanes = pair_place(pair)
        row = [atoms_ref[pencil, a : a + 1, lanes] for a in range(10)]
        charge, dip_x, dip_y, dip_z = row[6:10]
        first_row, window, origin = pair_window(pair, own, where_ref)
        dense_x = dense_rows(
            weight_rows(weights_ref, pencil, lanes, 0, 2), row[0] - origin, window
        )
        dense_y = dense_rows(weight_rows(weights_ref, pencil, lanes, 1, 2), row[1], 16)
        value, first = weight_rows(weights_ref, pencil, lanes, 2, 2)
        mixed = [charge * value[t] + dip_z * first[t] for t in range(6)]
        right = []
        for re, im in z_waves(row[2], (mixed, value), base_ref, taps_ref):
            re, im = halves(re), halves(im)
            right.append(
                [
                    jnp.concatenate([re[n], gap, im[n], gap, im[n], gap, -re[n], gap], axis=0)
                    for n in range(2)
                ]
            )
        high, low = [jnp.concatenate([right[0][n], right[1][n]], axis=1) for n in range(2)]
        right = jnp.concatenate([high, low, high], axis=1)
        left = []
        for r in rows:
            value, first = dense_y[0][r : r + 1], dense_y[1][r : r + 1]
            left.append(
                jnp.concatenate(
                    [
                        value * dense_x[0],
                        (dip_x * value) * dense_x[1] + (dip_y * first) * dense_x[0],
                    ],
                    axis=1,
                )
            )
        high, low = halves(jnp.concatenate(left, axis=0))
        left = jnp.concatenate([high, high, low], axis=1)
        added = lax.dot_general(
            left, right, (((1,), (1,)), ((), ())), preferred_element_type=f32
        )
        at = pl.ds(first_row, window)
        for n in range(len(rows)):
            piece = added[n * window : (n + 1) * window]
            grid_ref[at, n * LANES : (n + 1) * LANES] += piece[:, :LANES]
            grid_ref[at, part + n * LANES : part + (n + 1) * LANES] += piece[:, LANES:]
        return carry

    lax.fori_loop(0, PENCILS * PAIRS, pair_body, 0, unroll=6)
    if own:
        return
    grid_ref[0:WIDE] += grid_ref[NX:EXTENDED]
    table_copy.wait()
    sign = lane_sign((NX, LANES))
    totals = []
    for first in range(0, CY, 2):
        lanes = slice(first * LANES, (first + 2) * LANES)
        below = slice(part + lanes.start, part + lanes.stop)
        line = jnp.concatenate(
            forward_line(
                table_ref, quarters_of(grid_ref[:NX, lanes]), quarters_of(grid_ref[:NX, below])
            ),
            axis=0,
        )
        for n, y in enumerate((first, first + 1)):
            one = line[:, n * LANES : (n + 1) * LANES]
            totals.append(one * cos_ref[:, y : y + 1] + turned(one, sign) * sin_ref[:, y : y + 1])
    for group in range(GROUPS):
        blocks = []
        for block in range(4 * group, 4 * group + 4):
            j, y = block // CY, block % CY
            blocks.append(totals[y][j * SLABS : (j + 1) * SLABS])
        for c, carrier in enumerate(pack_blocks(blocks)):
            out_ref[rows_of(3 * group + c), :] = carrier

    @pl.when(where_ref[1] % 2 == 1)
    def _():
        make_green(where_ref, green_ref)
        green_copy = fetch(green_ref, green_out_ref, semaphores.at[3])
        for start, some_ref in ((0, slab_atoms_ref), (PENCILS * PAIRS, atoms_ref)):
            sampling_weights(
                start, start == 0, where_ref, some_ref, weights_ref, base_ref, taps_ref, *kept
            )
        copies = [fetch(kept[n], results[n], semaphores.at[n]) for n in range(3)]
        for copy in [green_copy, *copies]:
            copy.wait()


def spline_modulus(turns):
    cosine, _ = unit_phase(turns)
    return (64.0 + 52.0 * cosine + 4.0 * cosine * cosine) * (1.0 / 120.0)


def folded_mode(row):
    residue = (
        (row >= QUARTER).astype(jnp.int32)
        + (row >= 2 * QUARTER).astype(jnp.int32)
        + (row >= 3 * QUARTER).astype(jnp.int32)
    )
    mode = 4 * (row - QUARTER * residue) + residue
    return jnp.where(mode < NX // 2, mode, mode - NX)


def make_green(where_ref, out_ref):
    slab, pencil, shear = where_ref[0], where_ref[1], where_ref[3].astype(f32)
    decay = (math.pi / screening) ** 2
    column = lax.broadcasted_iota(jnp.int32, (1, LANES), 1)
    own_x = folded_mode(jnp.minimum(column, PART_X) * SLABS + slab)
    own_y = folded_mode(lax.broadcasted_iota(jnp.int32, (NY, LANES), 0))
    float_x = own_x.astype(f32)
    wave_y = own_y.astype(f32) + float_x * shear * (1.0 / NX)
    part_x, part_y = float_x * (1.0 / NX), wave_y * (1.0 / NY)
    norm = part_x * part_x + part_y * part_y
    moduli = spline_modulus(part_x) * spline_modulus(part_y)
    top = jnp.exp(-decay * norm) / (math.pi * moduli * moduli)
    top = jnp.where((own_x == -(NX // 2)) | (own_y == -(NY // 2)), 0.0, top)
    lane = jnp.where(column < HALF, column, column - HALF)
    mode = pencil * PART_Z + lane
    part_z = mode.astype(f32) * (1.0 / NZ)
    modulus = spline_modulus(part_z)
    norm_z = part_z * part_z
    twice = jnp.where(mode == 0, 1.0, 2.0) * (1.0 / (NX * NY * NZ))
    mode_top = jnp.where(
        lane < PART_Z, twice * jnp.exp(-decay * norm_z) / (modulus * modulus), 0.0
    )
    mode_norm = jnp.where(lane < PART_Z, norm_z, 1.0)
    for j in range(PART_X):
        square = norm[:, j : j + 1] + mode_norm
        green = top[:, j : j + 1] * mode_top / jnp.where(square == 0.0, 1.0, square)
        out_ref[:, j * LANES : (j + 1) * LANES] = jnp.where(square == 0.0, 0.0, green)


def green_kernel(where_ref, _, result_ref, green_ref, semaphore):
    @pl.when(where_ref[1] % 2 == 0)
    def _():
        make_green(where_ref, green_ref)
        fetch(green_ref, result_ref, semaphore).wait()


def filter_kernel(
    in_ref, tables_ref, backs_ref, greens_ref, out_ref, table_ref, back_ref, green_ref, semaphores
):
    copies = [
        fetch(tables_ref, table_ref, semaphores.at[0]),
        fetch(backs_ref, back_ref, semaphores.at[1]),
    ]
    for first in range(0, PART_X, 2):
        lanes = pl.ds(first * LANES, 2 * LANES)
        copies.append(
            fetch(greens_ref.at[:, lanes], green_ref.at[:, lanes], semaphores.at[2 + first // 2])
        )
    sign = lane_sign((NY, LANES))
    energy = jnp.zeros((8, LANES), f32)
    blocks = []
    for first in range(0, PART_X, 2):
        lines = []
        for j in (first, first + 1):
            found = [block_at(in_ref, j, y) for y in range(CY)]
            lines.append(
                jnp.concatenate(
                    [one[16 * part : 16 * part + 16] for part in range(4) for one in found], axis=0
                )
            )
        swapped = jnp.concatenate([turned(one, sign) for one in lines], axis=1)
        lines = jnp.concatenate(lines, axis=1)
        if first == 0:
            copies[0].wait()
        spectrum = jnp.concatenate(
            forward_line(table_ref, quarters_of(lines), quarters_of(swapped)), axis=0
        )
        modes = []
        copies[2 + first // 2].wait()
        for n in range(2):
            j = first + n
            one = spectrum[:, n * LANES : (n + 1) * LANES]
            scaled = green_ref[:, j * LANES : (j + 1) * LANES] * one
            share = scaled * one
            energy = energy + sum(share[8 * i : 8 * i + 8] for i in range(NY // 8))
            modes.append(scaled)
        swapped = jnp.concatenate([turned(one, sign) for one in modes], axis=1)
        modes = jnp.concatenate(modes, axis=1)
        if first == 0:
            copies[1].wait()
        parts = inverse_line(back_ref, quarters_of(modes), quarters_of(swapped))
        for n in range(2):
            for y in range(CY):
                blocks.append(
                    jnp.concatenate(
                        [
                            one[16 * y : 16 * y + 16, n * LANES : (n + 1) * LANES]
                            for one in parts
                        ],
                        axis=0,
                    )
                )
        for group in range(first * CY // 4, (first + 2) * CY // 4):
            for c, carrier in enumerate(pack_blocks(blocks[4 * group : 4 * group + 4])):
                out_ref[rows_of(3 * group + c), :] = carrier
    lane = lax.broadcasted_iota(jnp.int32, (SLABS, LANES), 1)
    share = 0.5 * jnp.sum(energy)
    out_ref[rows_of(0), :] = jnp.where(lane == PART_Z, share, out_ref[rows_of(0), :])


def sample_kernel(own, *refs):
    if own:
        atoms_ref, where_ref, waves_ref, x_ref, y_ref, grid_ref, out_ref = refs
    else:
        atoms_ref, where_ref, base_ref, taps_ref = refs[:4]
        kept = refs[4:7]
        in_ref, cos_ref, sin_ref, tables_ref, slab_atoms_ref, out_ref, grid_ref = refs[7:14]
        slab_weights, below_weights = refs[14:17], refs[17:20]
        waves_ref, x_ref, y_ref = below_weights
        table_ref, weights_ref, semaphores = refs[20:]
        table_copy = fetch(tables_ref, table_ref, semaphores.at[6])
        later = where_ref[1] % 2 == 0
        pairs = PENCILS * PAIRS
        copies = [
            pltpu.make_async_copy(source.at[pl.ds(start, pairs)], target, semaphores.at[n])
            for n, (source, start, target) in enumerate(
                [(kept[n], pairs, below_weights[n]) for n in range(3)]
                + [(kept[n], 0, slab_weights[n]) for n in range(3)]
            )
        ]

        @pl.when(later)
        def _():
            for slab, some_ref, targets in (
                (False, atoms_ref, below_weights),
                (True, slab_atoms_ref, slab_weights),
            ):
                sampling_weights(
                    0, slab, where_ref, some_ref, weights_ref, base_ref, taps_ref, *targets
                )

        @pl.when(jnp.logical_not(later))
        def _():
            for copy in copies:
                copy.start()

    rows = list(range(CY)) if own else list(range(CY, 2 * CY - 1))
    energy = 0.0
    if not own:
        sign = lane_sign((NX, LANES))
        for first in range(0, CY, 2):
            modes, swapped = [], []
            for y in range(first, first + 2):
                line = jnp.concatenate([block_at(in_ref, j, y) for j in range(PART_X)], axis=0)
                other = turned(line, sign)
                cos_y, sin_y = cos_ref[:, y : y + 1], sin_ref[:, y : y + 1]
                modes.append(line * cos_y - other * sin_y)
                swapped.append(other * cos_y + line * sin_y)
            swapped = jnp.concatenate(swapped, axis=1)
            modes = jnp.concatenate(modes, axis=1)
            if first == 0:
                table_copy.wait()
            cells = jnp.concatenate(
                inverse_line(table_ref, quarters_of(modes), quarters_of(swapped)), axis=0
            )
            lanes = slice(first * LANES, (first + 2) * LANES)
            grid_ref[:NX, lanes] = cells
            grid_ref[NX:, lanes] = cells[:WIDE]
        lane = lax.broadcasted_iota(jnp.int32, (SLABS, LANES), 1)
        energy = jnp.sum(jnp.where(lane == PART_Z, in_ref[rows_of(0), :], 0.0))
    gap = jnp.zeros((HALF - PADDED_Z, 3 * LANES), bf16)

    if not own:

        @pl.when(jnp.logical_not(later))
        def _():
            for copy in copies[:3]:
                copy.wait()

    def pair_body(pair, carry):
        pencil, lanes = pair_place(pair)
        waves = [
            jnp.concatenate(
                [waves_ref[pair, n, :PADDED_Z], gap, waves_ref[pair, n, PADDED_Z:], gap],
                axis=0,
            )
            for n in range(2)
        ]
        first_row, window, _ = pair_window(pair, own, where_ref)
        at = pl.ds(first_row, window)
        cells = jnp.concatenate(
            [grid_ref[at, n * LANES : (n + 1) * LANES] for n in range(len(rows))], axis=0
        )
        read = product(halves(cells), waves)
        dense_x = [x_ref[pair, p, :window] for p in range(3)]
        dense_y = [y_ref[pair, p] for p in range(3)]
        lined = {}
        for order_y, order_z in ((0, 0), (1, 0), (2, 0), (0, 1), (1, 1), (0, 2)):
            lined[order_y, order_z] = sum(
                dense_y[order_y][r : r + 1]
                * read[n * window : (n + 1) * window, order_z * LANES : (order_z + 1) * LANES]
                for n, r in enumerate(rows)
            )

        def sampled(p, r, s):
            return jnp.sum(dense_x[p] * lined[r, s], axis=0, keepdims=True)

        charge, dip_x, dip_y, dip_z, live = [
            atoms_ref[pencil, a : a + 1, lanes] for a in range(6, 11)
        ]
        s100 = sampled(1, 0, 0)
        s010 = sampled(0, 1, 0)
        s001 = sampled(0, 0, 1)
        s110 = sampled(1, 1, 0)
        s101 = sampled(1, 0, 1)
        s011 = sampled(0, 1, 1)
        out = [
            live * sampled(0, 0, 0),
            live * s100,
            live * s010,
            live * s001,
            charge * s100 + dip_x * sampled(2, 0, 0) + dip_y * s110 + dip_z * s101,
            charge * s010 + dip_x * s110 + dip_y * sampled(0, 2, 0) + dip_z * s011,
            charge * s001 + dip_x * s101 + dip_y * s011 + dip_z * sampled(0, 0, 2),
            jnp.full(live.shape, energy, f32),
        ]
        out_ref[pencil, :, lanes] = jnp.concatenate(out, axis=0)
        return carry

    lax.fori_loop(0, PENCILS * PAIRS, pair_body, 0, unroll=6)
    if not own:

        @pl.when(jnp.logical_not(later))
        def _():
            for copy in copies[3:]:
                copy.wait()


def finish_kernel(in_ref, charge_ref, dipole_ref, position_ref, energy_ref, row_ref, semaphore):
    total = (in_ref[0] + in_ref[1]) + (in_ref[2] + in_ref[3])
    row_ref[...] = total[0:1]
    copy = fetch(row_ref.at[0], charge_ref, semaphore)
    dipole_ref[...] = total[1:4]
    position_ref[...] = total[4:7]
    energy_ref[...] = total[7:8, 0:1]
    copy.wait()


SPACES = {"v": pltpu.VMEM, "h": pltpu.HBM, "s": pltpu.SMEM}
WORK = {"flops": 1_000_000_000, "bytes_accessed": 8_000_000}


def out_place(shape):
    pinned = isinstance(shape, type(pltpu.HBM((8, LANES), f32)))
    return pl.BlockSpec(memory_space=pltpu.HBM if pinned else pltpu.VMEM)


def call(kernel, inputs, out_shape, scratch=(), aliases=()):
    def run(*operands):
        placed = [
            pltpu.with_memory_space_constraint(one, pltpu.HBM) if where == "h" else one
            for one, where in zip(operands, inputs)
        ]
        return pl.pallas_call(
            kernel,
            out_shape=out_shape,
            in_specs=[pl.BlockSpec(memory_space=SPACES[one]) for one in inputs],
            out_specs=jax.tree.map(out_place, out_shape),
            scratch_shapes=list(scratch),
            input_output_aliases=dict(aliases),
            compiler_params=pltpu.CompilerParams(vmem_limit_bytes=28 * 1024 * 1024),
            cost_estimate=pl.CostEstimate(transcendentals=0, **WORK),
        )(*placed)

    return run


def next_slab(value, back=False):
    step = -1 if back else 1
    return lax.ppermute(value, "gy", [(i, (i + step) % SLABS) for i in range(SLABS)])


def swap_slabs(lines):
    lines = lines.reshape(SLABS, CARRIERS, 1, LANES)
    lines = lax.all_to_all(lines, "gy", split_axis=0, concat_axis=0, tiled=True)
    return lines.reshape(SLABS * CARRIERS, LANES)


def on_device(cell_index, offsets, charges, dipoles, block_count, shear_cells):
    pencil_index = lax.axis_index("gx")
    slab_index = lax.axis_index("gy")
    x_forward, x_inverse, y_forward, y_inverse = wave_tables()
    shape = jax.ShapeDtypeStruct
    shift = jnp.where(slab_index == 0, shear_cells[0], 0)
    where = jnp.stack([slab_index, pencil_index, shift, shear_cells[0]])

    mine, base, taps, cos_t, sin_t = call(
        prepare_kernel,
        "sshhhhh",
        (
            shape((16, ATOM_DEV), f32),
            shape((8, LANES), f32),
            shape((12, PADDED_Z, LANES), f32),
            shape((NX, LANES), f32),
            shape((NX, LANES), f32),
        ),
        [
            pltpu.SMEM(block_count.shape, jnp.int32),
            pltpu.VMEM((3, ATOM_DEV), jnp.int32),
            pltpu.VMEM((3, ATOM_DEV), f32),
            pltpu.VMEM((1, ATOM_DEV), f32),
            pltpu.VMEM((3, ATOM_DEV), f32),
            pltpu.SemaphoreType.DMA((5,)),
        ],
    )(
        where,
        shear_cells,
        block_count,
        cell_index,
        offsets,
        charges,
        dipoles,
    )
    atoms = lax.all_gather(mine, "gx", axis=0, tiled=False)
    below_atoms = next_slab(atoms)

    packed = shape((SLABS * CARRIERS, LANES), f32)
    table_space = pltpu.VMEM((NX, 6 * QUARTER), bf16)
    pairs = 2 * PENCILS * PAIRS
    held = [
        ((2, 2 * PADDED_Z, 3 * LANES), bf16),
        ((3, WIDE, LANES), f32),
        ((3, 16, LANES), f32),
    ]
    weights_space = pltpu.VMEM((PENCILS, 18, 8, ATOM_DEV), f32)
    four = pltpu.SemaphoreType.DMA((4,))
    grid_shape = shape((EXTENDED, 2 * CY * LANES), f32)
    slab_grid = call(
        lambda *refs: spread_kernel(True, *refs),
        "vsvv",
        grid_shape,
        [weights_space],
    )(atoms, where, base, taps)
    green_shape = pltpu.HBM((NY, PART_X * LANES), f32)
    green_space = pltpu.VMEM((NY, PART_X * LANES), f32)
    _, lines, *weights, green = call(
        lambda *refs: spread_kernel(False, *refs),
        "vsvvvhvvv",
        (
            grid_shape,
            packed,
            *(pltpu.HBM((pairs, *dims), kind) for dims, kind in held),
            green_shape,
        ),
        [
            *(pltpu.VMEM((pairs, *dims), kind) for dims, kind in held),
            green_space,
            table_space,
            weights_space,
            four,
        ],
        ((4, 0),),
    )(below_atoms, where, base, taps, slab_grid, x_forward, cos_t, sin_t, atoms)
    lines, where = lax.optimization_barrier((lines, where))
    green = call(
        green_kernel, "sh", green_shape, [green_space, pltpu.SemaphoreType.DMA], ((1, 0),)
    )(where, green)
    lines = swap_slabs(lines)
    filtered = call(
        filter_kernel,
        "vhhh",
        packed,
        [table_space, table_space, green_space, pltpu.SemaphoreType.DMA((5,))],
    )(
        lines, y_forward, y_inverse, green
    )
    filtered = swap_slabs(filtered)
    shares_shape = shape((PENCILS, 8, ATOM_DEV), f32)
    below_shares, potential, *weights = call(
        lambda *refs: sample_kernel(False, *refs),
        "vsvvhhhvvvhv",
        (
            shares_shape,
            shape((EXTENDED, CY * LANES), f32),
            *(shape((pairs // 2, *dims), kind) for dims, kind in held),
        ),
        [
            *(pltpu.VMEM((pairs // 2, *dims), kind) for dims, kind in held),
            table_space,
            weights_space,
            pltpu.SemaphoreType.DMA((7,)),
        ],
    )(below_atoms, where, base, taps, *weights, filtered, cos_t, sin_t, x_inverse, atoms)
    below_shares = next_slab(below_shares, back=True)
    shares = call(lambda *refs: sample_kernel(True, *refs), "vsvvvv", shares_shape)(
        atoms, where, *weights, potential
    )
    shares = lax.all_to_all(shares + below_shares, "gx", split_axis=0, concat_axis=0, tiled=True)
    charge_grad, dipole_grad, position_grad, energy = call(
        finish_kernel,
        "v",
        (
            pltpu.HBM((ATOM_DEV,), f32),
            shape((3, ATOM_DEV), f32),
            shape((3, ATOM_DEV), f32),
            shape((1, 1), f32),
        ),
        [pltpu.VMEM((1, ATOM_DEV), f32), pltpu.SemaphoreType.DMA],
    )(shares)
    return charge_grad, dipole_grad, position_grad, energy[0]


def solution(mesh):
    placed = (
        P(None, ("gy", "gx")),
        P(None, ("gy", "gx")),
        P(("gy", "gx")),
        P(None, ("gy", "gx")),
        P(("gy", "gx")),
        P(),
    )
    return jax.shard_map(
        on_device,
        mesh=mesh,
        in_specs=placed,
        out_specs=(P(("gy", "gx")), P(None, ("gy", "gx")), P(None, ("gy", "gx")), P()),
        check_vma=False,
    )
```

```python
import math

import jax
import jax.numpy as jnp
import ml_dtypes
import numpy as np
from jax import lax
from jax.experimental import pallas as pl
from jax.experimental.pallas import tpu as pltpu
from jax.sharding import PartitionSpec as P

NX = 384
NY = 384
NZ = 360
CY = 6
CX = 96
PENCILS = 4
SLABS = 64
PART_X = 6
PART_Z = 45
ATOM_BLK = 64
ATOM_DEV = 384
PAIRS = 3
WINDOW = 40
WIDE = 48
EXTENDED = NX + WIDE
HALF = 64
LANES = 128
PADDED_Z = 48
QUARTER = 96
screening = 0.9
f32 = jnp.float32
bf16 = jnp.bfloat16


def split_table(table):
    high = table.astype(ml_dtypes.bfloat16)
    low = (table - high.astype(np.float64)).astype(ml_dtypes.bfloat16)
    return np.concatenate([high, high, low], axis=1)


def wave_tables():
    quarter = np.arange(QUARTER)
    mode = np.arange(4)[:, None] + 4 * quarter[None, :]
    row_y = CY * (quarter % 16) + quarter // 16
    tables = []
    for place in (quarter, row_y):
        ticks = mode[:, :, None] * place % NX
        for table in (ticks, ticks.transpose(0, 2, 1)):
            angle = 2.0 * np.pi / NX * table.reshape(NX, QUARTER)
            tables.append(split_table(np.concatenate([np.cos(angle), np.sin(angle)], axis=1)))
    return tables


def spline_rows(fraction):
    levels = {2: [1.0 - fraction, fraction]}
    current = levels[2]
    for n in range(3, 7):
        inverse_n = 1.0 / (n - 1)
        updated = [None] * n
        updated[n - 1] = inverse_n * fraction * current[n - 2]
        for j in range(1, n - 1):
            updated[n - 1 - j] = inverse_n * (
                (fraction + j) * current[n - 2 - j] + (n - j - fraction) * current[n - 1 - j]
            )
        updated[0] = inverse_n * (1.0 - fraction) * current[0]
        current = updated
        levels[n] = current
    zero_row = jnp.zeros_like(fraction)

    def entry_at(values_list, k):
        return values_list[k] if 0 <= k < len(values_list) else zero_row

    first = [entry_at(levels[5], t - 1) - entry_at(levels[5], t) for t in range(6)]
    second = [
        entry_at(levels[4], t - 2) - 2.0 * entry_at(levels[4], t - 1) + entry_at(levels[4], t)
        for t in range(6)
    ]
    return levels[6], first, second


def dense_rows(tables, cell, length):
    away = lax.broadcasted_iota(jnp.int32, (length, cell.shape[1]), 0).astype(f32) - cell
    summed = [jnp.zeros(away.shape, f32) for _ in tables]
    for t in range(6):
        here = away == float(t)
        summed = [jnp.where(here, table[t], so_far) for table, so_far in zip(tables, summed)]
    return summed


def unit_phase(turns):
    turns = turns - jnp.floor(turns + 0.5)
    quarter = jnp.floor(4.0 * turns + 0.5)
    rest = turns - 0.25 * quarter
    theta = (2.0 * math.pi) * rest
    square = theta * theta
    sine = theta * (
        1.0
        + square
        * (-1.0 / 6 + square * (1.0 / 120 + square * (-1.0 / 5040 + square * (1.0 / 362880))))
    )
    cosine = 1.0 + square * (
        -0.5
        + square
        * (1.0 / 24 + square * (-1.0 / 720 + square * (1.0 / 40320 - square * (1.0 / 3628800))))
    )
    odd = jnp.abs(quarter) == 1.0
    cos_out = jnp.where(odd, sine, cosine)
    sin_out = jnp.where(odd, cosine, sine)
    cos_out = jnp.where((quarter == 1.0) | (jnp.abs(quarter) == 2.0), -cos_out, cos_out)
    sin_out = jnp.where((quarter == -1.0) | (jnp.abs(quarter) == 2.0), -sin_out, sin_out)
    return cos_out, sin_out


class Twist:
    def __init__(self, cos_ref, sin_ref):
        whole = (NX, LANES)
        self.cos = jnp.broadcast_to(cos_ref[:, 0:1], whole)
        self.sin = jnp.broadcast_to(sin_ref[:, 0:1], whole)
        self.cos_step = jnp.broadcast_to(cos_ref[:, CY : CY + 1], whole)
        self.sin_step = jnp.broadcast_to(sin_ref[:, CY : CY + 1], whole)
        self.row = 0

    def at(self, row):
        while self.row < row:
            self.cos, self.sin = (
                self.cos * self.cos_step - self.sin * self.sin_step,
                self.sin * self.cos_step + self.cos * self.sin_step,
            )
            self.row += 1
        return self.cos, self.sin


def halves(value):
    high = value.astype(bf16)
    return high, (value - high.astype(f32)).astype(bf16)


def joined(left, right):
    return (
        jnp.concatenate([left[0], left[0], left[1]], axis=1),
        jnp.concatenate([right[0], right[1], right[0]], axis=0),
    )


def product(left, right):
    left, right = joined(left, right)
    return jnp.dot(left, right, preferred_element_type=f32)


def product3(left, right):
    def one(a, b):
        return jnp.dot(a, b, preferred_element_type=f32)

    return one(left[0], right[0]) + (one(left[0], right[1]) + one(left[1], right[0]))


def lane_sign(shape):
    return jnp.where(lax.broadcasted_iota(jnp.int32, shape, 1) < HALF, 1.0, -1.0).astype(f32)


def turned(value, sign):
    return pltpu.roll(value, HALF, 1) * sign


def fetch(source, target, semaphore):
    copy = pltpu.make_async_copy(source, target, semaphore)
    copy.start()
    return copy


def line_product(table_ref, r, value):
    rows = slice(r * QUARTER, (r + 1) * QUARTER)
    table = table_ref[rows, : 2 * QUARTER], table_ref[rows, 4 * QUARTER :]
    return product3(table, halves(value))


def forward_line(table_ref, quarters, turned_quarters):
    g, h = quarters, turned_quarters
    a, b, c, d = g[0] + g[2], g[0] - g[2], g[1] + g[3], g[1] - g[3]
    ta, tb, tc, td = h[0] + h[2], h[0] - h[2], h[1] + h[3], h[1] - h[3]
    lines = []
    for r, (one, other) in enumerate(
        ((a + c, ta + tc), (b + td, tb - d), (a - c, ta - tc), (b - td, tb + d))
    ):
        stacked = jnp.concatenate([one, other], axis=0)
        lines.append(line_product(table_ref, r, stacked))
    return lines


def inverse_line(table_ref, modes, turned_modes):
    z = []
    for r in range(4):
        stacked = jnp.concatenate([modes[r], -turned_modes[r]], axis=0)
        z.append(line_product(table_ref, r, stacked))
    a, b, c, d = z[0] + z[2], z[0] - z[2], z[1] + z[3], z[1] - z[3]
    width = d.shape[1]
    sign = lane_sign((QUARTER, LANES))
    td = jnp.concatenate(
        [turned(d[:, n : n + LANES], sign) for n in range(0, width, LANES)], axis=1
    )
    return [a + c, b - td, a - c, b + td]


def quarters_of(value):
    return [value[r * QUARTER : (r + 1) * QUARTER] for r in range(4)]


PIECES = (0, 16, 32, 64, 80, 96)
GROUPS = PART_X * CY // 4
CARRIERS = 3 * GROUPS


def lane_range(first):
    lane = lax.broadcasted_iota(jnp.int32, (SLABS, LANES), 1)
    return (lane >= first) & (lane < first + 16)


def pack_blocks(blocks):
    carriers = []
    for c in range(3):
        value = blocks[c]
        for half in range(2):
            gap = PADDED_Z + half * HALF
            shift = (gap - PIECES[2 * c + half]) % LANES
            value = jnp.where(lane_range(gap), pltpu.roll(blocks[3], shift, 1), value)
        carriers.append(value)
    return carriers


def unpack_block(carriers):
    value = jnp.zeros((SLABS, LANES), f32)
    for p, source in enumerate(PIECES):
        gap = PADDED_Z + p % 2 * HALF
        shift = (source - gap) % LANES
        value = jnp.where(lane_range(source), pltpu.roll(carriers[p // 2], shift, 1), value)
    return value


def rows_of(carrier):
    return pl.ds(carrier, SLABS, stride=CARRIERS)


def block_at(ref, j, y):
    block = j * CY + y
    group, place = block // 4, block % 4
    if place < 3:
        return ref[rows_of(3 * group + place), :]
    return unpack_block([ref[rows_of(3 * group + c), :] for c in range(3)])


def prepare_kernel(
    where_ref, shear_ref, counts_ref, cells_ref, offsets_ref, charges_ref, dipoles_ref,
    atoms_ref, base_ref, taps_ref, cos_ref, sin_ref,
    count_ref, cell_ref, offset_ref, charge_ref, dipole_ref, semaphores
):
    copies = [
        fetch(source, target, semaphores.at[n])
        for n, (source, target) in enumerate(
            (
                (counts_ref, count_ref),
                (cells_ref, cell_ref),
                (offsets_ref, offset_ref),
                (charges_ref, charge_ref.at[0]),
                (dipoles_ref, dipole_ref),
            )
        )
    ]
    slab, pencil = where_ref[0], where_ref[1]
    first = pencil * PART_Z
    row = lax.broadcasted_iota(jnp.int32, (PADDED_Z, LANES), 0)
    mode = (row + first).astype(f32)
    base_ref[...] = mode[:8]
    for t in range(6):
        cos_t, sin_t = unit_phase(mode * float(t) * (1.0 / NZ))
        taps_ref[t] = jnp.where(row < PART_Z, cos_t, 0.0)
        taps_ref[6 + t] = jnp.where(row < PART_Z, sin_t, 0.0)
    column = lax.broadcasted_iota(jnp.int32, (1, LANES), 1)
    rows = jnp.where(column < CY, slab * CY + column, 1)
    index = lax.broadcasted_iota(jnp.int32, (NX, LANES), 0)
    folds = folded_mode(index)
    ticks = folds * (shear_ref[0] * rows)
    whole = jnp.floor(ticks.astype(f32) * (1.0 / (NX * NY))).astype(jnp.int32)
    rest = ticks - whole * (NX * NY)
    cos_t, sin_t = unit_phase(rest.astype(f32) * (1.0 / (NX * NY)))
    cos_ref[...] = cos_t
    sin_ref[...] = sin_t
    for copy in copies:
        copy.wait()
    slot = lax.broadcasted_iota(jnp.int32, (1, ATOM_DEV), 1)
    live = jnp.zeros((1, ATOM_DEV), f32)
    for b in range(ATOM_DEV // ATOM_BLK):
        inside = (slot >= b * ATOM_BLK) & (slot < b * ATOM_BLK + count_ref[b])
        live = jnp.where(inside, 1.0, live)
    atoms_ref[0:1, :] = cell_ref[0:1, :].astype(f32)
    atoms_ref[1:2, :] = (cell_ref[1:2, :] - slab * CY).astype(f32)
    atoms_ref[2:3, :] = cell_ref[2:3, :].astype(f32)
    atoms_ref[3:6, :] = offset_ref[...]
    atoms_ref[6:7, :] = charge_ref[...] * live
    atoms_ref[7:10, :] = dipole_ref[...] * live
    atoms_ref[10:11, :] = live
    atoms_ref[11:16, :] = jnp.zeros((5, ATOM_DEV), f32)


def spline_table(atoms_ref, table_ref, orders):
    def pencil_body(pencil, carry):
        tables = spline_rows(atoms_ref[pencil, 3:6, :])
        for o in range(orders):
            for t in range(6):
                table_ref[pencil, o * 6 + t, 0:3, :] = tables[o][t]
        return carry

    lax.fori_loop(0, PENCILS, pencil_body, 0)


def weight_rows(table_ref, pencil, lanes, dim, orders):
    row = slice(dim, dim + 1)
    return [[table_ref[pencil, o * 6 + t, row, lanes] for t in range(6)] for o in range(orders)]


def pair_place(pair):
    pencil = pair // PAIRS
    return pencil, pl.ds(pl.multiple_of(pair % PAIRS * LANES, LANES), LANES)


def pair_window(pair, own, where_ref):
    if own:
        return pl.multiple_of(pair * 32, 8), WINDOW, (pair * 32).astype(f32)
    place = pair * 32 + where_ref[2]
    place = jnp.where(place >= NX, place - NX, place)
    first = place // 8 * 8
    return pl.multiple_of(first, 8), WIDE, (pair * 32 - (place - first)).astype(f32)


def z_waves(cell_z, weights, base_ref, taps_ref):
    turn = base_ref[...] * cell_z
    turn = turn - 360.0 * jnp.floor(turn * (1.0 / 360.0))
    cos_k, sin_k = unit_phase(turn * (1.0 / 360.0))
    turn = 8.0 * cell_z
    turn = turn - 360.0 * jnp.floor(turn * (1.0 / 360.0))
    cos_8, sin_8 = unit_phase(jnp.broadcast_to(turn * (1.0 / 360.0), cos_k.shape))
    pieces = [[] for _ in weights]
    pieces_im = [[] for _ in weights]
    for q in range(PADDED_Z // 8):
        span = slice(q * 8, q * 8 + 8)
        cos_t = [taps_ref[t, span, :] for t in range(6)]
        sin_t = [taps_ref[6 + t, span, :] for t in range(6)]
        for s, weight in enumerate(weights):
            real = weight[0] * cos_t[0] + sum(weight[t] * cos_t[t] for t in range(1, 6))
            imag = sum(weight[t] * sin_t[t] for t in range(1, 6))
            pieces[s].append(real * cos_k - imag * sin_k)
            pieces_im[s].append(-(real * sin_k + imag * cos_k))
        cos_k, sin_k = cos_k * cos_8 - sin_k * sin_8, sin_k * cos_8 + cos_k * sin_8
    return [
        (jnp.concatenate(re, axis=0), jnp.concatenate(im, axis=0))
        for re, im in zip(pieces, pieces_im)
    ]


def sampling_weights(
    start, own, where_ref, some_ref, table_ref, base_ref, taps_ref, waves_ref, x_ref, y_ref
):
    spline_table(some_ref, table_ref, 3)

    def pair_body(pair, carry):
        pencil, lanes = pair_place(pair)
        row = [some_ref[pencil, a : a + 1, lanes] for a in range(3)]
        _, window, origin = pair_window(pair, own, where_ref)
        dense_x = dense_rows(weight_rows(table_ref, pencil, lanes, 0, 3), row[0] - origin, window)
        dense_y = dense_rows(weight_rows(table_ref, pencil, lanes, 1, 3), row[1], 16)
        for p in range(3):
            x_ref[start + pair, p, :window] = dense_x[p]
            y_ref[start + pair, p] = dense_y[p]
        waves = z_waves(row[2], weight_rows(table_ref, pencil, lanes, 2, 3), base_ref, taps_ref)
        for s, (re, im) in enumerate(waves):
            re, im = halves(re), halves(im)
            columns = slice(s * LANES, (s + 1) * LANES)
            for n in range(2):
                waves_ref[start + pair, n, :PADDED_Z, columns] = re[n]
                waves_ref[start + pair, n, PADDED_Z:, columns] = im[n]
        return carry

    lax.fori_loop(0, PENCILS * PAIRS, pair_body, 0, unroll=2)


def spread_kernel(own, *refs):
    atoms_ref, where_ref, base_ref, taps_ref = refs[:4]
    if own:
        grid_ref, weights_ref = refs[4:]
        grid_ref[...] = jnp.zeros_like(grid_ref)
    else:
        _, tables_ref, cos_ref, sin_ref, slab_atoms_ref, grid_ref, out_ref = refs[4:11]
        results, green_out_ref, kept = refs[11:14], refs[14], refs[15:18]
        green_ref, table_ref, weights_ref, semaphores = refs[18:]
        table_copy = fetch(tables_ref, table_ref, semaphores.at[0])
    rows = list(range(CY)) if own else list(range(CY, 2 * CY - 1))
    part = CY * LANES
    gap = jnp.zeros((HALF - PADDED_Z, LANES), bf16)
    spline_table(atoms_ref, weights_ref, 2)

    def pair_body(pair, carry):
        pencil, lanes = pair_place(pair)
        row = [atoms_ref[pencil, a : a + 1, lanes] for a in range(10)]
        charge, dip_x, dip_y, dip_z = row[6:10]
        first_row, window, origin = pair_window(pair, own, where_ref)
        dense_x = dense_rows(
            weight_rows(weights_ref, pencil, lanes, 0, 2), row[0] - origin, window
        )
        dense_y = dense_rows(weight_rows(weights_ref, pencil, lanes, 1, 2), row[1], 16)
        value, first = weight_rows(weights_ref, pencil, lanes, 2, 2)
        mixed = [charge * value[t] + dip_z * first[t] for t in range(6)]
        right = []
        for re, im in z_waves(row[2], (mixed, value), base_ref, taps_ref):
            re, im = halves(re), halves(im)
            right.append(
                [
                    jnp.concatenate([re[n], gap, im[n], gap, im[n], gap, -re[n], gap], axis=0)
                    for n in range(2)
                ]
            )
        high, low = [jnp.concatenate([right[0][n], right[1][n]], axis=1) for n in range(2)]
        right = jnp.concatenate([high, low, high], axis=1)
        left = []
        for r in rows:
            value, first = dense_y[0][r : r + 1], dense_y[1][r : r + 1]
            left.append(
                jnp.concatenate(
                    [
                        value * dense_x[0],
                        (dip_x * value) * dense_x[1] + (dip_y * first) * dense_x[0],
                    ],
                    axis=1,
                )
            )
        high, low = halves(jnp.concatenate(left, axis=0))
        left = jnp.concatenate([high, high, low], axis=1)
        added = lax.dot_general(
            left, right, (((1,), (1,)), ((), ())), preferred_element_type=f32
        )
        at = pl.ds(first_row, window)
        for n in range(len(rows)):
            piece = added[n * window : (n + 1) * window]
            grid_ref[at, n * LANES : (n + 1) * LANES] += piece[:, :LANES]
            grid_ref[at, part + n * LANES : part + (n + 1) * LANES] += piece[:, LANES:]
        return carry

    lax.fori_loop(0, PENCILS * PAIRS, pair_body, 0, unroll=12)
    if own:
        return
    grid_ref[0:WIDE] += grid_ref[NX:EXTENDED]
    table_copy.wait()
    sign = lane_sign((NX, LANES))
    twist = Twist(cos_ref, sin_ref)
    totals = []
    for first in range(0, CY, 2):
        lanes = slice(first * LANES, (first + 2) * LANES)
        below = slice(part + lanes.start, part + lanes.stop)
        line = jnp.concatenate(
            forward_line(
                table_ref, quarters_of(grid_ref[:NX, lanes]), quarters_of(grid_ref[:NX, below])
            ),
            axis=0,
        )
        for n, y in enumerate((first, first + 1)):
            one = line[:, n * LANES : (n + 1) * LANES]
            cos_y, sin_y = twist.at(y)
            totals.append(one * cos_y + turned(one, sign) * sin_y)
    for group in range(GROUPS):
        blocks = []
        for block in range(4 * group, 4 * group + 4):
            j, y = block // CY, block % CY
            blocks.append(totals[y][j * SLABS : (j + 1) * SLABS])
        for c, carrier in enumerate(pack_blocks(blocks)):
            out_ref[rows_of(3 * group + c), :] = carrier

    @pl.when(where_ref[1] % 2 == 1)
    def _():
        make_green(where_ref, green_ref)
        green_copy = fetch(green_ref, green_out_ref, semaphores.at[3])
        for start, some_ref in ((0, slab_atoms_ref), (PENCILS * PAIRS, atoms_ref)):
            sampling_weights(
                start, start == 0, where_ref, some_ref, weights_ref, base_ref, taps_ref, *kept
            )
        copies = [fetch(kept[n], results[n], semaphores.at[n]) for n in range(3)]
        for copy in [green_copy, *copies]:
            copy.wait()


def spline_modulus(turns):
    cosine, _ = unit_phase(turns)
    return (64.0 + 52.0 * cosine + 4.0 * cosine * cosine) * (1.0 / 120.0)


def folded_mode(row):
    residue = (
        (row >= QUARTER).astype(jnp.int32)
        + (row >= 2 * QUARTER).astype(jnp.int32)
        + (row >= 3 * QUARTER).astype(jnp.int32)
    )
    mode = 4 * (row - QUARTER * residue) + residue
    return jnp.where(mode < NX // 2, mode, mode - NX)


def make_green(where_ref, out_ref):
    slab, pencil, shear = where_ref[0], where_ref[1], where_ref[3].astype(f32)
    decay = (math.pi / screening) ** 2
    column = lax.broadcasted_iota(jnp.int32, (1, LANES), 1)
    own_x = folded_mode(jnp.minimum(column, PART_X) * SLABS + slab)
    own_y = folded_mode(lax.broadcasted_iota(jnp.int32, (NY, LANES), 0))
    float_x = own_x.astype(f32)
    wave_y = own_y.astype(f32) + float_x * shear * (1.0 / NX)
    part_x, part_y = float_x * (1.0 / NX), wave_y * (1.0 / NY)
    norm = part_x * part_x + part_y * part_y
    moduli = spline_modulus(part_x) * spline_modulus(part_y)
    top = jnp.exp(-decay * norm) / (math.pi * moduli * moduli)
    top = jnp.where((own_x == -(NX // 2)) | (own_y == -(NY // 2)), 0.0, top)
    lane = jnp.where(column < HALF, column, column - HALF)
    mode = pencil * PART_Z + lane
    part_z = mode.astype(f32) * (1.0 / NZ)
    modulus = spline_modulus(part_z)
    norm_z = part_z * part_z
    twice = jnp.where(mode == 0, 1.0, 2.0) * (1.0 / (NX * NY * NZ))
    mode_top = jnp.where(
        lane < PART_Z, twice * jnp.exp(-decay * norm_z) / (modulus * modulus), 0.0
    )
    mode_norm = jnp.where(lane < PART_Z, norm_z, 1.0)
    for j in range(PART_X):
        square = norm[:, j : j + 1] + mode_norm
        green = top[:, j : j + 1] * mode_top / jnp.where(square == 0.0, 1.0, square)
        out_ref[:, j * LANES : (j + 1) * LANES] = jnp.where(square == 0.0, 0.0, green)


def green_kernel(where_ref, _, result_ref, green_ref, semaphore):
    @pl.when(where_ref[1] % 2 == 0)
    def _():
        make_green(where_ref, green_ref)
        fetch(green_ref, result_ref, semaphore).wait()


def filter_kernel(
    in_ref, tables_ref, backs_ref, greens_ref, out_ref, table_ref, back_ref, green_ref, semaphores
):
    copies = [
        fetch(tables_ref, table_ref, semaphores.at[0]),
        fetch(backs_ref, back_ref, semaphores.at[1]),
    ]
    for first in range(0, PART_X, 2):
        lanes = pl.ds(first * LANES, 2 * LANES)
        copies.append(
            fetch(greens_ref.at[:, lanes], green_ref.at[:, lanes], semaphores.at[2 + first // 2])
        )
    sign = lane_sign((NY, LANES))
    energy = jnp.zeros((8, LANES), f32)
    blocks = []
    for first in range(0, PART_X, 2):
        lines = []
        for j in (first, first + 1):
            found = [block_at(in_ref, j, y) for y in range(CY)]
            lines.append(
                jnp.concatenate(
                    [one[16 * part : 16 * part + 16] for part in range(4) for one in found], axis=0
                )
            )
        swapped = jnp.concatenate([turned(one, sign) for one in lines], axis=1)
        lines = jnp.concatenate(lines, axis=1)
        if first == 0:
            copies[0].wait()
        spectrum = jnp.concatenate(
            forward_line(table_ref, quarters_of(lines), quarters_of(swapped)), axis=0
        )
        modes = []
        copies[2 + first // 2].wait()
        for n in range(2):
            j = first + n
            one = spectrum[:, n * LANES : (n + 1) * LANES]
            scaled = green_ref[:, j * LANES : (j + 1) * LANES] * one
            share = scaled * one
            energy = energy + sum(share[8 * i : 8 * i + 8] for i in range(NY // 8))
            modes.append(scaled)
        swapped = jnp.concatenate([turned(one, sign) for one in modes], axis=1)
        modes = jnp.concatenate(modes, axis=1)
        if first == 0:
            copies[1].wait()
        parts = inverse_line(back_ref, quarters_of(modes), quarters_of(swapped))
        for n in range(2):
            for y in range(CY):
                blocks.append(
                    jnp.concatenate(
                        [
                            one[16 * y : 16 * y + 16, n * LANES : (n + 1) * LANES]
                            for one in parts
                        ],
                        axis=0,
                    )
                )
        for group in range(first * CY // 4, (first + 2) * CY // 4):
            for c, carrier in enumerate(pack_blocks(blocks[4 * group : 4 * group + 4])):
                out_ref[rows_of(3 * group + c), :] = carrier
    lane = lax.broadcasted_iota(jnp.int32, (SLABS, LANES), 1)
    share = 0.5 * jnp.sum(energy)
    out_ref[rows_of(0), :] = jnp.where(lane == PART_Z, share, out_ref[rows_of(0), :])


def sample_kernel(own, *refs):
    if own:
        atoms_ref, where_ref, waves_ref, x_ref, y_ref, grid_ref, out_ref = refs
    else:
        atoms_ref, where_ref, base_ref, taps_ref = refs[:4]
        kept = refs[4:7]
        in_ref, cos_ref, sin_ref, tables_ref, slab_atoms_ref, out_ref, grid_ref = refs[7:14]
        slab_weights, below_weights = refs[14:17], refs[17:20]
        waves_ref, x_ref, y_ref = below_weights
        table_ref, weights_ref, semaphores = refs[20:]
        table_copy = fetch(tables_ref, table_ref, semaphores.at[6])
        later = where_ref[1] % 2 == 0
        pairs = PENCILS * PAIRS
        copies = [
            pltpu.make_async_copy(source.at[pl.ds(start, pairs)], target, semaphores.at[n])
            for n, (source, start, target) in enumerate(
                [(kept[n], pairs, below_weights[n]) for n in range(3)]
                + [(kept[n], 0, slab_weights[n]) for n in range(3)]
            )
        ]

        @pl.when(later)
        def _():
            for slab, some_ref, targets in (
                (False, atoms_ref, below_weights),
                (True, slab_atoms_ref, slab_weights),
            ):
                sampling_weights(
                    0, slab, where_ref, some_ref, weights_ref, base_ref, taps_ref, *targets
                )

        @pl.when(jnp.logical_not(later))
        def _():
            for copy in copies:
                copy.start()

    rows = list(range(CY)) if own else list(range(CY, 2 * CY - 1))
    energy = 0.0
    if not own:
        sign = lane_sign((NX, LANES))
        twist = Twist(cos_ref, sin_ref)
        for first in range(0, CY, 2):
            modes, swapped = [], []
            for y in range(first, first + 2):
                line = jnp.concatenate([block_at(in_ref, j, y) for j in range(PART_X)], axis=0)
                other = turned(line, sign)
                cos_y, sin_y = twist.at(y)
                modes.append(line * cos_y - other * sin_y)
                swapped.append(other * cos_y + line * sin_y)
            swapped = jnp.concatenate(swapped, axis=1)
            modes = jnp.concatenate(modes, axis=1)
            if first == 0:
                table_copy.wait()
            cells = jnp.concatenate(
                inverse_line(table_ref, quarters_of(modes), quarters_of(swapped)), axis=0
            )
            lanes = slice(first * LANES, (first + 2) * LANES)
            grid_ref[:NX, lanes] = cells
            grid_ref[NX:, lanes] = cells[:WIDE]
        lane = lax.broadcasted_iota(jnp.int32, (SLABS, LANES), 1)
        energy = jnp.sum(jnp.where(lane == PART_Z, in_ref[rows_of(0), :], 0.0))
    gap = jnp.zeros((HALF - PADDED_Z, 3 * LANES), bf16)

    if not own:

        @pl.when(jnp.logical_not(later))
        def _():
            for copy in copies[:3]:
                copy.wait()

    def pair_body(pair, carry):
        pencil, lanes = pair_place(pair)
        waves = [
            jnp.concatenate(
                [waves_ref[pair, n, :PADDED_Z], gap, waves_ref[pair, n, PADDED_Z:], gap],
                axis=0,
            )
            for n in range(2)
        ]
        first_row, window, _ = pair_window(pair, own, where_ref)
        at = pl.ds(first_row, window)
        cells = jnp.concatenate(
            [grid_ref[at, n * LANES : (n + 1) * LANES] for n in range(len(rows))], axis=0
        )
        read = product(halves(cells), waves)
        dense_x = [x_ref[pair, p, :window] for p in range(3)]
        dense_y = [y_ref[pair, p] for p in range(3)]
        lined = {}
        for order_y, order_z in ((0, 0), (1, 0), (2, 0), (0, 1), (1, 1), (0, 2)):
            lined[order_y, order_z] = sum(
                dense_y[order_y][r : r + 1]
                * read[n * window : (n + 1) * window, order_z * LANES : (order_z + 1) * LANES]
                for n, r in enumerate(rows)
            )

        def sampled(p, r, s):
            return jnp.sum(dense_x[p] * lined[r, s], axis=0, keepdims=True)

        charge, dip_x, dip_y, dip_z, live = [
            atoms_ref[pencil, a : a + 1, lanes] for a in range(6, 11)
        ]
        s100 = sampled(1, 0, 0)
        s010 = sampled(0, 1, 0)
        s001 = sampled(0, 0, 1)
        s110 = sampled(1, 1, 0)
        s101 = sampled(1, 0, 1)
        s011 = sampled(0, 1, 1)
        out = [
            live * sampled(0, 0, 0),
            live * s100,
            live * s010,
            live * s001,
            charge * s100 + dip_x * sampled(2, 0, 0) + dip_y * s110 + dip_z * s101,
            charge * s010 + dip_x * s110 + dip_y * sampled(0, 2, 0) + dip_z * s011,
            charge * s001 + dip_x * s101 + dip_y * s011 + dip_z * sampled(0, 0, 2),
            jnp.full(live.shape, energy, f32),
        ]
        ahead = lax.rem(pencil - where_ref[1] + PENCILS, PENCILS)
        out_ref[ahead, :, lanes] = jnp.concatenate(out, axis=0)
        return carry

    lax.fori_loop(0, PENCILS * PAIRS, pair_body, 0, unroll=12)
    if not own:

        @pl.when(jnp.logical_not(later))
        def _():
            for copy in copies[3:]:
                copy.wait()


def finish_kernel(
    own_ref, one_ref, two_ref, three_ref, charge_ref, dipole_ref, position_ref, energy_ref,
    row_ref, semaphore
):
    total = (own_ref[...] + one_ref[...]) + (two_ref[...] + three_ref[...])
    row_ref[...] = total[0:1]
    copy = fetch(row_ref.at[0], charge_ref, semaphore)
    dipole_ref[...] = total[1:4]
    position_ref[...] = total[4:7]
    energy_ref[...] = total[7:8, 0:1]
    copy.wait()


SPACES = {"v": pltpu.VMEM, "h": pltpu.HBM, "s": pltpu.SMEM}
WORK = {"flops": 1_000_000_000, "bytes_accessed": 8_000_000}


def out_place(shape):
    pinned = isinstance(shape, type(pltpu.HBM((8, LANES), f32)))
    return pl.BlockSpec(memory_space=pltpu.HBM if pinned else pltpu.VMEM)


def call(kernel, inputs, out_shape, scratch=(), aliases=()):
    def run(*operands):
        placed = [
            pltpu.with_memory_space_constraint(one, pltpu.HBM) if where == "h" else one
            for one, where in zip(operands, inputs)
        ]
        return pl.pallas_call(
            kernel,
            out_shape=out_shape,
            in_specs=[pl.BlockSpec(memory_space=SPACES[one]) for one in inputs],
            out_specs=jax.tree.map(out_place, out_shape),
            scratch_shapes=list(scratch),
            input_output_aliases=dict(aliases),
            compiler_params=pltpu.CompilerParams(vmem_limit_bytes=28 * 1024 * 1024),
            cost_estimate=pl.CostEstimate(transcendentals=0, **WORK),
        )(*placed)

    return run


def next_slab(value, back=False):
    step = -1 if back else 1
    return lax.ppermute(value, "gy", [(i, (i + step) % SLABS) for i in range(SLABS)])


def swap_slabs(lines):
    lines = lines.reshape(SLABS, CARRIERS, 1, LANES)
    lines = lax.all_to_all(lines, "gy", split_axis=0, concat_axis=0, tiled=True)
    return lines.reshape(SLABS * CARRIERS, LANES)


def on_device(cell_index, offsets, charges, dipoles, block_count, shear_cells):
    pencil_index = lax.axis_index("gx")
    slab_index = lax.axis_index("gy")
    x_forward, x_inverse, y_forward, y_inverse = wave_tables()
    shape = jax.ShapeDtypeStruct
    shift = jnp.where(slab_index == 0, shear_cells[0], 0)
    where = jnp.stack([slab_index, pencil_index, shift, shear_cells[0]])

    mine, base, taps, cos_t, sin_t = call(
        prepare_kernel,
        "sshhhhh",
        (
            shape((16, ATOM_DEV), f32),
            shape((8, LANES), f32),
            shape((12, PADDED_Z, LANES), f32),
            shape((NX, LANES), f32),
            shape((NX, LANES), f32),
        ),
        [
            pltpu.SMEM(block_count.shape, jnp.int32),
            pltpu.VMEM((3, ATOM_DEV), jnp.int32),
            pltpu.VMEM((3, ATOM_DEV), f32),
            pltpu.VMEM((1, ATOM_DEV), f32),
            pltpu.VMEM((3, ATOM_DEV), f32),
            pltpu.SemaphoreType.DMA((5,)),
        ],
    )(
        where,
        shear_cells,
        block_count,
        cell_index,
        offsets,
        charges,
        dipoles,
    )
    atoms = lax.all_gather(mine, "gx", axis=0, tiled=False)
    below_atoms = next_slab(atoms)

    packed = shape((SLABS * CARRIERS, LANES), f32)
    table_space = pltpu.VMEM((NX, 6 * QUARTER), bf16)
    pairs = 2 * PENCILS * PAIRS
    held = [
        ((2, 2 * PADDED_Z, 3 * LANES), bf16),
        ((3, WIDE, LANES), f32),
        ((3, 16, LANES), f32),
    ]
    weights_space = pltpu.VMEM((PENCILS, 18, 8, ATOM_DEV), f32)
    four = pltpu.SemaphoreType.DMA((4,))
    grid_shape = shape((EXTENDED, 2 * CY * LANES), f32)
    slab_grid = call(
        lambda *refs: spread_kernel(True, *refs),
        "vsvv",
        grid_shape,
        [weights_space],
    )(atoms, where, base, taps)
    green_shape = pltpu.HBM((NY, PART_X * LANES), f32)
    green_space = pltpu.VMEM((NY, PART_X * LANES), f32)
    _, lines, *weights, green = call(
        lambda *refs: spread_kernel(False, *refs),
        "vsvvvhvvv",
        (
            grid_shape,
            packed,
            *(pltpu.HBM((pairs, *dims), kind) for dims, kind in held),
            green_shape,
        ),
        [
            *(pltpu.VMEM((pairs, *dims), kind) for dims, kind in held),
            green_space,
            table_space,
            weights_space,
            four,
        ],
        ((4, 0),),
    )(below_atoms, where, base, taps, slab_grid, x_forward, cos_t, sin_t, atoms)
    lines, where = lax.optimization_barrier((lines, where))
    green = call(
        green_kernel, "sh", green_shape, [green_space, pltpu.SemaphoreType.DMA], ((1, 0),)
    )(where, green)
    lines = swap_slabs(lines)
    filtered = call(
        filter_kernel,
        "vhhh",
        packed,
        [table_space, table_space, green_space, pltpu.SemaphoreType.DMA((5,))],
    )(
        lines, y_forward, y_inverse, green
    )
    filtered = swap_slabs(filtered)
    shares_shape = shape((PENCILS, 8, ATOM_DEV), f32)
    below_shares, potential, *weights = call(
        lambda *refs: sample_kernel(False, *refs),
        "vsvvhhhvvvhv",
        (
            shares_shape,
            shape((EXTENDED, CY * LANES), f32),
            *(shape((pairs // 2, *dims), kind) for dims, kind in held),
        ),
        [
            *(pltpu.VMEM((pairs // 2, *dims), kind) for dims, kind in held),
            table_space,
            weights_space,
            pltpu.SemaphoreType.DMA((7,)),
        ],
    )(below_atoms, where, base, taps, *weights, filtered, cos_t, sin_t, x_inverse, atoms)
    below_shares = next_slab(below_shares, back=True)
    shares = call(lambda *refs: sample_kernel(True, *refs), "vsvvvv", shares_shape)(
        atoms, where, *weights, potential
    )
    shares = shares + below_shares
    arrived = [
        lax.ppermute(shares[ahead], "gx", [(i, (i + ahead) % PENCILS) for i in range(PENCILS)])
        for ahead in range(1, PENCILS)
    ]
    charge_grad, dipole_grad, position_grad, energy = call(
        finish_kernel,
        "vvvv",
        (
            pltpu.HBM((ATOM_DEV,), f32),
            shape((3, ATOM_DEV), f32),
            shape((3, ATOM_DEV), f32),
            shape((1, 1), f32),
        ),
        [pltpu.VMEM((1, ATOM_DEV), f32), pltpu.SemaphoreType.DMA],
    )(shares[0], *arrived)
    return charge_grad, dipole_grad, position_grad, energy[0]


def solution(mesh):
    placed = (
        P(None, ("gy", "gx")),
        P(None, ("gy", "gx")),
        P(("gy", "gx")),
        P(None, ("gy", "gx")),
        P(("gy", "gx")),
        P(),
    )
    return jax.shard_map(
        on_device,
        mesh=mesh,
        in_specs=placed,
        out_specs=(P(("gy", "gx")), P(None, ("gy", "gx")), P(None, ("gy", "gx")), P()),
        check_vma=False,
    )
```

```python
import math

import jax
import jax.numpy as jnp
import ml_dtypes
import numpy as np
from jax import lax
from jax.experimental import pallas as pl
from jax.experimental.pallas import tpu as pltpu
from jax.sharding import PartitionSpec as P

NX = 384
NY = 384
NZ = 360
CY = 6
CX = 96
PENCILS = 4
SLABS = 64
PART_X = 6
PART_Z = 45
ATOM_BLK = 64
ATOM_DEV = 384
PAIRS = 3
WINDOW = 40
WIDE = 48
EXTENDED = NX + WIDE
HALF = 64
LANES = 128
PADDED_Z = 48
QUARTER = 96
screening = 0.9
f32 = jnp.float32
bf16 = jnp.bfloat16


def split_table(table):
    high = table.astype(ml_dtypes.bfloat16)
    low = (table - high.astype(np.float64)).astype(ml_dtypes.bfloat16)
    return np.concatenate([high, high, low], axis=1)


def wave_tables():
    quarter = np.arange(QUARTER)
    mode = np.arange(4)[:, None] + 4 * quarter[None, :]
    row_y = CY * (quarter % 16) + quarter // 16
    tables = []
    for place in (quarter, row_y):
        ticks = mode[:, :, None] * place % NX
        for table in (ticks, ticks.transpose(0, 2, 1)):
            angle = 2.0 * np.pi / NX * table.reshape(NX, QUARTER)
            tables.append(split_table(np.concatenate([np.cos(angle), np.sin(angle)], axis=1)))
    return tables


def spline_rows(fraction):
    levels = {2: [1.0 - fraction, fraction]}
    current = levels[2]
    for n in range(3, 7):
        inverse_n = 1.0 / (n - 1)
        updated = [None] * n
        updated[n - 1] = inverse_n * fraction * current[n - 2]
        for j in range(1, n - 1):
            updated[n - 1 - j] = inverse_n * (
                (fraction + j) * current[n - 2 - j] + (n - j - fraction) * current[n - 1 - j]
            )
        updated[0] = inverse_n * (1.0 - fraction) * current[0]
        current = updated
        levels[n] = current
    zero_row = jnp.zeros_like(fraction)

    def entry_at(values_list, k):
        return values_list[k] if 0 <= k < len(values_list) else zero_row

    first = [entry_at(levels[5], t - 1) - entry_at(levels[5], t) for t in range(6)]
    second = [
        entry_at(levels[4], t - 2) - 2.0 * entry_at(levels[4], t - 1) + entry_at(levels[4], t)
        for t in range(6)
    ]
    return levels[6], first, second


def dense_rows(tables, cell, length):
    away = lax.broadcasted_iota(jnp.int32, (length, cell.shape[1]), 0).astype(f32) - cell
    summed = [jnp.zeros(away.shape, f32) for _ in tables]
    for t in range(6):
        here = away == float(t)
        summed = [jnp.where(here, table[t], so_far) for table, so_far in zip(tables, summed)]
    return summed


def unit_phase(turns):
    turns = turns - jnp.floor(turns + 0.5)
    quarter = jnp.floor(4.0 * turns + 0.5)
    rest = turns - 0.25 * quarter
    theta = (2.0 * math.pi) * rest
    square = theta * theta
    sine = theta * (
        1.0
        + square
        * (-1.0 / 6 + square * (1.0 / 120 + square * (-1.0 / 5040 + square * (1.0 / 362880))))
    )
    cosine = 1.0 + square * (
        -0.5
        + square
        * (1.0 / 24 + square * (-1.0 / 720 + square * (1.0 / 40320 - square * (1.0 / 3628800))))
    )
    odd = jnp.abs(quarter) == 1.0
    cos_out = jnp.where(odd, sine, cosine)
    sin_out = jnp.where(odd, cosine, sine)
    cos_out = jnp.where((quarter == 1.0) | (jnp.abs(quarter) == 2.0), -cos_out, cos_out)
    sin_out = jnp.where((quarter == -1.0) | (jnp.abs(quarter) == 2.0), -sin_out, sin_out)
    return cos_out, sin_out


class Twist:
    def __init__(self, cos_ref, sin_ref):
        whole = (NX, LANES)
        self.cos = jnp.broadcast_to(cos_ref[:, 0:1], whole)
        self.sin = jnp.broadcast_to(sin_ref[:, 0:1], whole)
        self.cos_step = jnp.broadcast_to(cos_ref[:, CY : CY + 1], whole)
        self.sin_step = jnp.broadcast_to(sin_ref[:, CY : CY + 1], whole)
        self.row = 0

    def at(self, row):
        while self.row < row:
            self.cos, self.sin = (
                self.cos * self.cos_step - self.sin * self.sin_step,
                self.sin * self.cos_step + self.cos * self.sin_step,
            )
            self.row += 1
        return self.cos, self.sin


def halves(value):
    high = value.astype(bf16)
    return high, (value - high.astype(f32)).astype(bf16)


def joined(left, right):
    return (
        jnp.concatenate([left[0], left[0], left[1]], axis=1),
        jnp.concatenate([right[0], right[1], right[0]], axis=0),
    )


def product(left, right):
    left, right = joined(left, right)
    return jnp.dot(left, right, preferred_element_type=f32)


def product3(left, right):
    def one(a, b):
        return jnp.dot(a, b, preferred_element_type=f32)

    return one(left[0], right[0]) + (one(left[0], right[1]) + one(left[1], right[0]))


def lane_sign(shape):
    return jnp.where(lax.broadcasted_iota(jnp.int32, shape, 1) < HALF, 1.0, -1.0).astype(f32)


def turned(value, sign):
    return pltpu.roll(value, HALF, 1) * sign


def fetch(source, target, semaphore):
    copy = pltpu.make_async_copy(source, target, semaphore)
    copy.start()
    return copy


def line_product(table_ref, r, value):
    rows = slice(r * QUARTER, (r + 1) * QUARTER)
    table = table_ref[rows, : 2 * QUARTER], table_ref[rows, 4 * QUARTER :]
    return product3(table, halves(value))


def forward_line(table_ref, quarters, turned_quarters):
    g, h = quarters, turned_quarters
    a, b, c, d = g[0] + g[2], g[0] - g[2], g[1] + g[3], g[1] - g[3]
    ta, tb, tc, td = h[0] + h[2], h[0] - h[2], h[1] + h[3], h[1] - h[3]
    lines = []
    for r, (one, other) in enumerate(
        ((a + c, ta + tc), (b + td, tb - d), (a - c, ta - tc), (b - td, tb + d))
    ):
        stacked = jnp.concatenate([one, other], axis=0)
        lines.append(line_product(table_ref, r, stacked))
    return lines


def inverse_line(table_ref, modes, turned_modes):
    z = []
    for r in range(4):
        stacked = jnp.concatenate([modes[r], -turned_modes[r]], axis=0)
        z.append(line_product(table_ref, r, stacked))
    a, b, c, d = z[0] + z[2], z[0] - z[2], z[1] + z[3], z[1] - z[3]
    width = d.shape[1]
    sign = lane_sign((QUARTER, LANES))
    td = jnp.concatenate(
        [turned(d[:, n : n + LANES], sign) for n in range(0, width, LANES)], axis=1
    )
    return [a + c, b - td, a - c, b + td]


def quarters_of(value):
    return [value[r * QUARTER : (r + 1) * QUARTER] for r in range(4)]


PIECES = (0, 16, 32, 64, 80, 96)
GROUPS = PART_X * CY // 4
CARRIERS = 3 * GROUPS


def lane_range(first):
    lane = lax.broadcasted_iota(jnp.int32, (SLABS, LANES), 1)
    return (lane >= first) & (lane < first + 16)


def pack_blocks(blocks):
    carriers = []
    for c in range(3):
        value = blocks[c]
        for half in range(2):
            gap = PADDED_Z + half * HALF
            shift = (gap - PIECES[2 * c + half]) % LANES
            value = jnp.where(lane_range(gap), pltpu.roll(blocks[3], shift, 1), value)
        carriers.append(value)
    return carriers


def unpack_block(carriers):
    value = jnp.zeros((SLABS, LANES), f32)
    for p, source in enumerate(PIECES):
        gap = PADDED_Z + p % 2 * HALF
        shift = (source - gap) % LANES
        value = jnp.where(lane_range(source), pltpu.roll(carriers[p // 2], shift, 1), value)
    return value


def rows_of(carrier):
    return pl.ds(carrier, SLABS, stride=CARRIERS)


def block_at(ref, j, y):
    block = j * CY + y
    group, place = block // 4, block % 4
    if place < 3:
        return ref[rows_of(3 * group + place), :]
    return unpack_block([ref[rows_of(3 * group + c), :] for c in range(3)])


def prepare_kernel(
    where_ref, shear_ref, counts_ref, cells_ref, offsets_ref, charges_ref, dipoles_ref,
    atoms_ref, base_ref, taps_ref, cos_ref, sin_ref,
    count_ref, cell_ref, offset_ref, charge_ref, dipole_ref, semaphores
):
    copies = [
        fetch(source, target, semaphores.at[n])
        for n, (source, target) in enumerate(
            (
                (counts_ref, count_ref),
                (cells_ref, cell_ref),
                (offsets_ref, offset_ref),
                (charges_ref, charge_ref.at[0]),
                (dipoles_ref, dipole_ref),
            )
        )
    ]
    slab, pencil = where_ref[0], where_ref[1]
    first = pencil * PART_Z
    row = lax.broadcasted_iota(jnp.int32, (PADDED_Z, LANES), 0)
    mode = (row + first).astype(f32)
    base_ref[...] = mode[:8]
    for t in range(3):
        cos_t, sin_t = unit_phase(mode * (t + 0.5) * (1.0 / NZ))
        taps_ref[t] = jnp.where(row < PART_Z, cos_t, 0.0)
        taps_ref[3 + t] = jnp.where(row < PART_Z, sin_t, 0.0)
    column = lax.broadcasted_iota(jnp.int32, (1, LANES), 1)
    rows = jnp.where(column < CY, slab * CY + column, 1)
    index = lax.broadcasted_iota(jnp.int32, (NX, LANES), 0)
    folds = folded_mode(index)
    ticks = folds * (shear_ref[0] * rows)
    whole = jnp.floor(ticks.astype(f32) * (1.0 / (NX * NY))).astype(jnp.int32)
    rest = ticks - whole * (NX * NY)
    cos_t, sin_t = unit_phase(rest.astype(f32) * (1.0 / (NX * NY)))
    cos_ref[...] = cos_t
    sin_ref[...] = sin_t
    for copy in copies:
        copy.wait()
    slot = lax.broadcasted_iota(jnp.int32, (1, ATOM_DEV), 1)
    live = jnp.zeros((1, ATOM_DEV), f32)
    for b in range(ATOM_DEV // ATOM_BLK):
        inside = (slot >= b * ATOM_BLK) & (slot < b * ATOM_BLK + count_ref[b])
        live = jnp.where(inside, 1.0, live)
    atoms_ref[0:1, :] = cell_ref[0:1, :].astype(f32)
    atoms_ref[1:2, :] = (cell_ref[1:2, :] - slab * CY).astype(f32)
    atoms_ref[2:3, :] = cell_ref[2:3, :].astype(f32)
    atoms_ref[3:6, :] = offset_ref[...]
    atoms_ref[6:7, :] = charge_ref[...] * live
    atoms_ref[7:10, :] = dipole_ref[...] * live
    atoms_ref[10:11, :] = live
    atoms_ref[11:16, :] = jnp.zeros((5, ATOM_DEV), f32)


def spline_table(atoms_ref, table_ref, orders):
    def pencil_body(pencil, carry):
        tables = spline_rows(atoms_ref[pencil, 3:6, :])
        for o in range(orders):
            for t in range(6):
                table_ref[pencil, o * 6 + t, 0:3, :] = tables[o][t]
        return carry

    lax.fori_loop(0, PENCILS, pencil_body, 0)


def weight_rows(table_ref, pencil, lanes, dim, orders):
    row = slice(dim, dim + 1)
    return [[table_ref[pencil, o * 6 + t, row, lanes] for t in range(6)] for o in range(orders)]


def pair_place(pair):
    pencil = pair // PAIRS
    return pencil, pl.ds(pl.multiple_of(pair % PAIRS * LANES, LANES), LANES)


def pair_window(pair, own, where_ref):
    if own:
        return pl.multiple_of(pair * 32, 8), WINDOW, (pair * 32).astype(f32)
    place = pair * 32 + where_ref[2]
    place = jnp.where(place >= NX, place - NX, place)
    first = place // 8 * 8
    return pl.multiple_of(first, 8), WIDE, (pair * 32 - (place - first)).astype(f32)


def z_waves(cell_z, weights, base_ref, taps_ref):
    centre = cell_z + 2.5
    turn = base_ref[...] * centre
    turn = turn - 360.0 * jnp.floor(turn * (1.0 / 360.0))
    cos_k, sin_k = unit_phase(turn * (1.0 / 360.0))
    turn = 8.0 * centre
    turn = turn - 360.0 * jnp.floor(turn * (1.0 / 360.0))
    cos_8, sin_8 = unit_phase(jnp.broadcast_to(turn * (1.0 / 360.0), cos_k.shape))
    folded = [
        (
            [weight[2 - t] + weight[3 + t] for t in range(3)],
            [weight[3 + t] - weight[2 - t] for t in range(3)],
        )
        for weight in weights
    ]
    pieces = [[] for _ in weights]
    pieces_im = [[] for _ in weights]
    for q in range(PADDED_Z // 8):
        span = slice(q * 8, q * 8 + 8)
        cos_t = [taps_ref[t, span, :] for t in range(3)]
        sin_t = [taps_ref[3 + t, span, :] for t in range(3)]
        for s, (even, odd) in enumerate(folded):
            real = even[0] * cos_t[0] + even[1] * cos_t[1] + even[2] * cos_t[2]
            imag = odd[0] * sin_t[0] + odd[1] * sin_t[1] + odd[2] * sin_t[2]
            pieces[s].append(real * cos_k - imag * sin_k)
            pieces_im[s].append(-(real * sin_k + imag * cos_k))
        cos_k, sin_k = cos_k * cos_8 - sin_k * sin_8, sin_k * cos_8 + cos_k * sin_8
    return [
        (jnp.concatenate(re, axis=0), jnp.concatenate(im, axis=0))
        for re, im in zip(pieces, pieces_im)
    ]


def sampling_weights(
    start, own, where_ref, some_ref, table_ref, base_ref, taps_ref, waves_ref, x_ref, y_ref
):
    spline_table(some_ref, table_ref, 3)

    def pair_body(pair, carry):
        pencil, lanes = pair_place(pair)
        row = [some_ref[pencil, a : a + 1, lanes] for a in range(3)]
        _, window, origin = pair_window(pair, own, where_ref)
        dense_x = dense_rows(weight_rows(table_ref, pencil, lanes, 0, 3), row[0] - origin, window)
        dense_y = dense_rows(weight_rows(table_ref, pencil, lanes, 1, 3), row[1], 16)
        for p in range(3):
            x_ref[start + pair, p, :window] = dense_x[p]
            y_ref[start + pair, p] = dense_y[p]
        waves = z_waves(row[2], weight_rows(table_ref, pencil, lanes, 2, 3), base_ref, taps_ref)
        for s, (re, im) in enumerate(waves):
            re, im = halves(re), halves(im)
            columns = slice(s * LANES, (s + 1) * LANES)
            for n in range(2):
                waves_ref[start + pair, n, :PADDED_Z, columns] = re[n]
                waves_ref[start + pair, n, PADDED_Z:, columns] = im[n]
        return carry

    lax.fori_loop(0, PENCILS * PAIRS, pair_body, 0, unroll=2)


def spread_kernel(own, *refs):
    atoms_ref, where_ref, base_ref, taps_ref = refs[:4]
    if own:
        grid_ref, weights_ref = refs[4:]
        grid_ref[...] = jnp.zeros_like(grid_ref)
    else:
        _, tables_ref, cos_ref, sin_ref, slab_atoms_ref, grid_ref, out_ref = refs[4:11]
        results, green_out_ref, kept = refs[11:14], refs[14], refs[15:18]
        green_ref, table_ref, weights_ref, semaphores = refs[18:]
        table_copy = fetch(tables_ref, table_ref, semaphores.at[0])
    rows = list(range(CY)) if own else list(range(CY, 2 * CY - 1))
    part = CY * LANES
    gap = jnp.zeros((HALF - PADDED_Z, LANES), bf16)
    spline_table(atoms_ref, weights_ref, 2)

    def pair_body(pair, carry):
        pencil, lanes = pair_place(pair)
        row = [atoms_ref[pencil, a : a + 1, lanes] for a in range(10)]
        charge, dip_x, dip_y, dip_z = row[6:10]
        first_row, window, origin = pair_window(pair, own, where_ref)
        dense_x = dense_rows(
            weight_rows(weights_ref, pencil, lanes, 0, 2), row[0] - origin, window
        )
        dense_y = dense_rows(weight_rows(weights_ref, pencil, lanes, 1, 2), row[1], 16)
        value, first = weight_rows(weights_ref, pencil, lanes, 2, 2)
        mixed = [charge * value[t] + dip_z * first[t] for t in range(6)]
        right = []
        for re, im in z_waves(row[2], (mixed, value), base_ref, taps_ref):
            re, im = halves(re), halves(im)
            right.append(
                [
                    jnp.concatenate([re[n], gap, im[n], gap, im[n], gap, -re[n], gap], axis=0)
                    for n in range(2)
                ]
            )
        high, low = [jnp.concatenate([right[0][n], right[1][n]], axis=1) for n in range(2)]
        right = jnp.concatenate([high, low, high], axis=1)
        left = []
        for r in rows:
            value, first = dense_y[0][r : r + 1], dense_y[1][r : r + 1]
            left.append(
                jnp.concatenate(
                    [
                        value * dense_x[0],
                        (dip_x * value) * dense_x[1] + (dip_y * first) * dense_x[0],
                    ],
                    axis=1,
                )
            )
        high, low = halves(jnp.concatenate(left, axis=0))
        left = jnp.concatenate([high, high, low], axis=1)
        added = lax.dot_general(
            left, right, (((1,), (1,)), ((), ())), preferred_element_type=f32
        )
        at = pl.ds(first_row, window)
        for n in range(len(rows)):
            piece = added[n * window : (n + 1) * window]
            grid_ref[at, n * LANES : (n + 1) * LANES] += piece[:, :LANES]
            grid_ref[at, part + n * LANES : part + (n + 1) * LANES] += piece[:, LANES:]
        return carry

    lax.fori_loop(0, PENCILS * PAIRS, pair_body, 0, unroll=12)
    if own:
        return
    grid_ref[0:WIDE] += grid_ref[NX:EXTENDED]
    table_copy.wait()
    sign = lane_sign((NX, LANES))
    twist = Twist(cos_ref, sin_ref)
    totals = []
    for first in range(0, CY, 2):
        lanes = slice(first * LANES, (first + 2) * LANES)
        below = slice(part + lanes.start, part + lanes.stop)
        line = jnp.concatenate(
            forward_line(
                table_ref, quarters_of(grid_ref[:NX, lanes]), quarters_of(grid_ref[:NX, below])
            ),
            axis=0,
        )
        for n, y in enumerate((first, first + 1)):
            one = line[:, n * LANES : (n + 1) * LANES]
            cos_y, sin_y = twist.at(y)
            totals.append(one * cos_y + turned(one, sign) * sin_y)
    for group in range(GROUPS):
        blocks = []
        for block in range(4 * group, 4 * group + 4):
            j, y = block // CY, block % CY
            blocks.append(totals[y][j * SLABS : (j + 1) * SLABS])
        for c, carrier in enumerate(pack_blocks(blocks)):
            out_ref[rows_of(3 * group + c), :] = carrier

    @pl.when(where_ref[1] % 2 == 1)
    def _():
        make_green(where_ref, green_ref)
        green_copy = fetch(green_ref, green_out_ref, semaphores.at[3])
        for start, some_ref in ((0, slab_atoms_ref), (PENCILS * PAIRS, atoms_ref)):
            sampling_weights(
                start, start == 0, where_ref, some_ref, weights_ref, base_ref, taps_ref, *kept
            )
        copies = [fetch(kept[n], results[n], semaphores.at[n]) for n in range(3)]
        for copy in [green_copy, *copies]:
            copy.wait()


def spline_modulus(turns):
    cosine, _ = unit_phase(turns)
    return (64.0 + 52.0 * cosine + 4.0 * cosine * cosine) * (1.0 / 120.0)


def folded_mode(row):
    residue = (
        (row >= QUARTER).astype(jnp.int32)
        + (row >= 2 * QUARTER).astype(jnp.int32)
        + (row >= 3 * QUARTER).astype(jnp.int32)
    )
    mode = 4 * (row - QUARTER * residue) + residue
    return jnp.where(mode < NX // 2, mode, mode - NX)


def make_green(where_ref, out_ref):
    slab, pencil, shear = where_ref[0], where_ref[1], where_ref[3].astype(f32)
    decay = (math.pi / screening) ** 2
    column = lax.broadcasted_iota(jnp.int32, (1, LANES), 1)
    own_x = folded_mode(jnp.minimum(column, PART_X) * SLABS + slab)
    own_y = folded_mode(lax.broadcasted_iota(jnp.int32, (NY, LANES), 0))
    float_x = own_x.astype(f32)
    wave_y = own_y.astype(f32) + float_x * shear * (1.0 / NX)
    part_x, part_y = float_x * (1.0 / NX), wave_y * (1.0 / NY)
    norm = part_x * part_x + part_y * part_y
    moduli = spline_modulus(part_x) * spline_modulus(part_y)
    top = jnp.exp(-decay * norm) / (math.pi * moduli * moduli)
    top = jnp.where((own_x == -(NX // 2)) | (own_y == -(NY // 2)), 0.0, top)
    lane = jnp.where(column < HALF, column, column - HALF)
    mode = pencil * PART_Z + lane
    part_z = mode.astype(f32) * (1.0 / NZ)
    modulus = spline_modulus(part_z)
    norm_z = part_z * part_z
    twice = jnp.where(mode == 0, 1.0, 2.0) * (1.0 / (NX * NY * NZ))
    mode_top = jnp.where(
        lane < PART_Z, twice * jnp.exp(-decay * norm_z) / (modulus * modulus), 0.0
    )
    mode_norm = jnp.where(lane < PART_Z, norm_z, 1.0)
    for j in range(PART_X):
        square = norm[:, j : j + 1] + mode_norm
        green = top[:, j : j + 1] * mode_top / jnp.where(square == 0.0, 1.0, square)
        out_ref[:, j * LANES : (j + 1) * LANES] = jnp.where(square == 0.0, 0.0, green)


def green_kernel(where_ref, _, result_ref, green_ref, semaphore):
    @pl.when(where_ref[1] % 2 == 0)
    def _():
        make_green(where_ref, green_ref)
        fetch(green_ref, result_ref, semaphore).wait()


def filter_kernel(
    in_ref, tables_ref, backs_ref, greens_ref, out_ref, table_ref, back_ref, green_ref, semaphores
):
    copies = [
        fetch(tables_ref, table_ref, semaphores.at[0]),
        fetch(backs_ref, back_ref, semaphores.at[1]),
    ]
    for first in range(0, PART_X, 2):
        lanes = pl.ds(first * LANES, 2 * LANES)
        copies.append(
            fetch(greens_ref.at[:, lanes], green_ref.at[:, lanes], semaphores.at[2 + first // 2])
        )
    sign = lane_sign((NY, LANES))
    energy = jnp.zeros((8, LANES), f32)
    blocks = []
    for first in range(0, PART_X, 2):
        lines = []
        for j in (first, first + 1):
            found = [block_at(in_ref, j, y) for y in range(CY)]
            lines.append(
                jnp.concatenate(
                    [one[16 * part : 16 * part + 16] for part in range(4) for one in found], axis=0
                )
            )
        swapped = jnp.concatenate([turned(one, sign) for one in lines], axis=1)
        lines = jnp.concatenate(lines, axis=1)
        if first == 0:
            copies[0].wait()
        spectrum = jnp.concatenate(
            forward_line(table_ref, quarters_of(lines), quarters_of(swapped)), axis=0
        )
        modes = []
        copies[2 + first // 2].wait()
        for n in range(2):
            j = first + n
            one = spectrum[:, n * LANES : (n + 1) * LANES]
            scaled = green_ref[:, j * LANES : (j + 1) * LANES] * one
            share = scaled * one
            energy = energy + sum(share[8 * i : 8 * i + 8] for i in range(NY // 8))
            modes.append(scaled)
        swapped = jnp.concatenate([turned(one, sign) for one in modes], axis=1)
        modes = jnp.concatenate(modes, axis=1)
        if first == 0:
            copies[1].wait()
        parts = inverse_line(back_ref, quarters_of(modes), quarters_of(swapped))
        for n in range(2):
            for y in range(CY):
                blocks.append(
                    jnp.concatenate(
                        [
                            one[16 * y : 16 * y + 16, n * LANES : (n + 1) * LANES]
                            for one in parts
                        ],
                        axis=0,
                    )
                )
        for group in range(first * CY // 4, (first + 2) * CY // 4):
            for c, carrier in enumerate(pack_blocks(blocks[4 * group : 4 * group + 4])):
                out_ref[rows_of(3 * group + c), :] = carrier
    lane = lax.broadcasted_iota(jnp.int32, (SLABS, LANES), 1)
    share = 0.5 * jnp.sum(energy)
    out_ref[rows_of(0), :] = jnp.where(lane == PART_Z, share, out_ref[rows_of(0), :])


def sample_kernel(own, *refs):
    if own:
        atoms_ref, where_ref, waves_ref, x_ref, y_ref, grid_ref, out_ref = refs
    else:
        atoms_ref, where_ref, base_ref, taps_ref = refs[:4]
        kept = refs[4:7]
        in_ref, cos_ref, sin_ref, tables_ref, slab_atoms_ref, out_ref, grid_ref = refs[7:14]
        slab_weights, below_weights = refs[14:17], refs[17:20]
        waves_ref, x_ref, y_ref = below_weights
        table_ref, weights_ref, semaphores = refs[20:]
        table_copy = fetch(tables_ref, table_ref, semaphores.at[6])
        later = where_ref[1] % 2 == 0
        pairs = PENCILS * PAIRS
        copies = [
            pltpu.make_async_copy(source.at[pl.ds(start, pairs)], target, semaphores.at[n])
            for n, (source, start, target) in enumerate(
                [(kept[n], pairs, below_weights[n]) for n in range(3)]
                + [(kept[n], 0, slab_weights[n]) for n in range(3)]
            )
        ]

        @pl.when(later)
        def _():
            for slab, some_ref, targets in (
                (False, atoms_ref, below_weights),
                (True, slab_atoms_ref, slab_weights),
            ):
                sampling_weights(
                    0, slab, where_ref, some_ref, weights_ref, base_ref, taps_ref, *targets
                )

        @pl.when(jnp.logical_not(later))
        def _():
            for copy in copies:
                copy.start()

    rows = list(range(CY)) if own else list(range(CY, 2 * CY - 1))
    energy = 0.0
    if not own:
        sign = lane_sign((NX, LANES))
        twist = Twist(cos_ref, sin_ref)
        for first in range(0, CY, 2):
            modes, swapped = [], []
            for y in range(first, first + 2):
                line = jnp.concatenate([block_at(in_ref, j, y) for j in range(PART_X)], axis=0)
                other = turned(line, sign)
                cos_y, sin_y = twist.at(y)
                modes.append(line * cos_y - other * sin_y)
                swapped.append(other * cos_y + line * sin_y)
            swapped = jnp.concatenate(swapped, axis=1)
            modes = jnp.concatenate(modes, axis=1)
            if first == 0:
                table_copy.wait()
            cells = jnp.concatenate(
                inverse_line(table_ref, quarters_of(modes), quarters_of(swapped)), axis=0
            )
            lanes = slice(first * LANES, (first + 2) * LANES)
            grid_ref[:NX, lanes] = cells
            grid_ref[NX:, lanes] = cells[:WIDE]
        lane = lax.broadcasted_iota(jnp.int32, (SLABS, LANES), 1)
        energy = jnp.sum(jnp.where(lane == PART_Z, in_ref[rows_of(0), :], 0.0))
    gap = jnp.zeros((HALF - PADDED_Z, 3 * LANES), bf16)

    if not own:

        @pl.when(jnp.logical_not(later))
        def _():
            for copy in copies[:3]:
                copy.wait()

    def pair_body(pair, carry):
        pencil, lanes = pair_place(pair)
        waves = [
            jnp.concatenate(
                [waves_ref[pair, n, :PADDED_Z], gap, waves_ref[pair, n, PADDED_Z:], gap],
                axis=0,
            )
            for n in range(2)
        ]
        first_row, window, _ = pair_window(pair, own, where_ref)
        at = pl.ds(first_row, window)
        cells = jnp.concatenate(
            [grid_ref[at, n * LANES : (n + 1) * LANES] for n in range(len(rows))], axis=0
        )
        read = product(halves(cells), waves)
        dense_x = [x_ref[pair, p, :window] for p in range(3)]
        dense_y = [y_ref[pair, p] for p in range(3)]
        lined = {}
        for order_y, order_z in ((0, 0), (1, 0), (2, 0), (0, 1), (1, 1), (0, 2)):
            lined[order_y, order_z] = sum(
                dense_y[order_y][r : r + 1]
                * read[n * window : (n + 1) * window, order_z * LANES : (order_z + 1) * LANES]
                for n, r in enumerate(rows)
            )

        def sampled(p, r, s):
            return jnp.sum(dense_x[p] * lined[r, s], axis=0, keepdims=True)

        charge, dip_x, dip_y, dip_z, live = [
            atoms_ref[pencil, a : a + 1, lanes] for a in range(6, 11)
        ]
        s100 = sampled(1, 0, 0)
        s010 = sampled(0, 1, 0)
        s001 = sampled(0, 0, 1)
        s110 = sampled(1, 1, 0)
        s101 = sampled(1, 0, 1)
        s011 = sampled(0, 1, 1)
        out = [
            live * sampled(0, 0, 0),
            live * s100,
            live * s010,
            live * s001,
            charge * s100 + dip_x * sampled(2, 0, 0) + dip_y * s110 + dip_z * s101,
            charge * s010 + dip_x * s110 + dip_y * sampled(0, 2, 0) + dip_z * s011,
            charge * s001 + dip_x * s101 + dip_y * s011 + dip_z * sampled(0, 0, 2),
            jnp.full(live.shape, energy, f32),
        ]
        ahead = lax.rem(pencil - where_ref[1] + PENCILS, PENCILS)
        out_ref[ahead, :, lanes] = jnp.concatenate(out, axis=0)
        return carry

    lax.fori_loop(0, PENCILS * PAIRS, pair_body, 0, unroll=12)
    if not own:

        @pl.when(jnp.logical_not(later))
        def _():
            for copy in copies[3:]:
                copy.wait()


def finish_kernel(
    own_ref, one_ref, two_ref, three_ref, charge_ref, dipole_ref, position_ref, energy_ref
):
    total = (own_ref[...] + one_ref[...]) + (two_ref[...] + three_ref[...])
    charge_ref[...] = total[0]
    dipole_ref[...] = total[1:4]
    position_ref[...] = total[4:7]
    energy_ref[...] = total[7:8, 0:1]


SPACES = {"v": pltpu.VMEM, "h": pltpu.HBM, "s": pltpu.SMEM}
WORK = {"flops": 1_000_000_000, "bytes_accessed": 8_000_000}


def out_place(shape):
    pinned = isinstance(shape, type(pltpu.HBM((8, LANES), f32)))
    return pl.BlockSpec(memory_space=pltpu.HBM if pinned else pltpu.VMEM)


def call(kernel, inputs, out_shape, scratch=(), aliases=()):
    def run(*operands):
        placed = [
            pltpu.with_memory_space_constraint(one, pltpu.HBM) if where == "h" else one
            for one, where in zip(operands, inputs)
        ]
        return pl.pallas_call(
            kernel,
            out_shape=out_shape,
            in_specs=[pl.BlockSpec(memory_space=SPACES[one]) for one in inputs],
            out_specs=jax.tree.map(out_place, out_shape),
            scratch_shapes=list(scratch),
            input_output_aliases=dict(aliases),
            compiler_params=pltpu.CompilerParams(vmem_limit_bytes=28 * 1024 * 1024),
            cost_estimate=pl.CostEstimate(transcendentals=0, **WORK),
        )(*placed)

    return run


def next_slab(value, back=False):
    step = -1 if back else 1
    return lax.ppermute(value, "gy", [(i, (i + step) % SLABS) for i in range(SLABS)])


def swap_slabs(lines):
    lines = lines.reshape(SLABS, CARRIERS, 1, LANES)
    lines = lax.all_to_all(lines, "gy", split_axis=0, concat_axis=0, tiled=True)
    return lines.reshape(SLABS * CARRIERS, LANES)


def on_device(cell_index, offsets, charges, dipoles, block_count, shear_cells):
    pencil_index = lax.axis_index("gx")
    slab_index = lax.axis_index("gy")
    x_forward, x_inverse, y_forward, y_inverse = wave_tables()
    shape = jax.ShapeDtypeStruct
    shift = jnp.where(slab_index == 0, shear_cells[0], 0)
    where = jnp.stack([slab_index, pencil_index, shift, shear_cells[0]])

    mine, base, taps, cos_t, sin_t = call(
        prepare_kernel,
        "sshhhhh",
        (
            shape((16, ATOM_DEV), f32),
            shape((8, LANES), f32),
            shape((6, PADDED_Z, LANES), f32),
            shape((NX, LANES), f32),
            shape((NX, LANES), f32),
        ),
        [
            pltpu.SMEM(block_count.shape, jnp.int32),
            pltpu.VMEM((3, ATOM_DEV), jnp.int32),
            pltpu.VMEM((3, ATOM_DEV), f32),
            pltpu.VMEM((1, ATOM_DEV), f32),
            pltpu.VMEM((3, ATOM_DEV), f32),
            pltpu.SemaphoreType.DMA((5,)),
        ],
    )(
        where,
        shear_cells,
        block_count,
        cell_index,
        offsets,
        charges,
        dipoles,
    )
    atoms = lax.all_gather(mine, "gx", axis=0, tiled=False)
    below_atoms = next_slab(atoms)

    packed = shape((SLABS * CARRIERS, LANES), f32)
    table_space = pltpu.VMEM((NX, 6 * QUARTER), bf16)
    pairs = 2 * PENCILS * PAIRS
    held = [
        ((2, 2 * PADDED_Z, 3 * LANES), bf16),
        ((3, WIDE, LANES), f32),
        ((3, 16, LANES), f32),
    ]
    weights_space = pltpu.VMEM((PENCILS, 18, 8, ATOM_DEV), f32)
    four = pltpu.SemaphoreType.DMA((4,))
    grid_shape = shape((EXTENDED, 2 * CY * LANES), f32)
    slab_grid = call(
        lambda *refs: spread_kernel(True, *refs),
        "vsvv",
        grid_shape,
        [weights_space],
    )(atoms, where, base, taps)
    green_shape = pltpu.HBM((NY, PART_X * LANES), f32)
    green_space = pltpu.VMEM((NY, PART_X * LANES), f32)
    _, lines, *weights, green = call(
        lambda *refs: spread_kernel(False, *refs),
        "vsvvvhvvv",
        (
            grid_shape,
            packed,
            *(pltpu.HBM((pairs, *dims), kind) for dims, kind in held),
            green_shape,
        ),
        [
            *(pltpu.VMEM((pairs, *dims), kind) for dims, kind in held),
            green_space,
            table_space,
            weights_space,
            four,
        ],
        ((4, 0),),
    )(below_atoms, where, base, taps, slab_grid, x_forward, cos_t, sin_t, atoms)
    lines, where = lax.optimization_barrier((lines, where))
    green = call(
        green_kernel, "sh", green_shape, [green_space, pltpu.SemaphoreType.DMA], ((1, 0),)
    )(where, green)
    lines = swap_slabs(lines)
    filtered = call(
        filter_kernel,
        "vhhh",
        packed,
        [table_space, table_space, green_space, pltpu.SemaphoreType.DMA((5,))],
    )(
        lines, y_forward, y_inverse, green
    )
    filtered = swap_slabs(filtered)
    shares_shape = shape((PENCILS, 8, ATOM_DEV), f32)
    below_shares, potential, *weights = call(
        lambda *refs: sample_kernel(False, *refs),
        "vsvvhhhvvvhv",
        (
            shares_shape,
            shape((EXTENDED, CY * LANES), f32),
            *(shape((pairs // 2, *dims), kind) for dims, kind in held),
        ),
        [
            *(pltpu.VMEM((pairs // 2, *dims), kind) for dims, kind in held),
            table_space,
            weights_space,
            pltpu.SemaphoreType.DMA((7,)),
        ],
    )(below_atoms, where, base, taps, *weights, filtered, cos_t, sin_t, x_inverse, atoms)
    below_shares = next_slab(below_shares, back=True)
    shares = call(lambda *refs: sample_kernel(True, *refs), "vsvvvv", shares_shape)(
        atoms, where, *weights, potential
    )
    shares = shares + below_shares
    arrived = [
        lax.ppermute(shares[ahead], "gx", [(i, (i + ahead) % PENCILS) for i in range(PENCILS)])
        for ahead in range(1, PENCILS)
    ]
    charge_grad, dipole_grad, position_grad, energy = call(
        finish_kernel,
        "vvvv",
        (
            shape((ATOM_DEV,), f32),
            shape((3, ATOM_DEV), f32),
            shape((3, ATOM_DEV), f32),
            shape((1, 1), f32),
        ),
    )(shares[0], *arrived)
    return charge_grad, dipole_grad, position_grad, energy[0]


def solution(mesh):
    placed = (
        P(None, ("gy", "gx")),
        P(None, ("gy", "gx")),
        P(("gy", "gx")),
        P(None, ("gy", "gx")),
        P(("gy", "gx")),
        P(),
    )
    return jax.shard_map(
        on_device,
        mesh=mesh,
        in_specs=placed,
        out_specs=(P(("gy", "gx")), P(None, ("gy", "gx")), P(None, ("gy", "gx")), P()),
        check_vma=False,
    )
```

```python
import math

import jax
import jax.numpy as jnp
import ml_dtypes
import numpy as np
from jax import lax
from jax.experimental import pallas as pl
from jax.experimental.pallas import tpu as pltpu
from jax.sharding import PartitionSpec as P

NX = 384
NY = 384
NZ = 360
CY = 6
CX = 96
PENCILS = 4
SLABS = 64
PART_X = 6
PART_Z = 45
ATOM_BLK = 64
ATOM_DEV = 384
PAIRS = 3
WINDOW = 40
WIDE = 48
EXTENDED = NX + WIDE
HALF = 64
LANES = 128
PADDED_Z = 48
QUARTER = 96
screening = 0.9
f32 = jnp.float32
bf16 = jnp.bfloat16


def split_table(table):
    high = table.astype(ml_dtypes.bfloat16)
    low = (table - high.astype(np.float64)).astype(ml_dtypes.bfloat16)
    return np.concatenate([high, high, low], axis=1)


def wave_tables():
    quarter = np.arange(QUARTER)
    mode = np.arange(4)[:, None] + 4 * quarter[None, :]
    row_y = CY * (quarter % 16) + quarter // 16
    tables = []
    for place in (quarter, row_y):
        ticks = mode[:, :, None] * place % NX
        for table in (ticks, ticks.transpose(0, 2, 1)):
            angle = 2.0 * np.pi / NX * table.reshape(NX, QUARTER)
            tables.append(split_table(np.concatenate([np.cos(angle), np.sin(angle)], axis=1)))
    return tables


def spline_rows(fraction):
    levels = {2: [1.0 - fraction, fraction]}
    current = levels[2]
    for n in range(3, 7):
        inverse_n = 1.0 / (n - 1)
        updated = [None] * n
        updated[n - 1] = inverse_n * fraction * current[n - 2]
        for j in range(1, n - 1):
            updated[n - 1 - j] = inverse_n * (
                (fraction + j) * current[n - 2 - j] + (n - j - fraction) * current[n - 1 - j]
            )
        updated[0] = inverse_n * (1.0 - fraction) * current[0]
        current = updated
        levels[n] = current
    zero_row = jnp.zeros_like(fraction)

    def entry_at(values_list, k):
        return values_list[k] if 0 <= k < len(values_list) else zero_row

    first = [entry_at(levels[5], t - 1) - entry_at(levels[5], t) for t in range(6)]
    second = [
        entry_at(levels[4], t - 2) - 2.0 * entry_at(levels[4], t - 1) + entry_at(levels[4], t)
        for t in range(6)
    ]
    return levels[6], first, second


def dense_rows(tables, cell, length):
    away = lax.broadcasted_iota(jnp.int32, (length, cell.shape[1]), 0).astype(f32) - cell
    summed = [jnp.zeros(away.shape, f32) for _ in tables]
    for t in range(6):
        here = away == float(t)
        summed = [jnp.where(here, table[t], so_far) for table, so_far in zip(tables, summed)]
    return summed


def unit_phase(turns):
    turns = turns - jnp.floor(turns + 0.5)
    quarter = jnp.floor(4.0 * turns + 0.5)
    rest = turns - 0.25 * quarter
    theta = (2.0 * math.pi) * rest
    square = theta * theta
    sine = theta * (
        1.0
        + square
        * (-1.0 / 6 + square * (1.0 / 120 + square * (-1.0 / 5040 + square * (1.0 / 362880))))
    )
    cosine = 1.0 + square * (
        -0.5
        + square
        * (1.0 / 24 + square * (-1.0 / 720 + square * (1.0 / 40320 - square * (1.0 / 3628800))))
    )
    odd = jnp.abs(quarter) == 1.0
    cos_out = jnp.where(odd, sine, cosine)
    sin_out = jnp.where(odd, cosine, sine)
    cos_out = jnp.where((quarter == 1.0) | (jnp.abs(quarter) == 2.0), -cos_out, cos_out)
    sin_out = jnp.where((quarter == -1.0) | (jnp.abs(quarter) == 2.0), -sin_out, sin_out)
    return cos_out, sin_out


class Twist:
    def __init__(self, cos_ref, sin_ref):
        whole = (NX, LANES)
        self.cos = jnp.broadcast_to(cos_ref[:, 0:1], whole)
        self.sin = jnp.broadcast_to(sin_ref[:, 0:1], whole)
        self.cos_step = jnp.broadcast_to(cos_ref[:, CY : CY + 1], whole)
        self.sin_step = jnp.broadcast_to(sin_ref[:, CY : CY + 1], whole)
        self.row = 0

    def at(self, row):
        while self.row < row:
            self.cos, self.sin = (
                self.cos * self.cos_step - self.sin * self.sin_step,
                self.sin * self.cos_step + self.cos * self.sin_step,
            )
            self.row += 1
        return self.cos, self.sin


def halves(value):
    high = value.astype(bf16)
    return high, (value - high.astype(f32)).astype(bf16)


def joined(left, right):
    return (
        jnp.concatenate([left[0], left[0], left[1]], axis=1),
        jnp.concatenate([right[0], right[1], right[0]], axis=0),
    )


def product(left, right):
    left, right = joined(left, right)
    return jnp.dot(left, right, preferred_element_type=f32)


def product3(left, right):
    def one(a, b):
        return jnp.dot(a, b, preferred_element_type=f32)

    return one(left[0], right[0]) + (one(left[0], right[1]) + one(left[1], right[0]))


def lane_sign(shape):
    return jnp.where(lax.broadcasted_iota(jnp.int32, shape, 1) < HALF, 1.0, -1.0).astype(f32)


def turned(value, sign):
    return pltpu.roll(value, HALF, 1) * sign


def fetch(source, target, semaphore):
    copy = pltpu.make_async_copy(source, target, semaphore)
    copy.start()
    return copy


def line_product(table_ref, r, value):
    rows = slice(r * QUARTER, (r + 1) * QUARTER)
    table = table_ref[rows, : 2 * QUARTER], table_ref[rows, 4 * QUARTER :]
    return product3(table, halves(value))


def forward_line(table_ref, quarters, turned_quarters):
    g, h = quarters, turned_quarters
    a, b, c, d = g[0] + g[2], g[0] - g[2], g[1] + g[3], g[1] - g[3]
    ta, tb, tc, td = h[0] + h[2], h[0] - h[2], h[1] + h[3], h[1] - h[3]
    lines = []
    for r, (one, other) in enumerate(
        ((a + c, ta + tc), (b + td, tb - d), (a - c, ta - tc), (b - td, tb + d))
    ):
        stacked = jnp.concatenate([one, other], axis=0)
        lines.append(line_product(table_ref, r, stacked))
    return lines


def inverse_line(table_ref, modes, turned_modes):
    z = []
    for r in range(4):
        stacked = jnp.concatenate([modes[r], -turned_modes[r]], axis=0)
        z.append(line_product(table_ref, r, stacked))
    a, b, c, d = z[0] + z[2], z[0] - z[2], z[1] + z[3], z[1] - z[3]
    width = d.shape[1]
    sign = lane_sign((QUARTER, LANES))
    td = jnp.concatenate(
        [turned(d[:, n : n + LANES], sign) for n in range(0, width, LANES)], axis=1
    )
    return [a + c, b - td, a - c, b + td]


def quarters_of(value):
    return [value[r * QUARTER : (r + 1) * QUARTER] for r in range(4)]


PIECES = (0, 16, 32, 64, 80, 96)
GROUPS = PART_X * CY // 4
CARRIERS = 3 * GROUPS


def lane_range(first):
    lane = lax.broadcasted_iota(jnp.int32, (SLABS, LANES), 1)
    return (lane >= first) & (lane < first + 16)


def pack_blocks(blocks):
    carriers = []
    for c in range(3):
        value = blocks[c]
        for half in range(2):
            gap = PADDED_Z + half * HALF
            shift = (gap - PIECES[2 * c + half]) % LANES
            value = jnp.where(lane_range(gap), pltpu.roll(blocks[3], shift, 1), value)
        carriers.append(value)
    return carriers


def unpack_block(carriers):
    value = jnp.zeros((SLABS, LANES), f32)
    for p, source in enumerate(PIECES):
        gap = PADDED_Z + p % 2 * HALF
        shift = (source - gap) % LANES
        value = jnp.where(lane_range(source), pltpu.roll(carriers[p // 2], shift, 1), value)
    return value


def rows_of(carrier):
    return pl.ds(carrier, SLABS, stride=CARRIERS)


def block_at(ref, j, y):
    block = j * CY + y
    group, place = block // 4, block % 4
    if place < 3:
        return ref[rows_of(3 * group + place), :]
    return unpack_block([ref[rows_of(3 * group + c), :] for c in range(3)])


def prepare_kernel(
    where_ref, shear_ref, counts_ref, cells_ref, offsets_ref, charges_ref, dipoles_ref,
    atoms_ref, base_ref, taps_ref, cos_ref, sin_ref,
    count_ref, cell_ref, offset_ref, charge_ref, dipole_ref, semaphores
):
    copies = [
        fetch(source, target, semaphores.at[n])
        for n, (source, target) in enumerate(
            (
                (counts_ref, count_ref),
                (cells_ref, cell_ref),
                (offsets_ref, offset_ref),
                (charges_ref, charge_ref.at[0]),
                (dipoles_ref, dipole_ref),
            )
        )
    ]
    slab, pencil = where_ref[0], where_ref[1]
    first = pencil * PART_Z
    row = lax.broadcasted_iota(jnp.int32, (PADDED_Z, LANES), 0)
    mode = (row + first).astype(f32)
    base_ref[...] = mode[:8]
    for t in range(3):
        cos_t, sin_t = unit_phase(mode * (t + 0.5) * (1.0 / NZ))
        taps_ref[t] = jnp.where(row < PART_Z, cos_t, 0.0)
        taps_ref[3 + t] = jnp.where(row < PART_Z, sin_t, 0.0)
    column = lax.broadcasted_iota(jnp.int32, (1, LANES), 1)
    rows = jnp.where(column < CY, slab * CY + column, 1)
    index = lax.broadcasted_iota(jnp.int32, (NX, LANES), 0)
    folds = folded_mode(index)
    ticks = folds * (shear_ref[0] * rows)
    whole = jnp.floor(ticks.astype(f32) * (1.0 / (NX * NY))).astype(jnp.int32)
    rest = ticks - whole * (NX * NY)
    cos_t, sin_t = unit_phase(rest.astype(f32) * (1.0 / (NX * NY)))
    cos_ref[...] = cos_t
    sin_ref[...] = sin_t
    for copy in copies:
        copy.wait()
    slot = lax.broadcasted_iota(jnp.int32, (1, ATOM_DEV), 1)
    live = jnp.zeros((1, ATOM_DEV), f32)
    for b in range(ATOM_DEV // ATOM_BLK):
        inside = (slot >= b * ATOM_BLK) & (slot < b * ATOM_BLK + count_ref[b])
        live = jnp.where(inside, 1.0, live)
    atoms_ref[0:1, :] = cell_ref[0:1, :].astype(f32)
    atoms_ref[1:2, :] = (cell_ref[1:2, :] - slab * CY).astype(f32)
    atoms_ref[2:3, :] = cell_ref[2:3, :].astype(f32)
    atoms_ref[3:6, :] = offset_ref[...]
    atoms_ref[6:7, :] = charge_ref[...] * live
    atoms_ref[7:10, :] = dipole_ref[...] * live
    atoms_ref[10:11, :] = live
    atoms_ref[11:16, :] = jnp.zeros((5, ATOM_DEV), f32)


def spline_table(atoms_ref, table_ref, orders):
    def pencil_body(pencil, carry):
        tables = spline_rows(atoms_ref[pencil, 3:6, :])
        for o in range(orders):
            for t in range(6):
                table_ref[pencil, o * 6 + t, 0:3, :] = tables[o][t]
        return carry

    lax.fori_loop(0, PENCILS, pencil_body, 0)


def weight_rows(table_ref, pencil, lanes, dim, orders):
    row = slice(dim, dim + 1)
    return [[table_ref[pencil, o * 6 + t, row, lanes] for t in range(6)] for o in range(orders)]


def pair_place(pair):
    pencil = pair // PAIRS
    return pencil, pl.ds(pl.multiple_of(pair % PAIRS * LANES, LANES), LANES)


def pair_window(pair, own, where_ref):
    if own:
        return pl.multiple_of(pair * 32, 8), WINDOW, (pair * 32).astype(f32)
    place = pair * 32 + where_ref[2]
    place = jnp.where(place >= NX, place - NX, place)
    first = place // 8 * 8
    return pl.multiple_of(first, 8), WIDE, (pair * 32 - (place - first)).astype(f32)


def z_waves(cell_z, weights, base_ref, taps_ref):
    centre = cell_z + 2.5
    turn = base_ref[...] * centre
    turn = turn - 360.0 * jnp.floor(turn * (1.0 / 360.0))
    cos_k, sin_k = unit_phase(turn * (1.0 / 360.0))
    turn = 8.0 * centre
    turn = turn - 360.0 * jnp.floor(turn * (1.0 / 360.0))
    cos_8, sin_8 = unit_phase(jnp.broadcast_to(turn * (1.0 / 360.0), cos_k.shape))
    folded = [
        (
            [weight[2 - t] + weight[3 + t] for t in range(3)],
            [weight[3 + t] - weight[2 - t] for t in range(3)],
        )
        for weight in weights
    ]
    pieces = [[] for _ in weights]
    pieces_im = [[] for _ in weights]
    for q in range(PADDED_Z // 8):
        span = slice(q * 8, q * 8 + 8)
        cos_t = [taps_ref[t, span, :] for t in range(3)]
        sin_t = [taps_ref[3 + t, span, :] for t in range(3)]
        for s, (even, odd) in enumerate(folded):
            real = even[0] * cos_t[0] + even[1] * cos_t[1] + even[2] * cos_t[2]
            imag = odd[0] * sin_t[0] + odd[1] * sin_t[1] + odd[2] * sin_t[2]
            pieces[s].append(real * cos_k - imag * sin_k)
            pieces_im[s].append(-(real * sin_k + imag * cos_k))
        cos_k, sin_k = cos_k * cos_8 - sin_k * sin_8, sin_k * cos_8 + cos_k * sin_8
    return [
        (jnp.concatenate(re, axis=0), jnp.concatenate(im, axis=0))
        for re, im in zip(pieces, pieces_im)
    ]


def sampling_weights(
    start, own, where_ref, some_ref, table_ref, base_ref, taps_ref, waves_ref, x_ref, y_ref
):
    spline_table(some_ref, table_ref, 3)

    def pair_body(pair, carry):
        pencil, lanes = pair_place(pair)
        row = [some_ref[pencil, a : a + 1, lanes] for a in range(3)]
        _, window, origin = pair_window(pair, own, where_ref)
        dense_x = dense_rows(weight_rows(table_ref, pencil, lanes, 0, 3), row[0] - origin, window)
        dense_y = dense_rows(weight_rows(table_ref, pencil, lanes, 1, 3), row[1], 16)
        for p in range(3):
            x_ref[start + pair, p, :window] = dense_x[p]
            y_ref[start + pair, p] = dense_y[p]
        waves = z_waves(row[2], weight_rows(table_ref, pencil, lanes, 2, 3), base_ref, taps_ref)
        for s, (re, im) in enumerate(waves):
            re, im = halves(re), halves(im)
            columns = slice(s * LANES, (s + 1) * LANES)
            for n in range(2):
                waves_ref[start + pair, n, :PADDED_Z, columns] = re[n]
                waves_ref[start + pair, n, PADDED_Z:, columns] = im[n]
        return carry

    lax.fori_loop(0, PENCILS * PAIRS, pair_body, 0, unroll=2)


def spread_kernel(own, *refs):
    atoms_ref, where_ref, base_ref, taps_ref = refs[:4]
    if own:
        grid_ref, weights_ref = refs[4:]
        grid_ref[...] = jnp.zeros_like(grid_ref)
    else:
        _, tables_ref, cos_ref, sin_ref, grid_ref, out_ref = refs[4:10]
        table_ref, weights_ref, semaphore = refs[10:]
        table_copy = fetch(tables_ref, table_ref, semaphore)
    rows = list(range(CY)) if own else list(range(CY, 2 * CY - 1))
    part = CY * LANES
    gap = jnp.zeros((HALF - PADDED_Z, LANES), bf16)
    spline_table(atoms_ref, weights_ref, 2)

    def pair_body(pair, carry):
        pencil, lanes = pair_place(pair)
        row = [atoms_ref[pencil, a : a + 1, lanes] for a in range(10)]
        charge, dip_x, dip_y, dip_z = row[6:10]
        first_row, window, origin = pair_window(pair, own, where_ref)
        dense_x = dense_rows(
            weight_rows(weights_ref, pencil, lanes, 0, 2), row[0] - origin, window
        )
        dense_y = dense_rows(weight_rows(weights_ref, pencil, lanes, 1, 2), row[1], 16)
        value, first = weight_rows(weights_ref, pencil, lanes, 2, 2)
        mixed = [charge * value[t] + dip_z * first[t] for t in range(6)]
        right = []
        for re, im in z_waves(row[2], (mixed, value), base_ref, taps_ref):
            re, im = halves(re), halves(im)
            right.append(
                [
                    jnp.concatenate([re[n], gap, im[n], gap, im[n], gap, -re[n], gap], axis=0)
                    for n in range(2)
                ]
            )
        high, low = [jnp.concatenate([right[0][n], right[1][n]], axis=1) for n in range(2)]
        right = jnp.concatenate([high, low, high], axis=1)
        left = []
        for r in rows:
            value, first = dense_y[0][r : r + 1], dense_y[1][r : r + 1]
            left.append(
                jnp.concatenate(
                    [
                        value * dense_x[0],
                        (dip_x * value) * dense_x[1] + (dip_y * first) * dense_x[0],
                    ],
                    axis=1,
                )
            )
        high, low = halves(jnp.concatenate(left, axis=0))
        left = jnp.concatenate([high, high, low], axis=1)
        added = lax.dot_general(
            left, right, (((1,), (1,)), ((), ())), preferred_element_type=f32
        )
        at = pl.ds(first_row, window)
        for n in range(len(rows)):
            piece = added[n * window : (n + 1) * window]
            grid_ref[at, n * LANES : (n + 1) * LANES] += piece[:, :LANES]
            grid_ref[at, part + n * LANES : part + (n + 1) * LANES] += piece[:, LANES:]
        return carry

    lax.fori_loop(0, PENCILS * PAIRS, pair_body, 0, unroll=12)
    if own:
        return
    grid_ref[0:WIDE] += grid_ref[NX:EXTENDED]
    table_copy.wait()
    sign = lane_sign((NX, LANES))
    twist = Twist(cos_ref, sin_ref)
    totals = []
    for first in range(0, CY, 2):
        lanes = slice(first * LANES, (first + 2) * LANES)
        below = slice(part + lanes.start, part + lanes.stop)
        line = jnp.concatenate(
            forward_line(
                table_ref, quarters_of(grid_ref[:NX, lanes]), quarters_of(grid_ref[:NX, below])
            ),
            axis=0,
        )
        for n, y in enumerate((first, first + 1)):
            one = line[:, n * LANES : (n + 1) * LANES]
            cos_y, sin_y = twist.at(y)
            totals.append(one * cos_y + turned(one, sign) * sin_y)
    for group in range(GROUPS):
        blocks = []
        for block in range(4 * group, 4 * group + 4):
            j, y = block // CY, block % CY
            blocks.append(totals[y][j * SLABS : (j + 1) * SLABS])
        for c, carrier in enumerate(pack_blocks(blocks)):
            out_ref[rows_of(3 * group + c), :] = carrier


def spline_modulus(turns):
    cosine, _ = unit_phase(turns)
    return (64.0 + 52.0 * cosine + 4.0 * cosine * cosine) * (1.0 / 120.0)


def folded_mode(row):
    residue = (
        (row >= QUARTER).astype(jnp.int32)
        + (row >= 2 * QUARTER).astype(jnp.int32)
        + (row >= 3 * QUARTER).astype(jnp.int32)
    )
    mode = 4 * (row - QUARTER * residue) + residue
    return jnp.where(mode < NX // 2, mode, mode - NX)


def make_green(where_ref, out_ref):
    slab, pencil, shear = where_ref[0], where_ref[1], where_ref[3].astype(f32)
    decay = (math.pi / screening) ** 2
    column = lax.broadcasted_iota(jnp.int32, (1, LANES), 1)
    own_x = folded_mode(jnp.minimum(column, PART_X) * SLABS + slab)
    own_y = folded_mode(lax.broadcasted_iota(jnp.int32, (NY, LANES), 0))
    float_x = own_x.astype(f32)
    wave_y = own_y.astype(f32) + float_x * shear * (1.0 / NX)
    part_x, part_y = float_x * (1.0 / NX), wave_y * (1.0 / NY)
    norm = part_x * part_x + part_y * part_y
    moduli = spline_modulus(part_x) * spline_modulus(part_y)
    top = jnp.exp(-decay * norm) / (math.pi * moduli * moduli)
    top = jnp.where((own_x == -(NX // 2)) | (own_y == -(NY // 2)), 0.0, top)
    lane = jnp.where(column < HALF, column, column - HALF)
    mode = pencil * PART_Z + lane
    part_z = mode.astype(f32) * (1.0 / NZ)
    modulus = spline_modulus(part_z)
    norm_z = part_z * part_z
    twice = jnp.where(mode == 0, 1.0, 2.0) * (1.0 / (NX * NY * NZ))
    mode_top = jnp.where(
        lane < PART_Z, twice * jnp.exp(-decay * norm_z) / (modulus * modulus), 0.0
    )
    mode_norm = jnp.where(lane < PART_Z, norm_z, 1.0)
    for j in range(PART_X):
        square = norm[:, j : j + 1] + mode_norm
        green = top[:, j : j + 1] * mode_top / jnp.where(square == 0.0, 1.0, square)
        out_ref[:, j * LANES : (j + 1) * LANES] = jnp.where(square == 0.0, 0.0, green)


def weights_kernel(where_ref, atoms_ref, below_ref, base_ref, taps_ref, *refs):
    results, green_out_ref, kept, green_ref, weights_ref, semaphores = (
        refs[:3], refs[3], refs[4:7], *refs[7:]
    )
    make_green(where_ref, green_ref)
    copies = [fetch(green_ref, green_out_ref, semaphores.at[6])]
    pairs = PENCILS * PAIRS
    for own, some_ref in ((True, atoms_ref), (False, below_ref)):
        start = 0 if own else pairs
        sampling_weights(start, own, where_ref, some_ref, weights_ref, base_ref, taps_ref, *kept)
        some = pl.ds(start, pairs)
        for n in range(3):
            semaphore = semaphores.at[n if own else 3 + n]
            copies.append(fetch(kept[n].at[some], results[n].at[some], semaphore))
    for copy in copies:
        copy.wait()


def filter_kernel(
    in_ref, tables_ref, backs_ref, greens_ref, out_ref, table_ref, back_ref, green_ref, semaphores
):
    copies = [
        fetch(tables_ref, table_ref, semaphores.at[0]),
        fetch(backs_ref, back_ref, semaphores.at[1]),
    ]
    for first in range(0, PART_X, 2):
        lanes = pl.ds(first * LANES, 2 * LANES)
        copies.append(
            fetch(greens_ref.at[:, lanes], green_ref.at[:, lanes], semaphores.at[2 + first // 2])
        )
    sign = lane_sign((NY, LANES))
    energy = jnp.zeros((8, LANES), f32)
    blocks = []
    for first in range(0, PART_X, 2):
        lines = []
        for j in (first, first + 1):
            found = [block_at(in_ref, j, y) for y in range(CY)]
            lines.append(
                jnp.concatenate(
                    [one[16 * part : 16 * part + 16] for part in range(4) for one in found], axis=0
                )
            )
        swapped = jnp.concatenate([turned(one, sign) for one in lines], axis=1)
        lines = jnp.concatenate(lines, axis=1)
        if first == 0:
            copies[0].wait()
        spectrum = jnp.concatenate(
            forward_line(table_ref, quarters_of(lines), quarters_of(swapped)), axis=0
        )
        modes = []
        copies[2 + first // 2].wait()
        for n in range(2):
            j = first + n
            one = spectrum[:, n * LANES : (n + 1) * LANES]
            scaled = green_ref[:, j * LANES : (j + 1) * LANES] * one
            share = scaled * one
            energy = energy + sum(share[8 * i : 8 * i + 8] for i in range(NY // 8))
            modes.append(scaled)
        swapped = jnp.concatenate([turned(one, sign) for one in modes], axis=1)
        modes = jnp.concatenate(modes, axis=1)
        if first == 0:
            copies[1].wait()
        parts = inverse_line(back_ref, quarters_of(modes), quarters_of(swapped))
        for n in range(2):
            for y in range(CY):
                blocks.append(
                    jnp.concatenate(
                        [
                            one[16 * y : 16 * y + 16, n * LANES : (n + 1) * LANES]
                            for one in parts
                        ],
                        axis=0,
                    )
                )
        for group in range(first * CY // 4, (first + 2) * CY // 4):
            for c, carrier in enumerate(pack_blocks(blocks[4 * group : 4 * group + 4])):
                out_ref[rows_of(3 * group + c), :] = carrier
    lane = lax.broadcasted_iota(jnp.int32, (SLABS, LANES), 1)
    share = 0.5 * jnp.sum(energy)
    out_ref[rows_of(0), :] = jnp.where(lane == PART_Z, share, out_ref[rows_of(0), :])


def sample_kernel(own, *refs):
    if own:
        atoms_ref, where_ref, waves_ref, x_ref, y_ref, grid_ref, out_ref = refs
    else:
        atoms_ref, where_ref = refs[:2]
        kept = refs[2:5]
        in_ref, cos_ref, sin_ref, tables_ref, out_ref, grid_ref = refs[5:11]
        slab_weights, below_weights = refs[11:14], refs[14:17]
        waves_ref, x_ref, y_ref = below_weights
        table_ref, semaphores = refs[17:]
        table_copy = fetch(tables_ref, table_ref, semaphores.at[6])
        pairs = PENCILS * PAIRS
        copies = [
            fetch(source.at[pl.ds(start, pairs)], target, semaphores.at[n])
            for n, (source, start, target) in enumerate(
                [(kept[n], pairs, below_weights[n]) for n in range(3)]
                + [(kept[n], 0, slab_weights[n]) for n in range(3)]
            )
        ]
    rows = list(range(CY)) if own else list(range(CY, 2 * CY - 1))
    energy = 0.0
    if not own:
        sign = lane_sign((NX, LANES))
        twist = Twist(cos_ref, sin_ref)
        for first in range(0, CY, 2):
            modes, swapped = [], []
            for y in range(first, first + 2):
                line = jnp.concatenate([block_at(in_ref, j, y) for j in range(PART_X)], axis=0)
                other = turned(line, sign)
                cos_y, sin_y = twist.at(y)
                modes.append(line * cos_y - other * sin_y)
                swapped.append(other * cos_y + line * sin_y)
            swapped = jnp.concatenate(swapped, axis=1)
            modes = jnp.concatenate(modes, axis=1)
            if first == 0:
                table_copy.wait()
            cells = jnp.concatenate(
                inverse_line(table_ref, quarters_of(modes), quarters_of(swapped)), axis=0
            )
            lanes = slice(first * LANES, (first + 2) * LANES)
            grid_ref[:NX, lanes] = cells
            grid_ref[NX:, lanes] = cells[:WIDE]
        lane = lax.broadcasted_iota(jnp.int32, (SLABS, LANES), 1)
        energy = jnp.sum(jnp.where(lane == PART_Z, in_ref[rows_of(0), :], 0.0))
    gap = jnp.zeros((HALF - PADDED_Z, 3 * LANES), bf16)

    if not own:
        for copy in copies[:3]:
            copy.wait()

    def pair_body(pair, carry):
        pencil, lanes = pair_place(pair)
        waves = [
            jnp.concatenate(
                [waves_ref[pair, n, :PADDED_Z], gap, waves_ref[pair, n, PADDED_Z:], gap],
                axis=0,
            )
            for n in range(2)
        ]
        first_row, window, _ = pair_window(pair, own, where_ref)
        at = pl.ds(first_row, window)
        cells = jnp.concatenate(
            [grid_ref[at, n * LANES : (n + 1) * LANES] for n in range(len(rows))], axis=0
        )
        read = product(halves(cells), waves)
        dense_x = [x_ref[pair, p, :window] for p in range(3)]
        dense_y = [y_ref[pair, p] for p in range(3)]
        lined = {}
        for order_y, order_z in ((0, 0), (1, 0), (2, 0), (0, 1), (1, 1), (0, 2)):
            lined[order_y, order_z] = sum(
                dense_y[order_y][r : r + 1]
                * read[n * window : (n + 1) * window, order_z * LANES : (order_z + 1) * LANES]
                for n, r in enumerate(rows)
            )

        def sampled(p, r, s):
            return jnp.sum(dense_x[p] * lined[r, s], axis=0, keepdims=True)

        charge, dip_x, dip_y, dip_z, live = [
            atoms_ref[pencil, a : a + 1, lanes] for a in range(6, 11)
        ]
        s100 = sampled(1, 0, 0)
        s010 = sampled(0, 1, 0)
        s001 = sampled(0, 0, 1)
        s110 = sampled(1, 1, 0)
        s101 = sampled(1, 0, 1)
        s011 = sampled(0, 1, 1)
        out = [
            live * sampled(0, 0, 0),
            live * s100,
            live * s010,
            live * s001,
            charge * s100 + dip_x * sampled(2, 0, 0) + dip_y * s110 + dip_z * s101,
            charge * s010 + dip_x * s110 + dip_y * sampled(0, 2, 0) + dip_z * s011,
            charge * s001 + dip_x * s101 + dip_y * s011 + dip_z * sampled(0, 0, 2),
            jnp.full(live.shape, energy, f32),
        ]
        ahead = lax.rem(pencil - where_ref[1] + PENCILS, PENCILS)
        out_ref[ahead, :, lanes] = jnp.concatenate(out, axis=0)
        return carry

    lax.fori_loop(0, PENCILS * PAIRS, pair_body, 0, unroll=12)
    if not own:
        for copy in copies[3:]:
            copy.wait()


def finish_kernel(
    own_ref, one_ref, two_ref, three_ref, charge_ref, dipole_ref, position_ref, energy_ref
):
    total = (own_ref[...] + one_ref[...]) + (two_ref[...] + three_ref[...])
    charge_ref[...] = total[0]
    dipole_ref[...] = total[1:4]
    position_ref[...] = total[4:7]
    energy_ref[...] = total[7:8, 0:1]


SPACES = {"v": pltpu.VMEM, "h": pltpu.HBM, "s": pltpu.SMEM}
WORK = {"flops": 1_000_000_000, "bytes_accessed": 8_000_000}


def out_place(shape):
    pinned = isinstance(shape, type(pltpu.HBM((8, LANES), f32)))
    return pl.BlockSpec(memory_space=pltpu.HBM if pinned else pltpu.VMEM)


def call(kernel, inputs, out_shape, scratch=(), aliases=()):
    def run(*operands):
        placed = [
            pltpu.with_memory_space_constraint(one, pltpu.HBM) if where == "h" else one
            for one, where in zip(operands, inputs)
        ]
        return pl.pallas_call(
            kernel,
            out_shape=out_shape,
            in_specs=[pl.BlockSpec(memory_space=SPACES[one]) for one in inputs],
            out_specs=jax.tree.map(out_place, out_shape),
            scratch_shapes=list(scratch),
            input_output_aliases=dict(aliases),
            compiler_params=pltpu.CompilerParams(vmem_limit_bytes=28 * 1024 * 1024),
            cost_estimate=pl.CostEstimate(transcendentals=0, **WORK),
        )(*placed)

    return run


def next_slab(value, back=False):
    step = -1 if back else 1
    return lax.ppermute(value, "gy", [(i, (i + step) % SLABS) for i in range(SLABS)])


def swap_slabs(lines):
    lines = lines.reshape(SLABS, CARRIERS, 1, LANES)
    lines = lax.all_to_all(lines, "gy", split_axis=0, concat_axis=0, tiled=True)
    return lines.reshape(SLABS * CARRIERS, LANES)


def on_device(cell_index, offsets, charges, dipoles, block_count, shear_cells):
    pencil_index = lax.axis_index("gx")
    slab_index = lax.axis_index("gy")
    x_forward, x_inverse, y_forward, y_inverse = wave_tables()
    shape = jax.ShapeDtypeStruct
    shift = jnp.where(slab_index == 0, shear_cells[0], 0)
    where = jnp.stack([slab_index, pencil_index, shift, shear_cells[0]])

    mine, base, taps, cos_t, sin_t = call(
        prepare_kernel,
        "sshhhhh",
        (
            shape((16, ATOM_DEV), f32),
            shape((8, LANES), f32),
            shape((6, PADDED_Z, LANES), f32),
            shape((NX, LANES), f32),
            shape((NX, LANES), f32),
        ),
        [
            pltpu.SMEM(block_count.shape, jnp.int32),
            pltpu.VMEM((3, ATOM_DEV), jnp.int32),
            pltpu.VMEM((3, ATOM_DEV), f32),
            pltpu.VMEM((1, ATOM_DEV), f32),
            pltpu.VMEM((3, ATOM_DEV), f32),
            pltpu.SemaphoreType.DMA((5,)),
        ],
    )(
        where,
        shear_cells,
        block_count,
        cell_index,
        offsets,
        charges,
        dipoles,
    )
    atoms = lax.all_gather(mine, "gx", axis=0, tiled=False)
    below_atoms = next_slab(atoms)

    packed = shape((SLABS * CARRIERS, LANES), f32)
    table_space = pltpu.VMEM((NX, 6 * QUARTER), bf16)
    pairs = 2 * PENCILS * PAIRS
    held = [
        ((2, 2 * PADDED_Z, 3 * LANES), bf16),
        ((3, WIDE, LANES), f32),
        ((3, 16, LANES), f32),
    ]
    weights_space = pltpu.VMEM((PENCILS, 18, 8, ATOM_DEV), f32)
    grid_shape = shape((EXTENDED, 2 * CY * LANES), f32)
    slab_grid = call(
        lambda *refs: spread_kernel(True, *refs),
        "vsvv",
        grid_shape,
        [weights_space],
    )(atoms, where, base, taps)
    green_shape = pltpu.HBM((NY, PART_X * LANES), f32)
    green_space = pltpu.VMEM((NY, PART_X * LANES), f32)
    _, lines = call(
        lambda *refs: spread_kernel(False, *refs),
        "vsvvvhvv",
        (grid_shape, packed),
        [table_space, weights_space, pltpu.SemaphoreType.DMA],
        ((4, 0),),
    )(below_atoms, where, base, taps, slab_grid, x_forward, cos_t, sin_t)
    lines, where, atoms, below_atoms = lax.optimization_barrier(
        (lines, where, atoms, below_atoms)
    )
    *weights, green = call(
        weights_kernel,
        "svvvv",
        (*(pltpu.HBM((pairs, *dims), kind) for dims, kind in held), green_shape),
        [
            *(pltpu.VMEM((pairs, *dims), kind) for dims, kind in held),
            green_space,
            weights_space,
            pltpu.SemaphoreType.DMA((7,)),
        ],
    )(where, atoms, below_atoms, base, taps)
    lines = swap_slabs(lines)
    filtered = call(
        filter_kernel,
        "vhhh",
        packed,
        [table_space, table_space, green_space, pltpu.SemaphoreType.DMA((5,))],
    )(
        lines, y_forward, y_inverse, green
    )
    filtered = swap_slabs(filtered)
    shares_shape = shape((PENCILS, 8, ATOM_DEV), f32)
    below_shares, potential, *weights = call(
        lambda *refs: sample_kernel(False, *refs),
        "vshhhvvvh",
        (
            shares_shape,
            shape((EXTENDED, CY * LANES), f32),
            *(shape((pairs // 2, *dims), kind) for dims, kind in held),
        ),
        [
            *(pltpu.VMEM((pairs // 2, *dims), kind) for dims, kind in held),
            table_space,
            pltpu.SemaphoreType.DMA((7,)),
        ],
    )(below_atoms, where, *weights, filtered, cos_t, sin_t, x_inverse)
    below_shares = next_slab(below_shares, back=True)
    shares = call(lambda *refs: sample_kernel(True, *refs), "vsvvvv", shares_shape)(
        atoms, where, *weights, potential
    )
    shares = shares + below_shares
    arrived = [
        lax.ppermute(shares[ahead], "gx", [(i, (i + ahead) % PENCILS) for i in range(PENCILS)])
        for ahead in range(1, PENCILS)
    ]
    charge_grad, dipole_grad, position_grad, energy = call(
        finish_kernel,
        "vvvv",
        (
            shape((ATOM_DEV,), f32),
            shape((3, ATOM_DEV), f32),
            shape((3, ATOM_DEV), f32),
            shape((1, 1), f32),
        ),
    )(shares[0], *arrived)
    return charge_grad, dipole_grad, position_grad, energy[0]


def solution(mesh):
    placed = (
        P(None, ("gy", "gx")),
        P(None, ("gy", "gx")),
        P(("gy", "gx")),
        P(None, ("gy", "gx")),
        P(("gy", "gx")),
        P(),
    )
    return jax.shard_map(
        on_device,
        mesh=mesh,
        in_specs=placed,
        out_specs=(P(("gy", "gx")), P(None, ("gy", "gx")), P(None, ("gy", "gx")), P()),
        check_vma=False,
    )
```

```python
import math

import jax
import jax.numpy as jnp
import ml_dtypes
import numpy as np
from jax import lax
from jax.experimental import pallas as pl
from jax.experimental.pallas import tpu as pltpu
from jax.sharding import PartitionSpec as P

NX = 384
NY = 384
NZ = 360
CY = 6
CX = 96
PENCILS = 4
SLABS = 64
PART_X = 6
PART_Z = 45
ATOM_BLK = 64
ATOM_DEV = 384
PAIRS = 3
WINDOW = 40
WIDE = 48
EXTENDED = NX + WIDE
HALF = 64
LANES = 128
PADDED_Z = 48
QUARTER = 96
screening = 0.9
f32 = jnp.float32
bf16 = jnp.bfloat16


def split_table(table):
    high = table.astype(ml_dtypes.bfloat16)
    low = (table - high.astype(np.float64)).astype(ml_dtypes.bfloat16)
    return np.concatenate([high, high, low], axis=1)


def wave_tables():
    quarter = np.arange(QUARTER)
    mode = np.arange(4)[:, None] + 4 * quarter[None, :]
    row_y = CY * (quarter % 16) + quarter // 16
    tables = []
    for place in (quarter, row_y):
        ticks = mode[:, :, None] * place % NX
        for table in (ticks, ticks.transpose(0, 2, 1)):
            angle = 2.0 * np.pi / NX * table.reshape(NX, QUARTER)
            tables.append(split_table(np.concatenate([np.cos(angle), np.sin(angle)], axis=1)))
    return tables


def spline_rows(fraction):
    levels = {2: [1.0 - fraction, fraction]}
    current = levels[2]
    for n in range(3, 7):
        inverse_n = 1.0 / (n - 1)
        updated = [None] * n
        updated[n - 1] = inverse_n * fraction * current[n - 2]
        for j in range(1, n - 1):
            updated[n - 1 - j] = inverse_n * (
                (fraction + j) * current[n - 2 - j] + (n - j - fraction) * current[n - 1 - j]
            )
        updated[0] = inverse_n * (1.0 - fraction) * current[0]
        current = updated
        levels[n] = current
    zero_row = jnp.zeros_like(fraction)

    def entry_at(values_list, k):
        return values_list[k] if 0 <= k < len(values_list) else zero_row

    first = [entry_at(levels[5], t - 1) - entry_at(levels[5], t) for t in range(6)]
    second = [
        entry_at(levels[4], t - 2) - 2.0 * entry_at(levels[4], t - 1) + entry_at(levels[4], t)
        for t in range(6)
    ]
    return levels[6], first, second


def dense_rows(tables, cell, length):
    away = lax.broadcasted_iota(jnp.int32, (length, cell.shape[1]), 0).astype(f32) - cell
    summed = [jnp.zeros(away.shape, f32) for _ in tables]
    for t in range(6):
        here = away == float(t)
        summed = [jnp.where(here, table[t], so_far) for table, so_far in zip(tables, summed)]
    return summed


def unit_phase(turns):
    turns = turns - jnp.floor(turns + 0.5)
    quarter = jnp.floor(4.0 * turns + 0.5)
    rest = turns - 0.25 * quarter
    theta = (2.0 * math.pi) * rest
    square = theta * theta
    sine = theta * (
        1.0
        + square
        * (-1.0 / 6 + square * (1.0 / 120 + square * (-1.0 / 5040 + square * (1.0 / 362880))))
    )
    cosine = 1.0 + square * (
        -0.5
        + square
        * (1.0 / 24 + square * (-1.0 / 720 + square * (1.0 / 40320 - square * (1.0 / 3628800))))
    )
    odd = jnp.abs(quarter) == 1.0
    cos_out = jnp.where(odd, sine, cosine)
    sin_out = jnp.where(odd, cosine, sine)
    cos_out = jnp.where((quarter == 1.0) | (jnp.abs(quarter) == 2.0), -cos_out, cos_out)
    sin_out = jnp.where((quarter == -1.0) | (jnp.abs(quarter) == 2.0), -sin_out, sin_out)
    return cos_out, sin_out


class Twist:
    def __init__(self, cos_ref, sin_ref):
        whole = (NX, LANES)
        self.cos = jnp.broadcast_to(cos_ref[:, 0:1], whole)
        self.sin = jnp.broadcast_to(sin_ref[:, 0:1], whole)
        self.cos_step = jnp.broadcast_to(cos_ref[:, CY : CY + 1], whole)
        self.sin_step = jnp.broadcast_to(sin_ref[:, CY : CY + 1], whole)
        self.row = 0

    def at(self, row):
        while self.row < row:
            self.cos, self.sin = (
                self.cos * self.cos_step - self.sin * self.sin_step,
                self.sin * self.cos_step + self.cos * self.sin_step,
            )
            self.row += 1
        return self.cos, self.sin


def halves(value):
    high = value.astype(bf16)
    return high, (value - high.astype(f32)).astype(bf16)


def joined(left, right):
    return (
        jnp.concatenate([left[0], left[0], left[1]], axis=1),
        jnp.concatenate([right[0], right[1], right[0]], axis=0),
    )


def product(left, right):
    left, right = joined(left, right)
    return jnp.dot(left, right, preferred_element_type=f32)


def product3(left, right):
    def one(a, b):
        return jnp.dot(a, b, preferred_element_type=f32)

    return one(left[0], right[0]) + (one(left[0], right[1]) + one(left[1], right[0]))


def lane_sign(shape):
    return jnp.where(lax.broadcasted_iota(jnp.int32, shape, 1) < HALF, 1.0, -1.0).astype(f32)


def turned(value, sign):
    return pltpu.roll(value, HALF, 1) * sign


def fetch(source, target, semaphore):
    copy = pltpu.make_async_copy(source, target, semaphore)
    copy.start()
    return copy


def line_product(table_ref, r, value):
    rows = slice(r * QUARTER, (r + 1) * QUARTER)
    table = table_ref[rows, : 2 * QUARTER], table_ref[rows, 4 * QUARTER :]
    return product3(table, halves(value))


def forward_line(table_ref, quarters, turned_quarters):
    g, h = quarters, turned_quarters
    a, b, c, d = g[0] + g[2], g[0] - g[2], g[1] + g[3], g[1] - g[3]
    ta, tb, tc, td = h[0] + h[2], h[0] - h[2], h[1] + h[3], h[1] - h[3]
    lines = []
    for r, (one, other) in enumerate(
        ((a + c, ta + tc), (b + td, tb - d), (a - c, ta - tc), (b - td, tb + d))
    ):
        stacked = jnp.concatenate([one, other], axis=0)
        lines.append(line_product(table_ref, r, stacked))
    return lines


def inverse_line(table_ref, modes, turned_modes):
    z = []
    for r in range(4):
        stacked = jnp.concatenate([modes[r], -turned_modes[r]], axis=0)
        z.append(line_product(table_ref, r, stacked))
    a, b, c, d = z[0] + z[2], z[0] - z[2], z[1] + z[3], z[1] - z[3]
    width = d.shape[1]
    sign = lane_sign((QUARTER, LANES))
    td = jnp.concatenate(
        [turned(d[:, n : n + LANES], sign) for n in range(0, width, LANES)], axis=1
    )
    return [a + c, b - td, a - c, b + td]


def quarters_of(value):
    return [value[r * QUARTER : (r + 1) * QUARTER] for r in range(4)]


PIECES = (0, 16, 32, 64, 80, 96)
GROUPS = PART_X * CY // 4
CARRIERS = 3 * GROUPS


def lane_range(first):
    lane = lax.broadcasted_iota(jnp.int32, (SLABS, LANES), 1)
    return (lane >= first) & (lane < first + 16)


def pack_blocks(blocks):
    carriers = []
    for c in range(3):
        value = blocks[c]
        for half in range(2):
            gap = PADDED_Z + half * HALF
            shift = (gap - PIECES[2 * c + half]) % LANES
            value = jnp.where(lane_range(gap), pltpu.roll(blocks[3], shift, 1), value)
        carriers.append(value)
    return carriers


def unpack_block(carriers):
    value = jnp.zeros((SLABS, LANES), f32)
    for p, source in enumerate(PIECES):
        gap = PADDED_Z + p % 2 * HALF
        shift = (source - gap) % LANES
        value = jnp.where(lane_range(source), pltpu.roll(carriers[p // 2], shift, 1), value)
    return value


def rows_of(carrier):
    return pl.ds(carrier, SLABS, stride=CARRIERS)


def block_at(ref, j, y):
    block = j * CY + y
    group, place = block // 4, block % 4
    if place < 3:
        return ref[rows_of(3 * group + place), :]
    return unpack_block([ref[rows_of(3 * group + c), :] for c in range(3)])


def prepare_kernel(
    where_ref, shear_ref, counts_ref, cells_ref, offsets_ref, charges_ref, dipoles_ref,
    atoms_ref, base_ref, taps_ref, cos_ref, sin_ref,
    count_ref, cell_ref, offset_ref, charge_ref, dipole_ref, semaphores
):
    copies = [
        fetch(source, target, semaphores.at[n])
        for n, (source, target) in enumerate(
            (
                (counts_ref, count_ref),
                (cells_ref, cell_ref),
                (offsets_ref, offset_ref),
                (charges_ref, charge_ref.at[0]),
                (dipoles_ref, dipole_ref),
            )
        )
    ]
    slab, pencil = where_ref[0], where_ref[1]
    first = pencil * PART_Z
    row = lax.broadcasted_iota(jnp.int32, (PADDED_Z, LANES), 0)
    mode = (row + first).astype(f32)
    base_ref[...] = mode[:8]
    for t in range(3):
        cos_t, sin_t = unit_phase(mode * (t + 0.5) * (1.0 / NZ))
        taps_ref[t] = jnp.where(row < PART_Z, cos_t, 0.0)
        taps_ref[3 + t] = jnp.where(row < PART_Z, sin_t, 0.0)
    column = lax.broadcasted_iota(jnp.int32, (1, LANES), 1)
    rows = jnp.where(column < CY, slab * CY + column, 1)
    index = lax.broadcasted_iota(jnp.int32, (NX, LANES), 0)
    folds = folded_mode(index)
    ticks = folds * (shear_ref[0] * rows)
    whole = jnp.floor(ticks.astype(f32) * (1.0 / (NX * NY))).astype(jnp.int32)
    rest = ticks - whole * (NX * NY)
    cos_t, sin_t = unit_phase(rest.astype(f32) * (1.0 / (NX * NY)))
    cos_ref[...] = cos_t
    sin_ref[...] = sin_t
    for copy in copies:
        copy.wait()
    slot = lax.broadcasted_iota(jnp.int32, (1, ATOM_DEV), 1)
    live = jnp.zeros((1, ATOM_DEV), f32)
    for b in range(ATOM_DEV // ATOM_BLK):
        inside = (slot >= b * ATOM_BLK) & (slot < b * ATOM_BLK + count_ref[b])
        live = jnp.where(inside, 1.0, live)
    atoms_ref[0:1, :] = cell_ref[0:1, :].astype(f32)
    atoms_ref[1:2, :] = (cell_ref[1:2, :] - slab * CY).astype(f32)
    atoms_ref[2:3, :] = cell_ref[2:3, :].astype(f32)
    atoms_ref[3:6, :] = offset_ref[...]
    atoms_ref[6:7, :] = charge_ref[...] * live
    atoms_ref[7:10, :] = dipole_ref[...] * live
    atoms_ref[10:11, :] = live
    atoms_ref[11:16, :] = jnp.zeros((5, ATOM_DEV), f32)


def spline_table(atoms_ref, table_ref, orders):
    def pencil_body(pencil, carry):
        tables = spline_rows(atoms_ref[pencil, 3:6, :])
        for o in range(orders):
            for t in range(6):
                table_ref[pencil, o * 6 + t, 0:3, :] = tables[o][t]
        return carry

    lax.fori_loop(0, PENCILS, pencil_body, 0)


def weight_rows(table_ref, pencil, lanes, dim, orders):
    row = slice(dim, dim + 1)
    return [[table_ref[pencil, o * 6 + t, row, lanes] for t in range(6)] for o in range(orders)]


def pair_place(pair):
    pencil = pair // PAIRS
    return pencil, pl.ds(pl.multiple_of(pair % PAIRS * LANES, LANES), LANES)


def pair_window(pair, own, where_ref):
    if own:
        return pl.multiple_of(pair * 32, 8), WINDOW, (pair * 32).astype(f32)
    place = pair * 32 + where_ref[2]
    place = jnp.where(place >= NX, place - NX, place)
    first = place // 8 * 8
    return pl.multiple_of(first, 8), WIDE, (pair * 32 - (place - first)).astype(f32)


def z_waves(cell_z, weights, base_ref, taps_ref):
    centre = cell_z + 2.5
    turn = base_ref[...] * centre
    turn = turn - 360.0 * jnp.floor(turn * (1.0 / 360.0))
    cos_k, sin_k = unit_phase(turn * (1.0 / 360.0))
    turn = 8.0 * centre
    turn = turn - 360.0 * jnp.floor(turn * (1.0 / 360.0))
    cos_8, sin_8 = unit_phase(jnp.broadcast_to(turn * (1.0 / 360.0), cos_k.shape))
    folded = [
        (
            [weight[2 - t] + weight[3 + t] for t in range(3)],
            [weight[3 + t] - weight[2 - t] for t in range(3)],
        )
        for weight in weights
    ]
    pieces = [[] for _ in weights]
    pieces_im = [[] for _ in weights]
    for q in range(PADDED_Z // 8):
        span = slice(q * 8, q * 8 + 8)
        cos_t = [taps_ref[t, span, :] for t in range(3)]
        sin_t = [taps_ref[3 + t, span, :] for t in range(3)]
        for s, (even, odd) in enumerate(folded):
            real = even[0] * cos_t[0] + even[1] * cos_t[1] + even[2] * cos_t[2]
            imag = odd[0] * sin_t[0] + odd[1] * sin_t[1] + odd[2] * sin_t[2]
            pieces[s].append(real * cos_k - imag * sin_k)
            pieces_im[s].append(-(real * sin_k + imag * cos_k))
        cos_k, sin_k = cos_k * cos_8 - sin_k * sin_8, sin_k * cos_8 + cos_k * sin_8
    return [
        (jnp.concatenate(re, axis=0), jnp.concatenate(im, axis=0))
        for re, im in zip(pieces, pieces_im)
    ]


def sampling_weights(
    start, own, where_ref, some_ref, table_ref, base_ref, taps_ref, waves_ref, x_ref, y_ref
):
    spline_table(some_ref, table_ref, 3)

    def pair_body(pair, carry):
        pencil, lanes = pair_place(pair)
        row = [some_ref[pencil, a : a + 1, lanes] for a in range(3)]
        _, window, origin = pair_window(pair, own, where_ref)
        dense_x = dense_rows(weight_rows(table_ref, pencil, lanes, 0, 3), row[0] - origin, window)
        dense_y = dense_rows(weight_rows(table_ref, pencil, lanes, 1, 3), row[1], 16)
        for p in range(3):
            x_ref[start + pair, p, :window] = dense_x[p]
            y_ref[start + pair, p] = dense_y[p]
        waves = z_waves(row[2], weight_rows(table_ref, pencil, lanes, 2, 3), base_ref, taps_ref)
        for s, (re, im) in enumerate(waves):
            re, im = halves(re), halves(im)
            columns = slice(s * LANES, (s + 1) * LANES)
            for n in range(2):
                waves_ref[start + pair, n, :PADDED_Z, columns] = re[n]
                waves_ref[start + pair, n, PADDED_Z:, columns] = im[n]
        return carry

    lax.fori_loop(0, PENCILS * PAIRS, pair_body, 0, unroll=2)


def spread_kernel(own, *refs):
    atoms_ref, where_ref, base_ref, taps_ref = refs[:4]
    if own:
        grid_ref, weights_ref = refs[4:]
        grid_ref[...] = jnp.zeros_like(grid_ref)
    else:
        _, tables_ref, cos_ref, sin_ref, grid_ref, out_ref = refs[4:10]
        table_ref, weights_ref, semaphore = refs[10:]
        table_copy = fetch(tables_ref, table_ref, semaphore)
    rows = list(range(CY)) if own else list(range(CY, 2 * CY - 1))
    part = CY * LANES
    gap = jnp.zeros((HALF - PADDED_Z, LANES), bf16)
    spline_table(atoms_ref, weights_ref, 2)

    def pair_body(pair, carry):
        pencil, lanes = pair_place(pair)
        row = [atoms_ref[pencil, a : a + 1, lanes] for a in range(10)]
        charge, dip_x, dip_y, dip_z = row[6:10]
        first_row, window, origin = pair_window(pair, own, where_ref)
        dense_x = dense_rows(
            weight_rows(weights_ref, pencil, lanes, 0, 2), row[0] - origin, window
        )
        dense_y = dense_rows(weight_rows(weights_ref, pencil, lanes, 1, 2), row[1], 16)
        value, first = weight_rows(weights_ref, pencil, lanes, 2, 2)
        mixed = [charge * value[t] + dip_z * first[t] for t in range(6)]
        right = []
        for re, im in z_waves(row[2], (mixed, value), base_ref, taps_ref):
            re, im = halves(re), halves(im)
            right.append(
                [
                    jnp.concatenate([re[n], gap, im[n], gap, im[n], gap, -re[n], gap], axis=0)
                    for n in range(2)
                ]
            )
        high, low = [jnp.concatenate([right[0][n], right[1][n]], axis=1) for n in range(2)]
        right = jnp.concatenate([high, low, high], axis=1)
        left = []
        for r in rows:
            value, first = dense_y[0][r : r + 1], dense_y[1][r : r + 1]
            left.append(
                jnp.concatenate(
                    [
                        value * dense_x[0],
                        (dip_x * value) * dense_x[1] + (dip_y * first) * dense_x[0],
                    ],
                    axis=1,
                )
            )
        high, low = halves(jnp.concatenate(left, axis=0))
        left = jnp.concatenate([high, high, low], axis=1)
        added = lax.dot_general(
            left, right, (((1,), (1,)), ((), ())), preferred_element_type=f32
        )
        at = pl.ds(first_row, window)
        for n in range(len(rows)):
            piece = added[n * window : (n + 1) * window]
            grid_ref[at, n * LANES : (n + 1) * LANES] += piece[:, :LANES]
            grid_ref[at, part + n * LANES : part + (n + 1) * LANES] += piece[:, LANES:]
        return carry

    lax.fori_loop(0, PENCILS * PAIRS, pair_body, 0, unroll=12)
    if own:
        return
    grid_ref[0:WIDE] += grid_ref[NX:EXTENDED]
    table_copy.wait()
    sign = lane_sign((NX, LANES))
    twist = Twist(cos_ref, sin_ref)
    totals = []
    for first in range(0, CY, 2):
        lanes = slice(first * LANES, (first + 2) * LANES)
        below = slice(part + lanes.start, part + lanes.stop)
        line = jnp.concatenate(
            forward_line(
                table_ref, quarters_of(grid_ref[:NX, lanes]), quarters_of(grid_ref[:NX, below])
            ),
            axis=0,
        )
        for n, y in enumerate((first, first + 1)):
            one = line[:, n * LANES : (n + 1) * LANES]
            cos_y, sin_y = twist.at(y)
            totals.append(one * cos_y + turned(one, sign) * sin_y)
    for group in range(GROUPS):
        blocks = []
        for block in range(4 * group, 4 * group + 4):
            j, y = block // CY, block % CY
            blocks.append(totals[y][j * SLABS : (j + 1) * SLABS])
        for c, carrier in enumerate(pack_blocks(blocks)):
            out_ref[rows_of(3 * group + c), :] = carrier


def spline_modulus(turns):
    cosine, _ = unit_phase(turns)
    return (64.0 + 52.0 * cosine + 4.0 * cosine * cosine) * (1.0 / 120.0)


def folded_mode(row):
    residue = (
        (row >= QUARTER).astype(jnp.int32)
        + (row >= 2 * QUARTER).astype(jnp.int32)
        + (row >= 3 * QUARTER).astype(jnp.int32)
    )
    mode = 4 * (row - QUARTER * residue) + residue
    return jnp.where(mode < NX // 2, mode, mode - NX)


def make_green(where_ref, out_ref):
    slab, pencil, shear = where_ref[0], where_ref[1], where_ref[3].astype(f32)
    decay = (math.pi / screening) ** 2
    column = lax.broadcasted_iota(jnp.int32, (1, LANES), 1)
    own_x = folded_mode(jnp.minimum(column, PART_X) * SLABS + slab)
    own_y = folded_mode(lax.broadcasted_iota(jnp.int32, (NY, LANES), 0))
    float_x = own_x.astype(f32)
    wave_y = own_y.astype(f32) + float_x * shear * (1.0 / NX)
    part_x, part_y = float_x * (1.0 / NX), wave_y * (1.0 / NY)
    norm = part_x * part_x + part_y * part_y
    moduli = spline_modulus(part_x) * spline_modulus(part_y)
    top = jnp.exp(-decay * norm) / (math.pi * moduli * moduli)
    top = jnp.where((own_x == -(NX // 2)) | (own_y == -(NY // 2)), 0.0, top)
    lane = jnp.where(column < HALF, column, column - HALF)
    mode = pencil * PART_Z + lane
    part_z = mode.astype(f32) * (1.0 / NZ)
    modulus = spline_modulus(part_z)
    norm_z = part_z * part_z
    twice = jnp.where(mode == 0, 1.0, 2.0) * (1.0 / (NX * NY * NZ))
    mode_top = jnp.where(
        lane < PART_Z, twice * jnp.exp(-decay * norm_z) / (modulus * modulus), 0.0
    )
    mode_norm = jnp.where(lane < PART_Z, norm_z, 1.0)
    for j in range(PART_X):
        square = norm[:, j : j + 1] + mode_norm
        green = top[:, j : j + 1] * mode_top / jnp.where(square == 0.0, 1.0, square)
        out_ref[:, j * LANES : (j + 1) * LANES] = jnp.where(square == 0.0, 0.0, green)


def weights_kernel(
    where_ref, atoms_ref, below_ref, base_ref, taps_ref, tables_ref, backs_ref, *refs
):
    results, (green_ref, table_ref, back_ref), kept = refs[:3], refs[3:6], refs[6:9]
    weights_ref, semaphores = refs[9:]
    copies = [
        fetch(tables_ref, table_ref, semaphores.at[6]),
        fetch(backs_ref, back_ref, semaphores.at[7]),
    ]
    make_green(where_ref, green_ref)
    pairs = PENCILS * PAIRS
    for own, some_ref in ((True, atoms_ref), (False, below_ref)):
        start = 0 if own else pairs
        sampling_weights(start, own, where_ref, some_ref, weights_ref, base_ref, taps_ref, *kept)
        some = pl.ds(start, pairs)
        for n in range(3):
            semaphore = semaphores.at[n if own else 3 + n]
            copies.append(fetch(kept[n].at[some], results[n].at[some], semaphore))
    for copy in copies:
        copy.wait()


def filter_kernel(in_ref, table_ref, back_ref, green_ref, out_ref):
    sign = lane_sign((NY, LANES))
    energy = jnp.zeros((8, LANES), f32)
    blocks = []
    for first in range(0, PART_X, 2):
        lines = []
        for j in (first, first + 1):
            found = [block_at(in_ref, j, y) for y in range(CY)]
            lines.append(
                jnp.concatenate(
                    [one[16 * part : 16 * part + 16] for part in range(4) for one in found], axis=0
                )
            )
        swapped = jnp.concatenate([turned(one, sign) for one in lines], axis=1)
        lines = jnp.concatenate(lines, axis=1)
        spectrum = jnp.concatenate(
            forward_line(table_ref, quarters_of(lines), quarters_of(swapped)), axis=0
        )
        modes = []
        for n in range(2):
            j = first + n
            one = spectrum[:, n * LANES : (n + 1) * LANES]
            scaled = green_ref[:, j * LANES : (j + 1) * LANES] * one
            share = scaled * one
            energy = energy + sum(share[8 * i : 8 * i + 8] for i in range(NY // 8))
            modes.append(scaled)
        swapped = jnp.concatenate([turned(one, sign) for one in modes], axis=1)
        modes = jnp.concatenate(modes, axis=1)
        parts = inverse_line(back_ref, quarters_of(modes), quarters_of(swapped))
        for n in range(2):
            for y in range(CY):
                blocks.append(
                    jnp.concatenate(
                        [
                            one[16 * y : 16 * y + 16, n * LANES : (n + 1) * LANES]
                            for one in parts
                        ],
                        axis=0,
                    )
                )
        for group in range(first * CY // 4, (first + 2) * CY // 4):
            for c, carrier in enumerate(pack_blocks(blocks[4 * group : 4 * group + 4])):
                out_ref[rows_of(3 * group + c), :] = carrier
    lane = lax.broadcasted_iota(jnp.int32, (SLABS, LANES), 1)
    share = 0.5 * jnp.sum(energy)
    out_ref[rows_of(0), :] = jnp.where(lane == PART_Z, share, out_ref[rows_of(0), :])


def sample_kernel(own, *refs):
    if own:
        atoms_ref, where_ref, waves_ref, x_ref, y_ref, grid_ref, out_ref = refs
    else:
        atoms_ref, where_ref = refs[:2]
        kept = refs[2:5]
        in_ref, cos_ref, sin_ref, tables_ref, out_ref, grid_ref = refs[5:11]
        slab_weights, below_weights = refs[11:14], refs[14:17]
        waves_ref, x_ref, y_ref = below_weights
        table_ref, semaphores = refs[17:]
        table_copy = fetch(tables_ref, table_ref, semaphores.at[6])
        pairs = PENCILS * PAIRS
        copies = [
            fetch(source.at[pl.ds(start, pairs)], target, semaphores.at[n])
            for n, (source, start, target) in enumerate(
                [(kept[n], pairs, below_weights[n]) for n in range(3)]
                + [(kept[n], 0, slab_weights[n]) for n in range(3)]
            )
        ]
    rows = list(range(CY)) if own else list(range(CY, 2 * CY - 1))
    energy = 0.0
    if not own:
        sign = lane_sign((NX, LANES))
        twist = Twist(cos_ref, sin_ref)
        for first in range(0, CY, 2):
            modes, swapped = [], []
            for y in range(first, first + 2):
                line = jnp.concatenate([block_at(in_ref, j, y) for j in range(PART_X)], axis=0)
                other = turned(line, sign)
                cos_y, sin_y = twist.at(y)
                modes.append(line * cos_y - other * sin_y)
                swapped.append(other * cos_y + line * sin_y)
            swapped = jnp.concatenate(swapped, axis=1)
            modes = jnp.concatenate(modes, axis=1)
            if first == 0:
                table_copy.wait()
            cells = jnp.concatenate(
                inverse_line(table_ref, quarters_of(modes), quarters_of(swapped)), axis=0
            )
            lanes = slice(first * LANES, (first + 2) * LANES)
            grid_ref[:NX, lanes] = cells
            grid_ref[NX:, lanes] = cells[:WIDE]
        lane = lax.broadcasted_iota(jnp.int32, (SLABS, LANES), 1)
        energy = jnp.sum(jnp.where(lane == PART_Z, in_ref[rows_of(0), :], 0.0))
    gap = jnp.zeros((HALF - PADDED_Z, 3 * LANES), bf16)

    if not own:
        for copy in copies[:3]:
            copy.wait()

    def pair_body(pair, carry):
        pencil, lanes = pair_place(pair)
        waves = [
            jnp.concatenate(
                [waves_ref[pair, n, :PADDED_Z], gap, waves_ref[pair, n, PADDED_Z:], gap],
                axis=0,
            )
            for n in range(2)
        ]
        first_row, window, _ = pair_window(pair, own, where_ref)
        at = pl.ds(first_row, window)
        cells = jnp.concatenate(
            [grid_ref[at, n * LANES : (n + 1) * LANES] for n in range(len(rows))], axis=0
        )
        read = product(halves(cells), waves)
        dense_x = [x_ref[pair, p, :window] for p in range(3)]
        dense_y = [y_ref[pair, p] for p in range(3)]
        lined = {}
        for order_y, order_z in ((0, 0), (1, 0), (2, 0), (0, 1), (1, 1), (0, 2)):
            lined[order_y, order_z] = sum(
                dense_y[order_y][r : r + 1]
                * read[n * window : (n + 1) * window, order_z * LANES : (order_z + 1) * LANES]
                for n, r in enumerate(rows)
            )

        def sampled(p, r, s):
            return jnp.sum(dense_x[p] * lined[r, s], axis=0, keepdims=True)

        charge, dip_x, dip_y, dip_z, live = [
            atoms_ref[pencil, a : a + 1, lanes] for a in range(6, 11)
        ]
        s100 = sampled(1, 0, 0)
        s010 = sampled(0, 1, 0)
        s001 = sampled(0, 0, 1)
        s110 = sampled(1, 1, 0)
        s101 = sampled(1, 0, 1)
        s011 = sampled(0, 1, 1)
        out = [
            live * sampled(0, 0, 0),
            live * s100,
            live * s010,
            live * s001,
            charge * s100 + dip_x * sampled(2, 0, 0) + dip_y * s110 + dip_z * s101,
            charge * s010 + dip_x * s110 + dip_y * sampled(0, 2, 0) + dip_z * s011,
            charge * s001 + dip_x * s101 + dip_y * s011 + dip_z * sampled(0, 0, 2),
            jnp.full(live.shape, energy, f32),
        ]
        ahead = lax.rem(pencil - where_ref[1] + PENCILS, PENCILS)
        out_ref[ahead, :, lanes] = jnp.concatenate(out, axis=0)
        return carry

    lax.fori_loop(0, PENCILS * PAIRS, pair_body, 0, unroll=12)
    if not own:
        for copy in copies[3:]:
            copy.wait()


def finish_kernel(
    own_ref, one_ref, two_ref, three_ref, charge_ref, dipole_ref, position_ref, energy_ref
):
    total = (own_ref[...] + one_ref[...]) + (two_ref[...] + three_ref[...])
    charge_ref[...] = total[0]
    dipole_ref[...] = total[1:4]
    position_ref[...] = total[4:7]
    energy_ref[...] = total[7:8, 0:1]


SPACES = {"v": pltpu.VMEM, "h": pltpu.HBM, "s": pltpu.SMEM}
WORK = {"flops": 1_000_000_000, "bytes_accessed": 8_000_000}


def out_place(shape):
    pinned = isinstance(shape, type(pltpu.HBM((8, LANES), f32)))
    return pl.BlockSpec(memory_space=pltpu.HBM if pinned else pltpu.VMEM)


def call(kernel, inputs, out_shape, scratch=(), aliases=()):
    def run(*operands):
        placed = [
            pltpu.with_memory_space_constraint(one, pltpu.HBM) if where == "h" else one
            for one, where in zip(operands, inputs)
        ]
        return pl.pallas_call(
            kernel,
            out_shape=out_shape,
            in_specs=[pl.BlockSpec(memory_space=SPACES[one]) for one in inputs],
            out_specs=jax.tree.map(out_place, out_shape),
            scratch_shapes=list(scratch),
            input_output_aliases=dict(aliases),
            compiler_params=pltpu.CompilerParams(vmem_limit_bytes=28 * 1024 * 1024),
            cost_estimate=pl.CostEstimate(transcendentals=0, **WORK),
        )(*placed)

    return run


def next_slab(value, back=False):
    step = -1 if back else 1
    return lax.ppermute(value, "gy", [(i, (i + step) % SLABS) for i in range(SLABS)])


def swap_slabs(lines):
    lines = lines.reshape(SLABS, CARRIERS, 1, LANES)
    lines = lax.all_to_all(lines, "gy", split_axis=0, concat_axis=0, tiled=True)
    return lines.reshape(SLABS * CARRIERS, LANES)


def on_device(cell_index, offsets, charges, dipoles, block_count, shear_cells):
    pencil_index = lax.axis_index("gx")
    slab_index = lax.axis_index("gy")
    x_forward, x_inverse, y_forward, y_inverse = wave_tables()
    shape = jax.ShapeDtypeStruct
    shift = jnp.where(slab_index == 0, shear_cells[0], 0)
    where = jnp.stack([slab_index, pencil_index, shift, shear_cells[0]])

    mine, base, taps, cos_t, sin_t = call(
        prepare_kernel,
        "sshhhhh",
        (
            shape((16, ATOM_DEV), f32),
            shape((8, LANES), f32),
            shape((6, PADDED_Z, LANES), f32),
            shape((NX, LANES), f32),
            shape((NX, LANES), f32),
        ),
        [
            pltpu.SMEM(block_count.shape, jnp.int32),
            pltpu.VMEM((3, ATOM_DEV), jnp.int32),
            pltpu.VMEM((3, ATOM_DEV), f32),
            pltpu.VMEM((1, ATOM_DEV), f32),
            pltpu.VMEM((3, ATOM_DEV), f32),
            pltpu.SemaphoreType.DMA((5,)),
        ],
    )(
        where,
        shear_cells,
        block_count,
        cell_index,
        offsets,
        charges,
        dipoles,
    )
    atoms = lax.all_gather(mine, "gx", axis=0, tiled=False)
    below_atoms = next_slab(atoms)

    packed = shape((SLABS * CARRIERS, LANES), f32)
    table_space = pltpu.VMEM((NX, 6 * QUARTER), bf16)
    pairs = 2 * PENCILS * PAIRS
    held = [
        ((2, 2 * PADDED_Z, 3 * LANES), bf16),
        ((3, WIDE, LANES), f32),
        ((3, 16, LANES), f32),
    ]
    weights_space = pltpu.VMEM((PENCILS, 18, 8, ATOM_DEV), f32)
    grid_shape = shape((EXTENDED, 2 * CY * LANES), f32)
    slab_grid = call(
        lambda *refs: spread_kernel(True, *refs),
        "vsvv",
        grid_shape,
        [weights_space],
    )(atoms, where, base, taps)
    green_shape = shape((NY, PART_X * LANES), f32)
    table_shape = shape((NX, 6 * QUARTER), bf16)
    _, lines = call(
        lambda *refs: spread_kernel(False, *refs),
        "vsvvvhvv",
        (grid_shape, packed),
        [table_space, weights_space, pltpu.SemaphoreType.DMA],
        ((4, 0),),
    )(below_atoms, where, base, taps, slab_grid, x_forward, cos_t, sin_t)
    lines, where, atoms, below_atoms = lax.optimization_barrier(
        (lines, where, atoms, below_atoms)
    )
    *weights, green, table, back = call(
        weights_kernel,
        "svvvvhh",
        (
            *(pltpu.HBM((pairs, *dims), kind) for dims, kind in held),
            green_shape,
            table_shape,
            table_shape,
        ),
        [
            *(pltpu.VMEM((pairs, *dims), kind) for dims, kind in held),
            weights_space,
            pltpu.SemaphoreType.DMA((8,)),
        ],
    )(where, atoms, below_atoms, base, taps, y_forward, y_inverse)
    lines = swap_slabs(lines)
    filtered = call(filter_kernel, "vvvv", packed)(lines, table, back, green)
    filtered = swap_slabs(filtered)
    shares_shape = shape((PENCILS, 8, ATOM_DEV), f32)
    below_shares, potential, *weights = call(
        lambda *refs: sample_kernel(False, *refs),
        "vshhhvvvh",
        (
            shares_shape,
            shape((EXTENDED, CY * LANES), f32),
            *(shape((pairs // 2, *dims), kind) for dims, kind in held),
        ),
        [
            *(pltpu.VMEM((pairs // 2, *dims), kind) for dims, kind in held),
            table_space,
            pltpu.SemaphoreType.DMA((7,)),
        ],
    )(below_atoms, where, *weights, filtered, cos_t, sin_t, x_inverse)
    below_shares = next_slab(below_shares, back=True)
    shares = call(lambda *refs: sample_kernel(True, *refs), "vsvvvv", shares_shape)(
        atoms, where, *weights, potential
    )
    shares = shares + below_shares
    arrived = [
        lax.ppermute(shares[ahead], "gx", [(i, (i + ahead) % PENCILS) for i in range(PENCILS)])
        for ahead in range(1, PENCILS)
    ]
    charge_grad, dipole_grad, position_grad, energy = call(
        finish_kernel,
        "vvvv",
        (
            shape((ATOM_DEV,), f32),
            shape((3, ATOM_DEV), f32),
            shape((3, ATOM_DEV), f32),
            shape((1, 1), f32),
        ),
    )(shares[0], *arrived)
    return charge_grad, dipole_grad, position_grad, energy[0]


def solution(mesh):
    placed = (
        P(None, ("gy", "gx")),
        P(None, ("gy", "gx")),
        P(("gy", "gx")),
        P(None, ("gy", "gx")),
        P(("gy", "gx")),
        P(),
    )
    return jax.shard_map(
        on_device,
        mesh=mesh,
        in_specs=placed,
        out_specs=(P(("gy", "gx")), P(None, ("gy", "gx")), P(None, ("gy", "gx")), P()),
        check_vma=False,
    )
```

```python
import math

import jax
import jax.numpy as jnp
import ml_dtypes
import numpy as np
from jax import lax
from jax.experimental import pallas as pl
from jax.experimental.pallas import tpu as pltpu
from jax.sharding import PartitionSpec as P

NX = 384
NY = 384
NZ = 360
CY = 6
CX = 96
PENCILS = 4
SLABS = 64
PART_X = 6
PART_Z = 45
ATOM_BLK = 64
ATOM_DEV = 384
PAIRS = 3
WINDOW = 40
WIDE = 48
EXTENDED = NX + WIDE
HALF = 64
LANES = 128
PADDED_Z = 48
QUARTER = 96
screening = 0.9
f32 = jnp.float32
bf16 = jnp.bfloat16


def split_table(table):
    high = table.astype(ml_dtypes.bfloat16)
    low = (table - high.astype(np.float64)).astype(ml_dtypes.bfloat16)
    return np.concatenate([high, high, low], axis=1)


def wave_tables():
    quarter = np.arange(QUARTER)
    mode = np.arange(4)[:, None] + 4 * quarter[None, :]
    row_y = CY * (quarter % 16) + quarter // 16
    tables = []
    for place in (quarter, row_y):
        ticks = mode[:, :, None] * place % NX
        for table in (ticks, ticks.transpose(0, 2, 1)):
            angle = 2.0 * np.pi / NX * table.reshape(NX, QUARTER)
            tables.append(split_table(np.concatenate([np.cos(angle), np.sin(angle)], axis=1)))
    return tables


def spline_rows(fraction):
    levels = {2: [1.0 - fraction, fraction]}
    current = levels[2]
    for n in range(3, 7):
        inverse_n = 1.0 / (n - 1)
        updated = [None] * n
        updated[n - 1] = inverse_n * fraction * current[n - 2]
        for j in range(1, n - 1):
            updated[n - 1 - j] = inverse_n * (
                (fraction + j) * current[n - 2 - j] + (n - j - fraction) * current[n - 1 - j]
            )
        updated[0] = inverse_n * (1.0 - fraction) * current[0]
        current = updated
        levels[n] = current
    zero_row = jnp.zeros_like(fraction)

    def entry_at(values_list, k):
        return values_list[k] if 0 <= k < len(values_list) else zero_row

    first = [entry_at(levels[5], t - 1) - entry_at(levels[5], t) for t in range(6)]
    second = [
        entry_at(levels[4], t - 2) - 2.0 * entry_at(levels[4], t - 1) + entry_at(levels[4], t)
        for t in range(6)
    ]
    return levels[6], first, second


def dense_rows(tables, cell, length):
    away = lax.broadcasted_iota(jnp.int32, (length, cell.shape[1]), 0).astype(f32) - cell
    summed = [jnp.zeros(away.shape, f32) for _ in tables]
    for t in range(6):
        here = away == float(t)
        summed = [jnp.where(here, table[t], so_far) for table, so_far in zip(tables, summed)]
    return summed


def unit_phase(turns):
    turns = turns - jnp.floor(turns + 0.5)
    quarter = jnp.floor(4.0 * turns + 0.5)
    rest = turns - 0.25 * quarter
    theta = (2.0 * math.pi) * rest
    square = theta * theta
    sine = theta * (
        1.0
        + square
        * (-1.0 / 6 + square * (1.0 / 120 + square * (-1.0 / 5040 + square * (1.0 / 362880))))
    )
    cosine = 1.0 + square * (
        -0.5
        + square
        * (1.0 / 24 + square * (-1.0 / 720 + square * (1.0 / 40320 - square * (1.0 / 3628800))))
    )
    odd = jnp.abs(quarter) == 1.0
    cos_out = jnp.where(odd, sine, cosine)
    sin_out = jnp.where(odd, cosine, sine)
    cos_out = jnp.where((quarter == 1.0) | (jnp.abs(quarter) == 2.0), -cos_out, cos_out)
    sin_out = jnp.where((quarter == -1.0) | (jnp.abs(quarter) == 2.0), -sin_out, sin_out)
    return cos_out, sin_out


class Twist:
    def __init__(self, cos_ref, sin_ref):
        whole = (NX, LANES)
        self.cos = jnp.broadcast_to(cos_ref[:, 0:1], whole)
        self.sin = jnp.broadcast_to(sin_ref[:, 0:1], whole)
        self.cos_step = jnp.broadcast_to(cos_ref[:, CY : CY + 1], whole)
        self.sin_step = jnp.broadcast_to(sin_ref[:, CY : CY + 1], whole)
        self.row = 0

    def at(self, row):
        while self.row < row:
            self.cos, self.sin = (
                self.cos * self.cos_step - self.sin * self.sin_step,
                self.sin * self.cos_step + self.cos * self.sin_step,
            )
            self.row += 1
        return self.cos, self.sin


def halves(value):
    high = value.astype(bf16)
    return high, (value - high.astype(f32)).astype(bf16)


def joined(left, right):
    return (
        jnp.concatenate([left[0], left[0], left[1]], axis=1),
        jnp.concatenate([right[0], right[1], right[0]], axis=0),
    )


def product(left, right):
    left, right = joined(left, right)
    return jnp.dot(left, right, preferred_element_type=f32)


def product3(left, right):
    def one(a, b):
        return jnp.dot(a, b, preferred_element_type=f32)

    return one(left[0], right[0]) + (one(left[0], right[1]) + one(left[1], right[0]))


def lane_sign(shape):
    return jnp.where(lax.broadcasted_iota(jnp.int32, shape, 1) < HALF, 1.0, -1.0).astype(f32)


def turned(value, sign):
    return pltpu.roll(value, HALF, 1) * sign


def fetch(source, target, semaphore):
    copy = pltpu.make_async_copy(source, target, semaphore)
    copy.start()
    return copy


def line_product(table_ref, r, value):
    rows = slice(r * QUARTER, (r + 1) * QUARTER)
    table = table_ref[rows, : 2 * QUARTER], table_ref[rows, 4 * QUARTER :]
    return product3(table, halves(value))


def forward_line(table_ref, quarters, turned_quarters):
    g, h = quarters, turned_quarters
    a, b, c, d = g[0] + g[2], g[0] - g[2], g[1] + g[3], g[1] - g[3]
    ta, tb, tc, td = h[0] + h[2], h[0] - h[2], h[1] + h[3], h[1] - h[3]
    lines = []
    for r, (one, other) in enumerate(
        ((a + c, ta + tc), (b + td, tb - d), (a - c, ta - tc), (b - td, tb + d))
    ):
        stacked = jnp.concatenate([one, other], axis=0)
        lines.append(line_product(table_ref, r, stacked))
    return lines


def inverse_line(table_ref, modes, turned_modes):
    z = []
    for r in range(4):
        stacked = jnp.concatenate([modes[r], -turned_modes[r]], axis=0)
        z.append(line_product(table_ref, r, stacked))
    a, b, c, d = z[0] + z[2], z[0] - z[2], z[1] + z[3], z[1] - z[3]
    width = d.shape[1]
    sign = lane_sign((QUARTER, LANES))
    td = jnp.concatenate(
        [turned(d[:, n : n + LANES], sign) for n in range(0, width, LANES)], axis=1
    )
    return [a + c, b - td, a - c, b + td]


def quarters_of(value):
    return [value[r * QUARTER : (r + 1) * QUARTER] for r in range(4)]


PIECES = (0, 16, 32, 64, 80, 96)
GROUPS = PART_X * CY // 4
CARRIERS = 3 * GROUPS


def lane_range(first):
    lane = lax.broadcasted_iota(jnp.int32, (SLABS, LANES), 1)
    return (lane >= first) & (lane < first + 16)


def pack_blocks(blocks):
    carriers = []
    for c in range(3):
        value = blocks[c]
        for half in range(2):
            gap = PADDED_Z + half * HALF
            shift = (gap - PIECES[2 * c + half]) % LANES
            value = jnp.where(lane_range(gap), pltpu.roll(blocks[3], shift, 1), value)
        carriers.append(value)
    return carriers


def unpack_block(carriers):
    value = jnp.zeros((SLABS, LANES), f32)
    for p, source in enumerate(PIECES):
        gap = PADDED_Z + p % 2 * HALF
        shift = (source - gap) % LANES
        value = jnp.where(lane_range(source), pltpu.roll(carriers[p // 2], shift, 1), value)
    return value


def rows_of(carrier):
    return pl.ds(carrier, SLABS, stride=CARRIERS)


def block_at(ref, j, y):
    block = j * CY + y
    group, place = block // 4, block % 4
    if place < 3:
        return ref[rows_of(3 * group + place), :]
    return unpack_block([ref[rows_of(3 * group + c), :] for c in range(3)])


def prepare_kernel(
    where_ref, shear_ref, counts_ref, cells_ref, offsets_ref, charges_ref, dipoles_ref,
    atoms_ref, base_ref, taps_ref, cos_ref, sin_ref,
    count_ref, cell_ref, offset_ref, charge_ref, dipole_ref, semaphores
):
    copies = [
        fetch(source, target, semaphores.at[n])
        for n, (source, target) in enumerate(
            (
                (counts_ref, count_ref),
                (cells_ref, cell_ref),
                (offsets_ref, offset_ref),
                (charges_ref, charge_ref.at[0]),
                (dipoles_ref, dipole_ref),
            )
        )
    ]
    slab, pencil = where_ref[0], where_ref[1]
    first = pencil * PART_Z
    row = lax.broadcasted_iota(jnp.int32, (PADDED_Z, LANES), 0)
    mode = (row + first).astype(f32)
    base_ref[...] = mode[:8]
    for t in range(3):
        cos_t, sin_t = unit_phase(mode * (t + 0.5) * (1.0 / NZ))
        taps_ref[t] = jnp.where(row < PART_Z, cos_t, 0.0)
        taps_ref[3 + t] = jnp.where(row < PART_Z, sin_t, 0.0)
    column = lax.broadcasted_iota(jnp.int32, (1, LANES), 1)
    rows = jnp.where(column < CY, slab * CY + column, 1)
    index = lax.broadcasted_iota(jnp.int32, (NX, LANES), 0)
    folds = folded_mode(index)
    ticks = folds * (shear_ref[0] * rows)
    whole = jnp.floor(ticks.astype(f32) * (1.0 / (NX * NY))).astype(jnp.int32)
    rest = ticks - whole * (NX * NY)
    cos_t, sin_t = unit_phase(rest.astype(f32) * (1.0 / (NX * NY)))
    cos_ref[...] = cos_t
    sin_ref[...] = sin_t
    for copy in copies:
        copy.wait()
    slot = lax.broadcasted_iota(jnp.int32, (1, ATOM_DEV), 1)
    live = jnp.zeros((1, ATOM_DEV), f32)
    for b in range(ATOM_DEV // ATOM_BLK):
        inside = (slot >= b * ATOM_BLK) & (slot < b * ATOM_BLK + count_ref[b])
        live = jnp.where(inside, 1.0, live)
    atoms_ref[0:1, :] = cell_ref[0:1, :].astype(f32)
    atoms_ref[1:2, :] = (cell_ref[1:2, :] - slab * CY).astype(f32)
    atoms_ref[2:3, :] = cell_ref[2:3, :].astype(f32)
    atoms_ref[3:6, :] = offset_ref[...]
    atoms_ref[6:7, :] = charge_ref[...] * live
    atoms_ref[7:10, :] = dipole_ref[...] * live
    atoms_ref[10:11, :] = live
    atoms_ref[11:16, :] = jnp.zeros((5, ATOM_DEV), f32)


def spline_table(atoms_ref, table_ref, orders):
    def pencil_body(pencil, carry):
        tables = spline_rows(atoms_ref[pencil, 3:6, :])
        for o in range(orders):
            for t in range(6):
                table_ref[pencil, o * 6 + t, 0:3, :] = tables[o][t]
        return carry

    lax.fori_loop(0, PENCILS, pencil_body, 0)


def weight_rows(table_ref, pencil, lanes, dim, orders):
    row = slice(dim, dim + 1)
    return [[table_ref[pencil, o * 6 + t, row, lanes] for t in range(6)] for o in range(orders)]


def pair_place(pair):
    pencil = pair // PAIRS
    return pencil, pl.ds(pl.multiple_of(pair % PAIRS * LANES, LANES), LANES)


def pair_window(pair, own, where_ref):
    if own:
        return pl.multiple_of(pair * 32, 8), WINDOW, (pair * 32).astype(f32)
    place = pair * 32 + where_ref[2]
    place = jnp.where(place >= NX, place - NX, place)
    first = place // 8 * 8
    return pl.multiple_of(first, 8), WIDE, (pair * 32 - (place - first)).astype(f32)


def z_waves(cell_z, weights, base_ref, taps_ref):
    centre = cell_z + 2.5
    turn = base_ref[...] * centre
    turn = turn - 360.0 * jnp.floor(turn * (1.0 / 360.0))
    cos_k, sin_k = unit_phase(turn * (1.0 / 360.0))
    turn = 8.0 * centre
    turn = turn - 360.0 * jnp.floor(turn * (1.0 / 360.0))
    cos_8, sin_8 = unit_phase(jnp.broadcast_to(turn * (1.0 / 360.0), cos_k.shape))
    folded = [
        (
            [weight[2 - t] + weight[3 + t] for t in range(3)],
            [weight[3 + t] - weight[2 - t] for t in range(3)],
        )
        for weight in weights
    ]
    pieces = [[] for _ in weights]
    pieces_im = [[] for _ in weights]
    for q in range(PADDED_Z // 8):
        span = slice(q * 8, q * 8 + 8)
        cos_t = [taps_ref[t, span, :] for t in range(3)]
        sin_t = [taps_ref[3 + t, span, :] for t in range(3)]
        for s, (even, odd) in enumerate(folded):
            real = even[0] * cos_t[0] + even[1] * cos_t[1] + even[2] * cos_t[2]
            imag = odd[0] * sin_t[0] + odd[1] * sin_t[1] + odd[2] * sin_t[2]
            pieces[s].append(real * cos_k - imag * sin_k)
            pieces_im[s].append(-(real * sin_k + imag * cos_k))
        cos_k, sin_k = cos_k * cos_8 - sin_k * sin_8, sin_k * cos_8 + cos_k * sin_8
    return [
        (jnp.concatenate(re, axis=0), jnp.concatenate(im, axis=0))
        for re, im in zip(pieces, pieces_im)
    ]


def sampling_weights(start, some_ref, table_ref, base_ref, taps_ref, waves_ref, rows_ref):
    spline_table(some_ref, table_ref, 3)

    def pair_body(pair, carry):
        pencil, lanes = pair_place(pair)
        for dim in range(2):
            for o, taps in enumerate(weight_rows(table_ref, pencil, lanes, dim, 3)):
                for t in range(6):
                    row = (dim * 3 + o) * 6 + t
                    rows_ref[start + pair, row : row + 1, :] = taps[t]
        weights = weight_rows(table_ref, pencil, lanes, 2, 3)
        waves = z_waves(some_ref[pencil, 2:3, lanes], weights, base_ref, taps_ref)
        for s, (re, im) in enumerate(waves):
            re, im = halves(re), halves(im)
            columns = slice(s * LANES, (s + 1) * LANES)
            for n in range(2):
                waves_ref[start + pair, n, :PADDED_Z, columns] = re[n]
                waves_ref[start + pair, n, PADDED_Z:, columns] = im[n]
        return carry

    lax.fori_loop(0, PENCILS * PAIRS, pair_body, 0, unroll=2)


def spread_kernel(own, *refs):
    atoms_ref, where_ref, base_ref, taps_ref = refs[:4]
    if own:
        grid_ref, weights_ref = refs[4:]
        grid_ref[...] = jnp.zeros_like(grid_ref)
    else:
        _, tables_ref, cos_ref, sin_ref, grid_ref, out_ref = refs[4:10]
        table_ref, weights_ref, semaphore = refs[10:]
        table_copy = fetch(tables_ref, table_ref, semaphore)
    rows = list(range(CY)) if own else list(range(CY, 2 * CY - 1))
    part = CY * LANES
    gap = jnp.zeros((HALF - PADDED_Z, LANES), bf16)
    spline_table(atoms_ref, weights_ref, 2)

    def pair_body(pair, carry):
        pencil, lanes = pair_place(pair)
        row = [atoms_ref[pencil, a : a + 1, lanes] for a in range(10)]
        charge, dip_x, dip_y, dip_z = row[6:10]
        first_row, window, origin = pair_window(pair, own, where_ref)
        dense_x = dense_rows(
            weight_rows(weights_ref, pencil, lanes, 0, 2), row[0] - origin, window
        )
        dense_y = dense_rows(weight_rows(weights_ref, pencil, lanes, 1, 2), row[1], 16)
        value, first = weight_rows(weights_ref, pencil, lanes, 2, 2)
        mixed = [charge * value[t] + dip_z * first[t] for t in range(6)]
        right = []
        for re, im in z_waves(row[2], (mixed, value), base_ref, taps_ref):
            re, im = halves(re), halves(im)
            right.append(
                [
                    jnp.concatenate([re[n], gap, im[n], gap, im[n], gap, -re[n], gap], axis=0)
                    for n in range(2)
                ]
            )
        high, low = [jnp.concatenate([right[0][n], right[1][n]], axis=1) for n in range(2)]
        right = jnp.concatenate([high, low, high], axis=1)
        left = []
        for r in rows:
            value, first = dense_y[0][r : r + 1], dense_y[1][r : r + 1]
            left.append(
                jnp.concatenate(
                    [
                        value * dense_x[0],
                        (dip_x * value) * dense_x[1] + (dip_y * first) * dense_x[0],
                    ],
                    axis=1,
                )
            )
        high, low = halves(jnp.concatenate(left, axis=0))
        left = jnp.concatenate([high, high, low], axis=1)
        added = lax.dot_general(
            left, right, (((1,), (1,)), ((), ())), preferred_element_type=f32
        )
        at = pl.ds(first_row, window)
        for n in range(len(rows)):
            piece = added[n * window : (n + 1) * window]
            grid_ref[at, n * LANES : (n + 1) * LANES] += piece[:, :LANES]
            grid_ref[at, part + n * LANES : part + (n + 1) * LANES] += piece[:, LANES:]
        return carry

    lax.fori_loop(0, PENCILS * PAIRS, pair_body, 0, unroll=12)
    if own:
        return
    grid_ref[0:WIDE] += grid_ref[NX:EXTENDED]
    table_copy.wait()
    sign = lane_sign((NX, LANES))
    twist = Twist(cos_ref, sin_ref)
    totals = []
    for first in range(0, CY, 2):
        lanes = slice(first * LANES, (first + 2) * LANES)
        below = slice(part + lanes.start, part + lanes.stop)
        line = jnp.concatenate(
            forward_line(
                table_ref, quarters_of(grid_ref[:NX, lanes]), quarters_of(grid_ref[:NX, below])
            ),
            axis=0,
        )
        for n, y in enumerate((first, first + 1)):
            one = line[:, n * LANES : (n + 1) * LANES]
            cos_y, sin_y = twist.at(y)
            totals.append(one * cos_y + turned(one, sign) * sin_y)
    for group in range(GROUPS):
        blocks = []
        for block in range(4 * group, 4 * group + 4):
            j, y = block // CY, block % CY
            blocks.append(totals[y][j * SLABS : (j + 1) * SLABS])
        for c, carrier in enumerate(pack_blocks(blocks)):
            out_ref[rows_of(3 * group + c), :] = carrier


def spline_modulus(turns):
    cosine, _ = unit_phase(turns)
    return (64.0 + 52.0 * cosine + 4.0 * cosine * cosine) * (1.0 / 120.0)


def folded_mode(row):
    residue = (
        (row >= QUARTER).astype(jnp.int32)
        + (row >= 2 * QUARTER).astype(jnp.int32)
        + (row >= 3 * QUARTER).astype(jnp.int32)
    )
    mode = 4 * (row - QUARTER * residue) + residue
    return jnp.where(mode < NX // 2, mode, mode - NX)


def make_green(where_ref, out_ref):
    slab, pencil, shear = where_ref[0], where_ref[1], where_ref[3].astype(f32)
    decay = (math.pi / screening) ** 2
    column = lax.broadcasted_iota(jnp.int32, (1, LANES), 1)
    own_x = folded_mode(jnp.minimum(column, PART_X) * SLABS + slab)
    own_y = folded_mode(lax.broadcasted_iota(jnp.int32, (NY, LANES), 0))
    float_x = own_x.astype(f32)
    wave_y = own_y.astype(f32) + float_x * shear * (1.0 / NX)
    part_x, part_y = float_x * (1.0 / NX), wave_y * (1.0 / NY)
    norm = part_x * part_x + part_y * part_y
    moduli = spline_modulus(part_x) * spline_modulus(part_y)
    top = jnp.exp(-decay * norm) / (math.pi * moduli * moduli)
    top = jnp.where((own_x == -(NX // 2)) | (own_y == -(NY // 2)), 0.0, top)
    lane = jnp.where(column < HALF, column, column - HALF)
    mode = pencil * PART_Z + lane
    part_z = mode.astype(f32) * (1.0 / NZ)
    modulus = spline_modulus(part_z)
    norm_z = part_z * part_z
    twice = jnp.where(mode == 0, 1.0, 2.0) * (1.0 / (NX * NY * NZ))
    mode_top = jnp.where(
        lane < PART_Z, twice * jnp.exp(-decay * norm_z) / (modulus * modulus), 0.0
    )
    mode_norm = jnp.where(lane < PART_Z, norm_z, 1.0)
    for j in range(PART_X):
        square = norm[:, j : j + 1] + mode_norm
        green = top[:, j : j + 1] * mode_top / jnp.where(square == 0.0, 1.0, square)
        out_ref[:, j * LANES : (j + 1) * LANES] = jnp.where(square == 0.0, 0.0, green)


def weights_kernel(
    where_ref, atoms_ref, below_ref, base_ref, taps_ref, tables_ref, backs_ref, *refs
):
    results, (green_ref, table_ref, back_ref), kept = refs[:2], refs[2:5], refs[5:7]
    weights_ref, semaphores = refs[7:]
    copies = [
        fetch(tables_ref, table_ref, semaphores.at[6]),
        fetch(backs_ref, back_ref, semaphores.at[7]),
    ]
    make_green(where_ref, green_ref)
    pairs = PENCILS * PAIRS
    for own, some_ref in ((True, atoms_ref), (False, below_ref)):
        start = 0 if own else pairs
        sampling_weights(start, some_ref, weights_ref, base_ref, taps_ref, *kept)
        some = pl.ds(start, pairs)
        for n in range(2):
            semaphore = semaphores.at[n if own else 2 + n]
            copies.append(fetch(kept[n].at[some], results[n].at[some], semaphore))
    for copy in copies:
        copy.wait()


def filter_kernel(in_ref, table_ref, back_ref, green_ref, out_ref):
    sign = lane_sign((NY, LANES))
    energy = jnp.zeros((8, LANES), f32)
    blocks = []
    for first in range(0, PART_X, 2):
        lines = []
        for j in (first, first + 1):
            found = [block_at(in_ref, j, y) for y in range(CY)]
            lines.append(
                jnp.concatenate(
                    [one[16 * part : 16 * part + 16] for part in range(4) for one in found], axis=0
                )
            )
        swapped = jnp.concatenate([turned(one, sign) for one in lines], axis=1)
        lines = jnp.concatenate(lines, axis=1)
        spectrum = jnp.concatenate(
            forward_line(table_ref, quarters_of(lines), quarters_of(swapped)), axis=0
        )
        modes = []
        for n in range(2):
            j = first + n
            one = spectrum[:, n * LANES : (n + 1) * LANES]
            scaled = green_ref[:, j * LANES : (j + 1) * LANES] * one
            share = scaled * one
            energy = energy + sum(share[8 * i : 8 * i + 8] for i in range(NY // 8))
            modes.append(scaled)
        swapped = jnp.concatenate([turned(one, sign) for one in modes], axis=1)
        modes = jnp.concatenate(modes, axis=1)
        parts = inverse_line(back_ref, quarters_of(modes), quarters_of(swapped))
        for n in range(2):
            for y in range(CY):
                blocks.append(
                    jnp.concatenate(
                        [
                            one[16 * y : 16 * y + 16, n * LANES : (n + 1) * LANES]
                            for one in parts
                        ],
                        axis=0,
                    )
                )
        for group in range(first * CY // 4, (first + 2) * CY // 4):
            for c, carrier in enumerate(pack_blocks(blocks[4 * group : 4 * group + 4])):
                out_ref[rows_of(3 * group + c), :] = carrier
    lane = lax.broadcasted_iota(jnp.int32, (SLABS, LANES), 1)
    share = 0.5 * jnp.sum(energy)
    out_ref[rows_of(0), :] = jnp.where(lane == PART_Z, share, out_ref[rows_of(0), :])


def sample_kernel(own, *refs):
    if own:
        atoms_ref, where_ref, waves_ref, rows_ref, grid_ref, out_ref = refs
    else:
        atoms_ref, where_ref = refs[:2]
        kept = refs[2:4]
        in_ref, cos_ref, sin_ref, tables_ref, out_ref, grid_ref = refs[4:10]
        slab_weights, below_weights = refs[10:12], refs[12:14]
        waves_ref, rows_ref = below_weights
        table_ref, semaphores = refs[14:]
        table_copy = fetch(tables_ref, table_ref, semaphores.at[6])
        pairs = PENCILS * PAIRS
        copies = [
            fetch(source.at[pl.ds(start, pairs)], target, semaphores.at[n])
            for n, (source, start, target) in enumerate(
                [(kept[n], pairs, below_weights[n]) for n in range(2)]
                + [(kept[n], 0, slab_weights[n]) for n in range(2)]
            )
        ]
    rows = list(range(CY)) if own else list(range(CY, 2 * CY - 1))
    energy = 0.0
    if not own:
        sign = lane_sign((NX, LANES))
        twist = Twist(cos_ref, sin_ref)
        for first in range(0, CY, 2):
            modes, swapped = [], []
            for y in range(first, first + 2):
                line = jnp.concatenate([block_at(in_ref, j, y) for j in range(PART_X)], axis=0)
                other = turned(line, sign)
                cos_y, sin_y = twist.at(y)
                modes.append(line * cos_y - other * sin_y)
                swapped.append(other * cos_y + line * sin_y)
            swapped = jnp.concatenate(swapped, axis=1)
            modes = jnp.concatenate(modes, axis=1)
            if first == 0:
                table_copy.wait()
            cells = jnp.concatenate(
                inverse_line(table_ref, quarters_of(modes), quarters_of(swapped)), axis=0
            )
            lanes = slice(first * LANES, (first + 2) * LANES)
            grid_ref[:NX, lanes] = cells
            grid_ref[NX:, lanes] = cells[:WIDE]
        lane = lax.broadcasted_iota(jnp.int32, (SLABS, LANES), 1)
        energy = jnp.sum(jnp.where(lane == PART_Z, in_ref[rows_of(0), :], 0.0))
    gap = jnp.zeros((HALF - PADDED_Z, 3 * LANES), bf16)

    if not own:
        for copy in copies[:2]:
            copy.wait()

    def pair_body(pair, carry):
        pencil, lanes = pair_place(pair)
        waves = [
            jnp.concatenate(
                [waves_ref[pair, n, :PADDED_Z], gap, waves_ref[pair, n, PADDED_Z:], gap],
                axis=0,
            )
            for n in range(2)
        ]
        first_row, window, origin = pair_window(pair, own, where_ref)
        at = pl.ds(first_row, window)
        cells = jnp.concatenate(
            [grid_ref[at, n * LANES : (n + 1) * LANES] for n in range(len(rows))], axis=0
        )
        read = product(halves(cells), waves)
        rows_x, rows_y = [
            [
                [rows_ref[pair, row + t : row + t + 1, :] for t in range(6)]
                for row in range(dim * 18, dim * 18 + 18, 6)
            ]
            for dim in range(2)
        ]
        dense_x = dense_rows(rows_x, atoms_ref[pencil, 0:1, lanes] - origin, window)
        dense_y = dense_rows(rows_y, atoms_ref[pencil, 1:2, lanes], 16)
        lined = {}
        for order_y, order_z in ((0, 0), (1, 0), (2, 0), (0, 1), (1, 1), (0, 2)):
            lined[order_y, order_z] = sum(
                dense_y[order_y][r : r + 1]
                * read[n * window : (n + 1) * window, order_z * LANES : (order_z + 1) * LANES]
                for n, r in enumerate(rows)
            )

        def sampled(p, r, s):
            return jnp.sum(dense_x[p] * lined[r, s], axis=0, keepdims=True)

        charge, dip_x, dip_y, dip_z, live = [
            atoms_ref[pencil, a : a + 1, lanes] for a in range(6, 11)
        ]
        s100 = sampled(1, 0, 0)
        s010 = sampled(0, 1, 0)
        s001 = sampled(0, 0, 1)
        s110 = sampled(1, 1, 0)
        s101 = sampled(1, 0, 1)
        s011 = sampled(0, 1, 1)
        out = [
            live * sampled(0, 0, 0),
            live * s100,
            live * s010,
            live * s001,
            charge * s100 + dip_x * sampled(2, 0, 0) + dip_y * s110 + dip_z * s101,
            charge * s010 + dip_x * s110 + dip_y * sampled(0, 2, 0) + dip_z * s011,
            charge * s001 + dip_x * s101 + dip_y * s011 + dip_z * sampled(0, 0, 2),
            jnp.full(live.shape, energy, f32),
        ]
        ahead = lax.rem(pencil - where_ref[1] + PENCILS, PENCILS)
        out_ref[ahead, :, lanes] = jnp.concatenate(out, axis=0)
        return carry

    lax.fori_loop(0, PENCILS * PAIRS, pair_body, 0, unroll=12)
    if not own:
        for copy in copies[2:]:
            copy.wait()


def finish_kernel(
    own_ref, one_ref, two_ref, three_ref, charge_ref, dipole_ref, position_ref, energy_ref
):
    total = (own_ref[...] + one_ref[...]) + (two_ref[...] + three_ref[...])
    charge_ref[...] = total[0]
    dipole_ref[...] = total[1:4]
    position_ref[...] = total[4:7]
    energy_ref[...] = total[7:8, 0:1]


SPACES = {"v": pltpu.VMEM, "h": pltpu.HBM, "s": pltpu.SMEM}
WORK = {"flops": 1_000_000_000, "bytes_accessed": 8_000_000}


def out_place(shape):
    pinned = isinstance(shape, type(pltpu.HBM((8, LANES), f32)))
    return pl.BlockSpec(memory_space=pltpu.HBM if pinned else pltpu.VMEM)


def call(kernel, inputs, out_shape, scratch=(), aliases=()):
    def run(*operands):
        placed = [
            pltpu.with_memory_space_constraint(one, pltpu.HBM) if where == "h" else one
            for one, where in zip(operands, inputs)
        ]
        return pl.pallas_call(
            kernel,
            out_shape=out_shape,
            in_specs=[pl.BlockSpec(memory_space=SPACES[one]) for one in inputs],
            out_specs=jax.tree.map(out_place, out_shape),
            scratch_shapes=list(scratch),
            input_output_aliases=dict(aliases),
            compiler_params=pltpu.CompilerParams(vmem_limit_bytes=28 * 1024 * 1024),
            cost_estimate=pl.CostEstimate(transcendentals=0, **WORK),
        )(*placed)

    return run


def next_slab(value, back=False):
    step = -1 if back else 1
    return lax.ppermute(value, "gy", [(i, (i + step) % SLABS) for i in range(SLABS)])


def swap_slabs(lines):
    lines = lines.reshape(SLABS, CARRIERS, 1, LANES)
    lines = lax.all_to_all(lines, "gy", split_axis=0, concat_axis=0, tiled=True)
    return lines.reshape(SLABS * CARRIERS, LANES)


def on_device(cell_index, offsets, charges, dipoles, block_count, shear_cells):
    pencil_index = lax.axis_index("gx")
    slab_index = lax.axis_index("gy")
    x_forward, x_inverse, y_forward, y_inverse = wave_tables()
    shape = jax.ShapeDtypeStruct
    shift = jnp.where(slab_index == 0, shear_cells[0], 0)
    where = jnp.stack([slab_index, pencil_index, shift, shear_cells[0]])

    mine, base, taps, cos_t, sin_t = call(
        prepare_kernel,
        "sshhhhh",
        (
            shape((16, ATOM_DEV), f32),
            shape((8, LANES), f32),
            shape((6, PADDED_Z, LANES), f32),
            shape((NX, LANES), f32),
            shape((NX, LANES), f32),
        ),
        [
            pltpu.SMEM(block_count.shape, jnp.int32),
            pltpu.VMEM((3, ATOM_DEV), jnp.int32),
            pltpu.VMEM((3, ATOM_DEV), f32),
            pltpu.VMEM((1, ATOM_DEV), f32),
            pltpu.VMEM((3, ATOM_DEV), f32),
            pltpu.SemaphoreType.DMA((5,)),
        ],
    )(
        where,
        shear_cells,
        block_count,
        cell_index,
        offsets,
        charges,
        dipoles,
    )
    atoms = lax.all_gather(mine, "gx", axis=0, tiled=False)
    below_atoms = next_slab(atoms)

    packed = shape((SLABS * CARRIERS, LANES), f32)
    table_space = pltpu.VMEM((NX, 6 * QUARTER), bf16)
    pairs = 2 * PENCILS * PAIRS
    held = [
        ((2, 2 * PADDED_Z, 3 * LANES), bf16),
        ((36, LANES), f32),
    ]
    weights_space = pltpu.VMEM((PENCILS, 18, 8, ATOM_DEV), f32)
    grid_shape = shape((EXTENDED, 2 * CY * LANES), f32)
    slab_grid = call(
        lambda *refs: spread_kernel(True, *refs),
        "vsvv",
        grid_shape,
        [weights_space],
    )(atoms, where, base, taps)
    green_shape = shape((NY, PART_X * LANES), f32)
    table_shape = shape((NX, 6 * QUARTER), bf16)
    _, lines = call(
        lambda *refs: spread_kernel(False, *refs),
        "vsvvvhvv",
        (grid_shape, packed),
        [table_space, weights_space, pltpu.SemaphoreType.DMA],
        ((4, 0),),
    )(below_atoms, where, base, taps, slab_grid, x_forward, cos_t, sin_t)
    lines, where, atoms, below_atoms = lax.optimization_barrier(
        (lines, where, atoms, below_atoms)
    )
    *weights, green, table, back = call(
        weights_kernel,
        "svvvvhh",
        (
            *(pltpu.HBM((pairs, *dims), kind) for dims, kind in held),
            green_shape,
            table_shape,
            table_shape,
        ),
        [
            *(pltpu.VMEM((pairs, *dims), kind) for dims, kind in held),
            weights_space,
            pltpu.SemaphoreType.DMA((8,)),
        ],
    )(where, atoms, below_atoms, base, taps, y_forward, y_inverse)
    lines = swap_slabs(lines)
    filtered = call(filter_kernel, "vvvv", packed)(lines, table, back, green)
    filtered = swap_slabs(filtered)
    shares_shape = shape((PENCILS, 8, ATOM_DEV), f32)
    below_shares, potential, *weights = call(
        lambda *refs: sample_kernel(False, *refs),
        "vshhvvvh",
        (
            shares_shape,
            shape((EXTENDED, CY * LANES), f32),
            *(shape((pairs // 2, *dims), kind) for dims, kind in held),
        ),
        [
            *(pltpu.VMEM((pairs // 2, *dims), kind) for dims, kind in held),
            table_space,
            pltpu.SemaphoreType.DMA((7,)),
        ],
    )(below_atoms, where, *weights, filtered, cos_t, sin_t, x_inverse)
    below_shares = next_slab(below_shares, back=True)
    shares = call(lambda *refs: sample_kernel(True, *refs), "vsvvv", shares_shape)(
        atoms, where, *weights, potential
    )
    shares = shares + below_shares
    arrived = [
        lax.ppermute(shares[ahead], "gx", [(i, (i + ahead) % PENCILS) for i in range(PENCILS)])
        for ahead in range(1, PENCILS)
    ]
    charge_grad, dipole_grad, position_grad, energy = call(
        finish_kernel,
        "vvvv",
        (
            shape((ATOM_DEV,), f32),
            shape((3, ATOM_DEV), f32),
            shape((3, ATOM_DEV), f32),
            shape((1, 1), f32),
        ),
    )(shares[0], *arrived)
    return charge_grad, dipole_grad, position_grad, energy[0]


def solution(mesh):
    placed = (
        P(None, ("gy", "gx")),
        P(None, ("gy", "gx")),
        P(("gy", "gx")),
        P(None, ("gy", "gx")),
        P(("gy", "gx")),
        P(),
    )
    return jax.shard_map(
        on_device,
        mesh=mesh,
        in_specs=placed,
        out_specs=(P(("gy", "gx")), P(None, ("gy", "gx")), P(None, ("gy", "gx")), P()),
        check_vma=False,
    )
```

```python
import math

import jax
import jax.numpy as jnp
import ml_dtypes
import numpy as np
from jax import lax
from jax.experimental import pallas as pl
from jax.experimental.pallas import tpu as pltpu
from jax.sharding import PartitionSpec as P

NX = 384
NY = 384
NZ = 360
CY = 6
CX = 96
PENCILS = 4
SLABS = 64
PART_X = 6
PART_Z = 45
ATOM_BLK = 64
ATOM_DEV = 384
PAIRS = 3
WINDOW = 40
WIDE = 48
EXTENDED = NX + WIDE
HALF = 64
LANES = 128
PADDED_Z = 48
QUARTER = 96
screening = 0.9
f32 = jnp.float32
bf16 = jnp.bfloat16


def split_table(table):
    high = table.astype(ml_dtypes.bfloat16)
    low = (table - high.astype(np.float64)).astype(ml_dtypes.bfloat16)
    return np.concatenate([high, high, low], axis=1)


def wave_tables():
    quarter = np.arange(QUARTER)
    mode = np.arange(4)[:, None] + 4 * quarter[None, :]
    row_y = CY * (quarter % 16) + quarter // 16
    tables = []
    for place in (quarter, row_y):
        ticks = mode[:, :, None] * place % NX
        for table in (ticks, ticks.transpose(0, 2, 1)):
            angle = 2.0 * np.pi / NX * table.reshape(NX, QUARTER)
            tables.append(split_table(np.concatenate([np.cos(angle), np.sin(angle)], axis=1)))
    return tables


def spline_rows(fraction):
    levels = {2: [1.0 - fraction, fraction]}
    current = levels[2]
    for n in range(3, 7):
        inverse_n = 1.0 / (n - 1)
        updated = [None] * n
        updated[n - 1] = inverse_n * fraction * current[n - 2]
        for j in range(1, n - 1):
            updated[n - 1 - j] = inverse_n * (
                (fraction + j) * current[n - 2 - j] + (n - j - fraction) * current[n - 1 - j]
            )
        updated[0] = inverse_n * (1.0 - fraction) * current[0]
        current = updated
        levels[n] = current
    zero_row = jnp.zeros_like(fraction)

    def entry_at(values_list, k):
        return values_list[k] if 0 <= k < len(values_list) else zero_row

    first = [entry_at(levels[5], t - 1) - entry_at(levels[5], t) for t in range(6)]
    second = [
        entry_at(levels[4], t - 2) - 2.0 * entry_at(levels[4], t - 1) + entry_at(levels[4], t)
        for t in range(6)
    ]
    return levels[6], first, second


def dense_rows(tables, cell, length):
    away = lax.broadcasted_iota(jnp.int32, (length, cell.shape[1]), 0).astype(f32) - cell
    summed = [jnp.zeros(away.shape, f32) for _ in tables]
    for t in range(6):
        here = away == float(t)
        summed = [jnp.where(here, table[t], so_far) for table, so_far in zip(tables, summed)]
    return summed


def unit_phase(turns):
    turns = turns - jnp.floor(turns + 0.5)
    quarter = jnp.floor(4.0 * turns + 0.5)
    rest = turns - 0.25 * quarter
    theta = (2.0 * math.pi) * rest
    square = theta * theta
    sine = theta * (
        1.0
        + square
        * (-1.0 / 6 + square * (1.0 / 120 + square * (-1.0 / 5040 + square * (1.0 / 362880))))
    )
    cosine = 1.0 + square * (
        -0.5
        + square
        * (1.0 / 24 + square * (-1.0 / 720 + square * (1.0 / 40320 - square * (1.0 / 3628800))))
    )
    odd = jnp.abs(quarter) == 1.0
    cos_out = jnp.where(odd, sine, cosine)
    sin_out = jnp.where(odd, cosine, sine)
    cos_out = jnp.where((quarter == 1.0) | (jnp.abs(quarter) == 2.0), -cos_out, cos_out)
    sin_out = jnp.where((quarter == -1.0) | (jnp.abs(quarter) == 2.0), -sin_out, sin_out)
    return cos_out, sin_out


class Twist:
    def __init__(self, cos_ref, sin_ref):
        whole = (NX, LANES)
        self.cos = jnp.broadcast_to(cos_ref[:, 0:1], whole)
        self.sin = jnp.broadcast_to(sin_ref[:, 0:1], whole)
        self.cos_step = jnp.broadcast_to(cos_ref[:, CY : CY + 1], whole)
        self.sin_step = jnp.broadcast_to(sin_ref[:, CY : CY + 1], whole)
        self.row = 0

    def at(self, row):
        while self.row < row:
            self.cos, self.sin = (
                self.cos * self.cos_step - self.sin * self.sin_step,
                self.sin * self.cos_step + self.cos * self.sin_step,
            )
            self.row += 1
        return self.cos, self.sin


def halves(value):
    high = value.astype(bf16)
    return high, (value - high.astype(f32)).astype(bf16)


def joined(left, right):
    return (
        jnp.concatenate([left[0], left[0], left[1]], axis=1),
        jnp.concatenate([right[0], right[1], right[0]], axis=0),
    )


def product(left, right):
    left, right = joined(left, right)
    return jnp.dot(left, right, preferred_element_type=f32)


def product3(left, right):
    def one(a, b):
        return jnp.dot(a, b, preferred_element_type=f32)

    return one(left[0], right[0]) + (one(left[0], right[1]) + one(left[1], right[0]))


def lane_sign(shape):
    return jnp.where(lax.broadcasted_iota(jnp.int32, shape, 1) < HALF, 1.0, -1.0).astype(f32)


def turned(value, sign):
    return pltpu.roll(value, HALF, 1) * sign


def fetch(source, target, semaphore):
    copy = pltpu.make_async_copy(source, target, semaphore)
    copy.start()
    return copy


def line_product(table_ref, r, value):
    rows = slice(r * QUARTER, (r + 1) * QUARTER)
    table = table_ref[rows, : 2 * QUARTER], table_ref[rows, 4 * QUARTER :]
    return product3(table, halves(value))


def forward_line(table_ref, quarters, turned_quarters):
    g, h = quarters, turned_quarters
    a, b, c, d = g[0] + g[2], g[0] - g[2], g[1] + g[3], g[1] - g[3]
    ta, tb, tc, td = h[0] + h[2], h[0] - h[2], h[1] + h[3], h[1] - h[3]
    lines = []
    for r, (one, other) in enumerate(
        ((a + c, ta + tc), (b + td, tb - d), (a - c, ta - tc), (b - td, tb + d))
    ):
        stacked = jnp.concatenate([one, other], axis=0)
        lines.append(line_product(table_ref, r, stacked))
    return lines


def inverse_line(table_ref, modes, turned_modes):
    z = []
    for r in range(4):
        stacked = jnp.concatenate([modes[r], -turned_modes[r]], axis=0)
        z.append(line_product(table_ref, r, stacked))
    a, b, c, d = z[0] + z[2], z[0] - z[2], z[1] + z[3], z[1] - z[3]
    width = d.shape[1]
    sign = lane_sign((QUARTER, LANES))
    td = jnp.concatenate(
        [turned(d[:, n : n + LANES], sign) for n in range(0, width, LANES)], axis=1
    )
    return [a + c, b - td, a - c, b + td]


def quarters_of(value):
    return [value[r * QUARTER : (r + 1) * QUARTER] for r in range(4)]


PIECES = (0, 16, 32, 64, 80, 96)
GROUPS = PART_X * CY // 4
CARRIERS = 3 * GROUPS


def lane_range(first):
    lane = lax.broadcasted_iota(jnp.int32, (SLABS, LANES), 1)
    return (lane >= first) & (lane < first + 16)


def pack_blocks(blocks):
    carriers = []
    for c in range(3):
        value = blocks[c]
        for half in range(2):
            gap = PADDED_Z + half * HALF
            shift = (gap - PIECES[2 * c + half]) % LANES
            value = jnp.where(lane_range(gap), pltpu.roll(blocks[3], shift, 1), value)
        carriers.append(value)
    return carriers


def unpack_block(carriers):
    value = jnp.zeros((SLABS, LANES), f32)
    for p, source in enumerate(PIECES):
        gap = PADDED_Z + p % 2 * HALF
        shift = (source - gap) % LANES
        value = jnp.where(lane_range(source), pltpu.roll(carriers[p // 2], shift, 1), value)
    return value


def rows_of(carrier):
    return pl.ds(carrier, SLABS, stride=CARRIERS)


def block_at(ref, j, y):
    block = j * CY + y
    group, place = block // 4, block % 4
    if place < 3:
        return ref[rows_of(3 * group + place), :]
    return unpack_block([ref[rows_of(3 * group + c), :] for c in range(3)])


def prepare_kernel(
    where_ref, shear_ref, counts_ref, cells_ref, offsets_ref, charges_ref, dipoles_ref,
    atoms_ref, base_ref, taps_ref, cos_ref, sin_ref,
    count_ref, cell_ref, offset_ref, charge_ref, dipole_ref, semaphores
):
    copies = [
        fetch(source, target, semaphores.at[n])
        for n, (source, target) in enumerate(
            (
                (counts_ref, count_ref),
                (cells_ref, cell_ref),
                (offsets_ref, offset_ref),
                (charges_ref, charge_ref.at[0]),
                (dipoles_ref, dipole_ref),
            )
        )
    ]
    slab, pencil = where_ref[0], where_ref[1]
    first = pencil * PART_Z
    row = lax.broadcasted_iota(jnp.int32, (PADDED_Z, LANES), 0)
    mode = (row + first).astype(f32)
    base_ref[...] = mode[:8]
    for t in range(3):
        cos_t, sin_t = unit_phase(mode * (t + 0.5) * (1.0 / NZ))
        taps_ref[t] = jnp.where(row < PART_Z, cos_t, 0.0)
        taps_ref[3 + t] = jnp.where(row < PART_Z, sin_t, 0.0)
    column = lax.broadcasted_iota(jnp.int32, (1, LANES), 1)
    rows = jnp.where(column < CY, slab * CY + column, 1)
    index = lax.broadcasted_iota(jnp.int32, (NX, LANES), 0)
    folds = folded_mode(index)
    ticks = folds * (shear_ref[0] * rows)
    whole = jnp.floor(ticks.astype(f32) * (1.0 / (NX * NY))).astype(jnp.int32)
    rest = ticks - whole * (NX * NY)
    cos_t, sin_t = unit_phase(rest.astype(f32) * (1.0 / (NX * NY)))
    cos_ref[...] = cos_t
    sin_ref[...] = sin_t
    for copy in copies:
        copy.wait()
    slot = lax.broadcasted_iota(jnp.int32, (1, ATOM_DEV), 1)
    live = jnp.zeros((1, ATOM_DEV), f32)
    for b in range(ATOM_DEV // ATOM_BLK):
        inside = (slot >= b * ATOM_BLK) & (slot < b * ATOM_BLK + count_ref[b])
        live = jnp.where(inside, 1.0, live)
    atoms_ref[0:1, :] = cell_ref[0:1, :].astype(f32)
    atoms_ref[1:2, :] = (cell_ref[1:2, :] - slab * CY).astype(f32)
    atoms_ref[2:3, :] = cell_ref[2:3, :].astype(f32)
    atoms_ref[3:6, :] = offset_ref[...]
    atoms_ref[6:7, :] = charge_ref[...] * live
    atoms_ref[7:10, :] = dipole_ref[...] * live
    atoms_ref[10:11, :] = live
    atoms_ref[11:16, :] = jnp.zeros((5, ATOM_DEV), f32)


def spline_table(atoms_ref, table_ref, orders):
    def pencil_body(pencil, carry):
        tables = spline_rows(atoms_ref[pencil, 3:6, :])
        for o in range(orders):
            for t in range(6):
                table_ref[pencil, o * 6 + t, 0:3, :] = tables[o][t]
        return carry

    lax.fori_loop(0, PENCILS, pencil_body, 0)


def weight_rows(table_ref, pencil, lanes, dim, orders):
    row = slice(dim, dim + 1)
    return [[table_ref[pencil, o * 6 + t, row, lanes] for t in range(6)] for o in range(orders)]


def pair_place(pair):
    pencil = pair // PAIRS
    return pencil, pl.ds(pl.multiple_of(pair % PAIRS * LANES, LANES), LANES)


def pair_window(pair, own, where_ref):
    if own:
        return pl.multiple_of(pair * 32, 8), WINDOW, (pair * 32).astype(f32)
    place = pair * 32 + where_ref[2]
    place = jnp.where(place >= NX, place - NX, place)
    first = place // 8 * 8
    return pl.multiple_of(first, 8), WIDE, (pair * 32 - (place - first)).astype(f32)


def z_waves(cell_z, weights, base_ref, taps_ref):
    centre = cell_z + 2.5
    turn = base_ref[...] * centre
    turn = turn - 360.0 * jnp.floor(turn * (1.0 / 360.0))
    cos_k, sin_k = unit_phase(turn * (1.0 / 360.0))
    turn = 8.0 * centre
    turn = turn - 360.0 * jnp.floor(turn * (1.0 / 360.0))
    cos_8, sin_8 = unit_phase(jnp.broadcast_to(turn * (1.0 / 360.0), cos_k.shape))
    folded = [
        (
            [weight[2 - t] + weight[3 + t] for t in range(3)],
            [weight[3 + t] - weight[2 - t] for t in range(3)],
        )
        for weight in weights
    ]
    pieces = [[] for _ in weights]
    pieces_im = [[] for _ in weights]
    for q in range(PADDED_Z // 8):
        span = slice(q * 8, q * 8 + 8)
        cos_t = [taps_ref[t, span, :] for t in range(3)]
        sin_t = [taps_ref[3 + t, span, :] for t in range(3)]
        for s, (even, odd) in enumerate(folded):
            real = even[0] * cos_t[0] + even[1] * cos_t[1] + even[2] * cos_t[2]
            imag = odd[0] * sin_t[0] + odd[1] * sin_t[1] + odd[2] * sin_t[2]
            pieces[s].append(real * cos_k - imag * sin_k)
            pieces_im[s].append(-(real * sin_k + imag * cos_k))
        cos_k, sin_k = cos_k * cos_8 - sin_k * sin_8, sin_k * cos_8 + cos_k * sin_8
    return [
        (jnp.concatenate(re, axis=0), jnp.concatenate(im, axis=0))
        for re, im in zip(pieces, pieces_im)
    ]


def sampling_weights(start, some_ref, table_ref, base_ref, taps_ref, waves_ref, rows_ref):
    spline_table(some_ref, table_ref, 3)

    def pair_body(pair, carry):
        pencil, lanes = pair_place(pair)
        for dim in range(2):
            for o, taps in enumerate(weight_rows(table_ref, pencil, lanes, dim, 3)):
                for t in range(6):
                    row = (dim * 3 + o) * 6 + t
                    rows_ref[start + pair, row : row + 1, :] = taps[t]
        weights = weight_rows(table_ref, pencil, lanes, 2, 3)
        waves = z_waves(some_ref[pencil, 2:3, lanes], weights, base_ref, taps_ref)
        for s, (re, im) in enumerate(waves):
            re, im = halves(re), halves(im)
            columns = slice(s * LANES, (s + 1) * LANES)
            for n in range(2):
                waves_ref[start + pair, n, :PADDED_Z, columns] = re[n]
                waves_ref[start + pair, n, PADDED_Z:, columns] = im[n]
        return carry

    lax.fori_loop(0, PENCILS * PAIRS, pair_body, 0, unroll=2)


def spread_kernel(own, *refs):
    atoms_ref, where_ref, base_ref, taps_ref = refs[:4]
    if own:
        grid_ref, weights_ref = refs[4:]
        grid_ref[...] = jnp.zeros_like(grid_ref)
    else:
        _, tables_ref, cos_ref, sin_ref, grid_ref, out_ref = refs[4:10]
        table_ref, weights_ref, semaphore = refs[10:]
        table_copy = fetch(tables_ref, table_ref, semaphore)
    rows = list(range(CY)) if own else list(range(CY, 2 * CY - 1))
    part = CY * LANES
    gap = jnp.zeros((HALF - PADDED_Z, LANES), bf16)
    spline_table(atoms_ref, weights_ref, 2)

    def pair_body(pair, carry):
        pencil, lanes = pair_place(pair)
        row = [atoms_ref[pencil, a : a + 1, lanes] for a in range(10)]
        charge, dip_x, dip_y, dip_z = row[6:10]
        first_row, window, origin = pair_window(pair, own, where_ref)
        dense_x = dense_rows(
            weight_rows(weights_ref, pencil, lanes, 0, 2), row[0] - origin, window
        )
        dense_y = dense_rows(weight_rows(weights_ref, pencil, lanes, 1, 2), row[1], 16)
        value, first = weight_rows(weights_ref, pencil, lanes, 2, 2)
        mixed = [charge * value[t] + dip_z * first[t] for t in range(6)]
        right = []
        for re, im in z_waves(row[2], (mixed, value), base_ref, taps_ref):
            re, im = halves(re), halves(im)
            right.append(
                [
                    jnp.concatenate([re[n], gap, im[n], gap, im[n], gap, -re[n], gap], axis=0)
                    for n in range(2)
                ]
            )
        high, low = [jnp.concatenate([right[0][n], right[1][n]], axis=1) for n in range(2)]
        right = jnp.concatenate([high, low, high], axis=1)
        left = []
        for r in rows:
            value, first = dense_y[0][r : r + 1], dense_y[1][r : r + 1]
            left.append(
                jnp.concatenate(
                    [
                        value * dense_x[0],
                        (dip_x * value) * dense_x[1] + (dip_y * first) * dense_x[0],
                    ],
                    axis=1,
                )
            )
        high, low = halves(jnp.concatenate(left, axis=0))
        left = jnp.concatenate([high, high, low], axis=1)
        added = lax.dot_general(
            left, right, (((1,), (1,)), ((), ())), preferred_element_type=f32
        )
        at = pl.ds(first_row, window)
        for n in range(len(rows)):
            piece = added[n * window : (n + 1) * window]
            grid_ref[at, n * LANES : (n + 1) * LANES] += piece[:, :LANES]
            grid_ref[at, part + n * LANES : part + (n + 1) * LANES] += piece[:, LANES:]
        return carry

    lax.fori_loop(0, PENCILS * PAIRS, pair_body, 0, unroll=12)
    if own:
        return
    grid_ref[0:WIDE] += grid_ref[NX:EXTENDED]
    table_copy.wait()
    sign = lane_sign((NX, LANES))
    twist = Twist(cos_ref, sin_ref)
    totals = []
    for first in range(0, CY, 2):
        lanes = slice(first * LANES, (first + 2) * LANES)
        below = slice(part + lanes.start, part + lanes.stop)
        line = jnp.concatenate(
            forward_line(
                table_ref, quarters_of(grid_ref[:NX, lanes]), quarters_of(grid_ref[:NX, below])
            ),
            axis=0,
        )
        for n, y in enumerate((first, first + 1)):
            one = line[:, n * LANES : (n + 1) * LANES]
            cos_y, sin_y = twist.at(y)
            totals.append(one * cos_y + turned(one, sign) * sin_y)
    for group in range(GROUPS):
        blocks = []
        for block in range(4 * group, 4 * group + 4):
            j, y = block // CY, block % CY
            blocks.append(totals[y][j * SLABS : (j + 1) * SLABS])
        for c, carrier in enumerate(pack_blocks(blocks)):
            out_ref[rows_of(3 * group + c), :] = carrier


def spline_modulus(turns):
    cosine, _ = unit_phase(turns)
    return (64.0 + 52.0 * cosine + 4.0 * cosine * cosine) * (1.0 / 120.0)


def folded_mode(row):
    residue = (
        (row >= QUARTER).astype(jnp.int32)
        + (row >= 2 * QUARTER).astype(jnp.int32)
        + (row >= 3 * QUARTER).astype(jnp.int32)
    )
    mode = 4 * (row - QUARTER * residue) + residue
    return jnp.where(mode < NX // 2, mode, mode - NX)


def make_green(where_ref, out_ref):
    slab, pencil, shear = where_ref[0], where_ref[1], where_ref[3].astype(f32)
    decay = (math.pi / screening) ** 2
    column = lax.broadcasted_iota(jnp.int32, (1, LANES), 1)
    own_x = folded_mode(jnp.minimum(column, PART_X) * SLABS + slab)
    own_y = folded_mode(lax.broadcasted_iota(jnp.int32, (NY, LANES), 0))
    float_x = own_x.astype(f32)
    wave_y = own_y.astype(f32) + float_x * shear * (1.0 / NX)
    part_x, part_y = float_x * (1.0 / NX), wave_y * (1.0 / NY)
    norm = part_x * part_x + part_y * part_y
    moduli = spline_modulus(part_x) * spline_modulus(part_y)
    top = jnp.exp(-decay * norm) / (math.pi * moduli * moduli)
    top = jnp.where((own_x == -(NX // 2)) | (own_y == -(NY // 2)), 0.0, top)
    lane = jnp.where(column < HALF, column, column - HALF)
    mode = pencil * PART_Z + lane
    part_z = mode.astype(f32) * (1.0 / NZ)
    modulus = spline_modulus(part_z)
    norm_z = part_z * part_z
    twice = jnp.where(mode == 0, 1.0, 2.0) * (1.0 / (NX * NY * NZ))
    mode_top = jnp.where(
        lane < PART_Z, twice * jnp.exp(-decay * norm_z) / (modulus * modulus), 0.0
    )
    mode_norm = jnp.where(lane < PART_Z, norm_z, 1.0)
    for j in range(PART_X):
        square = norm[:, j : j + 1] + mode_norm
        green = top[:, j : j + 1] * mode_top / jnp.where(square == 0.0, 1.0, square)
        out_ref[:, j * LANES : (j + 1) * LANES] = jnp.where(square == 0.0, 0.0, green)


def weights_kernel(
    where_ref, atoms_ref, below_ref, base_ref, taps_ref, tables_ref, backs_ref, *refs
):
    results, (green_ref, table_ref, back_ref), kept = refs[:2], refs[2:5], refs[5:7]
    weights_ref, semaphores = refs[7:]
    copies = [
        fetch(tables_ref, table_ref, semaphores.at[6]),
        fetch(backs_ref, back_ref, semaphores.at[7]),
    ]
    make_green(where_ref, green_ref)
    pairs = PENCILS * PAIRS
    for own, some_ref in ((True, atoms_ref), (False, below_ref)):
        start = 0 if own else pairs
        sampling_weights(start, some_ref, weights_ref, base_ref, taps_ref, *kept)
        some = pl.ds(start, pairs)
        for n in range(2):
            semaphore = semaphores.at[n if own else 2 + n]
            copies.append(fetch(kept[n].at[some], results[n].at[some], semaphore))
    for copy in copies:
        copy.wait()


def filter_kernel(in_ref, table_ref, back_ref, green_ref, out_ref):
    sign = lane_sign((NY, LANES))
    energy = jnp.zeros((8, LANES), f32)
    blocks = []
    for first in range(0, PART_X, 2):
        lines = []
        for j in (first, first + 1):
            found = [block_at(in_ref, j, y) for y in range(CY)]
            lines.append(
                jnp.concatenate(
                    [one[16 * part : 16 * part + 16] for part in range(4) for one in found], axis=0
                )
            )
        swapped = jnp.concatenate([turned(one, sign) for one in lines], axis=1)
        lines = jnp.concatenate(lines, axis=1)
        spectrum = jnp.concatenate(
            forward_line(table_ref, quarters_of(lines), quarters_of(swapped)), axis=0
        )
        modes = []
        for n in range(2):
            j = first + n
            one = spectrum[:, n * LANES : (n + 1) * LANES]
            scaled = green_ref[:, j * LANES : (j + 1) * LANES] * one
            share = scaled * one
            energy = energy + sum(share[8 * i : 8 * i + 8] for i in range(NY // 8))
            modes.append(scaled)
        swapped = jnp.concatenate([turned(one, sign) for one in modes], axis=1)
        modes = jnp.concatenate(modes, axis=1)
        parts = inverse_line(back_ref, quarters_of(modes), quarters_of(swapped))
        for n in range(2):
            for y in range(CY):
                blocks.append(
                    jnp.concatenate(
                        [
                            one[16 * y : 16 * y + 16, n * LANES : (n + 1) * LANES]
                            for one in parts
                        ],
                        axis=0,
                    )
                )
        for group in range(first * CY // 4, (first + 2) * CY // 4):
            for c, carrier in enumerate(pack_blocks(blocks[4 * group : 4 * group + 4])):
                out_ref[rows_of(3 * group + c), :] = carrier
    lane = lax.broadcasted_iota(jnp.int32, (SLABS, LANES), 1)
    share = 0.5 * jnp.sum(energy)
    out_ref[rows_of(0), :] = jnp.where(lane == PART_Z, share, out_ref[rows_of(0), :])


def sample_kernel(own, *refs):
    if own:
        atoms_ref, where_ref, waves_ref, rows_ref, grid_ref, out_ref = refs
    else:
        atoms_ref, where_ref = refs[:2]
        kept = refs[2:4]
        in_ref, cos_ref, sin_ref, tables_ref, out_ref, grid_ref = refs[4:10]
        slab_weights, below_weights = refs[10:12], refs[12:14]
        waves_ref, rows_ref = below_weights
        table_ref, semaphores = refs[14:]
        table_copy = fetch(tables_ref, table_ref, semaphores.at[6])
        pairs = PENCILS * PAIRS
        copies = [
            pltpu.make_async_copy(source.at[pl.ds(start, pairs)], target, semaphores.at[n])
            for n, (source, start, target) in enumerate(
                [(kept[n], pairs, below_weights[n]) for n in range(2)]
                + [(kept[n], 0, slab_weights[n]) for n in range(2)]
            )
        ]
    rows = list(range(CY)) if own else list(range(CY, 2 * CY - 1))
    energy = 0.0
    if not own:
        sign = lane_sign((NX, LANES))
        twist = Twist(cos_ref, sin_ref)
        for first in range(0, CY, 2):
            modes, swapped = [], []
            for y in range(first, first + 2):
                line = jnp.concatenate([block_at(in_ref, j, y) for j in range(PART_X)], axis=0)
                other = turned(line, sign)
                cos_y, sin_y = twist.at(y)
                modes.append(line * cos_y - other * sin_y)
                swapped.append(other * cos_y + line * sin_y)
            swapped = jnp.concatenate(swapped, axis=1)
            modes = jnp.concatenate(modes, axis=1)
            if first == 0:
                table_copy.wait()
                for copy in copies:
                    copy.start()
            cells = jnp.concatenate(
                inverse_line(table_ref, quarters_of(modes), quarters_of(swapped)), axis=0
            )
            lanes = slice(first * LANES, (first + 2) * LANES)
            grid_ref[:NX, lanes] = cells
            grid_ref[NX:, lanes] = cells[:WIDE]
        lane = lax.broadcasted_iota(jnp.int32, (SLABS, LANES), 1)
        energy = jnp.sum(jnp.where(lane == PART_Z, in_ref[rows_of(0), :], 0.0))
    gap = jnp.zeros((HALF - PADDED_Z, 3 * LANES), bf16)

    if not own:
        for copy in copies[:2]:
            copy.wait()

    def pair_body(pair, carry):
        pencil, lanes = pair_place(pair)
        waves = [
            jnp.concatenate(
                [waves_ref[pair, n, :PADDED_Z], gap, waves_ref[pair, n, PADDED_Z:], gap],
                axis=0,
            )
            for n in range(2)
        ]
        first_row, window, origin = pair_window(pair, own, where_ref)
        at = pl.ds(first_row, window)
        cells = jnp.concatenate(
            [grid_ref[at, n * LANES : (n + 1) * LANES] for n in range(len(rows))], axis=0
        )
        read = product(halves(cells), waves)
        rows_x, rows_y = [
            [
                [rows_ref[pair, row + t : row + t + 1, :] for t in range(6)]
                for row in range(dim * 18, dim * 18 + 18, 6)
            ]
            for dim in range(2)
        ]
        dense_x = dense_rows(rows_x, atoms_ref[pencil, 0:1, lanes] - origin, window)
        dense_y = dense_rows(rows_y, atoms_ref[pencil, 1:2, lanes], 16)
        lined = {}
        for order_y, order_z in ((0, 0), (1, 0), (2, 0), (0, 1), (1, 1), (0, 2)):
            lined[order_y, order_z] = sum(
                dense_y[order_y][r : r + 1]
                * read[n * window : (n + 1) * window, order_z * LANES : (order_z + 1) * LANES]
                for n, r in enumerate(rows)
            )

        def sampled(p, r, s):
            return jnp.sum(dense_x[p] * lined[r, s], axis=0, keepdims=True)

        charge, dip_x, dip_y, dip_z, live = [
            atoms_ref[pencil, a : a + 1, lanes] for a in range(6, 11)
        ]
        s100 = sampled(1, 0, 0)
        s010 = sampled(0, 1, 0)
        s001 = sampled(0, 0, 1)
        s110 = sampled(1, 1, 0)
        s101 = sampled(1, 0, 1)
        s011 = sampled(0, 1, 1)
        out = [
            live * sampled(0, 0, 0),
            live * s100,
            live * s010,
            live * s001,
            charge * s100 + dip_x * sampled(2, 0, 0) + dip_y * s110 + dip_z * s101,
            charge * s010 + dip_x * s110 + dip_y * sampled(0, 2, 0) + dip_z * s011,
            charge * s001 + dip_x * s101 + dip_y * s011 + dip_z * sampled(0, 0, 2),
            jnp.full(live.shape, energy, f32),
        ]
        ahead = lax.rem(pencil - where_ref[1] + PENCILS, PENCILS)
        out_ref[ahead, :, lanes] = jnp.concatenate(out, axis=0)
        return carry

    lax.fori_loop(0, PENCILS * PAIRS, pair_body, 0, unroll=12)
    if not own:
        for copy in copies[2:]:
            copy.wait()


def finish_kernel(
    own_ref, one_ref, two_ref, three_ref, charge_ref, dipole_ref, position_ref, energy_ref
):
    total = (own_ref[...] + one_ref[...]) + (two_ref[...] + three_ref[...])
    charge_ref[...] = total[0]
    dipole_ref[...] = total[1:4]
    position_ref[...] = total[4:7]
    energy_ref[...] = total[7:8, 0:1]


SPACES = {"v": pltpu.VMEM, "h": pltpu.HBM, "s": pltpu.SMEM}
WORK = {"flops": 1_000_000_000, "bytes_accessed": 8_000_000}


def out_place(shape):
    pinned = isinstance(shape, type(pltpu.HBM((8, LANES), f32)))
    return pl.BlockSpec(memory_space=pltpu.HBM if pinned else pltpu.VMEM)


def call(kernel, inputs, out_shape, scratch=(), aliases=()):
    def run(*operands):
        placed = [
            pltpu.with_memory_space_constraint(one, pltpu.HBM) if where == "h" else one
            for one, where in zip(operands, inputs)
        ]
        return pl.pallas_call(
            kernel,
            out_shape=out_shape,
            in_specs=[pl.BlockSpec(memory_space=SPACES[one]) for one in inputs],
            out_specs=jax.tree.map(out_place, out_shape),
            scratch_shapes=list(scratch),
            input_output_aliases=dict(aliases),
            compiler_params=pltpu.CompilerParams(vmem_limit_bytes=28 * 1024 * 1024),
            cost_estimate=pl.CostEstimate(transcendentals=0, **WORK),
        )(*placed)

    return run


def next_slab(value, back=False):
    step = -1 if back else 1
    return lax.ppermute(value, "gy", [(i, (i + step) % SLABS) for i in range(SLABS)])


def swap_slabs(lines):
    lines = lines.reshape(SLABS, CARRIERS, 1, LANES)
    lines = lax.all_to_all(lines, "gy", split_axis=0, concat_axis=0, tiled=True)
    return lines.reshape(SLABS * CARRIERS, LANES)


def on_device(cell_index, offsets, charges, dipoles, block_count, shear_cells):
    pencil_index = lax.axis_index("gx")
    slab_index = lax.axis_index("gy")
    x_forward, x_inverse, y_forward, y_inverse = wave_tables()
    shape = jax.ShapeDtypeStruct
    shift = jnp.where(slab_index == 0, shear_cells[0], 0)
    where = jnp.stack([slab_index, pencil_index, shift, shear_cells[0]])

    mine, base, taps, cos_t, sin_t = call(
        prepare_kernel,
        "sshhhhh",
        (
            shape((16, ATOM_DEV), f32),
            shape((8, LANES), f32),
            shape((6, PADDED_Z, LANES), f32),
            shape((NX, LANES), f32),
            shape((NX, LANES), f32),
        ),
        [
            pltpu.SMEM(block_count.shape, jnp.int32),
            pltpu.VMEM((3, ATOM_DEV), jnp.int32),
            pltpu.VMEM((3, ATOM_DEV), f32),
            pltpu.VMEM((1, ATOM_DEV), f32),
            pltpu.VMEM((3, ATOM_DEV), f32),
            pltpu.SemaphoreType.DMA((5,)),
        ],
    )(
        where,
        shear_cells,
        block_count,
        cell_index,
        offsets,
        charges,
        dipoles,
    )
    atoms = lax.all_gather(mine, "gx", axis=0, tiled=False)
    below_atoms = next_slab(atoms)

    packed = shape((SLABS * CARRIERS, LANES), f32)
    table_space = pltpu.VMEM((NX, 6 * QUARTER), bf16)
    pairs = 2 * PENCILS * PAIRS
    held = [
        ((2, 2 * PADDED_Z, 3 * LANES), bf16),
        ((36, LANES), f32),
    ]
    weights_space = pltpu.VMEM((PENCILS, 18, 8, ATOM_DEV), f32)
    grid_shape = shape((EXTENDED, 2 * CY * LANES), f32)
    slab_grid = call(
        lambda *refs: spread_kernel(True, *refs),
        "vsvv",
        grid_shape,
        [weights_space],
    )(atoms, where, base, taps)
    green_shape = shape((NY, PART_X * LANES), f32)
    table_shape = shape((NX, 6 * QUARTER), bf16)
    _, lines = call(
        lambda *refs: spread_kernel(False, *refs),
        "vsvvvhvv",
        (grid_shape, packed),
        [table_space, weights_space, pltpu.SemaphoreType.DMA],
        ((4, 0),),
    )(below_atoms, where, base, taps, slab_grid, x_forward, cos_t, sin_t)
    lines, where, atoms, below_atoms = lax.optimization_barrier(
        (lines, where, atoms, below_atoms)
    )
    *weights, green, table, back = call(
        weights_kernel,
        "svvvvhh",
        (
            *(pltpu.HBM((pairs, *dims), kind) for dims, kind in held),
            green_shape,
            table_shape,
            table_shape,
        ),
        [
            *(pltpu.VMEM((pairs, *dims), kind) for dims, kind in held),
            weights_space,
            pltpu.SemaphoreType.DMA((8,)),
        ],
    )(where, atoms, below_atoms, base, taps, y_forward, y_inverse)
    lines = swap_slabs(lines)
    filtered = call(filter_kernel, "vvvv", packed)(lines, table, back, green)
    filtered = swap_slabs(filtered)
    shares_shape = shape((PENCILS, 8, ATOM_DEV), f32)
    below_shares, potential, *weights = call(
        lambda *refs: sample_kernel(False, *refs),
        "vshhvvvh",
        (
            shares_shape,
            shape((EXTENDED, CY * LANES), f32),
            *(shape((pairs // 2, *dims), kind) for dims, kind in held),
        ),
        [
            *(pltpu.VMEM((pairs // 2, *dims), kind) for dims, kind in held),
            table_space,
            pltpu.SemaphoreType.DMA((7,)),
        ],
    )(below_atoms, where, *weights, filtered, cos_t, sin_t, x_inverse)
    below_shares = next_slab(below_shares, back=True)
    shares = call(lambda *refs: sample_kernel(True, *refs), "vsvvv", shares_shape)(
        atoms, where, *weights, potential
    )
    shares = shares + below_shares
    arrived = [
        lax.ppermute(shares[ahead], "gx", [(i, (i + ahead) % PENCILS) for i in range(PENCILS)])
        for ahead in range(1, PENCILS)
    ]
    charge_grad, dipole_grad, position_grad, energy = call(
        finish_kernel,
        "vvvv",
        (
            shape((ATOM_DEV,), f32),
            shape((3, ATOM_DEV), f32),
            shape((3, ATOM_DEV), f32),
            shape((1, 1), f32),
        ),
    )(shares[0], *arrived)
    return charge_grad, dipole_grad, position_grad, energy[0]


def solution(mesh):
    placed = (
        P(None, ("gy", "gx")),
        P(None, ("gy", "gx")),
        P(("gy", "gx")),
        P(None, ("gy", "gx")),
        P(("gy", "gx")),
        P(),
    )
    return jax.shard_map(
        on_device,
        mesh=mesh,
        in_specs=placed,
        out_specs=(P(("gy", "gx")), P(None, ("gy", "gx")), P(None, ("gy", "gx")), P()),
        check_vma=False,
    )
```
